32 devices in a mesh: blk: 8 (over z, y), head: 2 (over x), batch: 2 (over core).
Axes of the slice: x: 2, y: 2, z: 4, core: 2. Of those that a mesh axis runs over, the one named last changes fastest.
Arguments:
- query_rows: bfloat16 [4096, 3072], P(('batch', 'blk', 'head')), parts along dimension 0, may hold values from -16 to 16
- key_rows: bfloat16 [4096, 3072], P(('batch', 'blk', 'head')), parts along dimension 0, may hold values from -16 to 16
- value_rows: bfloat16 [4096, 3072], P(('batch', 'blk', 'head')), parts along dimension 0, may hold values from -6 to 6
- q_gain: float32 [3072], replicated, may hold values from 1 to 3
- k_gain: float32 [3072], replicated, may hold values from 1 to 3
- tile_mask: int32 [16, 16], replicated, may hold values from 0 to 1, as said below
Outputs:
- attended: bfloat16 [4096, 3072], P(('batch', 'blk', 'head')), parts along dimension 0
The draws below stay inside these ranges and needn't reach their ends.
There are 2 independent parts, one for each index of `batch`. The reference program is written for one: setup_inputs(seed, part) draws one part's arguments, and reference() takes and returns one part's arrays. A program takes and returns all parts, laid end to end along the dimension named above; an argument that names none is the same for every part. Nothing has to cross between parts.
Inputs may be any that keep to these rules, and one draw needn't show every extreme that they name: `tile_mask`: 1 where a block of 128 query positions may attend to a block of 128 key positions; the main diagonal and the two beside it are always 1.
All inputs are finite; a program needn't handle non-finite values.
Results may differ from the reference program's by a relative error of at most 0.012.
The reference program's roundings to bfloat16 on the way count: a program that leaves them out, or rounds other values in their place, can miss the bound.
Values may be sent and summed in bfloat16 or wider, within the bound.
No kernel may reach another device: no remote copies, remote signals or barrier semaphores. Data moves between devices by JAX's collectives and lax.ppermute only.
A program may use at most 128 MiB of HBM per device.

```python
import math
import jax
import jax.numpy as jnp
from jax import lax

HEADS = 24
HDIM = 128
TILE = 128
QTOK = 256
WIDTH = 3072
TOKENS = 2048
TILES = 16
N_BLK = 8


def paired_draw(key):
    base_key, other_key = jax.random.split(key, 2)
    shape = (TOKENS, HEADS * HDIM)
    query_out = jax.random.truncated_normal(other_key, -4.0, 4.0, shape, jnp.float32)
    key_out = jax.random.truncated_normal(base_key, -4.0, 4.0, shape, jnp.float32)
    return (query_out, key_out)


def draw_query_rows(key, part):
    return paired_draw(jax.random.fold_in(key, 7))[0].astype(jnp.bfloat16)


def draw_key_rows(key, part):
    return paired_draw(jax.random.fold_in(key, 7))[1].astype(jnp.bfloat16)


def draw_tile_mask(key, part):
    live_key, tile_key = jax.random.split(jax.random.fold_in(key, 11))
    indices = jnp.arange(TILES)
    distance = jnp.abs(indices[:, None] - indices[None, :])
    per_block = QTOK // TILE
    block_of = indices // per_block
    block_gap = jnp.abs(block_of[:, None] - block_of[None, :])
    gap_roll = jax.random.randint(live_key, (N_BLK,), 0, 1000)
    gap_values = jnp.arange(N_BLK)
    live_gap = (gap_values <= 1) | (gap_values == N_BLK // 2) | (gap_roll < 1800 // (gap_values + 1))
    live_pair = jnp.take(live_gap.astype(jnp.int32), block_gap) != 0
    rolled = jax.random.randint(tile_key, (TILES, TILES), 0, 1000)
    chosen = live_pair & (rolled < 500)
    return jnp.where((distance <= 1) | chosen, 1, 0).astype(jnp.int32)


def shard_levels(key, extent, cuts, smallest, top_value):
    def one(axis_at, shards_of):
        steps = jax.random.uniform(jax.random.fold_in(jax.random.fold_in(key, 6), axis_at), (shards_of,), jnp.float32, smallest / len(cuts), top_value / len(cuts))
        return jnp.repeat(jnp.exp(steps), extent[axis_at] // shards_of).reshape((-1,) + (1,) * (len(extent) - axis_at - 1))

    level = one(*cuts[0])
    for cut in cuts[1:]:
        level = level * one(*cut)
    return level


def gaussian(rng, shape, scale, bound, cuts=(), kind=jnp.bfloat16):
    drawn = jax.random.normal(rng, shape, jnp.float32) * scale
    if len(cuts) > 0:
        drawn = shard_levels(rng, shape, cuts, -0.22, 0.18) * drawn
    return jnp.clip(drawn, min=-bound, max=bound).astype(kind)


def setup_inputs(seed: int = 0, part: int = 0) -> dict:
    keys = jax.random.split(jax.random.key(seed), 7)
    part_splits = jax.random.split(jax.random.fold_in(keys[6], part), 7)
    return {
        "query_rows": draw_query_rows(jax.random.fold_in(jax.random.fold_in(keys[6], part), 71), part),
        "key_rows": draw_key_rows(jax.random.fold_in(jax.random.fold_in(keys[6], part), 71), part),
        "value_rows": gaussian(part_splits[2], (TOKENS, WIDTH), 1.0, 6.0, ((0, 16),)),
        "q_gain": jnp.clip(jnp.exp(jax.random.uniform(keys[3], (WIDTH,), jnp.float32, math.log(1.0), math.log(3.0))), 1.0, 3.0),
        "k_gain": jnp.clip(jnp.exp(jax.random.uniform(keys[4], (WIDTH,), jnp.float32, math.log(1.0), math.log(3.0))), 1.0, 3.0),
        "tile_mask": draw_tile_mask(jax.random.fold_in(keys[6], 71), part),
    }


def normalize(inputs, weights):
    widened = inputs.astype(jnp.float32)
    mean_square = lax.optimization_barrier(jnp.mean(widened * widened, axis=-1, keepdims=True))
    return (widened * lax.rsqrt(mean_square + 1e-06) * weights).astype(jnp.bfloat16)

def widen(inputs):
    return lax.optimization_barrier(inputs).astype(jnp.float32)

def reference(query_rows, key_rows, value_rows, q_gain, k_gain, tile_mask):
    queries = widen(normalize(query_rows, q_gain)).reshape(TOKENS, HEADS, HDIM)
    keys_all = widen(normalize(key_rows, k_gain)).reshape(TOKENS, HEADS, HDIM)
    values_all = value_rows.astype(jnp.float32).reshape(TOKENS, HEADS, HDIM)
    allowed_tiles = tile_mask != 0

    def one_block(block_index):
        first_row = (block_index * QTOK).astype(jnp.int32)
        block_queries = lax.dynamic_slice_in_dim(queries, first_row, QTOK, 0)
        mask_rows = lax.dynamic_slice_in_dim(allowed_tiles, (block_index * (QTOK // TILE)).astype(jnp.int32), QTOK // TILE, 0)
        allowed = jnp.repeat(jnp.repeat(mask_rows, TILE, axis=0), TILE, axis=1)
        scores = jnp.einsum('qhd,khd->hqk', block_queries, keys_all) * HDIM ** (-0.5)
        scores = jnp.where(allowed[None], scores, -1e+30)
        row_max = lax.optimization_barrier(jnp.max(scores, axis=-1, keepdims=True))
        weights = jnp.where(allowed[None], jnp.exp(scores - row_max), 0.0)
        totals = lax.optimization_barrier(jnp.sum(weights, axis=-1))
        rounded = widen(weights.astype(jnp.bfloat16))
        mixed = jnp.einsum('hqk,khd->qhd', rounded, values_all) / jnp.transpose(totals)[:, :, None]
        return mixed.astype(jnp.bfloat16)
    blocks_out = lax.map(one_block, jnp.arange(N_BLK, dtype=jnp.int32))
    return blocks_out.reshape(TOKENS, HEADS * HDIM)
```

```python
import functools

import jax
import jax.numpy as jnp
from jax import lax
from jax.experimental import pallas as pl
from jax.experimental.pallas import tpu as pltpu
from jax.sharding import Mesh, PartitionSpec as P

HEADS = 24
HDIM = 128
TILE = 128
EPS = 1e-06
MASKED = -1e30
VMEM_LIMIT = 48 * 1024 * 1024


def pack_kernel(shared, shared_heads, whole, whole_heads, q_ref, k_ref, v_ref, qg_ref, kg_ref, *outs):
    def normalize(ref, gain):
        widened = ref[...].astype(jnp.float32)
        mean_square = jnp.mean(widened * widened, axis=-1, keepdims=True)
        return (widened * lax.rsqrt(mean_square + EPS) * gain[...]).astype(jnp.bfloat16)

    outs = list(outs)
    shared_q, shared_kv = (outs.pop(0), outs.pop(0)) if shared_heads else (None, None)
    whole_qkv = outs.pop(0) if whole_heads else None
    first = shared * shared_heads * HDIM

    def place(block, shared_at, which):
        for d in range(shared if shared_heads else 0):
            width = shared_heads * HDIM
            shared_at(d)[...] = block[:, d * width : (d + 1) * width]
        for d in range(whole if whole_heads else 0):
            width = whole_heads * HDIM
            whole_qkv[d, which] = block[:, first + d * width : first + (d + 1) * width]

    place(normalize(q_ref, qg_ref), lambda d: shared_q.at[d], 0)
    place(normalize(k_ref, kg_ref), lambda d: shared_kv.at[d, 0], 1)
    place(v_ref[...], lambda d: shared_kv.at[d, 1], 2)


def attend_kernel(
    heads, key_blocks, key_token_block, query_token_block, read_q, read_kv, bm,
    place_ref, mask_ref, q_ref, kv_ref, out_ref, scores_ref,
):
    tiles = bm // TILE
    i, h = pl.program_id(0), pl.program_id(1)
    q_tile = query_token_block(i, place_ref) * tiles
    query = read_q(q_ref)
    scale = HDIM ** (-0.5)

    def score(c, running):
        key = read_kv(kv_ref, c, 0)
        k_tile = key_token_block(c) * tiles
        s = lax.dot_general(query, key, (((1,), (1,)), ((), ())), preferred_element_type=jnp.float32)
        rows = []
        for a in range(tiles):
            row = []
            for b in range(tiles):
                live = mask_ref[q_tile + a, k_tile + b] != 0
                bias = jnp.where(live, 0.0, MASKED).astype(jnp.float32)
                row.append(s[a * TILE : (a + 1) * TILE, b * TILE : (b + 1) * TILE] + bias)
            for b in range(tiles):
                scores_ref[c, a * TILE : (a + 1) * TILE, b * TILE : (b + 1) * TILE] = row[b]
            rows.append(functools.reduce(jnp.maximum, row))
        return jnp.maximum(running, jnp.concatenate(rows, axis=0))

    unroll = True if key_blocks <= 8 else 1
    largest = lax.fori_loop(0, key_blocks, score, jnp.full((bm, TILE), MASKED, jnp.float32), unroll=unroll)
    row_max = jnp.max(largest, axis=-1, keepdims=True)

    def mix(c, state):
        total, mixed = state
        weights = jnp.exp((scores_ref[c] - row_max) * scale)
        for b in range(tiles):
            total = total + weights[:, b * TILE : (b + 1) * TILE]
        value = read_kv(kv_ref, c, 1)
        mixed = mixed + jnp.dot(weights.astype(jnp.bfloat16), value, preferred_element_type=jnp.float32)
        return total, mixed

    zeros = jnp.zeros((bm, TILE), jnp.float32)
    total, mixed = lax.fori_loop(0, key_blocks, mix, (zeros, zeros), unroll=unroll)
    mixed = mixed / jnp.sum(total, axis=-1, keepdims=True)
    out_ref[...] = mixed.astype(out_ref.dtype).reshape(out_ref.shape)


def unpack_kernel(shared, shared_heads, whole, whole_heads, *refs):
    refs = list(refs)
    out_ref = refs.pop()
    first = 0
    for ref, count, heads in zip(refs, *zip(*[p for p in ((shared, shared_heads), (whole, whole_heads)) if p[1]])):
        width = heads * HDIM
        for d in range(count):
            out_ref[:, first + d * width : first + (d + 1) * width] = ref[d]
        first += count * width


def solution(mesh):
    n_blk, n_head = mesh.shape["blk"], mesh.shape["head"]
    clip = n_blk * n_head
    whole_heads = HEADS // clip
    left = HEADS - whole_heads * clip
    outer = max([d for d in range(1, n_blk + 1) if n_blk % d == 0 and left and left % (n_head * d) == 0] or [1])
    inner = n_blk // outer
    shared = outer * n_head
    shared_heads = left // shared
    named = Mesh(
        mesh.devices.reshape(outer, inner, n_head, mesh.shape["batch"]), ("outer", "inner", "head", "batch")
    )
    params = pltpu.CompilerParams(vmem_limit_bytes=VMEM_LIMIT)
    smem = pl.BlockSpec(memory_space=pltpu.SMEM)

    def per_device(query_rows, key_rows, value_rows, q_gain, k_gain, tile_mask):
        rows, features = query_rows.shape
        block = rows * n_head
        bf16 = jnp.bfloat16
        place = jnp.reshape(lax.axis_index("inner"), (1,)).astype(jnp.int32)

        packed_shapes = []
        if shared_heads:
            width = shared_heads * HDIM
            packed_shapes += [(shared, rows, width), (shared, 2, rows, width)]
        if whole_heads:
            packed_shapes += [(clip, 3, rows, whole_heads * HDIM)]
        packed = list(
            pl.pallas_call(
                functools.partial(pack_kernel, shared, shared_heads, clip, whole_heads),
                out_shape=[jax.ShapeDtypeStruct(s, bf16) for s in packed_shapes],
                compiler_params=params,
                name="pack",
            )(query_rows, key_rows, value_rows, q_gain.reshape(1, -1), k_gain.reshape(1, -1))
        )

        def exchange(x, axes):
            return lax.all_to_all(x, axes, split_axis=0, concat_axis=0, tiled=True)

        near, far = ("outer", "head"), ("outer", "inner", "head")
        if shared_heads:
            shared_kv = exchange(packed[1], near)
            shared_q = exchange(packed[0], near)
        if whole_heads:
            whole_qkv = exchange(packed[-1], far)

        returned = []
        if shared_heads:
            width = shared_heads * HDIM
            gathered = lax.all_gather(shared_kv, "inner").reshape(inner, outer, n_head, 2, rows, width)
            q5 = shared_q.reshape(outer, n_head, rows, width)
            mixed = pl.pallas_call(
                functools.partial(
                    attend_kernel,
                    shared_heads,
                    n_blk,
                    lambda c: lax.rem(c, outer) * inner + lax.div(c, outer),
                    lambda i, place_ref: i * inner + place_ref[0],
                    lambda ref: ref[0].reshape(block, HDIM),
                    lambda ref, c, which: ref[lax.div(c, outer), lax.rem(c, outer), :, which].reshape(block, HDIM),
                    block,
                ),
                grid=(outer, shared_heads),
                in_specs=[
                    smem,
                    smem,
                    pl.BlockSpec((1, n_head, rows, HDIM), lambda i, h: (i, 0, 0, h)),
                    pl.BlockSpec((inner, outer, n_head, 2, rows, HDIM), lambda i, h: (0, 0, 0, 0, 0, h)),
                ],
                out_specs=pl.BlockSpec((1, n_head, rows, HDIM), lambda i, h: (i, 0, 0, h)),
                out_shape=jax.ShapeDtypeStruct(q5.shape, bf16),
                scratch_shapes=[pltpu.VMEM((n_blk, block, block), jnp.float32)],
                compiler_params=params,
                cost_estimate=pl.CostEstimate(
                    flops=4 * outer * block * n_blk * block * width, bytes_accessed=q5.size * 8, transcendentals=0
                ),
                name="attend_shared",
            )(place, tile_mask, q5, gathered)
            returned.append(exchange(mixed.reshape(shared, rows, width), near))
        if whole_heads:
            width = whole_heads * HDIM
            qkv = whole_qkv.reshape(n_blk, n_head, 3, rows, width)
            mixed = pl.pallas_call(
                functools.partial(
                    attend_kernel,
                    whole_heads,
                    n_blk,
                    lambda c: c,
                    lambda i, place_ref: i,
                    lambda ref: ref[0, :, 0].reshape(block, HDIM),
                    lambda ref, c, which: ref[c, :, 1 + which].reshape(block, HDIM),
                    block,
                ),
                grid=(n_blk, whole_heads),
                in_specs=[
                    smem,
                    smem,
                    pl.BlockSpec((1, n_head, 1, rows, HDIM), lambda i, h: (i, 0, 0, 0, h)),
                    pl.BlockSpec((n_blk, n_head, 3, rows, HDIM), lambda i, h: (0, 0, 0, 0, h)),
                ],
                out_specs=pl.BlockSpec((1, n_head, rows, HDIM), lambda i, h: (i, 0, 0, h)),
                out_shape=jax.ShapeDtypeStruct((n_blk, n_head, rows, width), bf16),
                scratch_shapes=[pltpu.VMEM((n_blk, block, block), jnp.float32)],
                compiler_params=params,
                cost_estimate=pl.CostEstimate(
                    flops=4 * n_blk * block * n_blk * block * width, bytes_accessed=qkv.size * 2, transcendentals=0
                ),
                name="attend_whole",
            )(place, tile_mask, qkv, qkv)
            returned.append(exchange(mixed.reshape(clip, rows, width), far))

        return pl.pallas_call(
            functools.partial(unpack_kernel, shared, shared_heads, clip, whole_heads),
            out_shape=jax.ShapeDtypeStruct((rows, features), bf16),
            compiler_params=params,
            name="unpack",
        )(*returned)

    split = P(("batch", "outer", "inner", "head"), None)
    return jax.shard_map(
        per_device,
        mesh=named,
        in_specs=(split, split, split, P(), P(), P()),
        out_specs=split,
        check_vma=False,
    )
```

```python
import functools

import jax
import jax.numpy as jnp
from jax import lax
from jax.experimental import pallas as pl
from jax.experimental.pallas import tpu as pltpu
from jax.sharding import Mesh, PartitionSpec as P

HEADS = 24
HDIM = 128
TILE = 128
EPS = 1e-06
MASKED = -1e30
NEAR = ("outer", "head")
FAR = ("outer", "inner", "head")
PARAMS = pltpu.CompilerParams(vmem_limit_bytes=48 * 1024 * 1024)
BF16 = jnp.bfloat16


def partner(index, d, count, back=False):
    if count & (count - 1) == 0:
        return index ^ d
    return (index + (count - d if back else d)) % count


def swap(piece, axes, d, count, back=False):
    if d == 0:
        return piece
    pairs = [(i, partner(i, d, count, back)) for i in range(count)]
    return lax.ppermute(piece, axes, pairs)


def pack_kernel(near, near_heads, far, far_heads, q_hbm, k_hbm, v_hbm, qg_hbm, kg_hbm, *refs):
    outs, (q_in, k_in, v_in, qg, kg, by_head, sems) = list(refs[:-7]), refs[-7:]
    copies = [
        pltpu.make_async_copy(src, dst, sems.at[n])
        for n, (src, dst) in enumerate(
            ((q_hbm, q_in), (k_hbm, k_in), (v_hbm, v_in), (qg_hbm, qg), (kg_hbm, kg))
        )
    ]
    for copy in copies:
        copy.start()

    def keep(which, block):
        for h in range(HEADS):
            by_head[h, which] = block[:, h * HDIM : (h + 1) * HDIM]

    def normalize(ref, gain):
        widened = ref[...].astype(jnp.float32)
        mean_square = jnp.mean(widened * widened, axis=-1, keepdims=True)
        return (widened * lax.rsqrt(mean_square + EPS) * gain[...]).astype(BF16)

    copies[0].wait()
    copies[3].wait()
    keep(0, normalize(q_in, qg))
    copies[1].wait()
    copies[4].wait()
    keep(1, normalize(k_in, kg))
    copies[2].wait()
    keep(2, v_in[...])

    first = 0
    for axes, count, heads in ((NEAR, near, near_heads), (FAR, far, far_heads)):
        me = lax.axis_index(axes)
        for d in range(count if heads else 0):
            out = outs.pop(0)
            for h in range(heads):
                out[:, h] = by_head[first + partner(me, d, count) * heads + h]
        first += count * heads


def collect_kernel(near, rows, *refs):
    pieces, (q_out, kv_out) = refs[:near], refs[near:]
    me = lax.axis_index(NEAR)
    for d, piece in enumerate(pieces):
        at = pl.ds(pl.multiple_of(partner(me, d, near, True) * rows, rows), rows)
        q_out[:, at] = piece[0]
        kv_out[:, :, at] = piece[1:]


def attend(query, key_at, value_at, key_blocks, live_at, scores_ref):
    bm = query.shape[0]
    tiles = bm // TILE
    scale = HDIM ** (-0.5)

    def score(c, running):
        s = lax.dot_general(query, key_at(c), (((1,), (1,)), ((), ())), preferred_element_type=jnp.float32)
        largest = []
        for a in range(tiles):
            across = slice(a * TILE, (a + 1) * TILE)
            row = []
            for b in range(tiles):
                bias = jnp.where(live_at(c, a, b), 0.0, MASKED).astype(jnp.float32)
                row.append(s[across, b * TILE : (b + 1) * TILE] + bias)
                scores_ref[c, across, b * TILE : (b + 1) * TILE] = row[b]
            largest.append(functools.reduce(jnp.maximum, row))
        return jnp.maximum(running, jnp.concatenate(largest, axis=0))

    unroll = True if key_blocks <= 8 else 1
    largest = lax.fori_loop(0, key_blocks, score, jnp.full((bm, TILE), MASKED, jnp.float32), unroll=unroll)
    row_max = jnp.max(largest, axis=-1, keepdims=True)

    def mix(c, state):
        total, mixed = state
        weights = jnp.exp((scores_ref[c] - row_max) * scale)
        for b in range(tiles):
            total = total + weights[:, b * TILE : (b + 1) * TILE]
        mixed = mixed + jnp.dot(weights.astype(BF16), value_at(c), preferred_element_type=jnp.float32)
        return total, mixed

    zeros = jnp.zeros((bm, TILE), jnp.float32)
    total, mixed = lax.fori_loop(0, key_blocks, mix, (zeros, zeros), unroll=unroll)
    return (mixed / jnp.sum(total, axis=-1, keepdims=True)).astype(BF16)


def near_kernel(outer, inner, near, rows, mask_ref, q_ref, *refs):
    kv_refs, refs = refs[: len(refs) - near - 3], refs[len(refs) - near - 3 :]
    outs, (kv, mixed, scores_ref) = refs[:near], refs[near:]
    i, h = pl.program_id(0), pl.program_id(1)
    mine = lax.axis_index("inner")
    block = q_ref.shape[1]
    tiles = block // TILE

    @pl.when((i == 0) & (h == 0))
    def _():
        if len(kv_refs) == 1:
            kv[...] = kv_refs[0][...]
        else:
            for d, ref in enumerate(kv_refs):
                kv[mine ^ d] = ref[...]

    def at(c):
        return pl.ds(pl.multiple_of(lax.rem(c, outer) * block, block), block)

    mixed[h, pl.ds(pl.multiple_of(i * block, block), block)] = attend(
        q_ref[0],
        lambda c: kv[lax.div(c, outer), 0, h, at(c)],
        lambda c: kv[lax.div(c, outer), 1, h, at(c)],
        outer * inner,
        lambda c, a, b: mask_ref[
            (i * inner + mine) * tiles + a, (lax.rem(c, outer) * inner + lax.div(c, outer)) * tiles + b
        ]
        != 0,
        scores_ref,
    )

    @pl.when((i == pl.num_programs(0) - 1) & (h == pl.num_programs(1) - 1))
    def _():
        me = lax.axis_index(NEAR)
        for d, out in enumerate(outs):
            out[...] = mixed[:, pl.ds(pl.multiple_of(partner(me, d, near, True) * rows, rows), rows)]


def far_kernel(far, rows, block, mask_ref, *refs):
    pieces, outs, (qkv, mixed, scores_ref) = refs[:far], refs[far : 2 * far], refs[2 * far :]
    i, h = pl.program_id(0), pl.program_id(1)
    me = lax.axis_index(FAR)
    tiles = block // TILE

    def place(d):
        return pl.ds(pl.multiple_of(partner(me, d, far, True) * rows, rows), rows)

    @pl.when((i == 0) & (h == 0))
    def _():
        for d, piece in enumerate(pieces):
            qkv[:, :, place(d)] = piece[...]

    def at(c):
        return pl.ds(pl.multiple_of(c * block, block), block)

    mixed[h, at(i)] = attend(
        qkv[0, h, at(i)],
        lambda c: qkv[1, h, at(c)],
        lambda c: qkv[2, h, at(c)],
        far * rows // block,
        lambda c, a, b: mask_ref[i * tiles + a, c * tiles + b] != 0,
        scores_ref,
    )

    @pl.when((i == pl.num_programs(0) - 1) & (h == pl.num_programs(1) - 1))
    def _():
        for d, out in enumerate(outs):
            out[...] = mixed[:, place(d)]


def unpack_kernel(near, near_heads, far, far_heads, *refs):
    pieces, out_ref = list(refs[:-1]), refs[-1]
    first = 0
    for axes, count, heads in ((NEAR, near, near_heads), (FAR, far, far_heads)):
        me = lax.axis_index(axes)
        for d in range(count if heads else 0):
            piece = pieces.pop(0)
            for h in range(heads):
                at = (first + partner(me, d, count) * heads + h) * HDIM
                out_ref[:, pl.ds(pl.multiple_of(at, HDIM), HDIM)] = piece[h]
        first += count * heads


def solution(mesh):
    n_blk, n_head = mesh.shape["blk"], mesh.shape["head"]
    far = n_blk * n_head
    far_heads = HEADS // far
    left = HEADS - far_heads * far
    outer = max([d for d in range(1, n_blk + 1) if n_blk % d == 0 and left and left % (n_head * d) == 0] or [1])
    inner = n_blk // outer
    near = outer * n_head
    near_heads = left // near
    named = Mesh(
        mesh.devices.reshape(outer, inner, n_head, mesh.shape["batch"]), ("outer", "inner", "head", "batch")
    )
    smem = pl.BlockSpec(memory_space=pltpu.SMEM)

    def per_device(query_rows, key_rows, value_rows, q_gain, k_gain, tile_mask):
        rows, features = query_rows.shape
        block = rows * n_head

        def shape(*dims):
            return jax.ShapeDtypeStruct(dims, BF16)

        packed = pl.pallas_call(
            functools.partial(pack_kernel, near, near_heads, far, far_heads),
            in_specs=[pl.BlockSpec(memory_space=pltpu.HBM)] * 5,
            out_shape=[shape(3, near_heads, rows, HDIM)] * (near if near_heads else 0)
            + [shape(3, far_heads, rows, HDIM)] * (far if far_heads else 0),
            scratch_shapes=[pltpu.VMEM((rows, features), BF16)] * 3
            + [pltpu.VMEM((1, features), jnp.float32)] * 2
            + [pltpu.VMEM((HEADS, 3, rows, HDIM), BF16), pltpu.SemaphoreType.DMA((5,))],
            compiler_params=PARAMS,
            name="pack",
        )(query_rows, key_rows, value_rows, q_gain.reshape(1, -1), k_gain.reshape(1, -1))
        packed = list(packed)
        returned = []

        if near_heads:
            pieces = [swap(packed.pop(0), NEAR, d, near) for d in range(near)]
        if far_heads:
            far_pieces = [swap(packed.pop(0), FAR, d, far) for d in range(far)]

        if near_heads:
            q_near, kv_near = pl.pallas_call(
                functools.partial(collect_kernel, near, rows),
                out_shape=[shape(near_heads, near * rows, HDIM), shape(2, near_heads, near * rows, HDIM)],
                compiler_params=PARAMS,
                name="collect",
            )(*pieces)
            if inner == 2:
                kv_all = [kv_near, lax.ppermute(kv_near, "inner", [(0, 1), (1, 0)])]
            else:
                kv_all = [lax.all_gather(kv_near, "inner")]
            mixed = pl.pallas_call(
                functools.partial(near_kernel, outer, inner, near, rows),
                grid=(outer, near_heads),
                in_specs=[smem, pl.BlockSpec((1, block, HDIM), lambda i, h: (h, i, 0))]
                + [pl.BlockSpec(kv.shape, lambda i, h, n=kv.ndim: (0,) * n) for kv in kv_all],
                out_specs=[pl.BlockSpec((near_heads, rows, HDIM), lambda i, h: (0, 0, 0))] * near,
                out_shape=[shape(near_heads, rows, HDIM)] * near,
                scratch_shapes=[
                    pltpu.VMEM((inner, *kv_near.shape), BF16),
                    pltpu.VMEM((near_heads, near * rows, HDIM), BF16),
                    pltpu.VMEM((n_blk, block, block), jnp.float32),
                ],
                compiler_params=PARAMS,
                cost_estimate=pl.CostEstimate(
                    flops=4 * near_heads * near * rows * far * rows * HDIM, bytes_accessed=2**21, transcendentals=0
                ),
                name="attend_near",
            )(tile_mask, q_near, *kv_all)
            returned += [swap(mixed[d], NEAR, d, near, True) for d in range(near)]

        if far_heads:
            mixed = pl.pallas_call(
                functools.partial(far_kernel, far, rows, block),
                grid=(n_blk, far_heads),
                in_specs=[smem]
                + [pl.BlockSpec((3, far_heads, rows, HDIM), lambda i, h: (0, 0, 0, 0))] * far,
                out_specs=[pl.BlockSpec((far_heads, rows, HDIM), lambda i, h: (0, 0, 0))] * far,
                out_shape=[shape(far_heads, rows, HDIM)] * far,
                scratch_shapes=[
                    pltpu.VMEM((3, far_heads, far * rows, HDIM), BF16),
                    pltpu.VMEM((far_heads, far * rows, HDIM), BF16),
                    pltpu.VMEM((n_blk, block, block), jnp.float32),
                ],
                compiler_params=PARAMS,
                cost_estimate=pl.CostEstimate(
                    flops=4 * far_heads * (far * rows) ** 2 * HDIM, bytes_accessed=2**21, transcendentals=0
                ),
                name="attend_far",
            )(tile_mask, *far_pieces)
            returned += [swap(mixed[d], FAR, d, far, True) for d in range(far)]

        return pl.pallas_call(
            functools.partial(unpack_kernel, near, near_heads, far, far_heads),
            out_shape=shape(rows, features),
            compiler_params=PARAMS,
            name="unpack",
        )(*returned)

    split = P(("batch", "outer", "inner", "head"), None)
    return jax.shard_map(
        per_device,
        mesh=named,
        in_specs=(split, split, split, P(), P(), P()),
        out_specs=split,
        check_vma=False,
    )
```

```python
import functools

import jax
import jax.numpy as jnp
from jax import lax
from jax.experimental import pallas as pl
from jax.experimental.pallas import tpu as pltpu
from jax.sharding import Mesh, PartitionSpec as P

HEADS = 24
HDIM = 128
TILE = 128
EPS = 1e-06
MASKED = -1e30
NEAR = ("outer", "head")
FAR = ("outer", "inner", "head")
PARAMS = pltpu.CompilerParams(vmem_limit_bytes=48 * 1024 * 1024)
PACK_PARAMS = pltpu.CompilerParams(vmem_limit_bytes=61 * 1024 * 1024)
BF16 = jnp.bfloat16
SCALE = 1.4426950408889634 * HDIM ** (-0.5)


def shape(*dims):
    return jax.ShapeDtypeStruct(dims, BF16)


def exchange(x, axes):
    return lax.all_to_all(x, axes, split_axis=0, concat_axis=0, tiled=True)


def pack_kernel(write, q_hbm, k_hbm, v_hbm, qg_hbm, kg_hbm, *refs):
    outs, (q_in, k_in, v_in, qg, kg, sems) = refs[:-6], refs[-6:]
    copies = [
        pltpu.make_async_copy(src, dst, sems.at[n])
        for n, (src, dst) in enumerate(
            ((q_hbm, q_in), (k_hbm, k_in), (v_hbm, v_in), (qg_hbm, qg), (kg_hbm, kg))
        )
    ]
    for copy in copies:
        copy.start()

    def normalize(ref, gain):
        widened = ref[...].astype(jnp.float32)
        mean_square = jnp.mean(widened * widened, axis=-1, keepdims=True)
        return (widened * lax.rsqrt(mean_square + EPS) * gain[...]).astype(BF16)

    copies[0].wait()
    copies[3].wait()
    write(0, normalize(q_in, qg), *outs)
    copies[1].wait()
    copies[4].wait()
    write(1, normalize(k_in, kg), *outs)
    copies[2].wait()
    write(2, v_in[...], *outs)


def pack(write, out_shape, rows, features, arrays):
    q, k, v, q_gain, k_gain = arrays
    return pl.pallas_call(
        functools.partial(pack_kernel, write),
        in_specs=[pl.BlockSpec(memory_space=pltpu.HBM)] * 5,
        out_shape=out_shape,
        scratch_shapes=[pltpu.VMEM((rows, features), BF16)] * 3
        + [pltpu.VMEM((1, features), jnp.float32)] * 2
        + [pltpu.SemaphoreType.DMA((5,))],
        compiler_params=PACK_PARAMS,
        name="pack",
    )(q, k, v, q_gain.reshape(1, -1), k_gain.reshape(1, -1))


def attend(query, band, key_at, value_at, key_blocks, live_at, scores_ref):
    bm = query.shape[0]
    bands, tiles = bm // band, scores_ref.shape[2] // TILE

    def score(c, running):
        s = lax.dot_general(query, key_at(c), (((1,), (1,)), ((), ())), preferred_element_type=jnp.float32)
        largest = []
        for a in range(bands):
            across = slice(a * band, (a + 1) * band)
            row = []
            for b in range(tiles):
                bias = jnp.where(live_at(a, c * tiles + b), 0.0, MASKED).astype(jnp.float32)
                row.append(s[across, b * TILE : (b + 1) * TILE] + bias)
                scores_ref[c, across, b * TILE : (b + 1) * TILE] = row[b]
            largest.append(functools.reduce(jnp.maximum, row))
        return jnp.maximum(running, jnp.concatenate(largest, axis=0))

    unroll = True if key_blocks <= 8 else 1
    largest = lax.fori_loop(0, key_blocks, score, jnp.full((bm, TILE), MASKED, jnp.float32), unroll=unroll)
    row_max = jnp.max(largest, axis=-1, keepdims=True) * SCALE

    def mix(c, state):
        total, mixed = state
        weights = jnp.exp2(scores_ref[c] * SCALE - row_max)
        for b in range(tiles):
            total = total + weights[:, b * TILE : (b + 1) * TILE]
        mixed = mixed + jnp.dot(weights.astype(BF16), value_at(c), preferred_element_type=jnp.float32)
        return total, mixed

    zeros = jnp.zeros((bm, TILE), jnp.float32)
    total, mixed = lax.fori_loop(0, key_blocks, mix, (zeros, zeros), unroll=unroll)
    return (mixed / jnp.sum(total, axis=-1, keepdims=True)).astype(BF16)


def shared_kernel(sources, mask_ref, q_ref, own_ref, other_ref, out_ref, key, value, scores_ref):
    half = q_ref.shape[2]
    i = pl.program_id(0)

    @pl.when(i == 0)
    def _():
        mine = lax.axis_index("inner")
        here = pl.ds(pl.multiple_of(mine * half, half), half)
        there = pl.ds(pl.multiple_of((1 - mine) * half, half), half)
        key[:, here] = own_ref[:, 1]
        value[:, here] = own_ref[:, 2]
        key[:, there] = other_ref[:, 0]
        value[:, there] = other_ref[:, 1]

    bands = q_ref.shape[0]
    wide = scores_ref.shape[2]
    tiles = wide // TILE
    mixed = attend(
        q_ref[:, 0].reshape(bands * half, HDIM),
        half,
        lambda c: key[pl.ds(c * tiles, tiles)].reshape(wide, HDIM),
        lambda c: value[pl.ds(c * tiles, tiles)].reshape(wide, HDIM),
        sources // tiles,
        lambda a, t: mask_ref[i * bands + a, t] != 0,
        scores_ref,
    )
    out_ref[...] = mixed.reshape(out_ref.shape)


def whole_kernel(sources, mask_ref, q_ref, qkv_ref, shared_ref, out_ref, scores_ref):
    i = pl.program_id(0)
    bands, _, rows, _ = q_ref.shape
    wide = scores_ref.shape[2]
    tiles = wide // TILE
    mixed = attend(
        q_ref[:, 0].reshape(bands * rows, HDIM),
        TILE,
        lambda c: qkv_ref[pl.ds(c * tiles, tiles), 1].reshape(wide, HDIM),
        lambda c: qkv_ref[pl.ds(c * tiles, tiles), 2].reshape(wide, HDIM),
        sources // tiles,
        lambda a, t: mask_ref[i * bands + a, t] != 0,
        scores_ref,
    )
    out_ref[:, :rows] = mixed.reshape(bands, rows, HDIM)
    out_ref[:, rows:] = shared_ref[...]


def halved(n_head, far, near):
    def per_device(query_rows, key_rows, value_rows, q_gain, k_gain, tile_mask):
        rows, features = query_rows.shape
        half = rows // 2

        def near_of(d):
            return d // (2 * n_head) * n_head + d % n_head

        def half_of(d):
            return d // n_head % 2 * half

        def write(which, block, shared, whole):
            for d in range(far):
                at, head = half_of(d), near_of(d) * HDIM
                shared[d, which] = block[at : at + half, head : head + HDIM]
                head = (near + d) * HDIM
                whole[d, which] = block[:, head : head + HDIM]

        def read(got_ref, out_ref):
            for d in range(far):
                at, head = half_of(d), near_of(d) * HDIM
                out_ref[at : at + half, head : head + HDIM] = got_ref[d, rows:]
                head = (near + d) * HDIM
                out_ref[:, head : head + HDIM] = got_ref[d, :rows]

        shared, whole = pack(
            write,
            [shape(far, 3, half, HDIM), shape(far, 3, rows, HDIM)],
            rows,
            features,
            (query_rows, key_rows, value_rows, q_gain, k_gain),
        )
        shared = exchange(shared, FAR)
        other = lax.ppermute(shared[:, 1:], "inner", [(0, 1), (1, 0)])
        whole = exchange(whole, FAR)

        smem = pl.BlockSpec(memory_space=pltpu.SMEM)
        wide = 2 * TILE
        mixed = pl.pallas_call(
            functools.partial(shared_kernel, far),
            grid=(far // 4,),
            in_specs=[
                smem,
                pl.BlockSpec((4, 1, half, HDIM), lambda i: (i, 0, 0, 0)),
                pl.BlockSpec((far, 3, half, HDIM), lambda i: (0, 0, 0, 0)),
                pl.BlockSpec((far, 2, half, HDIM), lambda i: (0, 0, 0, 0)),
            ],
            out_specs=pl.BlockSpec((4, half, HDIM), lambda i: (i, 0, 0)),
            out_shape=shape(far, half, HDIM),
            scratch_shapes=[pltpu.VMEM((far, rows, HDIM), BF16)] * 2
            + [pltpu.VMEM((far // 2, 4 * half, wide), jnp.float32)],
            compiler_params=PARAMS,
            cost_estimate=pl.CostEstimate(
                flops=2 * (far * rows) ** 2 * HDIM, bytes_accessed=2**21, transcendentals=0
            ),
            name="attend_shared",
        )(tile_mask, shared, shared, other)
        mixed = pl.pallas_call(
            functools.partial(whole_kernel, far),
            grid=(far // 2,),
            in_specs=[
                smem,
                pl.BlockSpec((2, 1, rows, HDIM), lambda i: (i, 0, 0, 0)),
                pl.BlockSpec((far, 3, rows, HDIM), lambda i: (0, 0, 0, 0)),
                pl.BlockSpec((2, half, HDIM), lambda i: (i, 0, 0)),
            ],
            out_specs=pl.BlockSpec((2, rows + half, HDIM), lambda i: (i, 0, 0)),
            out_shape=shape(far, rows + half, HDIM),
            scratch_shapes=[pltpu.VMEM((far // 2, 2 * rows, wide), jnp.float32)],
            compiler_params=PARAMS,
            cost_estimate=pl.CostEstimate(
                flops=4 * (far * rows) ** 2 * HDIM, bytes_accessed=2**22, transcendentals=0
            ),
            name="attend_whole",
        )(tile_mask, whole, whole, mixed)
        return pl.pallas_call(
            read, out_shape=shape(rows, features), compiler_params=PARAMS, name="unpack"
        )(exchange(mixed, FAR))

    return per_device


def gathered_kernel(outer, inner, mask_ref, q_ref, kv_ref, out_ref, scores_ref):
    i = pl.program_id(0)
    block = out_ref.shape[0] * out_ref.shape[1] * out_ref.shape[2]
    tiles = block // TILE
    q_tile = (i * inner + lax.axis_index("inner")) * tiles
    mixed = attend(
        q_ref[0, :, 0].reshape(block, HDIM),
        TILE,
        lambda c: kv_ref[lax.rem(c, inner), lax.div(c, inner), :, 1].reshape(block, HDIM),
        lambda c: kv_ref[lax.rem(c, inner), lax.div(c, inner), :, 2].reshape(block, HDIM),
        outer * inner,
        lambda a, t: mask_ref[q_tile + a, t] != 0,
        scores_ref,
    )
    out_ref[...] = mixed.reshape(out_ref.shape)


def gathered(outer, inner, n_head, near):
    width = HEADS // near * HDIM

    def per_device(query_rows, key_rows, value_rows, q_gain, k_gain, tile_mask):
        rows, features = query_rows.shape
        block = rows * n_head

        def write(which, block, packed):
            for d in range(near):
                packed[d, which] = block[:, d * width : (d + 1) * width]

        def read(got_ref, out_ref):
            for d in range(near):
                out_ref[:, d * width : (d + 1) * width] = got_ref[d]

        (packed,) = pack(
            write,
            [shape(near, 3, rows, width)],
            rows,
            features,
            (query_rows, key_rows, value_rows, q_gain, k_gain),
        )
        own = exchange(packed, NEAR).reshape(outer, n_head, 3, rows, width)
        every = lax.all_gather(own, "inner")
        mixed = pl.pallas_call(
            functools.partial(gathered_kernel, outer, inner),
            grid=(outer, HEADS // near),
            in_specs=[
                pl.BlockSpec(memory_space=pltpu.SMEM),
                pl.BlockSpec((1, n_head, 1, rows, HDIM), lambda i, h: (i, 0, 0, 0, h)),
                pl.BlockSpec((inner, outer, n_head, 3, rows, HDIM), lambda i, h: (0, 0, 0, 0, 0, h)),
            ],
            out_specs=pl.BlockSpec((1, n_head, rows, HDIM), lambda i, h: (i, 0, 0, h)),
            out_shape=shape(outer, n_head, rows, width),
            scratch_shapes=[pltpu.VMEM((outer * inner, block, block), jnp.float32)],
            compiler_params=PARAMS,
            name="attend",
        )(tile_mask, own, every)
        return pl.pallas_call(
            read, out_shape=shape(rows, features), compiler_params=PARAMS, name="unpack"
        )(exchange(mixed.reshape(near, rows, width), NEAR))

    return per_device


def solution(mesh):
    n_blk, n_head = mesh.shape["blk"], mesh.shape["head"]
    outer = max(d for d in range(1, n_blk + 1) if n_blk % d == 0 and HEADS % (n_head * d) == 0)
    inner = n_blk // outer
    near, far = outer * n_head, n_blk * n_head

    def per_device(query_rows, *others):
        if inner == 2 and HEADS == near + far and far % 4 == 0 and query_rows.shape[0] == TILE:
            return halved(n_head, far, near)(query_rows, *others)
        return gathered(outer, inner, n_head, near)(query_rows, *others)

    split = P(("batch", "outer", "inner", "head"), None)
    return jax.shard_map(
        per_device,
        mesh=Mesh(
            mesh.devices.reshape(outer, inner, n_head, mesh.shape["batch"]), ("outer", "inner", "head", "batch")
        ),
        in_specs=(split, split, split, P(), P(), P()),
        out_specs=split,
        check_vma=False,
    )
```

```python
import functools

import jax
import jax.numpy as jnp
from jax import lax
from jax.experimental import pallas as pl
from jax.experimental.pallas import tpu as pltpu
from jax.sharding import Mesh, PartitionSpec as P

HEADS = 24
HDIM = 128
TILE = 128
EPS = 1e-06
MASKED = -1e30
NEAR = ("outer", "head")
FAR = ("outer", "inner", "head")
PARAMS = pltpu.CompilerParams(vmem_limit_bytes=48 * 1024 * 1024)
PACK_PARAMS = pltpu.CompilerParams(vmem_limit_bytes=61 * 1024 * 1024)
BF16 = jnp.bfloat16
SCALE = 1.4426950408889634 * HDIM ** (-0.5)


def shape(*dims):
    return jax.ShapeDtypeStruct(dims, BF16)


def exchange(x, axes):
    return lax.all_to_all(x, axes, split_axis=0, concat_axis=0, tiled=True)


def pack_kernel(write, n_out, q_hbm, k_hbm, v_hbm, qg_hbm, kg_hbm, *refs):
    outs, (q_in, k_in, v_in, qg, kg, sems, *kept) = refs[:n_out], refs[n_out:]
    outs = *kept, *outs
    copies = [
        pltpu.make_async_copy(src, dst, sems.at[n])
        for n, (src, dst) in enumerate(
            ((q_hbm, q_in), (k_hbm, k_in), (v_hbm, v_in), (qg_hbm, qg), (kg_hbm, kg))
        )
    ]
    for copy in copies:
        copy.start()

    def normalize(ref, gain):
        widened = ref[...].astype(jnp.float32)
        mean_square = jnp.mean(widened * widened, axis=-1, keepdims=True)
        return (widened * lax.rsqrt(mean_square + EPS) * gain[...]).astype(BF16)

    copies[0].wait()
    copies[3].wait()
    write(0, normalize(q_in, qg), *outs)
    copies[1].wait()
    copies[4].wait()
    write(1, normalize(k_in, kg), *outs)
    copies[2].wait()
    write(2, v_in[...], *outs)


def pack(write, out_shape, rows, features, arrays, kept=()):
    q, k, v, q_gain, k_gain = arrays
    return pl.pallas_call(
        functools.partial(pack_kernel, write, len(out_shape)),
        in_specs=[pl.BlockSpec(memory_space=pltpu.HBM)] * 5,
        out_shape=out_shape,
        scratch_shapes=[pltpu.VMEM((rows, features), BF16)] * 3
        + [pltpu.VMEM((1, features), jnp.float32)] * 2
        + [pltpu.SemaphoreType.DMA((5,)), *kept],
        compiler_params=PACK_PARAMS,
        name="pack",
    )(q, k, v, q_gain.reshape(1, -1), k_gain.reshape(1, -1))


def attend(query, band, key_at, value_at, key_blocks, live_at, scores_ref):
    bm = query.shape[0]
    bands, tiles = bm // band, scores_ref.shape[2] // TILE

    def score(c, running):
        s = lax.dot_general(query, key_at(c), (((1,), (1,)), ((), ())), preferred_element_type=jnp.float32)
        largest = []
        for a in range(bands):
            across = slice(a * band, (a + 1) * band)
            row = []
            for b in range(tiles):
                bias = jnp.where(live_at(a, c, b), 0.0, MASKED).astype(jnp.float32)
                row.append(s[across, b * TILE : (b + 1) * TILE] + bias)
                scores_ref[c, across, b * TILE : (b + 1) * TILE] = row[b]
            largest.append(functools.reduce(jnp.maximum, row))
        return jnp.maximum(running, jnp.concatenate(largest, axis=0))

    def over_keys(body, state):
        if key_blocks > 8:
            return lax.fori_loop(0, key_blocks, body, state)
        for c in range(key_blocks):
            state = body(c, state)
        return state

    largest = over_keys(score, jnp.full((bm, TILE), MASKED, jnp.float32))
    row_max = jnp.max(largest, axis=-1, keepdims=True) * SCALE

    def mix(c, state):
        total, mixed = state
        weights = jnp.exp2(scores_ref[c] * SCALE - row_max)
        for b in range(tiles):
            total = total + weights[:, b * TILE : (b + 1) * TILE]
        mixed = mixed + jnp.dot(weights.astype(BF16), value_at(c), preferred_element_type=jnp.float32)
        return total, mixed

    zeros = jnp.zeros((bm, TILE), jnp.float32)
    total, mixed = over_keys(mix, (zeros, zeros))
    return (mixed / jnp.sum(total, axis=-1, keepdims=True)).astype(BF16)


def collect_kernel(rows, *refs):
    pieces, (q_out, kv_out) = refs[:-2], refs[-2:]
    me = lax.axis_index(NEAR)
    for d, piece in enumerate(pieces):
        at = pl.ds(pl.multiple_of((me ^ d) * rows, rows), rows)
        q_out[at] = piece[0]
        kv_out[:, at] = piece[1:]


def shared_kernel(n_head, rows, mask_ref, q_ref, own_ref, other_ref, *refs):
    outs, (mixed, scores_ref) = refs[:-2], refs[-2:]
    mine = lax.axis_index("inner")
    wide = scores_ref.shape[2]
    blocks = q_ref.shape[0] // wide

    def at(c):
        return pl.ds(pl.multiple_of(lax.rem(c, blocks) * wide, wide), wide)

    def tile(block, inner, t):
        return (block * 2 + inner) * (wide // TILE) + t

    def kv_at(which, c):
        return own_ref[which, at(c)] if c < blocks else other_ref[which, at(c)]

    def one(i, _):
        mixed[at(i)] = attend(
            q_ref[at(i)],
            TILE,
            lambda c: kv_at(0, c),
            lambda c: kv_at(1, c),
            2 * blocks,
            lambda a, c, b: mask_ref[tile(i, mine, a), tile(c % blocks, mine if c < blocks else 1 - mine, b)] != 0,
            scores_ref,
        )
        return 0

    lax.fori_loop(0, blocks, one, 0)
    me = lax.axis_index(NEAR)
    for d, out in enumerate(outs):
        out[...] = mixed[pl.ds(pl.multiple_of((me ^ d) * rows, rows), rows)]


def whole_kernel(far, crossing, rows, near_of, mask_ref, *refs):
    pieces, shared, refs = refs[:far], refs[far : far + far // 4], refs[far + far // 4 :]
    outs, (qkv, mixed, scores_ref) = refs[:-3], refs[-3:]
    me = lax.axis_index(FAR)
    wide = scores_ref.shape[2]
    tiles = wide // TILE
    half = far // 2
    first = (me & half) ^ (half if crossing else 0)

    for d, piece in enumerate(pieces):
        qkv[:, pl.ds(pl.multiple_of((me ^ d) * rows, rows), rows)] = piece[...]

    def at(c):
        return pl.ds(c * wide if isinstance(c, int) else pl.multiple_of(c * wide, wide), wide)

    def one(i, _):
        block = lax.div(first, tiles) + i
        mixed[at(i)] = attend(
            qkv[0, at(block)],
            TILE,
            lambda c: qkv[1, at(c)],
            lambda c: qkv[2, at(c)],
            far // tiles,
            lambda a, c, b: mask_ref[block * tiles + a, c * tiles + b] != 0,
            scores_ref,
        )
        return 0

    lax.fori_loop(0, half // tiles, one, 0)
    shared = list(shared)
    for n, out in enumerate(outs):
        d = n + (half if crossing else 0)
        out[0] = mixed[pl.ds(pl.multiple_of(((me ^ d) & (half - 1)) * rows, rows), rows)]
        if near_of(d) is not None:
            out[1] = shared.pop(0)[...]


def swap(piece, axes, d, count):
    return lax.ppermute(piece, axes, [(i, i ^ d) for i in range(count)]) if d else piece


def halved(n_head, far, near):
    def near_of(d):
        return None if d // n_head % 2 else d // (2 * n_head) * n_head + d % n_head

    near_order = [*range(near // 2, near), *range(near // 2)]
    far_order = []
    for d in range(far // 2):
        far_order += [far // 2 + d, d]

    def per_device(query_rows, key_rows, value_rows, q_gain, k_gain, tile_mask):
        rows, features = query_rows.shape
        heads = shape(2, rows, HDIM), shape(1, rows, HDIM)

        def write(which, block, by_head, *outs):
            for h in range(HEADS):
                by_head[h, which] = block[:, h * HDIM : (h + 1) * HDIM]
            if which == 2:
                me_near, me_far = lax.axis_index(NEAR), lax.axis_index(FAR)
                for d in range(near):
                    outs[d][...] = by_head[me_near ^ d]
                for d in range(far):
                    outs[near + d][...] = by_head[near + (me_far ^ d)]

        def read(*refs):
            got, out_ref = refs[:-1], refs[-1]
            me_near, me_far = lax.axis_index(NEAR), lax.axis_index(FAR)

            def put(head, block):
                out_ref[:, pl.ds(pl.multiple_of(head * HDIM, HDIM), HDIM)] = block

            for d in range(far):
                put(near + (me_far ^ d), got[d][0])
                if near_of(d) is not None:
                    put(me_near ^ near_of(d), got[d][1])

        packed = pack(
            write,
            [shape(3, rows, HDIM)] * (near + far),
            rows,
            features,
            (query_rows, key_rows, value_rows, q_gain, k_gain),
            [pltpu.VMEM((HEADS, 3, rows, HDIM), BF16)],
        )
        near_got, far_got = [None] * near, [None] * far
        for d in near_order:
            near_got[d] = swap(packed[d], NEAR, d, near)
        for d in far_order:
            far_got[d] = swap(packed[near + d], FAR, d, far)

        q_near, kv_near = pl.pallas_call(
            functools.partial(collect_kernel, rows),
            out_shape=[shape(near * rows, HDIM), shape(2, near * rows, HDIM)],
            compiler_params=PARAMS,
            name="collect",
        )(*near_got)
        kv_other = lax.ppermute(kv_near, "inner", [(0, 1), (1, 0)])

        wide = 2 * TILE
        blocks = far * rows // wide
        smem, vmem = pl.BlockSpec(memory_space=pltpu.SMEM), pl.BlockSpec(memory_space=pltpu.VMEM)
        shared = pl.pallas_call(
            functools.partial(shared_kernel, n_head, rows),
            in_specs=[smem] + [vmem] * 3,
            out_shape=[shape(rows, HDIM)] * near,
            scratch_shapes=[
                pltpu.VMEM((near * rows, HDIM), BF16),
                pltpu.VMEM((blocks, wide, wide), jnp.float32),
            ],
            compiler_params=PARAMS,
            cost_estimate=pl.CostEstimate(
                flops=2 * (far * rows) ** 2 * HDIM, bytes_accessed=2**21, transcendentals=0
            ),
            name="attend_shared",
        )(tile_mask, q_near, kv_near, kv_other)

        mixed = [None] * far
        for crossing in (True, False):
            mine = range(far // 2, far) if crossing else range(far // 2)
            results = pl.pallas_call(
                functools.partial(whole_kernel, far, crossing, rows, near_of),
                in_specs=[smem] + [vmem] * (far + near // 2),
                out_shape=[heads[near_of(d) is None] for d in mine],
                scratch_shapes=[
                    pltpu.VMEM((3, far * rows, HDIM), BF16),
                    pltpu.VMEM((far // 2 * rows, HDIM), BF16),
                    pltpu.VMEM((blocks, wide, wide), jnp.float32),
                ],
                compiler_params=PARAMS,
                cost_estimate=pl.CostEstimate(
                    flops=2 * (far * rows) ** 2 * HDIM, bytes_accessed=2**22, transcendentals=0
                ),
                name="attend_crossing" if crossing else "attend_rest",
            )(tile_mask, *far_got, *[shared[near_of(d)] for d in mine if near_of(d) is not None])
            for d, result in zip(mine, results):
                mixed[d] = swap(result, FAR, d, far)
        return pl.pallas_call(
            read, out_shape=shape(rows, features), compiler_params=PARAMS, name="unpack"
        )(*mixed)

    return per_device


def gathered_kernel(outer, inner, mask_ref, q_ref, kv_ref, out_ref, scores_ref):
    i = pl.program_id(0)
    block = out_ref.shape[0] * out_ref.shape[1] * out_ref.shape[2]
    tiles = block // TILE
    q_tile = (i * inner + lax.axis_index("inner")) * tiles
    mixed = attend(
        q_ref[0, :, 0].reshape(block, HDIM),
        TILE,
        lambda c: kv_ref[lax.rem(c, inner), lax.div(c, inner), :, 1].reshape(block, HDIM),
        lambda c: kv_ref[lax.rem(c, inner), lax.div(c, inner), :, 2].reshape(block, HDIM),
        outer * inner,
        lambda a, c, b: mask_ref[q_tile + a, c * tiles + b] != 0,
        scores_ref,
    )
    out_ref[...] = mixed.reshape(out_ref.shape)


def gathered(outer, inner, n_head, near):
    width = HEADS // near * HDIM

    def per_device(query_rows, key_rows, value_rows, q_gain, k_gain, tile_mask):
        rows, features = query_rows.shape
        block = rows * n_head

        def write(which, block, packed):
            for d in range(near):
                packed[d, which] = block[:, d * width : (d + 1) * width]

        def read(got_ref, out_ref):
            for d in range(near):
                out_ref[:, d * width : (d + 1) * width] = got_ref[d]

        (packed,) = pack(
            write,
            [shape(near, 3, rows, width)],
            rows,
            features,
            (query_rows, key_rows, value_rows, q_gain, k_gain),
        )
        own = exchange(packed, NEAR).reshape(outer, n_head, 3, rows, width)
        every = lax.all_gather(own, "inner")
        mixed = pl.pallas_call(
            functools.partial(gathered_kernel, outer, inner),
            grid=(outer, HEADS // near),
            in_specs=[
                pl.BlockSpec(memory_space=pltpu.SMEM),
                pl.BlockSpec((1, n_head, 1, rows, HDIM), lambda i, h: (i, 0, 0, 0, h)),
                pl.BlockSpec((inner, outer, n_head, 3, rows, HDIM), lambda i, h: (0, 0, 0, 0, 0, h)),
            ],
            out_specs=pl.BlockSpec((1, n_head, rows, HDIM), lambda i, h: (i, 0, 0, h)),
            out_shape=shape(outer, n_head, rows, width),
            scratch_shapes=[pltpu.VMEM((outer * inner, block, block), jnp.float32)],
            compiler_params=PARAMS,
            name="attend",
        )(tile_mask, own, every)
        return pl.pallas_call(
            read, out_shape=shape(rows, features), compiler_params=PARAMS, name="unpack"
        )(exchange(mixed.reshape(near, rows, width), NEAR))

    return per_device


def solution(mesh):
    n_blk, n_head = mesh.shape["blk"], mesh.shape["head"]
    outer = max(d for d in range(1, n_blk + 1) if n_blk % d == 0 and HEADS % (n_head * d) == 0)
    inner = n_blk // outer
    near, far = outer * n_head, n_blk * n_head

    def per_device(query_rows, *others):
        in_pairs = inner == 2 and n_head == 2 and far & (far - 1) == 0
        if in_pairs and HEADS == near + far and query_rows.shape[0] == TILE:
            return halved(n_head, far, near)(query_rows, *others)
        return gathered(outer, inner, n_head, near)(query_rows, *others)

    split = P(("batch", "outer", "inner", "head"), None)
    return jax.shard_map(
        per_device,
        mesh=Mesh(
            mesh.devices.reshape(outer, inner, n_head, mesh.shape["batch"]), ("outer", "inner", "head", "batch")
        ),
        in_specs=(split, split, split, P(), P(), P()),
        out_specs=split,
        check_vma=False,
    )
```

```python
import functools

import jax
import jax.numpy as jnp
from jax import lax
from jax.experimental import pallas as pl
from jax.experimental.pallas import tpu as pltpu
from jax.sharding import Mesh, PartitionSpec as P

HEADS = 24
HDIM = 128
TILE = 128
EPS = 1e-06
MASKED = -1e30
NEAR = ("outer", "head")
FAR = ("outer", "inner", "head")
PARAMS = pltpu.CompilerParams(vmem_limit_bytes=48 * 1024 * 1024)
PACK_PARAMS = pltpu.CompilerParams(vmem_limit_bytes=61 * 1024 * 1024)
BF16 = jnp.bfloat16
SCALE = 1.4426950408889634 * HDIM ** (-0.5)


def shape(*dims):
    return jax.ShapeDtypeStruct(dims, BF16)


def exchange(x, axes):
    return lax.all_to_all(x, axes, split_axis=0, concat_axis=0, tiled=True)


def pack_kernel(write, n_out, q_hbm, k_hbm, v_hbm, qg_hbm, kg_hbm, *refs):
    outs, (q_in, k_in, v_in, qg, kg, sems, *kept) = refs[:n_out], refs[n_out:]
    outs = *kept, *outs
    copies = [
        pltpu.make_async_copy(src, dst, sems.at[n])
        for n, (src, dst) in enumerate(
            ((q_hbm, q_in), (k_hbm, k_in), (v_hbm, v_in), (qg_hbm, qg), (kg_hbm, kg))
        )
    ]
    for copy in copies:
        copy.start()

    def normalize(ref, gain):
        widened = ref[...].astype(jnp.float32)
        mean_square = jnp.mean(widened * widened, axis=-1, keepdims=True)
        return (widened * lax.rsqrt(mean_square + EPS) * gain[...]).astype(BF16)

    copies[0].wait()
    copies[3].wait()
    write(0, normalize(q_in, qg), *outs)
    copies[1].wait()
    copies[4].wait()
    write(1, normalize(k_in, kg), *outs)
    copies[2].wait()
    write(2, v_in[...], *outs)


def pack(write, out_shape, rows, features, arrays, kept=()):
    q, k, v, q_gain, k_gain = arrays
    return pl.pallas_call(
        functools.partial(pack_kernel, write, len(out_shape)),
        in_specs=[pl.BlockSpec(memory_space=pltpu.HBM)] * 5,
        out_shape=out_shape,
        scratch_shapes=[pltpu.VMEM((rows, features), BF16)] * 3
        + [pltpu.VMEM((1, features), jnp.float32)] * 2
        + [pltpu.SemaphoreType.DMA((5,)), *kept],
        compiler_params=PACK_PARAMS,
        name="pack",
    )(q, k, v, q_gain.reshape(1, -1), k_gain.reshape(1, -1))


def attend(query, band, key_at, value_at, key_blocks, live_at, scores_ref):
    bm = query.shape[0]
    bands, tiles = bm // band, scores_ref.shape[2] // TILE

    def score(c, running):
        s = lax.dot_general(query, key_at(c), (((1,), (1,)), ((), ())), preferred_element_type=jnp.float32)
        largest = []
        for a in range(bands):
            across = slice(a * band, (a + 1) * band)
            row = []
            for b in range(tiles):
                bias = jnp.where(live_at(a, c, b), 0.0, MASKED).astype(jnp.float32)
                row.append(s[across, b * TILE : (b + 1) * TILE] + bias)
                scores_ref[c, across, b * TILE : (b + 1) * TILE] = row[b]
            largest.append(functools.reduce(jnp.maximum, row))
        return jnp.maximum(running, jnp.concatenate(largest, axis=0))

    def over_keys(body, state):
        if key_blocks > 8:
            return lax.fori_loop(0, key_blocks, body, state)
        for c in range(key_blocks):
            state = body(c, state)
        return state

    largest = over_keys(score, jnp.full((bm, TILE), MASKED, jnp.float32))
    row_max = jnp.max(largest, axis=-1, keepdims=True) * SCALE

    def mix(c, state):
        total, mixed = state
        weights = jnp.exp2(scores_ref[c] * SCALE - row_max)
        for b in range(tiles):
            total = total + weights[:, b * TILE : (b + 1) * TILE]
        mixed = mixed + jnp.dot(weights.astype(BF16), value_at(c), preferred_element_type=jnp.float32)
        return total, mixed

    zeros = jnp.zeros((bm, TILE), jnp.float32)
    total, mixed = over_keys(mix, (zeros, zeros))
    return (mixed / jnp.sum(total, axis=-1, keepdims=True)).astype(BF16)


def collect_kernel(order, rows, *refs):
    pieces, (q_out, kv_out) = refs[:-2], refs[-2:]
    me = lax.axis_index(NEAR)
    for d, piece in zip(order, pieces):
        at = pl.ds(pl.multiple_of((me ^ d) * rows, rows), rows)
        q_out[at] = piece[0]
        kv_out[:, at] = piece[1:]


def shared_kernel(order, rows, mask_ref, q_ref, own_ref, other_ref, *refs):
    outs, (mixed, scores_ref) = refs[:-2], refs[-2:]
    mine = lax.axis_index("inner")
    wide = scores_ref.shape[2]
    blocks = q_ref.shape[0] // wide

    def at(c):
        return pl.ds(pl.multiple_of(lax.rem(c, blocks) * wide, wide), wide)

    def tile(block, inner, t):
        return (block * 2 + inner) * (wide // TILE) + t

    def kv_at(which, c):
        return own_ref[which, at(c)] if c < blocks else other_ref[which, at(c)]

    def one(i, _):
        mixed[at(i)] = attend(
            q_ref[at(i)],
            TILE,
            lambda c: kv_at(0, c),
            lambda c: kv_at(1, c),
            2 * blocks,
            lambda a, c, b: mask_ref[tile(i, mine, a), tile(c % blocks, mine if c < blocks else 1 - mine, b)] != 0,
            scores_ref,
        )
        return 0

    lax.fori_loop(0, blocks, one, 0)
    me = lax.axis_index(NEAR)
    for d, out in zip(order, outs):
        out[...] = mixed[pl.ds(pl.multiple_of((me ^ d) * rows, rows), rows)]


def whole_kernel(sources, mask_ref, q_ref, qkv_ref, out_ref, scores_ref):
    i = pl.program_id(0)
    bands, _, rows, _ = q_ref.shape
    wide = scores_ref.shape[2]
    tiles = wide // TILE
    mixed = attend(
        q_ref[:, 0].reshape(bands * rows, HDIM),
        TILE,
        lambda c: qkv_ref[pl.ds(c * tiles, tiles), 1].reshape(wide, HDIM),
        lambda c: qkv_ref[pl.ds(c * tiles, tiles), 2].reshape(wide, HDIM),
        sources // tiles,
        lambda a, c, b: mask_ref[i * bands + a, c * tiles + b] != 0,
        scores_ref,
    )
    out_ref[...] = mixed.reshape(bands, rows, HDIM)


def swap(piece, axes, d, count):
    return lax.ppermute(piece, axes, [(i, i ^ d) for i in range(count)]) if d else piece


def halved(far, near):
    order = [*range(near // 2, near), *range(near // 2)]

    def per_device(query_rows, key_rows, value_rows, q_gain, k_gain, tile_mask):
        rows, features = query_rows.shape

        def write(which, block, by_head, *outs):
            for h in range(near):
                by_head[h, which] = block[:, h * HDIM : (h + 1) * HDIM]
            for d in range(far):
                outs[-1][d, which] = block[:, (near + d) * HDIM : (near + d + 1) * HDIM]
            if which == 2:
                me = lax.axis_index(NEAR)
                for d, out in zip(order, outs):
                    out[...] = by_head[me ^ d]

        def read(*refs):
            shared, (whole, out_ref) = refs[:-2], refs[-2:]
            me = lax.axis_index(NEAR)
            for d, got in zip(order, shared):
                out_ref[:, pl.ds(pl.multiple_of((me ^ d) * HDIM, HDIM), HDIM)] = got[...]
            for d in range(far):
                out_ref[:, (near + d) * HDIM : (near + d + 1) * HDIM] = whole[d]

        *shared, whole = pack(
            write,
            [shape(3, rows, HDIM)] * near + [shape(far, 3, rows, HDIM)],
            rows,
            features,
            (query_rows, key_rows, value_rows, q_gain, k_gain),
            [pltpu.VMEM((near, 3, rows, HDIM), BF16)],
        )
        shared = [swap(piece, NEAR, d, near) for d, piece in zip(order, shared)]
        whole = exchange(whole, FAR)
        q_near, kv_near = pl.pallas_call(
            functools.partial(collect_kernel, order, rows),
            out_shape=[shape(near * rows, HDIM), shape(2, near * rows, HDIM)],
            compiler_params=PARAMS,
            name="collect",
        )(*shared)
        kv_other = lax.ppermute(kv_near, "inner", [(0, 1), (1, 0)])

        wide = 2 * TILE
        blocks = far * rows // wide
        smem, vmem = pl.BlockSpec(memory_space=pltpu.SMEM), pl.BlockSpec(memory_space=pltpu.VMEM)
        shared = pl.pallas_call(
            functools.partial(shared_kernel, order, rows),
            in_specs=[smem] + [vmem] * 3,
            out_shape=[shape(rows, HDIM)] * near,
            scratch_shapes=[
                pltpu.VMEM((near * rows, HDIM), BF16),
                pltpu.VMEM((blocks, wide, wide), jnp.float32),
            ],
            compiler_params=PARAMS,
            cost_estimate=pl.CostEstimate(
                flops=2 * (far * rows) ** 2 * HDIM, bytes_accessed=2**21, transcendentals=0
            ),
            name="attend_shared",
        )(tile_mask, q_near, kv_near, kv_other)
        shared = [swap(piece, NEAR, d, near) for d, piece in zip(order, shared)]

        whole = pl.pallas_call(
            functools.partial(whole_kernel, far),
            grid=(far // 2,),
            in_specs=[
                smem,
                pl.BlockSpec((2, 1, rows, HDIM), lambda i: (i, 0, 0, 0)),
                pl.BlockSpec((far, 3, rows, HDIM), lambda i: (0, 0, 0, 0)),
            ],
            out_specs=pl.BlockSpec((2, rows, HDIM), lambda i: (i, 0, 0)),
            out_shape=shape(far, rows, HDIM),
            scratch_shapes=[pltpu.VMEM((blocks, wide, wide), jnp.float32)],
            compiler_params=PARAMS,
            cost_estimate=pl.CostEstimate(
                flops=4 * (far * rows) ** 2 * HDIM, bytes_accessed=2**22, transcendentals=0
            ),
            name="attend_whole",
        )(tile_mask, whole, whole)
        return pl.pallas_call(
            read, out_shape=shape(rows, features), compiler_params=PARAMS, name="unpack"
        )(*shared, exchange(whole, FAR))

    return per_device


def gathered_kernel(outer, inner, mask_ref, q_ref, kv_ref, out_ref, scores_ref):
    i = pl.program_id(0)
    block = out_ref.shape[0] * out_ref.shape[1] * out_ref.shape[2]
    tiles = block // TILE
    q_tile = (i * inner + lax.axis_index("inner")) * tiles
    mixed = attend(
        q_ref[0, :, 0].reshape(block, HDIM),
        TILE,
        lambda c: kv_ref[lax.rem(c, inner), lax.div(c, inner), :, 1].reshape(block, HDIM),
        lambda c: kv_ref[lax.rem(c, inner), lax.div(c, inner), :, 2].reshape(block, HDIM),
        outer * inner,
        lambda a, c, b: mask_ref[q_tile + a, c * tiles + b] != 0,
        scores_ref,
    )
    out_ref[...] = mixed.reshape(out_ref.shape)


def gathered(outer, inner, n_head, near):
    width = HEADS // near * HDIM

    def per_device(query_rows, key_rows, value_rows, q_gain, k_gain, tile_mask):
        rows, features = query_rows.shape
        block = rows * n_head

        def write(which, block, packed):
            for d in range(near):
                packed[d, which] = block[:, d * width : (d + 1) * width]

        def read(got_ref, out_ref):
            for d in range(near):
                out_ref[:, d * width : (d + 1) * width] = got_ref[d]

        (packed,) = pack(
            write,
            [shape(near, 3, rows, width)],
            rows,
            features,
            (query_rows, key_rows, value_rows, q_gain, k_gain),
        )
        own = exchange(packed, NEAR).reshape(outer, n_head, 3, rows, width)
        every = lax.all_gather(own, "inner")
        mixed = pl.pallas_call(
            functools.partial(gathered_kernel, outer, inner),
            grid=(outer, HEADS // near),
            in_specs=[
                pl.BlockSpec(memory_space=pltpu.SMEM),
                pl.BlockSpec((1, n_head, 1, rows, HDIM), lambda i, h: (i, 0, 0, 0, h)),
                pl.BlockSpec((inner, outer, n_head, 3, rows, HDIM), lambda i, h: (0, 0, 0, 0, 0, h)),
            ],
            out_specs=pl.BlockSpec((1, n_head, rows, HDIM), lambda i, h: (i, 0, 0, h)),
            out_shape=shape(outer, n_head, rows, width),
            scratch_shapes=[pltpu.VMEM((outer * inner, block, block), jnp.float32)],
            compiler_params=PARAMS,
            name="attend",
        )(tile_mask, own, every)
        return pl.pallas_call(
            read, out_shape=shape(rows, features), compiler_params=PARAMS, name="unpack"
        )(exchange(mixed.reshape(near, rows, width), NEAR))

    return per_device


def solution(mesh):
    n_blk, n_head = mesh.shape["blk"], mesh.shape["head"]
    outer = max(d for d in range(1, n_blk + 1) if n_blk % d == 0 and HEADS % (n_head * d) == 0)
    inner = n_blk // outer
    near, far = outer * n_head, n_blk * n_head

    def per_device(query_rows, *others):
        in_pairs = inner == 2 and n_head == 2 and far & (far - 1) == 0
        if in_pairs and HEADS == near + far and query_rows.shape[0] == TILE:
            return halved(far, near)(query_rows, *others)
        return gathered(outer, inner, n_head, near)(query_rows, *others)

    split = P(("batch", "outer", "inner", "head"), None)
    return jax.shard_map(
        per_device,
        mesh=Mesh(
            mesh.devices.reshape(outer, inner, n_head, mesh.shape["batch"]), ("outer", "inner", "head", "batch")
        ),
        in_specs=(split, split, split, P(), P(), P()),
        out_specs=split,
        check_vma=False,
    )
```

```python
import functools

import jax
import jax.numpy as jnp
from jax import lax
from jax.experimental import pallas as pl
from jax.experimental.pallas import tpu as pltpu
from jax.sharding import Mesh, PartitionSpec as P

HEADS = 24
HDIM = 128
TILE = 128
EPS = 1e-06
MASKED = -1e30
NEAR = ("outer", "head")
FAR = ("outer", "inner", "head")
PARAMS = pltpu.CompilerParams(vmem_limit_bytes=48 * 1024 * 1024)
PACK_PARAMS = pltpu.CompilerParams(vmem_limit_bytes=61 * 1024 * 1024)
BF16 = jnp.bfloat16
SCALE = 1.4426950408889634 * HDIM ** (-0.5)


def shape(*dims):
    return jax.ShapeDtypeStruct(dims, BF16)


def exchange(x, axes):
    return lax.all_to_all(x, axes, split_axis=0, concat_axis=0, tiled=True)


def pack_kernel(write, n_out, q_hbm, k_hbm, v_hbm, qg_hbm, kg_hbm, *refs):
    outs, (q_in, k_in, v_in, qg, kg, sems, *kept) = refs[:n_out], refs[n_out:]
    outs = *kept, *outs
    copies = [
        pltpu.make_async_copy(src, dst, sems.at[n])
        for n, (src, dst) in enumerate(
            ((q_hbm, q_in), (k_hbm, k_in), (v_hbm, v_in), (qg_hbm, qg), (kg_hbm, kg))
        )
    ]
    for copy in copies:
        copy.start()

    def normalize(ref, gain):
        widened = ref[...].astype(jnp.float32)
        mean_square = jnp.mean(widened * widened, axis=-1, keepdims=True)
        return (widened * lax.rsqrt(mean_square + EPS) * gain[...]).astype(BF16)

    copies[0].wait()
    copies[3].wait()
    write(0, normalize(q_in, qg), *outs)
    copies[1].wait()
    copies[4].wait()
    write(1, normalize(k_in, kg), *outs)
    copies[2].wait()
    write(2, v_in[...], *outs)


def pack(write, out_shape, rows, features, arrays, kept=()):
    q, k, v, q_gain, k_gain = arrays
    return pl.pallas_call(
        functools.partial(pack_kernel, write, len(out_shape)),
        in_specs=[pl.BlockSpec(memory_space=pltpu.HBM)] * 5,
        out_shape=out_shape,
        scratch_shapes=[pltpu.VMEM((rows, features), BF16)] * 3
        + [pltpu.VMEM((1, features), jnp.float32)] * 2
        + [pltpu.SemaphoreType.DMA((5,)), *kept],
        compiler_params=PACK_PARAMS,
        name="pack",
    )(q, k, v, q_gain.reshape(1, -1), k_gain.reshape(1, -1))


def attend(query, band, key_at, value_at, key_blocks, live_at, scores_ref):
    bm = query.shape[0]
    bands, tiles = bm // band, scores_ref.shape[2] // TILE

    def score(c, running):
        s = lax.dot_general(query, key_at(c), (((1,), (1,)), ((), ())), preferred_element_type=jnp.float32)
        largest = []
        for a in range(bands):
            across = slice(a * band, (a + 1) * band)
            row = []
            for b in range(tiles):
                bias = jnp.where(live_at(a, c, b), 0.0, MASKED).astype(jnp.float32)
                row.append(s[across, b * TILE : (b + 1) * TILE] + bias)
                scores_ref[c, across, b * TILE : (b + 1) * TILE] = row[b]
            largest.append(functools.reduce(jnp.maximum, row))
        return jnp.maximum(running, jnp.concatenate(largest, axis=0))

    def over_keys(body, state):
        if key_blocks > 8:
            return lax.fori_loop(0, key_blocks, body, state)
        for c in range(key_blocks):
            state = body(c, state)
        return state

    largest = over_keys(score, jnp.full((bm, TILE), MASKED, jnp.float32))
    row_max = jnp.max(largest, axis=-1, keepdims=True) * SCALE

    def mix(c, state):
        total, mixed = state
        weights = jnp.exp2(scores_ref[c] * SCALE - row_max)
        for b in range(tiles):
            total = total + weights[:, b * TILE : (b + 1) * TILE]
        mixed = mixed + jnp.dot(weights.astype(BF16), value_at(c), preferred_element_type=jnp.float32)
        return total, mixed

    zeros = jnp.zeros((bm, TILE), jnp.float32)
    total, mixed = over_keys(mix, (zeros, zeros))
    return (mixed / jnp.sum(total, axis=-1, keepdims=True)).astype(BF16)


def collect_kernel(order, rows, *refs):
    pieces, (q_out, kv_out) = refs[:-2], refs[-2:]
    me = lax.axis_index(NEAR)
    for d, piece in zip(order, pieces):
        at = pl.ds(pl.multiple_of((me ^ d) * rows, rows), rows)
        q_out[at] = piece[0]
        kv_out[:, at] = piece[1:]


def shared_kernel(order, rows, mask_ref, q_ref, own_ref, other_ref, *refs):
    outs, (mixed, scores_ref) = refs[:-2], refs[-2:]
    mine = lax.axis_index("inner")
    wide = scores_ref.shape[2]
    blocks = q_ref.shape[0] // wide

    def at(c):
        return pl.ds(pl.multiple_of(lax.rem(c, blocks) * wide, wide), wide)

    def tile(block, inner, t):
        return (block * 2 + inner) * (wide // TILE) + t

    def kv_at(which, c):
        return own_ref[which, at(c)] if c < blocks else other_ref[which, at(c)]

    def one(i, _):
        mixed[at(i)] = attend(
            q_ref[at(i)],
            TILE,
            lambda c: kv_at(0, c),
            lambda c: kv_at(1, c),
            2 * blocks,
            lambda a, c, b: mask_ref[tile(i, mine, a), tile(c % blocks, mine if c < blocks else 1 - mine, b)] != 0,
            scores_ref,
        )
        return 0

    lax.fori_loop(0, blocks, one, 0)
    me = lax.axis_index(NEAR)
    for d, out in zip(order, outs):
        out[...] = mixed[pl.ds(pl.multiple_of((me ^ d) * rows, rows), rows)]


def whole_kernel(sources, mask_ref, q_ref, qkv_ref, after_ref, out_ref, scores_ref):
    i = pl.program_id(0)
    bands, _, rows, _ = q_ref.shape
    wide = scores_ref.shape[2]
    tiles = wide // TILE
    mixed = attend(
        q_ref[:, 0].reshape(bands * rows, HDIM),
        TILE,
        lambda c: qkv_ref[pl.ds(c * tiles, tiles), 1].reshape(wide, HDIM),
        lambda c: qkv_ref[pl.ds(c * tiles, tiles), 2].reshape(wide, HDIM),
        sources // tiles,
        lambda a, c, b: mask_ref[i * bands + a, c * tiles + b] != 0,
        scores_ref,
    )
    out_ref[...] = mixed.reshape(bands, rows, HDIM)


def swap(piece, axes, d, count):
    return lax.ppermute(piece, axes, [(i, i ^ d) for i in range(count)]) if d else piece


def halved(far, near):
    order = [*range(near // 2, near), *range(near // 2)]

    def per_device(query_rows, key_rows, value_rows, q_gain, k_gain, tile_mask):
        rows, features = query_rows.shape

        def write(which, block, by_head, *outs):
            for h in range(near):
                by_head[h, which] = block[:, h * HDIM : (h + 1) * HDIM]
            for d in range(far):
                outs[-1][d, which] = block[:, (near + d) * HDIM : (near + d + 1) * HDIM]
            if which == 2:
                me = lax.axis_index(NEAR)
                for d, out in zip(order, outs):
                    out[...] = by_head[me ^ d]

        def read(*refs):
            shared, (whole, out_ref) = refs[:-2], refs[-2:]
            me = lax.axis_index(NEAR)
            for d, got in zip(order, shared):
                out_ref[:, pl.ds(pl.multiple_of((me ^ d) * HDIM, HDIM), HDIM)] = got[...]
            for d in range(far):
                out_ref[:, (near + d) * HDIM : (near + d + 1) * HDIM] = whole[d]

        *shared, whole = pack(
            write,
            [shape(3, rows, HDIM)] * near + [shape(far, 3, rows, HDIM)],
            rows,
            features,
            (query_rows, key_rows, value_rows, q_gain, k_gain),
            [pltpu.VMEM((near, 3, rows, HDIM), BF16)],
        )
        shared = [swap(piece, NEAR, d, near) for d, piece in zip(order, shared)]
        whole = exchange(whole, FAR)
        q_near, kv_near = pl.pallas_call(
            functools.partial(collect_kernel, order, rows),
            out_shape=[shape(near * rows, HDIM), shape(2, near * rows, HDIM)],
            compiler_params=PARAMS,
            name="collect",
        )(*shared)
        kv_other = lax.ppermute(kv_near, "inner", [(0, 1), (1, 0)])

        wide = 2 * TILE
        blocks = far * rows // wide
        smem, vmem = pl.BlockSpec(memory_space=pltpu.SMEM), pl.BlockSpec(memory_space=pltpu.VMEM)
        shared = pl.pallas_call(
            functools.partial(shared_kernel, order, rows),
            in_specs=[smem] + [vmem] * 3,
            out_shape=[shape(rows, HDIM)] * near,
            scratch_shapes=[
                pltpu.VMEM((near * rows, HDIM), BF16),
                pltpu.VMEM((blocks, wide, wide), jnp.float32),
            ],
            compiler_params=PARAMS,
            cost_estimate=pl.CostEstimate(
                flops=2 * (far * rows) ** 2 * HDIM, bytes_accessed=2**21, transcendentals=0
            ),
            name="attend_shared",
        )(tile_mask, q_near, kv_near, kv_other)
        after = shared[0]
        shared = [swap(piece, NEAR, d, near) for d, piece in zip(order, shared)]

        whole = pl.pallas_call(
            functools.partial(whole_kernel, far),
            grid=(far // 2,),
            in_specs=[
                smem,
                pl.BlockSpec((2, 1, rows, HDIM), lambda i: (i, 0, 0, 0)),
                pl.BlockSpec((far, 3, rows, HDIM), lambda i: (0, 0, 0, 0)),
                pl.BlockSpec((16, HDIM), lambda i: (0, 0)),
            ],
            out_specs=pl.BlockSpec((2, rows, HDIM), lambda i: (i, 0, 0)),
            out_shape=shape(far, rows, HDIM),
            scratch_shapes=[pltpu.VMEM((blocks, wide, wide), jnp.float32)],
            compiler_params=PARAMS,
            cost_estimate=pl.CostEstimate(
                flops=4 * (far * rows) ** 2 * HDIM, bytes_accessed=2**22, transcendentals=0
            ),
            name="attend_whole",
        )(tile_mask, whole, whole, after)
        return pl.pallas_call(
            read, out_shape=shape(rows, features), compiler_params=PARAMS, name="unpack"
        )(*shared, exchange(whole, FAR))

    return per_device


def gathered_kernel(outer, inner, mask_ref, q_ref, kv_ref, out_ref, scores_ref):
    i = pl.program_id(0)
    block = out_ref.shape[0] * out_ref.shape[1] * out_ref.shape[2]
    tiles = block // TILE
    q_tile = (i * inner + lax.axis_index("inner")) * tiles
    mixed = attend(
        q_ref[0, :, 0].reshape(block, HDIM),
        TILE,
        lambda c: kv_ref[lax.rem(c, inner), lax.div(c, inner), :, 1].reshape(block, HDIM),
        lambda c: kv_ref[lax.rem(c, inner), lax.div(c, inner), :, 2].reshape(block, HDIM),
        outer * inner,
        lambda a, c, b: mask_ref[q_tile + a, c * tiles + b] != 0,
        scores_ref,
    )
    out_ref[...] = mixed.reshape(out_ref.shape)


def gathered(outer, inner, n_head, near):
    width = HEADS // near * HDIM

    def per_device(query_rows, key_rows, value_rows, q_gain, k_gain, tile_mask):
        rows, features = query_rows.shape
        block = rows * n_head

        def write(which, block, packed):
            for d in range(near):
                packed[d, which] = block[:, d * width : (d + 1) * width]

        def read(got_ref, out_ref):
            for d in range(near):
                out_ref[:, d * width : (d + 1) * width] = got_ref[d]

        (packed,) = pack(
            write,
            [shape(near, 3, rows, width)],
            rows,
            features,
            (query_rows, key_rows, value_rows, q_gain, k_gain),
        )
        own = exchange(packed, NEAR).reshape(outer, n_head, 3, rows, width)
        every = lax.all_gather(own, "inner")
        mixed = pl.pallas_call(
            functools.partial(gathered_kernel, outer, inner),
            grid=(outer, HEADS // near),
            in_specs=[
                pl.BlockSpec(memory_space=pltpu.SMEM),
                pl.BlockSpec((1, n_head, 1, rows, HDIM), lambda i, h: (i, 0, 0, 0, h)),
                pl.BlockSpec((inner, outer, n_head, 3, rows, HDIM), lambda i, h: (0, 0, 0, 0, 0, h)),
            ],
            out_specs=pl.BlockSpec((1, n_head, rows, HDIM), lambda i, h: (i, 0, 0, h)),
            out_shape=shape(outer, n_head, rows, width),
            scratch_shapes=[pltpu.VMEM((outer * inner, block, block), jnp.float32)],
            compiler_params=PARAMS,
            name="attend",
        )(tile_mask, own, every)
        return pl.pallas_call(
            read, out_shape=shape(rows, features), compiler_params=PARAMS, name="unpack"
        )(exchange(mixed.reshape(near, rows, width), NEAR))

    return per_device


def solution(mesh):
    n_blk, n_head = mesh.shape["blk"], mesh.shape["head"]
    outer = max(d for d in range(1, n_blk + 1) if n_blk % d == 0 and HEADS % (n_head * d) == 0)
    inner = n_blk // outer
    near, far = outer * n_head, n_blk * n_head

    def per_device(query_rows, *others):
        in_pairs = inner == 2 and n_head == 2 and far & (far - 1) == 0
        if in_pairs and HEADS == near + far and query_rows.shape[0] == TILE:
            return halved(far, near)(query_rows, *others)
        return gathered(outer, inner, n_head, near)(query_rows, *others)

    split = P(("batch", "outer", "inner", "head"), None)
    return jax.shard_map(
        per_device,
        mesh=Mesh(
            mesh.devices.reshape(outer, inner, n_head, mesh.shape["batch"]), ("outer", "inner", "head", "batch")
        ),
        in_specs=(split, split, split, P(), P(), P()),
        out_specs=split,
        check_vma=False,
    )
```

```python
import functools

import jax
import jax.numpy as jnp
from jax import lax
from jax.experimental import pallas as pl
from jax.experimental.pallas import tpu as pltpu
from jax.sharding import Mesh, PartitionSpec as P

HEADS = 24
HDIM = 128
TILE = 128
EPS = 1e-06
MASKED = -1e30
NEAR = ("outer", "head")
FAR = ("inner", "head", "outer")
PARAMS = pltpu.CompilerParams(vmem_limit_bytes=48 * 1024 * 1024)
PACK_PARAMS = pltpu.CompilerParams(vmem_limit_bytes=61 * 1024 * 1024)
BF16 = jnp.bfloat16
SCALE = 1.4426950408889634 * HDIM ** (-0.5)


def shape(*dims):
    return jax.ShapeDtypeStruct(dims, BF16)


def exchange(x, axes):
    return lax.all_to_all(x, axes, split_axis=0, concat_axis=0, tiled=True)


def pack_kernel(write, q_hbm, k_hbm, v_hbm, qg_hbm, kg_hbm, *refs):
    outs, (q_in, k_in, v_in, qg, kg, sems) = refs[:-6], refs[-6:]
    copies = [
        pltpu.make_async_copy(src, dst, sems.at[n])
        for n, (src, dst) in enumerate(
            ((q_hbm, q_in), (k_hbm, k_in), (v_hbm, v_in), (qg_hbm, qg), (kg_hbm, kg))
        )
    ]
    for copy in copies:
        copy.start()

    def normalize(ref, gain):
        widened = ref[...].astype(jnp.float32)
        mean_square = jnp.mean(widened * widened, axis=-1, keepdims=True)
        return (widened * lax.rsqrt(mean_square + EPS) * gain[...]).astype(BF16)

    copies[0].wait()
    copies[3].wait()
    write(0, normalize(q_in, qg), *outs)
    copies[1].wait()
    copies[4].wait()
    write(1, normalize(k_in, kg), *outs)
    copies[2].wait()
    write(2, v_in[...], *outs)


def pack(write, out_shape, rows, features, arrays):
    q, k, v, q_gain, k_gain = arrays
    return pl.pallas_call(
        functools.partial(pack_kernel, write),
        in_specs=[pl.BlockSpec(memory_space=pltpu.HBM)] * 5,
        out_shape=out_shape,
        scratch_shapes=[pltpu.VMEM((rows, features), BF16)] * 3
        + [pltpu.VMEM((1, features), jnp.float32)] * 2
        + [pltpu.SemaphoreType.DMA((5,))],
        compiler_params=PACK_PARAMS,
        name="pack",
    )(q, k, v, q_gain.reshape(1, -1), k_gain.reshape(1, -1))


def attend(query, band, key_at, value_at, key_blocks, live_at, scores_ref):
    bm = query.shape[0]
    bands, tiles = bm // band, scores_ref.shape[2] // TILE

    def score(c, running):
        s = lax.dot_general(query, key_at(c), (((1,), (1,)), ((), ())), preferred_element_type=jnp.float32)
        largest = []
        for a in range(bands):
            across = slice(a * band, (a + 1) * band)
            row = []
            for b in range(tiles):
                bias = jnp.where(live_at(a, c * tiles + b), 0.0, MASKED).astype(jnp.float32)
                row.append(s[across, b * TILE : (b + 1) * TILE] + bias)
                scores_ref[c, across, b * TILE : (b + 1) * TILE] = row[b]
            largest.append(functools.reduce(jnp.maximum, row))
        return jnp.maximum(running, jnp.concatenate(largest, axis=0))

    unroll = True if key_blocks <= 8 else 1
    largest = lax.fori_loop(0, key_blocks, score, jnp.full((bm, TILE), MASKED, jnp.float32), unroll=unroll)
    row_max = jnp.max(largest, axis=-1, keepdims=True) * SCALE

    def mix(c, state):
        total, mixed = state
        weights = jnp.exp2(scores_ref[c] * SCALE - row_max)
        for b in range(tiles):
            total = total + weights[:, b * TILE : (b + 1) * TILE]
        mixed = mixed + jnp.dot(weights.astype(BF16), value_at(c), preferred_element_type=jnp.float32)
        return total, mixed

    zeros = jnp.zeros((bm, TILE), jnp.float32)
    total, mixed = lax.fori_loop(0, key_blocks, mix, (zeros, zeros), unroll=unroll)
    return (mixed / jnp.sum(total, axis=-1, keepdims=True)).astype(BF16)


def shared_kernel(sources, tile_of, mask_ref, q_ref, own_ref, other_ref, out_ref, key, value, scores_ref):
    half = q_ref.shape[2]
    i = pl.program_id(0)

    @pl.when(i == 0)
    def _():
        mine = lax.axis_index("inner")
        here = pl.ds(pl.multiple_of(mine * half, half), half)
        there = pl.ds(pl.multiple_of((1 - mine) * half, half), half)
        key[:, here] = own_ref[:, 1]
        value[:, here] = own_ref[:, 2]
        key[:, there] = other_ref[:, 0]
        value[:, there] = other_ref[:, 1]

    bands = q_ref.shape[0]
    wide = scores_ref.shape[2]
    tiles = wide // TILE
    mixed = attend(
        q_ref[:, 0].reshape(bands * half, HDIM),
        half,
        lambda c: key[pl.ds(c * tiles, tiles)].reshape(wide, HDIM),
        lambda c: value[pl.ds(c * tiles, tiles)].reshape(wide, HDIM),
        sources // tiles,
        lambda a, t: mask_ref[tile_of(i * bands + a), tile_of(t)] != 0,
        scores_ref,
    )
    out_ref[...] = mixed.reshape(out_ref.shape)


def whole_kernel(sources, tile_of, mask_ref, q_ref, qkv_ref, shared_ref, out_ref, scores_ref):
    i = pl.program_id(0)
    bands, _, rows, _ = q_ref.shape
    wide = scores_ref.shape[2]
    tiles = wide // TILE
    mixed = attend(
        q_ref[:, 0].reshape(bands * rows, HDIM),
        TILE,
        lambda c: qkv_ref[pl.ds(c * tiles, tiles), 1].reshape(wide, HDIM),
        lambda c: qkv_ref[pl.ds(c * tiles, tiles), 2].reshape(wide, HDIM),
        sources // tiles,
        lambda a, t: mask_ref[tile_of(i * bands + a), tile_of(t)] != 0,
        scores_ref,
    )
    out_ref[:, :rows] = mixed.reshape(bands, rows, HDIM)
    out_ref[:, rows:] = shared_ref[...]


def halved(n_head, far, near):
    def per_device(query_rows, key_rows, value_rows, q_gain, k_gain, tile_mask):
        rows, features = query_rows.shape
        half = rows // 2

        outer = near // n_head

        def near_of(d):
            return d % outer * n_head + d // outer % n_head

        def half_of(d):
            return d // near * half

        def tile_of(d):
            return (d % outer * 2 + d // near) * n_head + d // outer % n_head

        def write(which, block, shared, whole):
            for d in range(far):
                at, head = half_of(d), near_of(d) * HDIM
                shared[d, which] = block[at : at + half, head : head + HDIM]
                head = (near + d) * HDIM
                whole[d, which] = block[:, head : head + HDIM]

        def read(got_ref, out_ref):
            for d in range(far):
                at, head = half_of(d), near_of(d) * HDIM
                out_ref[at : at + half, head : head + HDIM] = got_ref[d, rows:]
                head = (near + d) * HDIM
                out_ref[:, head : head + HDIM] = got_ref[d, :rows]

        shared, whole = pack(
            write,
            [shape(far, 3, half, HDIM), shape(far, 3, rows, HDIM)],
            rows,
            features,
            (query_rows, key_rows, value_rows, q_gain, k_gain),
        )
        shared = exchange(shared, FAR)
        other = lax.ppermute(shared[:, 1:], "inner", [(0, 1), (1, 0)])
        whole = exchange(whole, FAR)

        smem = pl.BlockSpec(memory_space=pltpu.SMEM)
        wide = 2 * TILE
        mixed = pl.pallas_call(
            functools.partial(shared_kernel, far, tile_of),
            grid=(far // 4,),
            in_specs=[
                smem,
                pl.BlockSpec((4, 1, half, HDIM), lambda i: (i, 0, 0, 0)),
                pl.BlockSpec((far, 3, half, HDIM), lambda i: (0, 0, 0, 0)),
                pl.BlockSpec((far, 2, half, HDIM), lambda i: (0, 0, 0, 0)),
            ],
            out_specs=pl.BlockSpec((4, half, HDIM), lambda i: (i, 0, 0)),
            out_shape=shape(far, half, HDIM),
            scratch_shapes=[pltpu.VMEM((far, rows, HDIM), BF16)] * 2
            + [pltpu.VMEM((far // 2, 4 * half, wide), jnp.float32)],
            compiler_params=PARAMS,
            cost_estimate=pl.CostEstimate(
                flops=2 * (far * rows) ** 2 * HDIM, bytes_accessed=2**21, transcendentals=0
            ),
            name="attend_shared",
        )(tile_mask, shared, shared, other)
        mixed = pl.pallas_call(
            functools.partial(whole_kernel, far, tile_of),
            grid=(far // 2,),
            in_specs=[
                smem,
                pl.BlockSpec((2, 1, rows, HDIM), lambda i: (i, 0, 0, 0)),
                pl.BlockSpec((far, 3, rows, HDIM), lambda i: (0, 0, 0, 0)),
                pl.BlockSpec((2, half, HDIM), lambda i: (i, 0, 0)),
            ],
            out_specs=pl.BlockSpec((2, rows + half, HDIM), lambda i: (i, 0, 0)),
            out_shape=shape(far, rows + half, HDIM),
            scratch_shapes=[pltpu.VMEM((far // 2, 2 * rows, wide), jnp.float32)],
            compiler_params=PARAMS,
            cost_estimate=pl.CostEstimate(
                flops=4 * (far * rows) ** 2 * HDIM, bytes_accessed=2**22, transcendentals=0
            ),
            name="attend_whole",
        )(tile_mask, whole, whole, mixed)
        return pl.pallas_call(
            read, out_shape=shape(rows, features), compiler_params=PARAMS, name="unpack"
        )(exchange(mixed, FAR))

    return per_device


def gathered_kernel(outer, inner, mask_ref, q_ref, kv_ref, out_ref, scores_ref):
    i = pl.program_id(0)
    block = out_ref.shape[0] * out_ref.shape[1] * out_ref.shape[2]
    tiles = block // TILE
    q_tile = (i * inner + lax.axis_index("inner")) * tiles
    mixed = attend(
        q_ref[0, :, 0].reshape(block, HDIM),
        TILE,
        lambda c: kv_ref[lax.rem(c, inner), lax.div(c, inner), :, 1].reshape(block, HDIM),
        lambda c: kv_ref[lax.rem(c, inner), lax.div(c, inner), :, 2].reshape(block, HDIM),
        outer * inner,
        lambda a, t: mask_ref[q_tile + a, t] != 0,
        scores_ref,
    )
    out_ref[...] = mixed.reshape(out_ref.shape)


def gathered(outer, inner, n_head, near):
    width = HEADS // near * HDIM

    def per_device(query_rows, key_rows, value_rows, q_gain, k_gain, tile_mask):
        rows, features = query_rows.shape
        block = rows * n_head

        def write(which, block, packed):
            for d in range(near):
                packed[d, which] = block[:, d * width : (d + 1) * width]

        def read(got_ref, out_ref):
            for d in range(near):
                out_ref[:, d * width : (d + 1) * width] = got_ref[d]

        (packed,) = pack(
            write,
            [shape(near, 3, rows, width)],
            rows,
            features,
            (query_rows, key_rows, value_rows, q_gain, k_gain),
        )
        own = exchange(packed, NEAR).reshape(outer, n_head, 3, rows, width)
        every = lax.all_gather(own, "inner")
        mixed = pl.pallas_call(
            functools.partial(gathered_kernel, outer, inner),
            grid=(outer, HEADS // near),
            in_specs=[
                pl.BlockSpec(memory_space=pltpu.SMEM),
                pl.BlockSpec((1, n_head, 1, rows, HDIM), lambda i, h: (i, 0, 0, 0, h)),
                pl.BlockSpec((inner, outer, n_head, 3, rows, HDIM), lambda i, h: (0, 0, 0, 0, 0, h)),
            ],
            out_specs=pl.BlockSpec((1, n_head, rows, HDIM), lambda i, h: (i, 0, 0, h)),
            out_shape=shape(outer, n_head, rows, width),
            scratch_shapes=[pltpu.VMEM((outer * inner, block, block), jnp.float32)],
            compiler_params=PARAMS,
            name="attend",
        )(tile_mask, own, every)
        return pl.pallas_call(
            read, out_shape=shape(rows, features), compiler_params=PARAMS, name="unpack"
        )(exchange(mixed.reshape(near, rows, width), NEAR))

    return per_device


def solution(mesh):
    n_blk, n_head = mesh.shape["blk"], mesh.shape["head"]
    outer = max(d for d in range(1, n_blk + 1) if n_blk % d == 0 and HEADS % (n_head * d) == 0)
    inner = n_blk // outer
    near, far = outer * n_head, n_blk * n_head

    def per_device(query_rows, *others):
        if inner == 2 and HEADS == near + far and far % 4 == 0 and query_rows.shape[0] == TILE:
            return halved(n_head, far, near)(query_rows, *others)
        return gathered(outer, inner, n_head, near)(query_rows, *others)

    split = P(("batch", "outer", "inner", "head"), None)
    return jax.shard_map(
        per_device,
        mesh=Mesh(
            mesh.devices.reshape(outer, inner, n_head, mesh.shape["batch"]), ("outer", "inner", "head", "batch")
        ),
        in_specs=(split, split, split, P(), P(), P()),
        out_specs=split,
        check_vma=False,
    )
```

```python
import functools
import itertools

import jax
import jax.numpy as jnp
from jax import lax
from jax.experimental import pallas as pl
from jax.experimental.pallas import tpu as pltpu
from jax.sharding import Mesh, PartitionSpec as P

HEADS = 24
HDIM = 128
TILE = 128
EPS = 1e-06
MASKED = -1e30
NEAR = ("outer", "head")
FAR = ("outer", "inner", "head")
PARAMS = pltpu.CompilerParams(vmem_limit_bytes=48 * 1024 * 1024)
PACK_PARAMS = pltpu.CompilerParams(vmem_limit_bytes=61 * 1024 * 1024)
BF16 = jnp.bfloat16
SCALE = 1.4426950408889634 * HDIM ** (-0.5)


def shape(*dims):
    return jax.ShapeDtypeStruct(dims, BF16)


def exchange(x, axes):
    return lax.all_to_all(x, axes, split_axis=0, concat_axis=0, tiled=True)


def pack_kernel(write, n_out, q_hbm, k_hbm, v_hbm, qg_hbm, kg_hbm, *refs):
    outs, (q_in, k_in, v_in, qg, kg, sems, *kept) = refs[:n_out], refs[n_out:]
    outs = *kept, *outs
    copies = [
        pltpu.make_async_copy(src, dst, sems.at[n])
        for n, (src, dst) in enumerate(
            ((q_hbm, q_in), (k_hbm, k_in), (v_hbm, v_in), (qg_hbm, qg), (kg_hbm, kg))
        )
    ]
    for copy in copies:
        copy.start()

    def normalize(ref, gain):
        widened = ref[...].astype(jnp.float32)
        mean_square = jnp.mean(widened * widened, axis=-1, keepdims=True)
        return (widened * lax.rsqrt(mean_square + EPS) * gain[...]).astype(BF16)

    copies[0].wait()
    copies[3].wait()
    write(0, normalize(q_in, qg), *outs)
    copies[1].wait()
    copies[4].wait()
    write(1, normalize(k_in, kg), *outs)
    copies[2].wait()
    write(2, v_in[...], *outs)


def pack(write, out_shape, rows, features, arrays, kept=()):
    q, k, v, q_gain, k_gain = arrays
    return pl.pallas_call(
        functools.partial(pack_kernel, write, len(out_shape)),
        in_specs=[pl.BlockSpec(memory_space=pltpu.HBM)] * 5,
        out_shape=out_shape,
        scratch_shapes=[pltpu.VMEM((rows, features), BF16)] * 3
        + [pltpu.VMEM((1, features), jnp.float32)] * 2
        + [pltpu.SemaphoreType.DMA((5,)), *kept],
        compiler_params=PACK_PARAMS,
        name="pack",
    )(q, k, v, q_gain.reshape(1, -1), k_gain.reshape(1, -1))


def attend(query, band, key_at, value_at, key_blocks, live_at, scores_ref):
    bm = query.shape[0]
    bands, tiles = bm // band, scores_ref.shape[2] // TILE

    def score(c, running):
        s = lax.dot_general(query, key_at(c), (((1,), (1,)), ((), ())), preferred_element_type=jnp.float32)
        largest = []
        for a in range(bands):
            across = slice(a * band, (a + 1) * band)
            row = []
            for b in range(tiles):
                bias = jnp.where(live_at(a, c, b), 0.0, MASKED).astype(jnp.float32)
                row.append(s[across, b * TILE : (b + 1) * TILE] + bias)
                scores_ref[c, across, b * TILE : (b + 1) * TILE] = row[b]
            largest.append(functools.reduce(jnp.maximum, row))
        return jnp.maximum(running, jnp.concatenate(largest, axis=0))

    def over_keys(body, state):
        if key_blocks > 8:
            return lax.fori_loop(0, key_blocks, body, state)
        for c in range(key_blocks):
            state = body(c, state)
        return state

    largest = over_keys(score, jnp.full((bm, TILE), MASKED, jnp.float32))
    row_max = jnp.max(largest, axis=-1, keepdims=True) * SCALE

    def mix(c, state):
        total, mixed = state
        weights = jnp.exp2(scores_ref[c] * SCALE - row_max)
        for b in range(tiles):
            total = total + weights[:, b * TILE : (b + 1) * TILE]
        mixed = mixed + jnp.dot(weights.astype(BF16), value_at(c), preferred_element_type=jnp.float32)
        return total, mixed

    zeros = jnp.zeros((bm, TILE), jnp.float32)
    total, mixed = over_keys(mix, (zeros, zeros))
    return (mixed / jnp.sum(total, axis=-1, keepdims=True)).astype(BF16)


def pick(step):
    first, second = step
    return jnp.where(lax.axis_index("batch") == 0, first, second)


def rows_of(me, step, rows):
    return pl.ds(pl.multiple_of((me ^ pick(step)) * rows, rows), rows)


def collect_kernel(steps, rows, *refs):
    pieces, (q_out, kv_out) = refs[:-2], refs[-2:]
    me = lax.axis_index(NEAR)
    for step, piece in zip(steps, pieces):
        at = rows_of(me, step, rows)
        q_out[at] = piece[0]
        kv_out[:, at] = piece[1:]


def shared_kernel(steps, rows, mask_ref, q_ref, own_ref, other_ref, *refs):
    outs, (mixed, scores_ref) = refs[:-2], refs[-2:]
    mine = lax.axis_index("inner")
    wide = scores_ref.shape[2]
    blocks = q_ref.shape[0] // wide

    def at(c):
        return pl.ds(pl.multiple_of(lax.rem(c, blocks) * wide, wide), wide)

    def tile(block, inner, t):
        return (block * 2 + inner) * (wide // TILE) + t

    def kv_at(which, c):
        return own_ref[which, at(c)] if c < blocks else other_ref[which, at(c)]

    def one(i, _):
        mixed[at(i)] = attend(
            q_ref[at(i)],
            TILE,
            lambda c: kv_at(0, c),
            lambda c: kv_at(1, c),
            2 * blocks,
            lambda a, c, b: mask_ref[tile(i, mine, a), tile(c % blocks, mine if c < blocks else 1 - mine, b)] != 0,
            scores_ref,
        )
        return 0

    lax.fori_loop(0, blocks, one, 0)
    me = lax.axis_index(NEAR)
    for step, out in zip(steps, outs):
        out[...] = mixed[rows_of(me, step, rows)]


def whole_kernel(far_steps, steps, with_shared, rows, mask_ref, *refs):
    far = len(far_steps)
    pieces, shared, refs = refs[:far], refs[far : far + sum(with_shared)], refs[far + sum(with_shared) :]
    outs, (qkv, mixed, scores_ref) = refs[-3 - len(steps) : -3], refs[-3:]
    me = lax.axis_index(FAR)
    wide = scores_ref.shape[2]
    tiles = wide // TILE
    half = far // 2
    first = (me ^ pick(steps[0])) & half

    for step, piece in zip(far_steps, pieces):
        qkv[:, rows_of(me, step, rows)] = piece[...]

    def at(c):
        return pl.ds(c * wide if isinstance(c, int) else pl.multiple_of(c * wide, wide), wide)

    def one(i, _):
        block = lax.div(first, tiles) + i
        mixed[at(i)] = attend(
            qkv[0, at(block)],
            TILE,
            lambda c: qkv[1, at(c)],
            lambda c: qkv[2, at(c)],
            far // tiles,
            lambda a, c, b: mask_ref[block * tiles + a, c * tiles + b] != 0,
            scores_ref,
        )
        return 0

    lax.fori_loop(0, half // tiles, one, 0)
    shared = list(shared)
    for step, both, out in zip(steps, with_shared, outs):
        out[0] = mixed[pl.ds(pl.multiple_of(((me ^ pick(step)) & (half - 1)) * rows, rows), rows)]
        if both:
            out[1] = shared.pop(0)[...]


def swap(piece, axes, step, sizes):
    outer, inner, head, batch = sizes
    pairs = []
    for o, i, h, b in itertools.product(*map(range, sizes)):
        if axes == NEAR:
            to_o, to_h = divmod((o * head + h) ^ step[b], head)
            to_i = i
        else:
            to, to_h = divmod(((o * inner + i) * head + h) ^ step[b], head)
            to_o, to_i = divmod(to, inner)
        pairs.append((((o * inner + i) * head + h) * batch + b, ((to_o * inner + to_i) * head + to_h) * batch + b))
    return lax.ppermute(piece, ("outer", "inner", "head", "batch"), pairs)


def staggered(count):
    half = count // 2
    steps = []
    for d in range(half):
        steps += [(half + d, d), (d, half + d)]
    return steps


def halved(n_head, far, near):
    sizes = near // n_head, 2, n_head, 2
    near_steps, far_steps = staggered(near), staggered(far)

    def near_step(step):
        if step[0] // n_head % 2:
            return None
        return tuple(d // (2 * n_head) * n_head + d % n_head for d in step)

    def per_device(query_rows, key_rows, value_rows, q_gain, k_gain, tile_mask):
        rows, features = query_rows.shape
        heads = shape(2, rows, HDIM), shape(1, rows, HDIM)
        back = [far_steps[0::2], far_steps[1::2]]

        def write(which, block, by_head, *outs):
            for h in range(HEADS):
                by_head[h, which] = block[:, h * HDIM : (h + 1) * HDIM]
            if which == 2:
                me_near, me_far = lax.axis_index(NEAR), lax.axis_index(FAR)
                for step, out in zip(near_steps, outs):
                    out[...] = by_head[me_near ^ pick(step)]
                for step, out in zip(far_steps, outs[near:]):
                    out[...] = by_head[near + (me_far ^ pick(step))]

        def read(*refs):
            got, out_ref = refs[:-1], refs[-1]
            me_near, me_far = lax.axis_index(NEAR), lax.axis_index(FAR)

            def put(head, block):
                out_ref[:, pl.ds(pl.multiple_of(head * HDIM, HDIM), HDIM)] = block

            for step, ref in zip(back[0] + back[1], got):
                put(near + (me_far ^ pick(step)), ref[0])
                if near_step(step):
                    put(me_near ^ pick(near_step(step)), ref[1])

        packed = pack(
            write,
            [shape(3, rows, HDIM)] * (near + far),
            rows,
            features,
            (query_rows, key_rows, value_rows, q_gain, k_gain),
            [pltpu.VMEM((HEADS, 3, rows, HDIM), BF16)],
        )
        near_got = [swap(piece, NEAR, step, sizes) for piece, step in zip(packed, near_steps)]
        far_got = [swap(piece, FAR, step, sizes) for piece, step in zip(packed[near:], far_steps)]

        q_near, kv_near = pl.pallas_call(
            functools.partial(collect_kernel, near_steps, rows),
            out_shape=[shape(near * rows, HDIM), shape(2, near * rows, HDIM)],
            compiler_params=PARAMS,
            name="collect",
        )(*near_got)
        kv_other = lax.ppermute(kv_near, "inner", [(0, 1), (1, 0)])

        wide = 2 * TILE
        blocks = far * rows // wide
        smem, vmem = pl.BlockSpec(memory_space=pltpu.SMEM), pl.BlockSpec(memory_space=pltpu.VMEM)
        shared_steps = [near_step(step) for step in back[0] + back[1] if near_step(step)]
        shared = pl.pallas_call(
            functools.partial(shared_kernel, shared_steps, rows),
            in_specs=[smem] + [vmem] * 3,
            out_shape=[shape(rows, HDIM)] * near,
            scratch_shapes=[
                pltpu.VMEM((near * rows, HDIM), BF16),
                pltpu.VMEM((blocks, wide, wide), jnp.float32),
            ],
            compiler_params=PARAMS,
            cost_estimate=pl.CostEstimate(
                flops=2 * (far * rows) ** 2 * HDIM, bytes_accessed=2**21, transcendentals=0
            ),
            name="attend_shared",
        )(tile_mask, q_near, kv_near, kv_other)

        shared, returned, after = list(shared), [], []
        for steps in back:
            with_shared = [near_step(step) is not None for step in steps]
            mine = [shared.pop(0) for both in with_shared if both]
            mixed = pl.pallas_call(
                functools.partial(whole_kernel, far_steps, steps, with_shared, rows),
                in_specs=[smem] + [vmem] * (far + len(mine) + len(after)),
                out_shape=[heads[0 if both else 1] for both in with_shared],
                scratch_shapes=[
                    pltpu.VMEM((3, far * rows, HDIM), BF16),
                    pltpu.VMEM((far // 2 * rows, HDIM), BF16),
                    pltpu.VMEM((blocks, wide, wide), jnp.float32),
                ],
                compiler_params=PARAMS,
                cost_estimate=pl.CostEstimate(
                    flops=2 * (far * rows) ** 2 * HDIM, bytes_accessed=2**22, transcendentals=0
                ),
                name="attend_rest" if after else "attend_first",
            )(tile_mask, *far_got, *mine, *after)
            after = [mixed[-1]]
            returned += [swap(piece, FAR, step, sizes) for piece, step in zip(mixed, steps)]
        return pl.pallas_call(
            read, out_shape=shape(rows, features), compiler_params=PARAMS, name="unpack"
        )(*returned)

    return per_device


def gathered_kernel(outer, inner, mask_ref, q_ref, kv_ref, out_ref, scores_ref):
    i = pl.program_id(0)
    block = out_ref.shape[0] * out_ref.shape[1] * out_ref.shape[2]
    tiles = block // TILE
    q_tile = (i * inner + lax.axis_index("inner")) * tiles
    mixed = attend(
        q_ref[0, :, 0].reshape(block, HDIM),
        TILE,
        lambda c: kv_ref[lax.rem(c, inner), lax.div(c, inner), :, 1].reshape(block, HDIM),
        lambda c: kv_ref[lax.rem(c, inner), lax.div(c, inner), :, 2].reshape(block, HDIM),
        outer * inner,
        lambda a, c, b: mask_ref[q_tile + a, c * tiles + b] != 0,
        scores_ref,
    )
    out_ref[...] = mixed.reshape(out_ref.shape)


def gathered(outer, inner, n_head, near):
    width = HEADS // near * HDIM

    def per_device(query_rows, key_rows, value_rows, q_gain, k_gain, tile_mask):
        rows, features = query_rows.shape
        block = rows * n_head

        def write(which, block, packed):
            for d in range(near):
                packed[d, which] = block[:, d * width : (d + 1) * width]

        def read(got_ref, out_ref):
            for d in range(near):
                out_ref[:, d * width : (d + 1) * width] = got_ref[d]

        (packed,) = pack(
            write,
            [shape(near, 3, rows, width)],
            rows,
            features,
            (query_rows, key_rows, value_rows, q_gain, k_gain),
        )
        own = exchange(packed, NEAR).reshape(outer, n_head, 3, rows, width)
        every = lax.all_gather(own, "inner")
        mixed = pl.pallas_call(
            functools.partial(gathered_kernel, outer, inner),
            grid=(outer, HEADS // near),
            in_specs=[
                pl.BlockSpec(memory_space=pltpu.SMEM),
                pl.BlockSpec((1, n_head, 1, rows, HDIM), lambda i, h: (i, 0, 0, 0, h)),
                pl.BlockSpec((inner, outer, n_head, 3, rows, HDIM), lambda i, h: (0, 0, 0, 0, 0, h)),
            ],
            out_specs=pl.BlockSpec((1, n_head, rows, HDIM), lambda i, h: (i, 0, 0, h)),
            out_shape=shape(outer, n_head, rows, width),
            scratch_shapes=[pltpu.VMEM((outer * inner, block, block), jnp.float32)],
            compiler_params=PARAMS,
            name="attend",
        )(tile_mask, own, every)
        return pl.pallas_call(
            read, out_shape=shape(rows, features), compiler_params=PARAMS, name="unpack"
        )(exchange(mixed.reshape(near, rows, width), NEAR))

    return per_device


def solution(mesh):
    n_blk, n_head = mesh.shape["blk"], mesh.shape["head"]
    outer = max(d for d in range(1, n_blk + 1) if n_blk % d == 0 and HEADS % (n_head * d) == 0)
    inner = n_blk // outer
    near, far = outer * n_head, n_blk * n_head

    def per_device(query_rows, *others):
        in_pairs = inner == 2 and n_head == 2 and far & (far - 1) == 0 and mesh.shape["batch"] == 2
        if in_pairs and HEADS == near + far and query_rows.shape[0] == TILE:
            return halved(n_head, far, near)(query_rows, *others)
        return gathered(outer, inner, n_head, near)(query_rows, *others)

    split = P(("batch", "outer", "inner", "head"), None)
    return jax.shard_map(
        per_device,
        mesh=Mesh(
            mesh.devices.reshape(outer, inner, n_head, mesh.shape["batch"]), ("outer", "inner", "head", "batch")
        ),
        in_specs=(split, split, split, P(), P(), P()),
        out_specs=split,
        check_vma=False,
    )
```

```python
import functools

import jax
import jax.numpy as jnp
from jax import lax
from jax.experimental import pallas as pl
from jax.experimental.pallas import tpu as pltpu
from jax.sharding import Mesh, PartitionSpec as P

HEADS = 24
HDIM = 128
TILE = 128
EPS = 1e-06
MASKED = -1e30
NEAR = ("outer", "head")
FAR = ("outer", "inner", "head")
PARAMS = pltpu.CompilerParams(vmem_limit_bytes=48 * 1024 * 1024)
PACK_PARAMS = pltpu.CompilerParams(vmem_limit_bytes=61 * 1024 * 1024)
BF16 = jnp.bfloat16
SCALE = 1.4426950408889634 * HDIM ** (-0.5)


def shape(*dims):
    return jax.ShapeDtypeStruct(dims, BF16)


def exchange(x, axes):
    return lax.all_to_all(x, axes, split_axis=0, concat_axis=0, tiled=True)


def pack_kernel(write, q_hbm, k_hbm, v_hbm, qg_hbm, kg_hbm, *refs):
    outs, (q_in, k_in, v_in, qg, kg, sems) = refs[:-6], refs[-6:]
    copies = [
        pltpu.make_async_copy(src, dst, sems.at[n])
        for n, (src, dst) in enumerate(
            ((q_hbm, q_in), (k_hbm, k_in), (v_hbm, v_in), (qg_hbm, qg), (kg_hbm, kg))
        )
    ]
    for copy in copies:
        copy.start()

    def normalize(ref, gain):
        widened = ref[...].astype(jnp.float32)
        mean_square = jnp.mean(widened * widened, axis=-1, keepdims=True)
        return (widened * lax.rsqrt(mean_square + EPS) * gain[...]).astype(BF16)

    copies[0].wait()
    copies[3].wait()
    write(0, normalize(q_in, qg), *outs)
    copies[1].wait()
    copies[4].wait()
    write(1, normalize(k_in, kg), *outs)
    copies[2].wait()
    write(2, v_in[...], *outs)


def pack(write, out_shape, rows, features, arrays):
    q, k, v, q_gain, k_gain = arrays
    return pl.pallas_call(
        functools.partial(pack_kernel, write),
        in_specs=[pl.BlockSpec(memory_space=pltpu.HBM)] * 5,
        out_shape=out_shape,
        scratch_shapes=[pltpu.VMEM((rows, features), BF16)] * 3
        + [pltpu.VMEM((1, features), jnp.float32)] * 2
        + [pltpu.SemaphoreType.DMA((5,))],
        compiler_params=PACK_PARAMS,
        name="pack",
    )(q, k, v, q_gain.reshape(1, -1), k_gain.reshape(1, -1))


def attend(query, band, key_at, value_at, key_blocks, live_at, scores_ref):
    bm, wide = query.shape[0], scores_ref.shape[2]

    def score(c, running):
        return first_pass(query, band, key_at(c), lambda a, b: live_at(a, c * (wide // TILE) + b), scores_ref, c, running)

    def mix(c, state):
        return second_pass(scores_ref, c, row_max, value_at(c), state)

    largest = lax.fori_loop(0, key_blocks, score, jnp.full((bm, TILE), MASKED, jnp.float32))
    row_max = jnp.max(largest, axis=-1, keepdims=True) * SCALE
    zeros = jnp.zeros((bm, TILE), jnp.float32)
    return divide(*lax.fori_loop(0, key_blocks, mix, (zeros, zeros)))


def first_pass(query, band, key, live_at, scores_ref, c, running):
    s = lax.dot_general(query, key, (((1,), (1,)), ((), ())), preferred_element_type=jnp.float32)
    largest = []
    for a in range(query.shape[0] // band):
        across = slice(a * band, (a + 1) * band)
        best = running[across]
        for b in range(key.shape[0] // TILE):
            along = slice(b * TILE, (b + 1) * TILE)
            masked = s[across, along] + jnp.where(live_at(a, b), 0.0, MASKED).astype(jnp.float32)
            scores_ref[c, across, along] = masked
            best = jnp.maximum(best, masked)
        largest.append(best)
    return jnp.concatenate(largest, axis=0)


def second_pass(scores_ref, c, row_max, value, state):
    total, mixed = state
    weights = jnp.exp2(scores_ref[c] * SCALE - row_max)
    for b in range(value.shape[0] // TILE):
        total = total + weights[:, b * TILE : (b + 1) * TILE]
    return total, mixed + jnp.dot(weights.astype(BF16), value, preferred_element_type=jnp.float32)


def divide(total, mixed):
    return (mixed / jnp.sum(total, axis=-1, keepdims=True)).astype(BF16)


def attend_blocks(blocks, band, query_at, key_at, value_at, key_blocks, live_at, finish, scores):
    bm = scores[0].shape[1]
    empty = jnp.full((bm, TILE), MASKED, jnp.float32)
    zeros = jnp.zeros((bm, TILE), jnp.float32)

    def both(i, row_max, now, following):
        later = jnp.minimum(i + 1, blocks - 1)
        query = query_at(later)
        largest, state = empty, (zeros, zeros)
        for c in range(key_blocks):
            largest = first_pass(query, band, key_at(c), lambda a, b: live_at(later, a, c, b), following, c, largest)
            state = second_pass(now, c, row_max, value_at(c), state)
        finish(i, divide(*state))
        return jnp.max(largest, axis=-1, keepdims=True) * SCALE

    largest = empty
    query = query_at(0)
    for c in range(key_blocks):
        largest = first_pass(query, band, key_at(c), lambda a, b: live_at(0, a, c, b), scores[0], c, largest)

    def pair(n, row_max):
        row_max = both(2 * n, row_max, scores[0], scores[1])
        return both(2 * n + 1, row_max, scores[1], scores[0])

    lax.fori_loop(0, blocks // 2, pair, jnp.max(largest, axis=-1, keepdims=True) * SCALE)


def shared_kernel(sources, mask_ref, own_ref, other_ref, out_ref, key, value, *scores):
    half = own_ref.shape[2]
    mine = lax.axis_index("inner")
    here = pl.ds(pl.multiple_of(mine * half, half), half)
    there = pl.ds(pl.multiple_of((1 - mine) * half, half), half)
    key[:, here] = own_ref[:, 1]
    value[:, here] = own_ref[:, 2]
    key[:, there] = other_ref[:, 0]
    value[:, there] = other_ref[:, 1]
    _, bm, wide = scores[0].shape
    bands, tiles = bm // half, wide // TILE

    def finish(i, mixed):
        out_ref[pl.ds(i * bands, bands)] = mixed.reshape(bands, half, HDIM)

    attend_blocks(
        sources // bands,
        half,
        lambda i: own_ref[pl.ds(i * bands, bands), 0].reshape(bm, HDIM),
        lambda c: key[c * tiles : (c + 1) * tiles].reshape(wide, HDIM),
        lambda c: value[c * tiles : (c + 1) * tiles].reshape(wide, HDIM),
        sources // tiles,
        lambda i, a, c, b: mask_ref[i * bands + a, c * tiles + b] != 0,
        finish,
        scores,
    )


def whole_kernel(sources, mask_ref, qkv_ref, shared_ref, out_ref, *scores):
    rows = qkv_ref.shape[2]
    _, bm, wide = scores[0].shape
    bands, tiles = bm // rows, wide // TILE
    out_ref[:, rows:] = shared_ref[...]

    def finish(i, mixed):
        out_ref[pl.ds(i * bands, bands), :rows] = mixed.reshape(bands, rows, HDIM)

    attend_blocks(
        sources // bands,
        rows,
        lambda i: qkv_ref[pl.ds(i * bands, bands), 0].reshape(bm, HDIM),
        lambda c: qkv_ref[c * tiles : (c + 1) * tiles, 1].reshape(wide, HDIM),
        lambda c: qkv_ref[c * tiles : (c + 1) * tiles, 2].reshape(wide, HDIM),
        sources // tiles,
        lambda i, a, c, b: mask_ref[i * bands + a, c * tiles + b] != 0,
        finish,
        scores,
    )


def halved(n_head, far, near):
    def per_device(query_rows, key_rows, value_rows, q_gain, k_gain, tile_mask):
        rows, features = query_rows.shape
        half = rows // 2

        def near_of(d):
            return d // (2 * n_head) * n_head + d % n_head

        def half_of(d):
            return d // n_head % 2 * half

        def write(which, block, shared, whole):
            for d in range(far):
                at, head = half_of(d), near_of(d) * HDIM
                shared[d, which] = block[at : at + half, head : head + HDIM]
                head = (near + d) * HDIM
                whole[d, which] = block[:, head : head + HDIM]

        def read(got_ref, out_ref):
            for d in range(far):
                at, head = half_of(d), near_of(d) * HDIM
                out_ref[at : at + half, head : head + HDIM] = got_ref[d, rows:]
                head = (near + d) * HDIM
                out_ref[:, head : head + HDIM] = got_ref[d, :rows]

        shared, whole = pack(
            write,
            [shape(far, 3, half, HDIM), shape(far, 3, rows, HDIM)],
            rows,
            features,
            (query_rows, key_rows, value_rows, q_gain, k_gain),
        )
        shared = exchange(shared, FAR)
        other = lax.ppermute(shared[:, 1:], "inner", [(0, 1), (1, 0)])
        whole = exchange(whole, FAR)

        smem, vmem = pl.BlockSpec(memory_space=pltpu.SMEM), pl.BlockSpec(memory_space=pltpu.VMEM)
        wide = 2 * TILE
        scores = [pltpu.VMEM((far // 2, wide, wide), jnp.float32)] * 2
        mixed = pl.pallas_call(
            functools.partial(shared_kernel, far),
            in_specs=[smem, vmem, vmem],
            out_shape=shape(far, half, HDIM),
            scratch_shapes=[pltpu.VMEM((far, rows, HDIM), BF16)] * 2 + scores,
            compiler_params=PARAMS,
            cost_estimate=pl.CostEstimate(
                flops=2 * (far * rows) ** 2 * HDIM, bytes_accessed=2**21, transcendentals=0
            ),
            name="attend_shared",
        )(tile_mask, shared, other)
        mixed = pl.pallas_call(
            functools.partial(whole_kernel, far),
            in_specs=[smem, vmem, vmem],
            out_shape=shape(far, rows + half, HDIM),
            scratch_shapes=scores,
            compiler_params=PARAMS,
            cost_estimate=pl.CostEstimate(
                flops=4 * (far * rows) ** 2 * HDIM, bytes_accessed=2**22, transcendentals=0
            ),
            name="attend_whole",
        )(tile_mask, whole, mixed)
        return pl.pallas_call(
            read, out_shape=shape(rows, features), compiler_params=PARAMS, name="unpack"
        )(exchange(mixed, FAR))

    return per_device


def gathered_kernel(outer, inner, mask_ref, q_ref, kv_ref, out_ref, scores_ref):
    i = pl.program_id(0)
    block = out_ref.shape[0] * out_ref.shape[1] * out_ref.shape[2]
    tiles = block // TILE
    q_tile = (i * inner + lax.axis_index("inner")) * tiles
    mixed = attend(
        q_ref[0, :, 0].reshape(block, HDIM),
        TILE,
        lambda c: kv_ref[lax.rem(c, inner), lax.div(c, inner), :, 1].reshape(block, HDIM),
        lambda c: kv_ref[lax.rem(c, inner), lax.div(c, inner), :, 2].reshape(block, HDIM),
        outer * inner,
        lambda a, t: mask_ref[q_tile + a, t] != 0,
        scores_ref,
    )
    out_ref[...] = mixed.reshape(out_ref.shape)


def gathered(outer, inner, n_head, near):
    width = HEADS // near * HDIM

    def per_device(query_rows, key_rows, value_rows, q_gain, k_gain, tile_mask):
        rows, features = query_rows.shape
        block = rows * n_head

        def write(which, block, packed):
            for d in range(near):
                packed[d, which] = block[:, d * width : (d + 1) * width]

        def read(got_ref, out_ref):
            for d in range(near):
                out_ref[:, d * width : (d + 1) * width] = got_ref[d]

        (packed,) = pack(
            write,
            [shape(near, 3, rows, width)],
            rows,
            features,
            (query_rows, key_rows, value_rows, q_gain, k_gain),
        )
        own = exchange(packed, NEAR).reshape(outer, n_head, 3, rows, width)
        every = lax.all_gather(own, "inner")
        mixed = pl.pallas_call(
            functools.partial(gathered_kernel, outer, inner),
            grid=(outer, HEADS // near),
            in_specs=[
                pl.BlockSpec(memory_space=pltpu.SMEM),
                pl.BlockSpec((1, n_head, 1, rows, HDIM), lambda i, h: (i, 0, 0, 0, h)),
                pl.BlockSpec((inner, outer, n_head, 3, rows, HDIM), lambda i, h: (0, 0, 0, 0, 0, h)),
            ],
            out_specs=pl.BlockSpec((1, n_head, rows, HDIM), lambda i, h: (i, 0, 0, h)),
            out_shape=shape(outer, n_head, rows, width),
            scratch_shapes=[pltpu.VMEM((outer * inner, block, block), jnp.float32)],
            compiler_params=PARAMS,
            name="attend",
        )(tile_mask, own, every)
        return pl.pallas_call(
            read, out_shape=shape(rows, features), compiler_params=PARAMS, name="unpack"
        )(exchange(mixed.reshape(near, rows, width), NEAR))

    return per_device


def solution(mesh):
    n_blk, n_head = mesh.shape["blk"], mesh.shape["head"]
    outer = max(d for d in range(1, n_blk + 1) if n_blk % d == 0 and HEADS % (n_head * d) == 0)
    inner = n_blk // outer
    near, far = outer * n_head, n_blk * n_head

    def per_device(query_rows, *others):
        if inner == 2 and HEADS == near + far and far % 4 == 0 and query_rows.shape[0] == TILE:
            return halved(n_head, far, near)(query_rows, *others)
        return gathered(outer, inner, n_head, near)(query_rows, *others)

    split = P(("batch", "outer", "inner", "head"), None)
    return jax.shard_map(
        per_device,
        mesh=Mesh(
            mesh.devices.reshape(outer, inner, n_head, mesh.shape["batch"]), ("outer", "inner", "head", "batch")
        ),
        in_specs=(split, split, split, P(), P(), P()),
        out_specs=split,
        check_vma=False,
    )
```

```python
import functools

import jax
import jax.numpy as jnp
from jax import lax
from jax.experimental import pallas as pl
from jax.experimental.pallas import tpu as pltpu
from jax.sharding import Mesh, PartitionSpec as P

HEADS = 24
HDIM = 128
TILE = 128
EPS = 1e-06
MASKED = -1e30
NEAR = ("outer", "head")
FAR = ("outer", "inner", "head")
PARAMS = pltpu.CompilerParams(vmem_limit_bytes=48 * 1024 * 1024)
PACK_PARAMS = pltpu.CompilerParams(vmem_limit_bytes=61 * 1024 * 1024)
BF16 = jnp.bfloat16
SCALE = 1.4426950408889634 * HDIM ** (-0.5)


def shape(*dims):
    return jax.ShapeDtypeStruct(dims, BF16)


def exchange(x, axes):
    return lax.all_to_all(x, axes, split_axis=0, concat_axis=0, tiled=True)


def pack_kernel(write, q_hbm, k_hbm, v_hbm, qg_hbm, kg_hbm, *refs):
    outs, (q_in, k_in, v_in, qg, kg, sems) = refs[:-6], refs[-6:]
    copies = [
        pltpu.make_async_copy(src, dst, sems.at[n])
        for n, (src, dst) in enumerate(
            ((q_hbm, q_in), (k_hbm, k_in), (v_hbm, v_in), (qg_hbm, qg), (kg_hbm, kg))
        )
    ]
    for copy in copies:
        copy.start()

    def normalize(ref, gain):
        widened = ref[...].astype(jnp.float32)
        mean_square = jnp.mean(widened * widened, axis=-1, keepdims=True)
        return (widened * lax.rsqrt(mean_square + EPS) * gain[...]).astype(BF16)

    copies[0].wait()
    copies[3].wait()
    write(0, normalize(q_in, qg), *outs)
    copies[1].wait()
    copies[4].wait()
    write(1, normalize(k_in, kg), *outs)
    copies[2].wait()
    write(2, v_in[...], *outs)


def pack(write, out_shape, rows, features, arrays):
    q, k, v, q_gain, k_gain = arrays
    return pl.pallas_call(
        functools.partial(pack_kernel, write),
        in_specs=[pl.BlockSpec(memory_space=pltpu.HBM)] * 5,
        out_shape=out_shape,
        scratch_shapes=[pltpu.VMEM((rows, features), BF16)] * 3
        + [pltpu.VMEM((1, features), jnp.float32)] * 2
        + [pltpu.SemaphoreType.DMA((5,))],
        compiler_params=PACK_PARAMS,
        name="pack",
    )(q, k, v, q_gain.reshape(1, -1), k_gain.reshape(1, -1))


def first_pass(query, key, bias_at, scores_ref, c, largest):
    s = lax.dot_general(key, query, (((1,), (1,)), ((), ())), preferred_element_type=jnp.float32)
    for t in range(key.shape[0] // TILE):
        down = slice(t * TILE, (t + 1) * TILE)
        masked = s[down].reshape(TILE // 8, 8, -1) + bias_at(t)[None]
        scores_ref[c, down] = masked.reshape(TILE, -1)
        largest = jnp.maximum(largest, jnp.max(masked, axis=0))
    return largest


def second_pass(scores_ref, c, col_max, value_t, state):
    total, mixed = state
    wide, bm = scores_ref.shape[1:]
    weights = jnp.exp2(scores_ref[c].reshape(wide // 8, 8, bm) * SCALE - col_max[None])
    total = total + jnp.sum(weights, axis=0)
    weights = weights.reshape(wide, bm).astype(BF16)
    return total, mixed + jnp.dot(value_t, weights, preferred_element_type=jnp.float32)


def over_all(largest):
    return jnp.broadcast_to(jnp.max(largest, axis=0, keepdims=True) * SCALE, largest.shape)


def divide(total, mixed):
    return (mixed / jnp.sum(total, axis=0, keepdims=True)).T.astype(BF16)


def bias_of(band, bm, live_at):
    lane = lax.broadcasted_iota(jnp.int32, (8, bm), 1)
    bias = jnp.zeros((8, bm), jnp.float32)
    for a in range(bm // band):
        dead = jnp.where(live_at(a), 0.0, MASKED).astype(jnp.float32)
        bias = jnp.where((lane >= a * band) & (lane < (a + 1) * band), dead, bias)
    return bias


def attend(query, band, key_at, value_at, key_blocks, live_at, scores_ref):
    wide, bm = scores_ref.shape[1:]

    def score(c, largest):
        def bias_at(t):
            return bias_of(band, bm, lambda a: live_at(a, c * (wide // TILE) + t))

        return first_pass(query, key_at(c), bias_at, scores_ref, c, largest)

    largest = lax.fori_loop(0, key_blocks, score, jnp.full((8, bm), MASKED, jnp.float32))
    col_max = over_all(largest)

    def mix(c, state):
        return second_pass(scores_ref, c, col_max, transposed(value_at(c)), state)

    state = jnp.zeros((8, bm), jnp.float32), jnp.zeros((HDIM, bm), jnp.float32)
    return divide(*lax.fori_loop(0, key_blocks, mix, state))


def transposed(block):
    return block.astype(jnp.float32).T.astype(BF16)


def attend_blocks(blocks, band, query_at, key_at, value_t, key_blocks, live_at, finish, scores):
    wide, bm = scores[0].shape[1:]
    empty = jnp.full((8, bm), MASKED, jnp.float32)
    nothing = jnp.zeros((8, bm), jnp.float32), jnp.zeros((HDIM, bm), jnp.float32)

    def bias_at(i, c):
        return lambda t: bias_of(band, bm, lambda a: live_at(i, a, c, t))

    def both(i, col_max, now, following):
        later = jnp.minimum(i + 1, blocks - 1)
        query = query_at(later)
        largest, state = empty, nothing
        for c in range(key_blocks):
            largest = first_pass(query, key_at(c), bias_at(later, c), following, c, largest)
            state = second_pass(now, c, col_max, value_t[:, c * wide : (c + 1) * wide], state)
        finish(i, divide(*state))
        return over_all(largest)

    largest = empty
    query = query_at(0)
    for c in range(key_blocks):
        largest = first_pass(query, key_at(c), bias_at(0, c), scores[0], c, largest)

    def pair(n, col_max):
        col_max = both(2 * n, col_max, scores[0], scores[1])
        return both(2 * n + 1, col_max, scores[1], scores[0])

    lax.fori_loop(0, blocks // 2, pair, over_all(largest))


def shared_kernel(sources, mask_ref, own_ref, other_ref, out_ref, key, value, value_t, *scores):
    half = own_ref.shape[2]
    mine = lax.axis_index("inner")
    here = pl.ds(pl.multiple_of(mine * half, half), half)
    there = pl.ds(pl.multiple_of((1 - mine) * half, half), half)
    key[:, here] = own_ref[:, 1]
    value[:, here] = own_ref[:, 2]
    key[:, there] = other_ref[:, 0]
    value[:, there] = other_ref[:, 1]
    for t in range(sources):
        value_t[:, t * TILE : (t + 1) * TILE] = transposed(value[t])
    _, wide, bm = scores[0].shape
    bands, tiles = bm // half, wide // TILE

    def finish(i, mixed):
        out_ref[pl.ds(i * bands, bands)] = mixed.reshape(bands, half, HDIM)

    attend_blocks(
        sources // bands,
        half,
        lambda i: own_ref[pl.ds(i * bands, bands), 0].reshape(bm, HDIM),
        lambda c: key[c * tiles : (c + 1) * tiles].reshape(wide, HDIM),
        value_t,
        sources // tiles,
        lambda i, a, c, t: mask_ref[i * bands + a, c * tiles + t] != 0,
        finish,
        scores,
    )


def whole_kernel(sources, mask_ref, qkv_ref, shared_ref, out_ref, value_t, *scores):
    rows = qkv_ref.shape[2]
    _, wide, bm = scores[0].shape
    bands, tiles = bm // rows, wide // TILE
    out_ref[:, rows:] = shared_ref[...]
    for t in range(sources):
        value_t[:, t * TILE : (t + 1) * TILE] = transposed(qkv_ref[t, 2])

    def finish(i, mixed):
        out_ref[pl.ds(i * bands, bands), :rows] = mixed.reshape(bands, rows, HDIM)

    attend_blocks(
        sources // bands,
        rows,
        lambda i: qkv_ref[pl.ds(i * bands, bands), 0].reshape(bm, HDIM),
        lambda c: qkv_ref[c * tiles : (c + 1) * tiles, 1].reshape(wide, HDIM),
        value_t,
        sources // tiles,
        lambda i, a, c, t: mask_ref[i * bands + a, c * tiles + t] != 0,
        finish,
        scores,
    )


def halved(n_head, far, near):
    def per_device(query_rows, key_rows, value_rows, q_gain, k_gain, tile_mask):
        rows, features = query_rows.shape
        half = rows // 2

        def near_of(d):
            return d // (2 * n_head) * n_head + d % n_head

        def half_of(d):
            return d // n_head % 2 * half

        def write(which, block, shared, whole):
            for d in range(far):
                at, head = half_of(d), near_of(d) * HDIM
                shared[d, which] = block[at : at + half, head : head + HDIM]
                head = (near + d) * HDIM
                whole[d, which] = block[:, head : head + HDIM]

        def read(got_ref, out_ref):
            for d in range(far):
                at, head = half_of(d), near_of(d) * HDIM
                out_ref[at : at + half, head : head + HDIM] = got_ref[d, rows:]
                head = (near + d) * HDIM
                out_ref[:, head : head + HDIM] = got_ref[d, :rows]

        shared, whole = pack(
            write,
            [shape(far, 3, half, HDIM), shape(far, 3, rows, HDIM)],
            rows,
            features,
            (query_rows, key_rows, value_rows, q_gain, k_gain),
        )
        shared = exchange(shared, FAR)
        other = lax.ppermute(shared[:, 1:], "inner", [(0, 1), (1, 0)])
        whole = exchange(whole, FAR)

        smem, vmem = pl.BlockSpec(memory_space=pltpu.SMEM), pl.BlockSpec(memory_space=pltpu.VMEM)
        wide = 2 * TILE
        scores = [pltpu.VMEM((far // 2, wide, wide), jnp.float32)] * 2
        mixed = pl.pallas_call(
            functools.partial(shared_kernel, far),
            in_specs=[smem, vmem, vmem],
            out_shape=shape(far, half, HDIM),
            scratch_shapes=[pltpu.VMEM((far, rows, HDIM), BF16)] * 2
            + [pltpu.VMEM((HDIM, far * rows), BF16), *scores],
            compiler_params=PARAMS,
            cost_estimate=pl.CostEstimate(
                flops=2 * (far * rows) ** 2 * HDIM, bytes_accessed=2**21, transcendentals=0
            ),
            name="attend_shared",
        )(tile_mask, shared, other)
        mixed = pl.pallas_call(
            functools.partial(whole_kernel, far),
            in_specs=[smem, vmem, vmem],
            out_shape=shape(far, rows + half, HDIM),
            scratch_shapes=[pltpu.VMEM((HDIM, far * rows), BF16), *scores],
            compiler_params=PARAMS,
            cost_estimate=pl.CostEstimate(
                flops=4 * (far * rows) ** 2 * HDIM, bytes_accessed=2**22, transcendentals=0
            ),
            name="attend_whole",
        )(tile_mask, whole, mixed)
        return pl.pallas_call(
            read, out_shape=shape(rows, features), compiler_params=PARAMS, name="unpack"
        )(exchange(mixed, FAR))

    return per_device


def gathered_kernel(outer, inner, mask_ref, q_ref, kv_ref, out_ref, scores_ref):
    i = pl.program_id(0)
    block = out_ref.shape[0] * out_ref.shape[1] * out_ref.shape[2]
    tiles = block // TILE
    q_tile = (i * inner + lax.axis_index("inner")) * tiles
    mixed = attend(
        q_ref[0, :, 0].reshape(block, HDIM),
        TILE,
        lambda c: kv_ref[lax.rem(c, inner), lax.div(c, inner), :, 1].reshape(block, HDIM),
        lambda c: kv_ref[lax.rem(c, inner), lax.div(c, inner), :, 2].reshape(block, HDIM),
        outer * inner,
        lambda a, t: mask_ref[q_tile + a, t] != 0,
        scores_ref,
    )
    out_ref[...] = mixed.reshape(out_ref.shape)


def gathered(outer, inner, n_head, near):
    width = HEADS // near * HDIM

    def per_device(query_rows, key_rows, value_rows, q_gain, k_gain, tile_mask):
        rows, features = query_rows.shape
        block = rows * n_head

        def write(which, block, packed):
            for d in range(near):
                packed[d, which] = block[:, d * width : (d + 1) * width]

        def read(got_ref, out_ref):
            for d in range(near):
                out_ref[:, d * width : (d + 1) * width] = got_ref[d]

        (packed,) = pack(
            write,
            [shape(near, 3, rows, width)],
            rows,
            features,
            (query_rows, key_rows, value_rows, q_gain, k_gain),
        )
        own = exchange(packed, NEAR).reshape(outer, n_head, 3, rows, width)
        every = lax.all_gather(own, "inner")
        mixed = pl.pallas_call(
            functools.partial(gathered_kernel, outer, inner),
            grid=(outer, HEADS // near),
            in_specs=[
                pl.BlockSpec(memory_space=pltpu.SMEM),
                pl.BlockSpec((1, n_head, 1, rows, HDIM), lambda i, h: (i, 0, 0, 0, h)),
                pl.BlockSpec((inner, outer, n_head, 3, rows, HDIM), lambda i, h: (0, 0, 0, 0, 0, h)),
            ],
            out_specs=pl.BlockSpec((1, n_head, rows, HDIM), lambda i, h: (i, 0, 0, h)),
            out_shape=shape(outer, n_head, rows, width),
            scratch_shapes=[pltpu.VMEM((outer * inner, block, block), jnp.float32)],
            compiler_params=PARAMS,
            name="attend",
        )(tile_mask, own, every)
        return pl.pallas_call(
            read, out_shape=shape(rows, features), compiler_params=PARAMS, name="unpack"
        )(exchange(mixed.reshape(near, rows, width), NEAR))

    return per_device


def solution(mesh):
    n_blk, n_head = mesh.shape["blk"], mesh.shape["head"]
    outer = max(d for d in range(1, n_blk + 1) if n_blk % d == 0 and HEADS % (n_head * d) == 0)
    inner = n_blk // outer
    near, far = outer * n_head, n_blk * n_head

    def per_device(query_rows, *others):
        if inner == 2 and HEADS == near + far and far % 4 == 0 and query_rows.shape[0] == TILE:
            return halved(n_head, far, near)(query_rows, *others)
        return gathered(outer, inner, n_head, near)(query_rows, *others)

    split = P(("batch", "outer", "inner", "head"), None)
    return jax.shard_map(
        per_device,
        mesh=Mesh(
            mesh.devices.reshape(outer, inner, n_head, mesh.shape["batch"]), ("outer", "inner", "head", "batch")
        ),
        in_specs=(split, split, split, P(), P(), P()),
        out_specs=split,
        check_vma=False,
    )
```

```python
import functools

import jax
import jax.numpy as jnp
from jax import lax
from jax.experimental import pallas as pl
from jax.experimental.pallas import tpu as pltpu
from jax.sharding import Mesh, PartitionSpec as P

HEADS = 24
HDIM = 128
TILE = 128
EPS = 1e-06
MASKED = -1e30
NEAR = ("outer", "head")
FAR = ("outer", "inner", "head")
PARAMS = pltpu.CompilerParams(vmem_limit_bytes=48 * 1024 * 1024)
PACK_PARAMS = pltpu.CompilerParams(vmem_limit_bytes=61 * 1024 * 1024)
BF16 = jnp.bfloat16
SCALE = 1.4426950408889634 * HDIM ** (-0.5)


def shape(*dims):
    return jax.ShapeDtypeStruct(dims, BF16)


def exchange(x, axes):
    return lax.all_to_all(x, axes, split_axis=0, concat_axis=0, tiled=True)


def pack_kernel(write, n_out, q_hbm, k_hbm, v_hbm, qg_hbm, kg_hbm, *refs):
    outs, (q_in, k_in, v_in, qg, kg, sems, *kept) = refs[:n_out], refs[n_out:]
    outs = *kept, *outs
    copies = [
        pltpu.make_async_copy(src, dst, sems.at[n])
        for n, (src, dst) in enumerate(
            ((q_hbm, q_in), (k_hbm, k_in), (v_hbm, v_in), (qg_hbm, qg), (kg_hbm, kg))
        )
    ]
    for copy in copies:
        copy.start()

    def normalize(ref, gain):
        widened = ref[...].astype(jnp.float32)
        mean_square = jnp.mean(widened * widened, axis=-1, keepdims=True)
        return (widened * lax.rsqrt(mean_square + EPS) * gain[...]).astype(BF16)

    copies[0].wait()
    copies[3].wait()
    write(0, normalize(q_in, qg), *outs)
    copies[1].wait()
    copies[4].wait()
    write(1, normalize(k_in, kg), *outs)
    copies[2].wait()
    write(2, v_in[...], *outs)


def pack(write, out_shape, rows, features, arrays, kept=()):
    q, k, v, q_gain, k_gain = arrays
    return pl.pallas_call(
        functools.partial(pack_kernel, write, len(out_shape)),
        in_specs=[pl.BlockSpec(memory_space=pltpu.HBM)] * 5,
        out_shape=out_shape,
        scratch_shapes=[pltpu.VMEM((rows, features), BF16)] * 3
        + [pltpu.VMEM((1, features), jnp.float32)] * 2
        + [pltpu.SemaphoreType.DMA((5,)), *kept],
        compiler_params=PACK_PARAMS,
        name="pack",
    )(q, k, v, q_gain.reshape(1, -1), k_gain.reshape(1, -1))


def first_pass(query, key, bias_at, scores_ref, c, largest):
    s = lax.dot_general(key, query, (((1,), (1,)), ((), ())), preferred_element_type=jnp.float32)
    for t in range(key.shape[0] // TILE):
        down = slice(t * TILE, (t + 1) * TILE)
        masked = s[down].reshape(TILE // 8, 8, -1) + bias_at(t)[None]
        scores_ref[c, down] = masked.reshape(TILE, -1)
        largest = jnp.maximum(largest, jnp.max(masked, axis=0))
    return largest


def second_pass(scores_ref, c, col_max, value_t, state):
    total, mixed = state
    wide, bm = scores_ref.shape[1:]
    weights = jnp.exp2(scores_ref[c].reshape(wide // 8, 8, bm) * SCALE - col_max[None])
    total = total + jnp.sum(weights, axis=0)
    weights = weights.reshape(wide, bm).astype(BF16)
    return total, mixed + jnp.dot(value_t, weights, preferred_element_type=jnp.float32)


def over_all(largest):
    return jnp.broadcast_to(jnp.max(largest, axis=0, keepdims=True) * SCALE, largest.shape)


def divide(total, mixed):
    return (mixed / jnp.sum(total, axis=0, keepdims=True)).T.astype(BF16)


def bias_of(band, bm, live_at):
    lane = lax.broadcasted_iota(jnp.int32, (8, bm), 1)
    bias = jnp.zeros((8, bm), jnp.float32)
    for a in range(bm // band):
        dead = jnp.where(live_at(a), 0.0, MASKED).astype(jnp.float32)
        bias = jnp.where((lane >= a * band) & (lane < (a + 1) * band), dead, bias)
    return bias


def attend(query, band, key_at, value_at, key_blocks, live_at, scores_ref):
    wide, bm = scores_ref.shape[1:]

    def score(c, largest):
        def bias_at(t):
            return bias_of(band, bm, lambda a: live_at(a, c * (wide // TILE) + t))

        return first_pass(query, key_at(c), bias_at, scores_ref, c, largest)

    largest = lax.fori_loop(0, key_blocks, score, jnp.full((8, bm), MASKED, jnp.float32))
    col_max = over_all(largest)

    def mix(c, state):
        return second_pass(scores_ref, c, col_max, transposed(value_at(c)), state)

    state = jnp.zeros((8, bm), jnp.float32), jnp.zeros((HDIM, bm), jnp.float32)
    return divide(*lax.fori_loop(0, key_blocks, mix, state))


def transposed(block):
    return block.astype(jnp.float32).T.astype(BF16)


def attend_blocks(blocks, band, query_at, key_at, value_t, key_blocks, live_at, finish, scores):
    wide, bm = scores[0].shape[1:]
    empty = jnp.full((8, bm), MASKED, jnp.float32)
    nothing = jnp.zeros((8, bm), jnp.float32), jnp.zeros((HDIM, bm), jnp.float32)

    def bias_at(i, c):
        return lambda t: bias_of(band, bm, lambda a: live_at(i, a, c, t))

    def both(i, col_max, now, following):
        later = jnp.minimum(i + 1, blocks - 1)
        query = query_at(later)
        largest, state = empty, nothing
        for c in range(key_blocks):
            largest = first_pass(query, key_at(c), bias_at(later, c), following, c, largest)
            state = second_pass(now, c, col_max, value_t[:, c * wide : (c + 1) * wide], state)
        finish(i, divide(*state))
        return over_all(largest)

    largest = empty
    query = query_at(0)
    for c in range(key_blocks):
        largest = first_pass(query, key_at(c), bias_at(0, c), scores[0], c, largest)

    def pair(n, col_max):
        col_max = both(2 * n, col_max, scores[0], scores[1])
        return both(2 * n + 1, col_max, scores[1], scores[0])

    lax.fori_loop(0, blocks // 2, pair, over_all(largest))


def collect_kernel(order, rows, *refs):
    pieces, (q_out, kv_out) = refs[:-2], refs[-2:]
    me = lax.axis_index(NEAR)
    for d, piece in zip(order, pieces):
        at = pl.ds(pl.multiple_of((me ^ d) * rows, rows), rows)
        q_out[at] = piece[0]
        kv_out[:, at] = piece[1:]


def shared_kernel(order, rows, mask_ref, q_ref, own_ref, other_ref, *refs):
    outs, (value_t, mixed, *scores) = refs[: len(order)], refs[len(order) :]
    mine = lax.axis_index("inner")
    _, wide, bm = scores[0].shape
    blocks = q_ref.shape[0] // wide

    def key_at(c):
        ref = own_ref if c < blocks else other_ref
        return ref[0, c % blocks * wide : (c % blocks + 1) * wide]

    for n, ref in enumerate((own_ref, other_ref)):
        for t in range(blocks * wide // TILE):
            at = (n * blocks * wide) + t * TILE
            value_t[:, at : at + TILE] = transposed(ref[1, t * TILE : (t + 1) * TILE])

    def tile(block, inner, t):
        return (block * 2 + inner) * (wide // TILE) + t

    def finish(i, block):
        mixed[pl.ds(pl.multiple_of(i * bm, bm), bm)] = block

    attend_blocks(
        blocks,
        TILE,
        lambda i: q_ref[pl.ds(pl.multiple_of(i * bm, bm), bm)],
        key_at,
        value_t,
        2 * blocks,
        lambda i, a, c, t: mask_ref[tile(i, mine, a), tile(c % blocks, mine if c < blocks else 1 - mine, t)] != 0,
        finish,
        scores,
    )
    me = lax.axis_index(NEAR)
    for d, out in zip(order, outs):
        out[...] = mixed[pl.ds(pl.multiple_of((me ^ d) * rows, rows), rows)]


def whole_kernel(sources, mask_ref, qkv_ref, *refs):
    out_ref, value_t, *scores = refs[-4:]
    rows = qkv_ref.shape[2]
    _, wide, bm = scores[0].shape
    bands, tiles = bm // rows, wide // TILE
    for t in range(sources):
        value_t[:, t * TILE : (t + 1) * TILE] = transposed(qkv_ref[t, 2])

    def finish(i, mixed):
        out_ref[pl.ds(i * bands, bands)] = mixed.reshape(bands, rows, HDIM)

    attend_blocks(
        sources // bands,
        rows,
        lambda i: qkv_ref[pl.ds(i * bands, bands), 0].reshape(bm, HDIM),
        lambda c: qkv_ref[c * tiles : (c + 1) * tiles, 1].reshape(wide, HDIM),
        value_t,
        sources // tiles,
        lambda i, a, c, t: mask_ref[i * bands + a, c * tiles + t] != 0,
        finish,
        scores,
    )


def swap(piece, axes, d, count):
    return lax.ppermute(piece, axes, [(i, i ^ d) for i in range(count)]) if d else piece


def halved(far, near):
    order = [*range(near // 2, near), *range(near // 2)]

    def per_device(query_rows, key_rows, value_rows, q_gain, k_gain, tile_mask):
        rows, features = query_rows.shape

        def write(which, block, by_head, *outs):
            for h in range(near):
                by_head[h, which] = block[:, h * HDIM : (h + 1) * HDIM]
            for d in range(far):
                outs[-1][d, which] = block[:, (near + d) * HDIM : (near + d + 1) * HDIM]
            if which == 2:
                me = lax.axis_index(NEAR)
                for d, out in zip(order, outs):
                    out[...] = by_head[me ^ d]

        def read(*refs):
            shared, (whole, out_ref) = refs[:-2], refs[-2:]
            me = lax.axis_index(NEAR)
            for d, got in zip(order, shared):
                out_ref[:, pl.ds(pl.multiple_of((me ^ d) * HDIM, HDIM), HDIM)] = got[...]
            for d in range(far):
                out_ref[:, (near + d) * HDIM : (near + d + 1) * HDIM] = whole[d]

        *shared, whole = pack(
            write,
            [shape(3, rows, HDIM)] * near + [shape(far, 3, rows, HDIM)],
            rows,
            features,
            (query_rows, key_rows, value_rows, q_gain, k_gain),
            [pltpu.VMEM((near, 3, rows, HDIM), BF16)],
        )
        shared = [swap(piece, NEAR, d, near) for d, piece in zip(order, shared)]
        whole = exchange(whole, FAR)
        q_near, kv_near = pl.pallas_call(
            functools.partial(collect_kernel, order, rows),
            out_shape=[shape(near * rows, HDIM), shape(2, near * rows, HDIM)],
            compiler_params=PARAMS,
            name="collect",
        )(*shared)
        kv_other = lax.ppermute(kv_near, "inner", [(0, 1), (1, 0)])

        wide = 2 * TILE
        blocks = far * rows // wide
        smem, vmem = pl.BlockSpec(memory_space=pltpu.SMEM), pl.BlockSpec(memory_space=pltpu.VMEM)
        scratch = [pltpu.VMEM((HDIM, far * rows), BF16)]
        scores = [pltpu.VMEM((blocks, wide, wide), jnp.float32)] * 2
        shared = pl.pallas_call(
            functools.partial(shared_kernel, order, rows),
            in_specs=[smem] + [vmem] * 3,
            out_shape=[shape(rows, HDIM)] * near,
            scratch_shapes=scratch + [pltpu.VMEM((near * rows, HDIM), BF16)] + scores,
            compiler_params=PARAMS,
            cost_estimate=pl.CostEstimate(flops=2**32, bytes_accessed=2**21, transcendentals=0),
            name="attend_shared",
        )(tile_mask, q_near, kv_near, kv_other)
        shared = [swap(piece, NEAR, d, near) for d, piece in zip(order, shared)]

        whole = pl.pallas_call(
            functools.partial(whole_kernel, far),
            in_specs=[smem, vmem] + [pl.BlockSpec(memory_space=pl.ANY)] * near,
            out_shape=shape(far, rows, HDIM),
            scratch_shapes=scratch + scores,
            compiler_params=PARAMS,
            cost_estimate=pl.CostEstimate(flops=2**33, bytes_accessed=2**22, transcendentals=0),
            name="attend_whole",
        )(tile_mask, whole, *shared)
        return pl.pallas_call(
            read, out_shape=shape(rows, features), compiler_params=PARAMS, name="unpack"
        )(*shared, exchange(whole, FAR))

    return per_device


def gathered_kernel(outer, inner, mask_ref, q_ref, kv_ref, out_ref, scores_ref):
    i = pl.program_id(0)
    block = out_ref.shape[0] * out_ref.shape[1] * out_ref.shape[2]
    tiles = block // TILE
    q_tile = (i * inner + lax.axis_index("inner")) * tiles
    mixed = attend(
        q_ref[0, :, 0].reshape(block, HDIM),
        TILE,
        lambda c: kv_ref[lax.rem(c, inner), lax.div(c, inner), :, 1].reshape(block, HDIM),
        lambda c: kv_ref[lax.rem(c, inner), lax.div(c, inner), :, 2].reshape(block, HDIM),
        outer * inner,
        lambda a, t: mask_ref[q_tile + a, t] != 0,
        scores_ref,
    )
    out_ref[...] = mixed.reshape(out_ref.shape)


def gathered(outer, inner, n_head, near):
    width = HEADS // near * HDIM

    def per_device(query_rows, key_rows, value_rows, q_gain, k_gain, tile_mask):
        rows, features = query_rows.shape
        block = rows * n_head

        def write(which, block, packed):
            for d in range(near):
                packed[d, which] = block[:, d * width : (d + 1) * width]

        def read(got_ref, out_ref):
            for d in range(near):
                out_ref[:, d * width : (d + 1) * width] = got_ref[d]

        (packed,) = pack(
            write,
            [shape(near, 3, rows, width)],
            rows,
            features,
            (query_rows, key_rows, value_rows, q_gain, k_gain),
        )
        own = exchange(packed, NEAR).reshape(outer, n_head, 3, rows, width)
        every = lax.all_gather(own, "inner")
        mixed = pl.pallas_call(
            functools.partial(gathered_kernel, outer, inner),
            grid=(outer, HEADS // near),
            in_specs=[
                pl.BlockSpec(memory_space=pltpu.SMEM),
                pl.BlockSpec((1, n_head, 1, rows, HDIM), lambda i, h: (i, 0, 0, 0, h)),
                pl.BlockSpec((inner, outer, n_head, 3, rows, HDIM), lambda i, h: (0, 0, 0, 0, 0, h)),
            ],
            out_specs=pl.BlockSpec((1, n_head, rows, HDIM), lambda i, h: (i, 0, 0, h)),
            out_shape=shape(outer, n_head, rows, width),
            scratch_shapes=[pltpu.VMEM((outer * inner, block, block), jnp.float32)],
            compiler_params=PARAMS,
            name="attend",
        )(tile_mask, own, every)
        return pl.pallas_call(
            read, out_shape=shape(rows, features), compiler_params=PARAMS, name="unpack"
        )(exchange(mixed.reshape(near, rows, width), NEAR))

    return per_device


def solution(mesh):
    n_blk, n_head = mesh.shape["blk"], mesh.shape["head"]
    outer = max(d for d in range(1, n_blk + 1) if n_blk % d == 0 and HEADS % (n_head * d) == 0)
    inner = n_blk // outer
    near, far = outer * n_head, n_blk * n_head

    def per_device(query_rows, *others):
        in_pairs = inner == 2 and n_head == 2 and near & (near - 1) == 0
        if in_pairs and HEADS == near + far and query_rows.shape[0] == TILE:
            return halved(far, near)(query_rows, *others)
        return gathered(outer, inner, n_head, near)(query_rows, *others)

    split = P(("batch", "outer", "inner", "head"), None)
    return jax.shard_map(
        per_device,
        mesh=Mesh(
            mesh.devices.reshape(outer, inner, n_head, mesh.shape["batch"]), ("outer", "inner", "head", "batch")
        ),
        in_specs=(split, split, split, P(), P(), P()),
        out_specs=split,
        check_vma=False,
    )
```

```python
import functools

import jax
import jax.numpy as jnp
from jax import lax
from jax.experimental import pallas as pl
from jax.experimental.pallas import tpu as pltpu
from jax.sharding import Mesh, PartitionSpec as P

HEADS = 24
HDIM = 128
TILE = 128
EPS = 1e-06
MASKED = -1e30
NEAR = ("outer", "head")
FAR = ("outer", "inner", "head")
PARAMS = pltpu.CompilerParams(vmem_limit_bytes=48 * 1024 * 1024)
PACK_PARAMS = pltpu.CompilerParams(vmem_limit_bytes=61 * 1024 * 1024)
BF16 = jnp.bfloat16
SCALE = 1.4426950408889634 * HDIM ** (-0.5)


def shape(*dims):
    return jax.ShapeDtypeStruct(dims, BF16)


def exchange(x, axes):
    return lax.all_to_all(x, axes, split_axis=0, concat_axis=0, tiled=True)


def pack_kernel(write, n_out, q_hbm, k_hbm, v_hbm, qg_hbm, kg_hbm, *refs):
    outs, (q_in, k_in, v_in, qg, kg, sems, *kept) = refs[:n_out], refs[n_out:]
    outs = *kept, *outs
    copies = [
        pltpu.make_async_copy(src, dst, sems.at[n])
        for n, (src, dst) in enumerate(
            ((q_hbm, q_in), (k_hbm, k_in), (v_hbm, v_in), (qg_hbm, qg), (kg_hbm, kg))
        )
    ]
    for copy in copies:
        copy.start()

    def normalize(ref, gain):
        widened = ref[...].astype(jnp.float32)
        mean_square = jnp.mean(widened * widened, axis=-1, keepdims=True)
        return (widened * lax.rsqrt(mean_square + EPS) * gain[...]).astype(BF16)

    copies[0].wait()
    copies[3].wait()
    write(0, normalize(q_in, qg), *outs)
    copies[1].wait()
    copies[4].wait()
    write(1, normalize(k_in, kg), *outs)
    copies[2].wait()
    write(2, v_in[...], *outs)


def pack(write, out_shape, rows, features, arrays, kept=()):
    q, k, v, q_gain, k_gain = arrays
    return pl.pallas_call(
        functools.partial(pack_kernel, write, len(out_shape)),
        in_specs=[pl.BlockSpec(memory_space=pltpu.HBM)] * 5,
        out_shape=out_shape,
        scratch_shapes=[pltpu.VMEM((rows, features), BF16)] * 3
        + [pltpu.VMEM((1, features), jnp.float32)] * 2
        + [pltpu.SemaphoreType.DMA((5,)), *kept],
        compiler_params=PACK_PARAMS,
        name="pack",
    )(q, k, v, q_gain.reshape(1, -1), k_gain.reshape(1, -1))


def first_pass(query, key, bias_at, scores_ref, c, largest):
    s = lax.dot_general(key, query, (((1,), (1,)), ((), ())), preferred_element_type=jnp.float32)
    for t in range(key.shape[0] // TILE):
        down = slice(t * TILE, (t + 1) * TILE)
        masked = s[down].reshape(TILE // 8, 8, -1) + bias_at(t)[None]
        scores_ref[c, down] = masked.reshape(TILE, -1)
        largest = jnp.maximum(largest, jnp.max(masked, axis=0))
    return largest


def second_pass(scores_ref, c, col_max, value_t, state):
    total, mixed = state
    wide, bm = scores_ref.shape[1:]
    weights = jnp.exp2(scores_ref[c].reshape(wide // 8, 8, bm) * SCALE - col_max[None])
    total = total + jnp.sum(weights, axis=0)
    weights = weights.reshape(wide, bm).astype(BF16)
    return total, mixed + jnp.dot(value_t, weights, preferred_element_type=jnp.float32)


def over_all(largest):
    return jnp.broadcast_to(jnp.max(largest, axis=0, keepdims=True) * SCALE, largest.shape)


def divide(total, mixed):
    return (mixed / jnp.sum(total, axis=0, keepdims=True)).T.astype(BF16)


def bias_of(band, bm, live_at):
    lane = lax.broadcasted_iota(jnp.int32, (8, bm), 1)
    bias = jnp.zeros((8, bm), jnp.float32)
    for a in range(bm // band):
        dead = jnp.where(live_at(a), 0.0, MASKED).astype(jnp.float32)
        bias = jnp.where((lane >= a * band) & (lane < (a + 1) * band), dead, bias)
    return bias


def attend(query, band, key_at, value_at, key_blocks, live_at, scores_ref):
    wide, bm = scores_ref.shape[1:]

    def score(c, largest):
        def bias_at(t):
            return bias_of(band, bm, lambda a: live_at(a, c * (wide // TILE) + t))

        return first_pass(query, key_at(c), bias_at, scores_ref, c, largest)

    largest = lax.fori_loop(0, key_blocks, score, jnp.full((8, bm), MASKED, jnp.float32))
    col_max = over_all(largest)

    def mix(c, state):
        return second_pass(scores_ref, c, col_max, transposed(value_at(c)), state)

    state = jnp.zeros((8, bm), jnp.float32), jnp.zeros((HDIM, bm), jnp.float32)
    return divide(*lax.fori_loop(0, key_blocks, mix, state))


def transposed(block):
    return block.astype(jnp.float32).T.astype(BF16)


def attend_blocks(blocks, band, query_at, key_at, value_t, key_blocks, live_at, finish, scores):
    wide, bm = scores[0].shape[1:]
    empty = jnp.full((8, bm), MASKED, jnp.float32)
    nothing = jnp.zeros((8, bm), jnp.float32), jnp.zeros((HDIM, bm), jnp.float32)

    def bias_at(i, c):
        return lambda t: bias_of(band, bm, lambda a: live_at(i, a, c, t))

    def both(i, col_max, now, following):
        later = jnp.minimum(i + 1, blocks - 1)
        query = query_at(later)
        largest, state = empty, nothing
        for c in range(key_blocks):
            largest = first_pass(query, key_at(c), bias_at(later, c), following, c, largest)
            state = second_pass(now, c, col_max, value_t[:, c * wide : (c + 1) * wide], state)
        finish(i, divide(*state))
        return over_all(largest)

    largest = empty
    query = query_at(0)
    for c in range(key_blocks):
        largest = first_pass(query, key_at(c), bias_at(0, c), scores[0], c, largest)

    def pair(n, col_max):
        col_max = both(2 * n, col_max, scores[0], scores[1])
        return both(2 * n + 1, col_max, scores[1], scores[0])

    lax.fori_loop(0, blocks // 2, pair, over_all(largest))


def collect_kernel(order, rows, *refs):
    pieces, (q_out, kv_out) = refs[:-2], refs[-2:]
    me = lax.axis_index(NEAR)
    for d, piece in zip(order, pieces):
        at = pl.ds(pl.multiple_of((me ^ d) * rows, rows), rows)
        q_out[at] = piece[0]
        kv_out[:, at] = piece[1:]


def shared_kernel(order, rows, mask_ref, q_ref, own_ref, other_ref, *refs):
    outs, (value_t, mixed, *scores) = refs[: len(order)], refs[len(order) :]
    mine = lax.axis_index("inner")
    _, wide, bm = scores[0].shape
    blocks = q_ref.shape[0] // wide

    def key_at(c):
        ref = own_ref if c < blocks else other_ref
        return ref[0, c % blocks * wide : (c % blocks + 1) * wide]

    for n, ref in enumerate((own_ref, other_ref)):
        for t in range(blocks * wide // TILE):
            at = (n * blocks * wide) + t * TILE
            value_t[:, at : at + TILE] = transposed(ref[1, t * TILE : (t + 1) * TILE])

    def tile(block, inner, t):
        return (block * 2 + inner) * (wide // TILE) + t

    def finish(i, block):
        mixed[pl.ds(pl.multiple_of(i * bm, bm), bm)] = block

    attend_blocks(
        blocks,
        TILE,
        lambda i: q_ref[pl.ds(pl.multiple_of(i * bm, bm), bm)],
        key_at,
        value_t,
        2 * blocks,
        lambda i, a, c, t: mask_ref[tile(i, mine, a), tile(c % blocks, mine if c < blocks else 1 - mine, t)] != 0,
        finish,
        scores,
    )
    me = lax.axis_index(NEAR)
    for d, out in zip(order, outs):
        out[...] = mixed[pl.ds(pl.multiple_of((me ^ d) * rows, rows), rows)]


def whole_kernel(sources, mask_ref, qkv_ref, *refs):
    out_ref, value_t, *scores = refs[-4:]
    rows = qkv_ref.shape[2]
    _, wide, bm = scores[0].shape
    bands, tiles = bm // rows, wide // TILE
    for t in range(sources):
        value_t[:, t * TILE : (t + 1) * TILE] = transposed(qkv_ref[t, 2])

    def finish(i, mixed):
        out_ref[pl.ds(i * bands, bands)] = mixed.reshape(bands, rows, HDIM)

    attend_blocks(
        sources // bands,
        rows,
        lambda i: qkv_ref[pl.ds(i * bands, bands), 0].reshape(bm, HDIM),
        lambda c: qkv_ref[c * tiles : (c + 1) * tiles, 1].reshape(wide, HDIM),
        value_t,
        sources // tiles,
        lambda i, a, c, t: mask_ref[i * bands + a, c * tiles + t] != 0,
        finish,
        scores,
    )


def swap(piece, axes, d, count):
    return lax.ppermute(piece, axes, [(i, i ^ d) for i in range(count)]) if d else piece


def halved(far, near):
    order = [*range(near // 2, near), *range(near // 2)]

    def per_device(query_rows, key_rows, value_rows, q_gain, k_gain, tile_mask):
        rows, features = query_rows.shape

        def write(which, block, by_head, *outs):
            for h in range(near):
                by_head[h, which] = block[:, h * HDIM : (h + 1) * HDIM]
            for d in range(far):
                outs[-1][d, which] = block[:, (near + d) * HDIM : (near + d + 1) * HDIM]
            if which == 2:
                me = lax.axis_index(NEAR)
                for d, out in zip(order, outs):
                    out[...] = by_head[me ^ d]

        def read(*refs):
            shared, (whole, out_ref) = refs[:-2], refs[-2:]
            me = lax.axis_index(NEAR)
            for d, got in zip(order, shared):
                out_ref[:, pl.ds(pl.multiple_of((me ^ d) * HDIM, HDIM), HDIM)] = got[...]
            for d in range(far):
                out_ref[:, (near + d) * HDIM : (near + d + 1) * HDIM] = whole[d]

        *shared, whole = pack(
            write,
            [shape(3, rows, HDIM)] * near + [shape(far, 3, rows, HDIM)],
            rows,
            features,
            (query_rows, key_rows, value_rows, q_gain, k_gain),
            [pltpu.VMEM((near, 3, rows, HDIM), BF16)],
        )
        shared = [swap(piece, NEAR, d, near) for d, piece in zip(order, shared)]
        whole = exchange(whole, FAR)
        q_near, kv_near = pl.pallas_call(
            functools.partial(collect_kernel, order, rows),
            out_shape=[shape(near * rows, HDIM), shape(2, near * rows, HDIM)],
            compiler_params=PARAMS,
            name="collect",
        )(*shared)
        kv_other = lax.ppermute(kv_near, "inner", [(0, 1), (1, 0)])

        wide = 2 * TILE
        blocks = far * rows // wide
        smem, vmem = pl.BlockSpec(memory_space=pltpu.SMEM), pl.BlockSpec(memory_space=pltpu.VMEM)
        scratch = [pltpu.VMEM((HDIM, far * rows), BF16)]
        scores = [pltpu.VMEM((blocks, wide, wide), jnp.float32)] * 2
        shared = pl.pallas_call(
            functools.partial(shared_kernel, order, rows),
            in_specs=[smem] + [vmem] * 3,
            out_shape=[shape(rows, HDIM)] * near,
            scratch_shapes=scratch + [pltpu.VMEM((near * rows, HDIM), BF16)] + scores,
            compiler_params=PARAMS,
            cost_estimate=pl.CostEstimate(flops=2**35, bytes_accessed=2**21, transcendentals=0),
            name="attend_shared",
        )(tile_mask, q_near, kv_near, kv_other)
        shared = [swap(piece, NEAR, d, near) for d, piece in zip(order, shared)]

        whole = pl.pallas_call(
            functools.partial(whole_kernel, far),
            in_specs=[smem, vmem] + [pl.BlockSpec(memory_space=pl.ANY)] * near,
            out_shape=shape(far, rows, HDIM),
            scratch_shapes=scratch + scores,
            compiler_params=PARAMS,
            cost_estimate=pl.CostEstimate(flops=2**33, bytes_accessed=2**22, transcendentals=0),
            name="attend_whole",
        )(tile_mask, whole, *shared)
        return pl.pallas_call(
            read, out_shape=shape(rows, features), compiler_params=PARAMS, name="unpack"
        )(*shared, exchange(whole, FAR))

    return per_device


def gathered_kernel(outer, inner, mask_ref, q_ref, kv_ref, out_ref, scores_ref):
    i = pl.program_id(0)
    block = out_ref.shape[0] * out_ref.shape[1] * out_ref.shape[2]
    tiles = block // TILE
    q_tile = (i * inner + lax.axis_index("inner")) * tiles
    mixed = attend(
        q_ref[0, :, 0].reshape(block, HDIM),
        TILE,
        lambda c: kv_ref[lax.rem(c, inner), lax.div(c, inner), :, 1].reshape(block, HDIM),
        lambda c: kv_ref[lax.rem(c, inner), lax.div(c, inner), :, 2].reshape(block, HDIM),
        outer * inner,
        lambda a, t: mask_ref[q_tile + a, t] != 0,
        scores_ref,
    )
    out_ref[...] = mixed.reshape(out_ref.shape)


def gathered(outer, inner, n_head, near):
    width = HEADS // near * HDIM

    def per_device(query_rows, key_rows, value_rows, q_gain, k_gain, tile_mask):
        rows, features = query_rows.shape
        block = rows * n_head

        def write(which, block, packed):
            for d in range(near):
                packed[d, which] = block[:, d * width : (d + 1) * width]

        def read(got_ref, out_ref):
            for d in range(near):
                out_ref[:, d * width : (d + 1) * width] = got_ref[d]

        (packed,) = pack(
            write,
            [shape(near, 3, rows, width)],
            rows,
            features,
            (query_rows, key_rows, value_rows, q_gain, k_gain),
        )
        own = exchange(packed, NEAR).reshape(outer, n_head, 3, rows, width)
        every = lax.all_gather(own, "inner")
        mixed = pl.pallas_call(
            functools.partial(gathered_kernel, outer, inner),
            grid=(outer, HEADS // near),
            in_specs=[
                pl.BlockSpec(memory_space=pltpu.SMEM),
                pl.BlockSpec((1, n_head, 1, rows, HDIM), lambda i, h: (i, 0, 0, 0, h)),
                pl.BlockSpec((inner, outer, n_head, 3, rows, HDIM), lambda i, h: (0, 0, 0, 0, 0, h)),
            ],
            out_specs=pl.BlockSpec((1, n_head, rows, HDIM), lambda i, h: (i, 0, 0, h)),
            out_shape=shape(outer, n_head, rows, width),
            scratch_shapes=[pltpu.VMEM((outer * inner, block, block), jnp.float32)],
            compiler_params=PARAMS,
            name="attend",
        )(tile_mask, own, every)
        return pl.pallas_call(
            read, out_shape=shape(rows, features), compiler_params=PARAMS, name="unpack"
        )(exchange(mixed.reshape(near, rows, width), NEAR))

    return per_device


def solution(mesh):
    n_blk, n_head = mesh.shape["blk"], mesh.shape["head"]
    outer = max(d for d in range(1, n_blk + 1) if n_blk % d == 0 and HEADS % (n_head * d) == 0)
    inner = n_blk // outer
    near, far = outer * n_head, n_blk * n_head

    def per_device(query_rows, *others):
        in_pairs = inner == 2 and n_head == 2 and near & (near - 1) == 0
        if in_pairs and HEADS == near + far and query_rows.shape[0] == TILE:
            return halved(far, near)(query_rows, *others)
        return gathered(outer, inner, n_head, near)(query_rows, *others)

    split = P(("batch", "outer", "inner", "head"), None)
    return jax.shard_map(
        per_device,
        mesh=Mesh(
            mesh.devices.reshape(outer, inner, n_head, mesh.shape["batch"]), ("outer", "inner", "head", "batch")
        ),
        in_specs=(split, split, split, P(), P(), P()),
        out_specs=split,
        check_vma=False,
    )
```

```python
import functools

import jax
import jax.numpy as jnp
from jax import lax
from jax.experimental import pallas as pl
from jax.experimental.pallas import tpu as pltpu
from jax.sharding import Mesh, PartitionSpec as P

HEADS = 24
HDIM = 128
TILE = 128
EPS = 1e-06
MASKED = -1e30
NEAR = ("outer", "head")
FAR = ("outer", "inner", "head")
PARAMS = pltpu.CompilerParams(vmem_limit_bytes=48 * 1024 * 1024)
PACK_PARAMS = pltpu.CompilerParams(vmem_limit_bytes=61 * 1024 * 1024)
BF16 = jnp.bfloat16
SCALE = 1.4426950408889634 * HDIM ** (-0.5)


def shape(*dims):
    return jax.ShapeDtypeStruct(dims, BF16)


def exchange(x, axes):
    return lax.all_to_all(x, axes, split_axis=0, concat_axis=0, tiled=True)


def pack_kernel(write, n_out, q_hbm, k_hbm, v_hbm, qg_hbm, kg_hbm, *refs):
    outs, (q_in, k_in, v_in, qg, kg, sems, *kept) = refs[:n_out], refs[n_out:]
    outs = *kept, *outs
    copies = [
        pltpu.make_async_copy(src, dst, sems.at[n])
        for n, (src, dst) in enumerate(
            ((q_hbm, q_in), (k_hbm, k_in), (v_hbm, v_in), (qg_hbm, qg), (kg_hbm, kg))
        )
    ]
    for copy in copies:
        copy.start()

    def normalize(ref, gain):
        widened = ref[...].astype(jnp.float32)
        mean_square = jnp.mean(widened * widened, axis=-1, keepdims=True)
        return (widened * lax.rsqrt(mean_square + EPS) * gain[...]).astype(BF16)

    copies[0].wait()
    copies[3].wait()
    write(0, normalize(q_in, qg), *outs)
    copies[1].wait()
    copies[4].wait()
    write(1, normalize(k_in, kg), *outs)
    copies[2].wait()
    write(2, v_in[...], *outs)


def pack(write, out_shape, rows, features, arrays, kept=()):
    q, k, v, q_gain, k_gain = arrays
    return pl.pallas_call(
        functools.partial(pack_kernel, write, len(out_shape)),
        in_specs=[pl.BlockSpec(memory_space=pltpu.HBM)] * 5,
        out_shape=out_shape,
        scratch_shapes=[pltpu.VMEM((rows, features), BF16)] * 3
        + [pltpu.VMEM((1, features), jnp.float32)] * 2
        + [pltpu.SemaphoreType.DMA((5,)), *kept],
        compiler_params=PACK_PARAMS,
        name="pack",
    )(q, k, v, q_gain.reshape(1, -1), k_gain.reshape(1, -1))


def first_pass(query, key, bias_at, scores_ref, c, largest):
    s = lax.dot_general(key, query, (((1,), (1,)), ((), ())), preferred_element_type=jnp.float32)
    for t in range(key.shape[0] // TILE):
        down = slice(t * TILE, (t + 1) * TILE)
        masked = s[down].reshape(TILE // 8, 8, -1) + bias_at(t)[None]
        scores_ref[c, down] = masked.reshape(TILE, -1)
        largest = jnp.maximum(largest, jnp.max(masked, axis=0))
    return largest


def second_pass(scores_ref, c, col_max, value_t, state):
    total, mixed = state
    wide, bm = scores_ref.shape[1:]
    weights = jnp.exp2(scores_ref[c].reshape(wide // 8, 8, bm) * SCALE - col_max[None])
    total = total + jnp.sum(weights, axis=0)
    weights = weights.reshape(wide, bm).astype(BF16)
    return total, mixed + jnp.dot(value_t, weights, preferred_element_type=jnp.float32)


def over_all(largest):
    return jnp.broadcast_to(jnp.max(largest, axis=0, keepdims=True) * SCALE, largest.shape)


def divide(total, mixed):
    return (mixed / jnp.sum(total, axis=0, keepdims=True)).T.astype(BF16)


def bias_of(band, bm, live_at):
    lane = lax.broadcasted_iota(jnp.int32, (8, bm), 1)
    bias = jnp.zeros((8, bm), jnp.float32)
    for a in range(bm // band):
        dead = jnp.where(live_at(a), 0.0, MASKED).astype(jnp.float32)
        bias = jnp.where((lane >= a * band) & (lane < (a + 1) * band), dead, bias)
    return bias


def attend(query, band, key_at, value_at, key_blocks, live_at, scores_ref):
    wide, bm = scores_ref.shape[1:]

    def score(c, largest):
        def bias_at(t):
            return bias_of(band, bm, lambda a: live_at(a, c * (wide // TILE) + t))

        return first_pass(query, key_at(c), bias_at, scores_ref, c, largest)

    largest = lax.fori_loop(0, key_blocks, score, jnp.full((8, bm), MASKED, jnp.float32))
    col_max = over_all(largest)

    def mix(c, state):
        return second_pass(scores_ref, c, col_max, transposed(value_at(c)), state)

    state = jnp.zeros((8, bm), jnp.float32), jnp.zeros((HDIM, bm), jnp.float32)
    return divide(*lax.fori_loop(0, key_blocks, mix, state))


def transposed(block):
    return block.astype(jnp.float32).T.astype(BF16)


def attend_blocks(blocks, band, query_at, key_at, value_t, key_blocks, live_at, finish, scores):
    wide, bm = scores[0].shape[1:]
    empty = jnp.full((8, bm), MASKED, jnp.float32)
    nothing = jnp.zeros((8, bm), jnp.float32), jnp.zeros((HDIM, bm), jnp.float32)

    def bias_at(i, c):
        return lambda t: bias_of(band, bm, lambda a: live_at(i, a, c, t))

    def both(i, col_max, now, following):
        later = jnp.minimum(i + 1, blocks - 1)
        query = query_at(later)
        largest, state = empty, nothing
        for c in range(key_blocks):
            largest = first_pass(query, key_at(c), bias_at(later, c), following, c, largest)
            state = second_pass(now, c, col_max, value_t[:, c * wide : (c + 1) * wide], state)
        finish(i, divide(*state))
        return over_all(largest)

    largest = empty
    query = query_at(0)
    for c in range(key_blocks):
        largest = first_pass(query, key_at(c), bias_at(0, c), scores[0], c, largest)

    def pair(n, col_max):
        col_max = both(2 * n, col_max, scores[0], scores[1])
        return both(2 * n + 1, col_max, scores[1], scores[0])

    lax.fori_loop(0, blocks // 2, pair, over_all(largest))


def collect_kernel(order, rows, *refs):
    pieces, (q_out, kv_out) = refs[:-2], refs[-2:]
    me = lax.axis_index(NEAR)
    for d, piece in zip(order, pieces):
        at = pl.ds(pl.multiple_of((me ^ d) * rows, rows), rows)
        q_out[at] = piece[0]
        kv_out[:, at] = piece[1:]


def shared_kernel(order, rows, mask_ref, q_ref, own_ref, other_ref, *refs):
    outs, (value_t, mixed, *scores) = refs[: len(order)], refs[len(order) :]
    mine = lax.axis_index("inner")
    _, wide, bm = scores[0].shape
    blocks = q_ref.shape[0] // wide

    def key_at(c):
        ref = own_ref if c < blocks else other_ref
        return ref[0, c % blocks * wide : (c % blocks + 1) * wide]

    for n, ref in enumerate((own_ref, other_ref)):
        for t in range(blocks * wide // TILE):
            at = (n * blocks * wide) + t * TILE
            value_t[:, at : at + TILE] = transposed(ref[1, t * TILE : (t + 1) * TILE])

    def tile(block, inner, t):
        return (block * 2 + inner) * (wide // TILE) + t

    def finish(i, block):
        mixed[pl.ds(pl.multiple_of(i * bm, bm), bm)] = block

    attend_blocks(
        blocks,
        TILE,
        lambda i: q_ref[pl.ds(pl.multiple_of(i * bm, bm), bm)],
        key_at,
        value_t,
        2 * blocks,
        lambda i, a, c, t: mask_ref[tile(i, mine, a), tile(c % blocks, mine if c < blocks else 1 - mine, t)] != 0,
        finish,
        scores,
    )
    me = lax.axis_index(NEAR)
    for d, out in zip(order, outs):
        out[...] = mixed[pl.ds(pl.multiple_of((me ^ d) * rows, rows), rows)]


def whole_kernel(sources, mask_ref, qkv_ref, *refs):
    out_ref, value_t, *scores = refs[-4:]
    rows = qkv_ref.shape[2]
    _, wide, bm = scores[0].shape
    bands, tiles = bm // rows, wide // TILE
    for t in range(sources):
        value_t[:, t * TILE : (t + 1) * TILE] = transposed(qkv_ref[t, 2])

    def finish(i, mixed):
        out_ref[pl.ds(i * bands, bands)] = mixed.reshape(bands, rows, HDIM)

    attend_blocks(
        sources // bands,
        rows,
        lambda i: qkv_ref[pl.ds(i * bands, bands), 0].reshape(bm, HDIM),
        lambda c: qkv_ref[c * tiles : (c + 1) * tiles, 1].reshape(wide, HDIM),
        value_t,
        sources // tiles,
        lambda i, a, c, t: mask_ref[i * bands + a, c * tiles + t] != 0,
        finish,
        scores,
    )


def swap(piece, axes, d, count):
    return lax.ppermute(piece, axes, [(i, i ^ d) for i in range(count)]) if d else piece


def halved(far, near):
    order = [*range(near // 2, near), *range(near // 2)]

    def per_device(query_rows, key_rows, value_rows, q_gain, k_gain, tile_mask):
        rows, features = query_rows.shape

        def write(which, block, by_head, *outs):
            for h in range(near):
                by_head[h, which] = block[:, h * HDIM : (h + 1) * HDIM]
            for d in range(far):
                outs[-1][d, which] = block[:, (near + d) * HDIM : (near + d + 1) * HDIM]
            if which == 2:
                me = lax.axis_index(NEAR)
                for d, out in zip(order, outs):
                    out[...] = by_head[me ^ d]

        def read(*refs):
            shared, (whole, out_ref) = refs[:-2], refs[-2:]
            me = lax.axis_index(NEAR)
            for d, got in zip(order, shared):
                out_ref[:, pl.ds(pl.multiple_of((me ^ d) * HDIM, HDIM), HDIM)] = got[...]
            for d in range(far):
                out_ref[:, (near + d) * HDIM : (near + d + 1) * HDIM] = whole[d]

        *shared, whole = pack(
            write,
            [shape(3, rows, HDIM)] * near + [shape(far, 3, rows, HDIM)],
            rows,
            features,
            (query_rows, key_rows, value_rows, q_gain, k_gain),
            [pltpu.VMEM((near, 3, rows, HDIM), BF16)],
        )
        shared = [swap(piece, NEAR, d, near) for d, piece in zip(order, shared)]
        whole = exchange(whole, FAR)
        q_near, kv_near = pl.pallas_call(
            functools.partial(collect_kernel, order, rows),
            out_shape=[shape(near * rows, HDIM), shape(2, near * rows, HDIM)],
            compiler_params=PARAMS,
            name="collect",
        )(*shared)
        kv_other = lax.ppermute(kv_near, "inner", [(0, 1), (1, 0)])

        wide = 2 * TILE
        blocks = far * rows // wide
        smem, vmem = pl.BlockSpec(memory_space=pltpu.SMEM), pl.BlockSpec(memory_space=pltpu.VMEM)
        scratch = [pltpu.VMEM((HDIM, far * rows), BF16)]
        scores = [pltpu.VMEM((blocks, wide, wide), jnp.float32)] * 2
        shared = pl.pallas_call(
            functools.partial(shared_kernel, order, rows),
            in_specs=[smem] + [vmem] * 3,
            out_shape=[shape(rows, HDIM)] * near,
            scratch_shapes=scratch + [pltpu.VMEM((near * rows, HDIM), BF16)] + scores,
            compiler_params=PARAMS,
            cost_estimate=pl.CostEstimate(flops=21 * 2**30, bytes_accessed=2**21, transcendentals=0),
            name="attend_shared",
        )(tile_mask, q_near, kv_near, kv_other)
        shared = [swap(piece, NEAR, d, near) for d, piece in zip(order, shared)]

        whole = pl.pallas_call(
            functools.partial(whole_kernel, far),
            in_specs=[smem, vmem] + [pl.BlockSpec(memory_space=pl.ANY)] * near,
            out_shape=shape(far, rows, HDIM),
            scratch_shapes=scratch + scores,
            compiler_params=PARAMS,
            cost_estimate=pl.CostEstimate(flops=2**33, bytes_accessed=2**22, transcendentals=0),
            name="attend_whole",
        )(tile_mask, whole, *shared)
        return pl.pallas_call(
            read, out_shape=shape(rows, features), compiler_params=PARAMS, name="unpack"
        )(*shared, exchange(whole, FAR))

    return per_device


def gathered_kernel(outer, inner, mask_ref, q_ref, kv_ref, out_ref, scores_ref):
    i = pl.program_id(0)
    block = out_ref.shape[0] * out_ref.shape[1] * out_ref.shape[2]
    tiles = block // TILE
    q_tile = (i * inner + lax.axis_index("inner")) * tiles
    mixed = attend(
        q_ref[0, :, 0].reshape(block, HDIM),
        TILE,
        lambda c: kv_ref[lax.rem(c, inner), lax.div(c, inner), :, 1].reshape(block, HDIM),
        lambda c: kv_ref[lax.rem(c, inner), lax.div(c, inner), :, 2].reshape(block, HDIM),
        outer * inner,
        lambda a, t: mask_ref[q_tile + a, t] != 0,
        scores_ref,
    )
    out_ref[...] = mixed.reshape(out_ref.shape)


def gathered(outer, inner, n_head, near):
    width = HEADS // near * HDIM

    def per_device(query_rows, key_rows, value_rows, q_gain, k_gain, tile_mask):
        rows, features = query_rows.shape
        block = rows * n_head

        def write(which, block, packed):
            for d in range(near):
                packed[d, which] = block[:, d * width : (d + 1) * width]

        def read(got_ref, out_ref):
            for d in range(near):
                out_ref[:, d * width : (d + 1) * width] = got_ref[d]

        (packed,) = pack(
            write,
            [shape(near, 3, rows, width)],
            rows,
            features,
            (query_rows, key_rows, value_rows, q_gain, k_gain),
        )
        own = exchange(packed, NEAR).reshape(outer, n_head, 3, rows, width)
        every = lax.all_gather(own, "inner")
        mixed = pl.pallas_call(
            functools.partial(gathered_kernel, outer, inner),
            grid=(outer, HEADS // near),
            in_specs=[
                pl.BlockSpec(memory_space=pltpu.SMEM),
                pl.BlockSpec((1, n_head, 1, rows, HDIM), lambda i, h: (i, 0, 0, 0, h)),
                pl.BlockSpec((inner, outer, n_head, 3, rows, HDIM), lambda i, h: (0, 0, 0, 0, 0, h)),
            ],
            out_specs=pl.BlockSpec((1, n_head, rows, HDIM), lambda i, h: (i, 0, 0, h)),
            out_shape=shape(outer, n_head, rows, width),
            scratch_shapes=[pltpu.VMEM((outer * inner, block, block), jnp.float32)],
            compiler_params=PARAMS,
            name="attend",
        )(tile_mask, own, every)
        return pl.pallas_call(
            read, out_shape=shape(rows, features), compiler_params=PARAMS, name="unpack"
        )(exchange(mixed.reshape(near, rows, width), NEAR))

    return per_device


def solution(mesh):
    n_blk, n_head = mesh.shape["blk"], mesh.shape["head"]
    outer = max(d for d in range(1, n_blk + 1) if n_blk % d == 0 and HEADS % (n_head * d) == 0)
    inner = n_blk // outer
    near, far = outer * n_head, n_blk * n_head

    def per_device(query_rows, *others):
        in_pairs = inner == 2 and n_head == 2 and near & (near - 1) == 0
        if in_pairs and HEADS == near + far and query_rows.shape[0] == TILE:
            return halved(far, near)(query_rows, *others)
        return gathered(outer, inner, n_head, near)(query_rows, *others)

    split = P(("batch", "outer", "inner", "head"), None)
    return jax.shard_map(
        per_device,
        mesh=Mesh(
            mesh.devices.reshape(outer, inner, n_head, mesh.shape["batch"]), ("outer", "inner", "head", "batch")
        ),
        in_specs=(split, split, split, P(), P(), P()),
        out_specs=split,
        check_vma=False,
    )
```

```python
import functools

import jax
import jax.numpy as jnp
from jax import lax
from jax.experimental import pallas as pl
from jax.experimental.pallas import tpu as pltpu
from jax.sharding import Mesh, PartitionSpec as P

HEADS = 24
HDIM = 128
TILE = 128
EPS = 1e-06
MASKED = -1e30
NEAR = ("outer", "head")
FAR = ("outer", "inner", "head")
PARAMS = pltpu.CompilerParams(vmem_limit_bytes=48 * 1024 * 1024)
PACK_PARAMS = pltpu.CompilerParams(vmem_limit_bytes=61 * 1024 * 1024)
BF16 = jnp.bfloat16
SCALE = 1.4426950408889634 * HDIM ** (-0.5)


def shape(*dims):
    return jax.ShapeDtypeStruct(dims, BF16)


def exchange(x, axes):
    return lax.all_to_all(x, axes, split_axis=0, concat_axis=0, tiled=True)


def pack_kernel(write, n_out, q_hbm, k_hbm, v_hbm, qg_hbm, kg_hbm, *refs):
    outs, (q_in, k_in, v_in, qg, kg, sems, *kept) = refs[:n_out], refs[n_out:]
    outs = *kept, *outs
    copies = [
        pltpu.make_async_copy(src, dst, sems.at[n])
        for n, (src, dst) in enumerate(
            ((q_hbm, q_in), (k_hbm, k_in), (v_hbm, v_in), (qg_hbm, qg), (kg_hbm, kg))
        )
    ]
    for copy in copies:
        copy.start()

    def normalize(ref, gain):
        widened = ref[...].astype(jnp.float32)
        mean_square = jnp.mean(widened * widened, axis=-1, keepdims=True)
        return (widened * lax.rsqrt(mean_square + EPS) * gain[...]).astype(BF16)

    copies[0].wait()
    copies[3].wait()
    write(0, normalize(q_in, qg), *outs)
    copies[1].wait()
    copies[4].wait()
    write(1, normalize(k_in, kg), *outs)
    copies[2].wait()
    write(2, v_in[...], *outs)


def pack(write, out_shape, rows, features, arrays, kept=()):
    q, k, v, q_gain, k_gain = arrays
    return pl.pallas_call(
        functools.partial(pack_kernel, write, len(out_shape)),
        in_specs=[pl.BlockSpec(memory_space=pltpu.HBM)] * 5,
        out_shape=out_shape,
        scratch_shapes=[pltpu.VMEM((rows, features), BF16)] * 3
        + [pltpu.VMEM((1, features), jnp.float32)] * 2
        + [pltpu.SemaphoreType.DMA((5,)), *kept],
        compiler_params=PACK_PARAMS,
        name="pack",
    )(q, k, v, q_gain.reshape(1, -1), k_gain.reshape(1, -1))


def first_pass(query, key, bias_at, scores_ref, c, largest):
    s = lax.dot_general(key, query, (((1,), (1,)), ((), ())), preferred_element_type=jnp.float32)
    for t in range(key.shape[0] // TILE):
        down = slice(t * TILE, (t + 1) * TILE)
        masked = s[down].reshape(TILE // 8, 8, -1) + bias_at(t)[None]
        scores_ref[c, down] = masked.reshape(TILE, -1)
        largest = jnp.maximum(largest, jnp.max(masked, axis=0))
    return largest


def second_pass(scores_ref, c, col_max, value_t, state):
    total, mixed = state
    wide, bm = scores_ref.shape[1:]
    weights = jnp.exp2(scores_ref[c].reshape(wide // 8, 8, bm) * SCALE - col_max[None])
    total = total + jnp.sum(weights, axis=0)
    weights = weights.reshape(wide, bm).astype(BF16)
    return total, mixed + jnp.dot(value_t, weights, preferred_element_type=jnp.float32)


def over_all(largest):
    return jnp.broadcast_to(jnp.max(largest, axis=0, keepdims=True) * SCALE, largest.shape)


def divide(total, mixed):
    return (mixed / jnp.sum(total, axis=0, keepdims=True)).T.astype(BF16)


def bias_of(band, bm, live_at):
    lane = lax.broadcasted_iota(jnp.int32, (8, bm), 1)
    bias = jnp.zeros((8, bm), jnp.float32)
    for a in range(bm // band):
        dead = jnp.where(live_at(a), 0.0, MASKED).astype(jnp.float32)
        bias = jnp.where((lane >= a * band) & (lane < (a + 1) * band), dead, bias)
    return bias


def attend(query, band, key_at, value_at, key_blocks, live_at, scores_ref):
    wide, bm = scores_ref.shape[1:]

    def score(c, largest):
        def bias_at(t):
            return bias_of(band, bm, lambda a: live_at(a, c * (wide // TILE) + t))

        return first_pass(query, key_at(c), bias_at, scores_ref, c, largest)

    largest = lax.fori_loop(0, key_blocks, score, jnp.full((8, bm), MASKED, jnp.float32))
    col_max = over_all(largest)

    def mix(c, state):
        return second_pass(scores_ref, c, col_max, transposed(value_at(c)), state)

    state = jnp.zeros((8, bm), jnp.float32), jnp.zeros((HDIM, bm), jnp.float32)
    return divide(*lax.fori_loop(0, key_blocks, mix, state))


def transposed(block):
    return block.astype(jnp.float32).T.astype(BF16)


def attend_blocks(blocks, band, query_at, key_at, value_t, key_blocks, live_at, finish, scores):
    wide, bm = scores[0].shape[1:]
    empty = jnp.full((8, bm), MASKED, jnp.float32)
    nothing = jnp.zeros((8, bm), jnp.float32), jnp.zeros((HDIM, bm), jnp.float32)

    def bias_at(i, c):
        return lambda t: bias_of(band, bm, lambda a: live_at(i, a, c, t))

    def both(i, col_max, now, following):
        later = jnp.minimum(i + 1, blocks - 1)
        query = query_at(later)
        largest, state = empty, nothing
        for c in range(key_blocks):
            largest = first_pass(query, key_at(c), bias_at(later, c), following, c, largest)
            state = second_pass(now, c, col_max, value_t[:, c * wide : (c + 1) * wide], state)
        finish(i, divide(*state))
        return over_all(largest)

    largest = empty
    query = query_at(0)
    for c in range(key_blocks):
        largest = first_pass(query, key_at(c), bias_at(0, c), scores[0], c, largest)

    def pair(n, col_max):
        col_max = both(2 * n, col_max, scores[0], scores[1])
        return both(2 * n + 1, col_max, scores[1], scores[0])

    lax.fori_loop(0, blocks // 2, pair, over_all(largest))


def collect_kernel(order, rows, *refs):
    pieces, (q_out, kv_out) = refs[:-2], refs[-2:]
    me = lax.axis_index(NEAR)
    for d, piece in zip(order, pieces):
        at = pl.ds(pl.multiple_of((me ^ d) * rows, rows), rows)
        q_out[at] = piece[0]
        kv_out[:, at] = piece[1:]


def shared_kernel(order, rows, mask_ref, q_ref, own_ref, other_ref, *refs):
    outs, (value_t, mixed, *scores) = refs[: len(order)], refs[len(order) :]
    mine = lax.axis_index("inner")
    _, wide, bm = scores[0].shape
    blocks = q_ref.shape[0] // wide

    def key_at(c):
        ref = own_ref if c < blocks else other_ref
        return ref[0, c % blocks * wide : (c % blocks + 1) * wide]

    for n, ref in enumerate((own_ref, other_ref)):
        for t in range(blocks * wide // TILE):
            at = (n * blocks * wide) + t * TILE
            value_t[:, at : at + TILE] = transposed(ref[1, t * TILE : (t + 1) * TILE])

    def tile(block, inner, t):
        return (block * 2 + inner) * (wide // TILE) + t

    def finish(i, block):
        mixed[pl.ds(pl.multiple_of(i * bm, bm), bm)] = block

    attend_blocks(
        blocks,
        TILE,
        lambda i: q_ref[pl.ds(pl.multiple_of(i * bm, bm), bm)],
        key_at,
        value_t,
        2 * blocks,
        lambda i, a, c, t: mask_ref[tile(i, mine, a), tile(c % blocks, mine if c < blocks else 1 - mine, t)] != 0,
        finish,
        scores,
    )
    me = lax.axis_index(NEAR)
    for d, out in zip(order, outs):
        out[...] = mixed[pl.ds(pl.multiple_of((me ^ d) * rows, rows), rows)]


def whole_kernel(sources, mask_ref, qkv_ref, *refs):
    out_ref, value_t, *scores = refs[-4:]
    rows = qkv_ref.shape[2]
    _, wide, bm = scores[0].shape
    bands, tiles = bm // rows, wide // TILE
    for t in range(sources):
        value_t[:, t * TILE : (t + 1) * TILE] = transposed(qkv_ref[t, 2])

    def finish(i, mixed):
        out_ref[pl.ds(i * bands, bands)] = mixed.reshape(bands, rows, HDIM)

    attend_blocks(
        sources // bands,
        rows,
        lambda i: qkv_ref[pl.ds(i * bands, bands), 0].reshape(bm, HDIM),
        lambda c: qkv_ref[c * tiles : (c + 1) * tiles, 1].reshape(wide, HDIM),
        value_t,
        sources // tiles,
        lambda i, a, c, t: mask_ref[i * bands + a, c * tiles + t] != 0,
        finish,
        scores,
    )


def swap(piece, axes, d, count):
    return lax.ppermute(piece, axes, [(i, i ^ d) for i in range(count)]) if d else piece


def halved(far, near):
    order = [*range(near // 2, near), *range(near // 2)]

    def per_device(query_rows, key_rows, value_rows, q_gain, k_gain, tile_mask):
        rows, features = query_rows.shape

        def write(which, block, by_head, *outs):
            for h in range(near):
                by_head[h, which] = block[:, h * HDIM : (h + 1) * HDIM]
            for d in range(far):
                outs[-1][d, which] = block[:, (near + d) * HDIM : (near + d + 1) * HDIM]
            if which == 2:
                me = lax.axis_index(NEAR)
                for d, out in zip(order, outs):
                    out[...] = by_head[me ^ d]

        def read(*refs):
            shared, (whole, out_ref) = refs[:-2], refs[-2:]
            me = lax.axis_index(NEAR)
            for d, got in zip(order, shared):
                out_ref[:, pl.ds(pl.multiple_of((me ^ d) * HDIM, HDIM), HDIM)] = got[...]
            for d in range(far):
                out_ref[:, (near + d) * HDIM : (near + d + 1) * HDIM] = whole[d]

        *shared, whole = pack(
            write,
            [shape(3, rows, HDIM)] * near + [shape(far, 3, rows, HDIM)],
            rows,
            features,
            (query_rows, key_rows, value_rows, q_gain, k_gain),
            [pltpu.VMEM((near, 3, rows, HDIM), BF16)],
        )
        shared = [swap(piece, NEAR, d, near) for d, piece in zip(order, shared)]
        whole = exchange(whole, FAR)
        q_near, kv_near = pl.pallas_call(
            functools.partial(collect_kernel, order, rows),
            out_shape=[shape(near * rows, HDIM), shape(2, near * rows, HDIM)],
            compiler_params=PARAMS,
            name="collect",
        )(*shared)
        kv_other = lax.ppermute(kv_near, "inner", [(0, 1), (1, 0)])

        wide = 2 * TILE
        blocks = far * rows // wide
        smem, vmem = pl.BlockSpec(memory_space=pltpu.SMEM), pl.BlockSpec(memory_space=pltpu.VMEM)
        scratch = [pltpu.VMEM((HDIM, far * rows), BF16)]
        scores = [pltpu.VMEM((blocks, wide, wide), jnp.float32)] * 2
        shared = pl.pallas_call(
            functools.partial(shared_kernel, order, rows),
            in_specs=[smem] + [vmem] * 3,
            out_shape=[shape(rows, HDIM)] * near,
            scratch_shapes=scratch + [pltpu.VMEM((near * rows, HDIM), BF16)] + scores,
            compiler_params=PARAMS,
            cost_estimate=pl.CostEstimate(flops=27 * 2**30, bytes_accessed=2**21, transcendentals=0),
            name="attend_shared",
        )(tile_mask, q_near, kv_near, kv_other)
        shared = [swap(piece, NEAR, d, near) for d, piece in zip(order, shared)]

        whole = pl.pallas_call(
            functools.partial(whole_kernel, far),
            in_specs=[smem, vmem] + [pl.BlockSpec(memory_space=pl.ANY)] * near,
            out_shape=shape(far, rows, HDIM),
            scratch_shapes=scratch + scores,
            compiler_params=PARAMS,
            cost_estimate=pl.CostEstimate(flops=2**33, bytes_accessed=2**22, transcendentals=0),
            name="attend_whole",
        )(tile_mask, whole, *shared)
        return pl.pallas_call(
            read, out_shape=shape(rows, features), compiler_params=PARAMS, name="unpack"
        )(*shared, exchange(whole, FAR))

    return per_device


def gathered_kernel(outer, inner, mask_ref, q_ref, kv_ref, out_ref, scores_ref):
    i = pl.program_id(0)
    block = out_ref.shape[0] * out_ref.shape[1] * out_ref.shape[2]
    tiles = block // TILE
    q_tile = (i * inner + lax.axis_index("inner")) * tiles
    mixed = attend(
        q_ref[0, :, 0].reshape(block, HDIM),
        TILE,
        lambda c: kv_ref[lax.rem(c, inner), lax.div(c, inner), :, 1].reshape(block, HDIM),
        lambda c: kv_ref[lax.rem(c, inner), lax.div(c, inner), :, 2].reshape(block, HDIM),
        outer * inner,
        lambda a, t: mask_ref[q_tile + a, t] != 0,
        scores_ref,
    )
    out_ref[...] = mixed.reshape(out_ref.shape)


def gathered(outer, inner, n_head, near):
    width = HEADS // near * HDIM

    def per_device(query_rows, key_rows, value_rows, q_gain, k_gain, tile_mask):
        rows, features = query_rows.shape
        block = rows * n_head

        def write(which, block, packed):
            for d in range(near):
                packed[d, which] = block[:, d * width : (d + 1) * width]

        def read(got_ref, out_ref):
            for d in range(near):
                out_ref[:, d * width : (d + 1) * width] = got_ref[d]

        (packed,) = pack(
            write,
            [shape(near, 3, rows, width)],
            rows,
            features,
            (query_rows, key_rows, value_rows, q_gain, k_gain),
        )
        own = exchange(packed, NEAR).reshape(outer, n_head, 3, rows, width)
        every = lax.all_gather(own, "inner")
        mixed = pl.pallas_call(
            functools.partial(gathered_kernel, outer, inner),
            grid=(outer, HEADS // near),
            in_specs=[
                pl.BlockSpec(memory_space=pltpu.SMEM),
                pl.BlockSpec((1, n_head, 1, rows, HDIM), lambda i, h: (i, 0, 0, 0, h)),
                pl.BlockSpec((inner, outer, n_head, 3, rows, HDIM), lambda i, h: (0, 0, 0, 0, 0, h)),
            ],
            out_specs=pl.BlockSpec((1, n_head, rows, HDIM), lambda i, h: (i, 0, 0, h)),
            out_shape=shape(outer, n_head, rows, width),
            scratch_shapes=[pltpu.VMEM((outer * inner, block, block), jnp.float32)],
            compiler_params=PARAMS,
            name="attend",
        )(tile_mask, own, every)
        return pl.pallas_call(
            read, out_shape=shape(rows, features), compiler_params=PARAMS, name="unpack"
        )(exchange(mixed.reshape(near, rows, width), NEAR))

    return per_device


def solution(mesh):
    n_blk, n_head = mesh.shape["blk"], mesh.shape["head"]
    outer = max(d for d in range(1, n_blk + 1) if n_blk % d == 0 and HEADS % (n_head * d) == 0)
    inner = n_blk // outer
    near, far = outer * n_head, n_blk * n_head

    def per_device(query_rows, *others):
        in_pairs = inner == 2 and n_head == 2 and near & (near - 1) == 0
        if in_pairs and HEADS == near + far and query_rows.shape[0] == TILE:
            return halved(far, near)(query_rows, *others)
        return gathered(outer, inner, n_head, near)(query_rows, *others)

    split = P(("batch", "outer", "inner", "head"), None)
    return jax.shard_map(
        per_device,
        mesh=Mesh(
            mesh.devices.reshape(outer, inner, n_head, mesh.shape["batch"]), ("outer", "inner", "head", "batch")
        ),
        in_specs=(split, split, split, P(), P(), P()),
        out_specs=split,
        check_vma=False,
    )
```

```python
import functools

import jax
import jax.numpy as jnp
from jax import lax
from jax.experimental import pallas as pl
from jax.experimental.pallas import tpu as pltpu
from jax.sharding import Mesh, PartitionSpec as P

HEADS = 24
HDIM = 128
TILE = 128
EPS = 1e-06
MASKED = -1e30
NEAR = ("outer", "head")
FAR = ("outer", "inner", "head")
PARAMS = pltpu.CompilerParams(vmem_limit_bytes=48 * 1024 * 1024)
PACK_PARAMS = pltpu.CompilerParams(vmem_limit_bytes=61 * 1024 * 1024)
BF16 = jnp.bfloat16
SCALE = 1.4426950408889634 * HDIM ** (-0.5)


def shape(*dims):
    return jax.ShapeDtypeStruct(dims, BF16)


def exchange(x, axes):
    return lax.all_to_all(x, axes, split_axis=0, concat_axis=0, tiled=True)


def pack_kernel(write, n_out, q_hbm, k_hbm, v_hbm, qg_hbm, kg_hbm, *refs):
    outs, (q_in, k_in, v_in, qg, kg, sems, *kept) = refs[:n_out], refs[n_out:]
    outs = *kept, *outs
    copies = [
        pltpu.make_async_copy(src, dst, sems.at[n])
        for n, (src, dst) in enumerate(
            ((q_hbm, q_in), (k_hbm, k_in), (v_hbm, v_in), (qg_hbm, qg), (kg_hbm, kg))
        )
    ]
    for copy in copies:
        copy.start()

    def normalize(ref, gain):
        widened = ref[...].astype(jnp.float32)
        mean_square = jnp.mean(widened * widened, axis=-1, keepdims=True)
        return (widened * lax.rsqrt(mean_square + EPS) * gain[...]).astype(BF16)

    copies[0].wait()
    copies[3].wait()
    write(0, normalize(q_in, qg), *outs)
    copies[1].wait()
    copies[4].wait()
    write(1, normalize(k_in, kg), *outs)
    copies[2].wait()
    write(2, v_in[...], *outs)


def pack(write, out_shape, rows, features, arrays, kept=()):
    q, k, v, q_gain, k_gain = arrays
    return pl.pallas_call(
        functools.partial(pack_kernel, write, len(out_shape)),
        in_specs=[pl.BlockSpec(memory_space=pltpu.HBM)] * 5,
        out_shape=out_shape,
        scratch_shapes=[pltpu.VMEM((rows, features), BF16)] * 3
        + [pltpu.VMEM((1, features), jnp.float32)] * 2
        + [pltpu.SemaphoreType.DMA((5,)), *kept],
        compiler_params=PACK_PARAMS,
        name="pack",
    )(q, k, v, q_gain.reshape(1, -1), k_gain.reshape(1, -1))


def first_pass(query, key, bias_at, scores_ref, c, largest):
    s = lax.dot_general(key, query, (((1,), (1,)), ((), ())), preferred_element_type=jnp.float32)
    for t in range(key.shape[0] // TILE):
        down = slice(t * TILE, (t + 1) * TILE)
        masked = s[down].reshape(TILE // 8, 8, -1) + bias_at(t)[None]
        scores_ref[c, down] = masked.reshape(TILE, -1)
        largest = jnp.maximum(largest, jnp.max(masked, axis=0))
    return largest


def second_pass(scores_ref, c, col_max, value_t, state):
    total, mixed = state
    wide, bm = scores_ref.shape[1:]
    weights = jnp.exp2(scores_ref[c].reshape(wide // 8, 8, bm) * SCALE - col_max[None])
    total = total + jnp.sum(weights, axis=0)
    weights = weights.reshape(wide, bm).astype(BF16)
    return total, mixed + jnp.dot(value_t, weights, preferred_element_type=jnp.float32)


def over_all(largest):
    return jnp.broadcast_to(jnp.max(largest, axis=0, keepdims=True) * SCALE, largest.shape)


def divide(total, mixed):
    return (mixed / jnp.sum(total, axis=0, keepdims=True)).T.astype(BF16)


def bias_of(band, bm, live_at):
    lane = lax.broadcasted_iota(jnp.int32, (8, bm), 1)
    bias = jnp.zeros((8, bm), jnp.float32)
    for a in range(bm // band):
        dead = jnp.where(live_at(a), 0.0, MASKED).astype(jnp.float32)
        bias = jnp.where((lane >= a * band) & (lane < (a + 1) * band), dead, bias)
    return bias


def attend(query, band, key_at, value_at, key_blocks, live_at, scores_ref):
    wide, bm = scores_ref.shape[1:]

    def score(c, largest):
        def bias_at(t):
            return bias_of(band, bm, lambda a: live_at(a, c * (wide // TILE) + t))

        return first_pass(query, key_at(c), bias_at, scores_ref, c, largest)

    largest = lax.fori_loop(0, key_blocks, score, jnp.full((8, bm), MASKED, jnp.float32))
    col_max = over_all(largest)

    def mix(c, state):
        return second_pass(scores_ref, c, col_max, transposed(value_at(c)), state)

    state = jnp.zeros((8, bm), jnp.float32), jnp.zeros((HDIM, bm), jnp.float32)
    return divide(*lax.fori_loop(0, key_blocks, mix, state))


def transposed(block):
    return block.astype(jnp.float32).T.astype(BF16)


def attend_blocks(blocks, band, query_at, key_at, value_t, key_blocks, live_at, finish, scores):
    wide, bm = scores[0].shape[1:]
    empty = jnp.full((8, bm), MASKED, jnp.float32)
    nothing = jnp.zeros((8, bm), jnp.float32), jnp.zeros((HDIM, bm), jnp.float32)

    def bias_at(i, c):
        return lambda t: bias_of(band, bm, lambda a: live_at(i, a, c, t))

    def both(i, col_max, now, following):
        later = jnp.minimum(i + 1, blocks - 1)
        query = query_at(later)
        largest, state = empty, nothing
        for c in range(key_blocks):
            largest = first_pass(query, key_at(c), bias_at(later, c), following, c, largest)
            state = second_pass(now, c, col_max, value_t[:, c * wide : (c + 1) * wide], state)
        finish(i, divide(*state))
        return over_all(largest)

    largest = empty
    query = query_at(0)
    for c in range(key_blocks):
        largest = first_pass(query, key_at(c), bias_at(0, c), scores[0], c, largest)

    def pair(n, col_max):
        col_max = both(2 * n, col_max, scores[0], scores[1])
        return both(2 * n + 1, col_max, scores[1], scores[0])

    lax.fori_loop(0, blocks // 2, pair, over_all(largest))


def collect_kernel(order, rows, *refs):
    pieces, (q_out, kv_out) = refs[:-2], refs[-2:]
    me = lax.axis_index(NEAR)
    for d, piece in zip(order, pieces):
        at = pl.ds(pl.multiple_of((me ^ d) * rows, rows), rows)
        q_out[at] = piece[0]
        kv_out[:, at] = piece[1:]


def shared_kernel(order, rows, mask_ref, q_ref, own_ref, other_ref, *refs):
    outs, (value_t, mixed, *scores) = refs[: len(order)], refs[len(order) :]
    mine = lax.axis_index("inner")
    _, wide, bm = scores[0].shape
    blocks = q_ref.shape[0] // wide

    def key_at(c):
        ref = own_ref if c < blocks else other_ref
        return ref[0, c % blocks * wide : (c % blocks + 1) * wide]

    for n, ref in enumerate((own_ref, other_ref)):
        for t in range(blocks * wide // TILE):
            at = (n * blocks * wide) + t * TILE
            value_t[:, at : at + TILE] = transposed(ref[1, t * TILE : (t + 1) * TILE])

    def tile(block, inner, t):
        return (block * 2 + inner) * (wide // TILE) + t

    def finish(i, block):
        mixed[pl.ds(pl.multiple_of(i * bm, bm), bm)] = block

    attend_blocks(
        blocks,
        TILE,
        lambda i: q_ref[pl.ds(pl.multiple_of(i * bm, bm), bm)],
        key_at,
        value_t,
        2 * blocks,
        lambda i, a, c, t: mask_ref[tile(i, mine, a), tile(c % blocks, mine if c < blocks else 1 - mine, t)] != 0,
        finish,
        scores,
    )
    me = lax.axis_index(NEAR)
    for d, out in zip(order, outs):
        out[...] = mixed[pl.ds(pl.multiple_of((me ^ d) * rows, rows), rows)]


def whole_kernel(sources, mask_ref, qkv_ref, *refs):
    out_ref, value_t, *scores = refs[-4:]
    rows = qkv_ref.shape[2]
    _, wide, bm = scores[0].shape
    bands, tiles = bm // rows, wide // TILE
    for t in range(sources):
        value_t[:, t * TILE : (t + 1) * TILE] = transposed(qkv_ref[t, 2])

    def finish(i, mixed):
        out_ref[pl.ds(i * bands, bands)] = mixed.reshape(bands, rows, HDIM)

    attend_blocks(
        sources // bands,
        rows,
        lambda i: qkv_ref[pl.ds(i * bands, bands), 0].reshape(bm, HDIM),
        lambda c: qkv_ref[c * tiles : (c + 1) * tiles, 1].reshape(wide, HDIM),
        value_t,
        sources // tiles,
        lambda i, a, c, t: mask_ref[i * bands + a, c * tiles + t] != 0,
        finish,
        scores,
    )


def swap(piece, axes, d, count):
    return lax.ppermute(piece, axes, [(i, i ^ d) for i in range(count)]) if d else piece


def halved(far, near):
    order = [*range(near // 2, near), *range(near // 2)]

    def per_device(query_rows, key_rows, value_rows, q_gain, k_gain, tile_mask):
        rows, features = query_rows.shape

        def write(which, block, by_head, *outs):
            for h in range(near):
                by_head[h, which] = block[:, h * HDIM : (h + 1) * HDIM]
            for d in range(far):
                outs[-1][d, which] = block[:, (near + d) * HDIM : (near + d + 1) * HDIM]
            if which == 2:
                me = lax.axis_index(NEAR)
                for d, out in zip(order, outs):
                    out[...] = by_head[me ^ d]

        def read(*refs):
            shared, (whole, out_ref) = refs[:-2], refs[-2:]
            me = lax.axis_index(NEAR)
            for d, got in zip(order, shared):
                out_ref[:, pl.ds(pl.multiple_of((me ^ d) * HDIM, HDIM), HDIM)] = got[...]
            for d in range(far):
                out_ref[:, (near + d) * HDIM : (near + d + 1) * HDIM] = whole[d]

        *shared, whole = pack(
            write,
            [shape(3, rows, HDIM)] * near + [shape(far, 3, rows, HDIM)],
            rows,
            features,
            (query_rows, key_rows, value_rows, q_gain, k_gain),
            [pltpu.VMEM((near, 3, rows, HDIM), BF16)],
        )
        shared = [swap(piece, NEAR, d, near) for d, piece in zip(order, shared)]
        whole = exchange(whole, FAR)
        q_near, kv_near = pl.pallas_call(
            functools.partial(collect_kernel, order, rows),
            out_shape=[shape(near * rows, HDIM), shape(2, near * rows, HDIM)],
            compiler_params=PARAMS,
            name="collect",
        )(*shared)
        kv_other = lax.ppermute(kv_near, "inner", [(0, 1), (1, 0)])

        wide = 2 * TILE
        blocks = far * rows // wide
        smem, vmem = pl.BlockSpec(memory_space=pltpu.SMEM), pl.BlockSpec(memory_space=pltpu.VMEM)
        scratch = [pltpu.VMEM((HDIM, far * rows), BF16)]
        scores = [pltpu.VMEM((blocks, wide, wide), jnp.float32)] * 2
        shared = pl.pallas_call(
            functools.partial(shared_kernel, order, rows),
            in_specs=[smem] + [vmem] * 3,
            out_shape=[shape(rows, HDIM)] * near,
            scratch_shapes=scratch + [pltpu.VMEM((near * rows, HDIM), BF16)] + scores,
            compiler_params=PARAMS,
            cost_estimate=pl.CostEstimate(flops=23 * 2**30, bytes_accessed=2**21, transcendentals=0),
            name="attend_shared",
        )(tile_mask, q_near, kv_near, kv_other)
        shared = [swap(piece, NEAR, d, near) for d, piece in zip(order, shared)]

        whole = pl.pallas_call(
            functools.partial(whole_kernel, far),
            in_specs=[smem, vmem] + [pl.BlockSpec(memory_space=pl.ANY)] * near,
            out_shape=shape(far, rows, HDIM),
            scratch_shapes=scratch + scores,
            compiler_params=PARAMS,
            cost_estimate=pl.CostEstimate(flops=2**33, bytes_accessed=2**22, transcendentals=0),
            name="attend_whole",
        )(tile_mask, whole, *shared)
        return pl.pallas_call(
            read, out_shape=shape(rows, features), compiler_params=PARAMS, name="unpack"
        )(*shared, exchange(whole, FAR))

    return per_device


def gathered_kernel(outer, inner, mask_ref, q_ref, kv_ref, out_ref, scores_ref):
    i = pl.program_id(0)
    block = out_ref.shape[0] * out_ref.shape[1] * out_ref.shape[2]
    tiles = block // TILE
    q_tile = (i * inner + lax.axis_index("inner")) * tiles
    mixed = attend(
        q_ref[0, :, 0].reshape(block, HDIM),
        TILE,
        lambda c: kv_ref[lax.rem(c, inner), lax.div(c, inner), :, 1].reshape(block, HDIM),
        lambda c: kv_ref[lax.rem(c, inner), lax.div(c, inner), :, 2].reshape(block, HDIM),
        outer * inner,
        lambda a, t: mask_ref[q_tile + a, t] != 0,
        scores_ref,
    )
    out_ref[...] = mixed.reshape(out_ref.shape)


def gathered(outer, inner, n_head, near):
    width = HEADS // near * HDIM

    def per_device(query_rows, key_rows, value_rows, q_gain, k_gain, tile_mask):
        rows, features = query_rows.shape
        block = rows * n_head

        def write(which, block, packed):
            for d in range(near):
                packed[d, which] = block[:, d * width : (d + 1) * width]

        def read(got_ref, out_ref):
            for d in range(near):
                out_ref[:, d * width : (d + 1) * width] = got_ref[d]

        (packed,) = pack(
            write,
            [shape(near, 3, rows, width)],
            rows,
            features,
            (query_rows, key_rows, value_rows, q_gain, k_gain),
        )
        own = exchange(packed, NEAR).reshape(outer, n_head, 3, rows, width)
        every = lax.all_gather(own, "inner")
        mixed = pl.pallas_call(
            functools.partial(gathered_kernel, outer, inner),
            grid=(outer, HEADS // near),
            in_specs=[
                pl.BlockSpec(memory_space=pltpu.SMEM),
                pl.BlockSpec((1, n_head, 1, rows, HDIM), lambda i, h: (i, 0, 0, 0, h)),
                pl.BlockSpec((inner, outer, n_head, 3, rows, HDIM), lambda i, h: (0, 0, 0, 0, 0, h)),
            ],
            out_specs=pl.BlockSpec((1, n_head, rows, HDIM), lambda i, h: (i, 0, 0, h)),
            out_shape=shape(outer, n_head, rows, width),
            scratch_shapes=[pltpu.VMEM((outer * inner, block, block), jnp.float32)],
            compiler_params=PARAMS,
            name="attend",
        )(tile_mask, own, every)
        return pl.pallas_call(
            read, out_shape=shape(rows, features), compiler_params=PARAMS, name="unpack"
        )(exchange(mixed.reshape(near, rows, width), NEAR))

    return per_device


def solution(mesh):
    n_blk, n_head = mesh.shape["blk"], mesh.shape["head"]
    outer = max(d for d in range(1, n_blk + 1) if n_blk % d == 0 and HEADS % (n_head * d) == 0)
    inner = n_blk // outer
    near, far = outer * n_head, n_blk * n_head

    def per_device(query_rows, *others):
        in_pairs = inner == 2 and n_head == 2 and near & (near - 1) == 0
        if in_pairs and HEADS == near + far and query_rows.shape[0] == TILE:
            return halved(far, near)(query_rows, *others)
        return gathered(outer, inner, n_head, near)(query_rows, *others)

    split = P(("batch", "outer", "inner", "head"), None)
    return jax.shard_map(
        per_device,
        mesh=Mesh(
            mesh.devices.reshape(outer, inner, n_head, mesh.shape["batch"]), ("outer", "inner", "head", "batch")
        ),
        in_specs=(split, split, split, P(), P(), P()),
        out_specs=split,
        check_vma=False,
    )
```

```python
import functools

import jax
import jax.numpy as jnp
from jax import lax
from jax.experimental import pallas as pl
from jax.experimental.pallas import tpu as pltpu
from jax.sharding import Mesh, PartitionSpec as P

HEADS = 24
HDIM = 128
TILE = 128
EPS = 1e-06
MASKED = -1e30
NEAR = ("outer", "head")
FAR = ("outer", "inner", "head")
PARAMS = pltpu.CompilerParams(vmem_limit_bytes=48 * 1024 * 1024)
PACK_PARAMS = pltpu.CompilerParams(vmem_limit_bytes=61 * 1024 * 1024)
BF16 = jnp.bfloat16
SHARED_COST = 26 * 2**30
SCALE = 1.4426950408889634 * HDIM ** (-0.5)


def shape(*dims):
    return jax.ShapeDtypeStruct(dims, BF16)


def exchange(x, axes):
    return lax.all_to_all(x, axes, split_axis=0, concat_axis=0, tiled=True)


def pack_kernel(write, inputs, outputs, scratch):
    q_hbm, k_hbm, v_hbm, qg_hbm, kg_hbm = inputs
    q_in, k_in, v_in, qg, kg, sems, *kept = scratch
    copies = [
        pltpu.make_async_copy(src, dst, sems.at[n])
        for n, (src, dst) in enumerate(
            ((v_hbm, v_in), (q_hbm, q_in), (qg_hbm, qg), (k_hbm, k_in), (kg_hbm, kg))
        )
    ]
    for copy in copies:
        copy.start()

    def normalize(first, ref, gain):
        copies[first].wait()
        copies[first + 1].wait()
        widened = ref[...].astype(jnp.float32)
        mean_square = jnp.mean(widened * widened, axis=-1, keepdims=True)
        return (widened * lax.rsqrt(mean_square + EPS) * gain[...]).astype(BF16)

    copies[0].wait()
    sent = write(2, v_in[...], outputs, kept)
    sent += write(0, normalize(1, q_in, qg), outputs, kept)
    sent += write(1, normalize(3, k_in, kg), outputs, kept)
    for copy in sent:
        copy.wait()


def pack(write, out_shape, rows, features, arrays, kept=()):
    q, k, v, q_gain, k_gain = arrays
    hbm = pl.BlockSpec(memory_space=pltpu.HBM)

    def kernel(*refs):
        pack_kernel(write, refs[:5], refs[5 : 5 + len(out_shape)], refs[5 + len(out_shape) :])

    return pl.pallas_call(
        kernel,
        in_specs=[hbm] * 5,
        out_specs=[hbm] * len(out_shape),
        out_shape=out_shape,
        scratch_shapes=[pltpu.VMEM((rows, features), BF16)] * 3
        + [pltpu.VMEM((1, features), jnp.float32)] * 2
        + [pltpu.SemaphoreType.DMA((5,)), *kept],
        compiler_params=PACK_PARAMS,
        name="pack",
    )(q, k, v, q_gain.reshape(1, -1), k_gain.reshape(1, -1))


def first_pass(query, key, bias_at, scores_ref, c, largest):
    s = lax.dot_general(key, query, (((1,), (1,)), ((), ())), preferred_element_type=jnp.float32)
    for t in range(key.shape[0] // TILE):
        down = slice(t * TILE, (t + 1) * TILE)
        masked = s[down].reshape(TILE // 8, 8, -1) + bias_at(t)[None]
        scores_ref[c, down] = masked.reshape(TILE, -1)
        largest = jnp.maximum(largest, jnp.max(masked, axis=0))
    return largest


def second_pass(scores_ref, c, col_max, value_t, state):
    total, mixed = state
    wide, bm = scores_ref.shape[1:]
    weights = jnp.exp2(scores_ref[c].reshape(wide // 8, 8, bm) * SCALE - col_max[None])
    total = total + jnp.sum(weights, axis=0)
    weights = weights.reshape(wide, bm).astype(BF16)
    return total, mixed + jnp.dot(value_t, weights, preferred_element_type=jnp.float32)


def over_all(largest):
    return jnp.broadcast_to(jnp.max(largest, axis=0, keepdims=True) * SCALE, largest.shape)


def divide(total, mixed):
    return (mixed / jnp.sum(total, axis=0, keepdims=True)).T.astype(BF16)


def bias_of(band, bm, live_at):
    lane = lax.broadcasted_iota(jnp.int32, (8, bm), 1)
    bias = jnp.zeros((8, bm), jnp.float32)
    for a in range(bm // band):
        dead = jnp.where(live_at(a), 0.0, MASKED).astype(jnp.float32)
        bias = jnp.where((lane >= a * band) & (lane < (a + 1) * band), dead, bias)
    return bias


def attend(query, band, key_at, value_at, key_blocks, live_at, scores_ref):
    wide, bm = scores_ref.shape[1:]

    def score(c, largest):
        def bias_at(t):
            return bias_of(band, bm, lambda a: live_at(a, c * (wide // TILE) + t))

        return first_pass(query, key_at(c), bias_at, scores_ref, c, largest)

    largest = lax.fori_loop(0, key_blocks, score, jnp.full((8, bm), MASKED, jnp.float32))
    col_max = over_all(largest)

    def mix(c, state):
        return second_pass(scores_ref, c, col_max, transposed(value_at(c)), state)

    state = jnp.zeros((8, bm), jnp.float32), jnp.zeros((HDIM, bm), jnp.float32)
    return divide(*lax.fori_loop(0, key_blocks, mix, state))


def transposed(block):
    return block.astype(jnp.float32).T.astype(BF16)


def attend_blocks(blocks, band, query_at, key_at, value_t, key_blocks, live_at, finish, scores):
    wide, bm = scores[0].shape[1:]
    empty = jnp.full((8, bm), MASKED, jnp.float32)
    nothing = jnp.zeros((8, bm), jnp.float32), jnp.zeros((HDIM, bm), jnp.float32)

    def bias_at(i, c):
        return lambda t: bias_of(band, bm, lambda a: live_at(i, a, c, t))

    def both(i, col_max, now, following):
        later = jnp.minimum(i + 1, blocks - 1)
        query = query_at(later)
        largest, state = empty, nothing
        for c in range(key_blocks):
            largest = first_pass(query, key_at(c), bias_at(later, c), following, c, largest)
            state = second_pass(now, c, col_max, value_t[:, c * wide : (c + 1) * wide], state)
        finish(i, divide(*state))
        return over_all(largest)

    largest = empty
    query = query_at(0)
    for c in range(key_blocks):
        largest = first_pass(query, key_at(c), bias_at(0, c), scores[0], c, largest)

    def pair(n, col_max):
        col_max = both(2 * n, col_max, scores[0], scores[1])
        return both(2 * n + 1, col_max, scores[1], scores[0])

    lax.fori_loop(0, blocks // 2, pair, over_all(largest))


def collect_kernel(order, rows, *refs):
    pieces, (q_out, kv_out) = refs[:-2], refs[-2:]
    me = lax.axis_index(NEAR)
    for d, piece in zip(order, pieces):
        at = pl.ds(pl.multiple_of((me ^ d) * rows, rows), rows)
        q_out[at] = piece[0]
        kv_out[:, at] = piece[1:]


def shared_kernel(mask_ref, q_ref, own_ref, other_ref, out_ref, value_t, *scores):
    mine = lax.axis_index("inner")
    _, wide, bm = scores[0].shape
    blocks = q_ref.shape[0] // wide

    def key_at(c):
        ref = own_ref if c < blocks else other_ref
        return ref[0, c % blocks * wide : (c % blocks + 1) * wide]

    for n, ref in enumerate((own_ref, other_ref)):
        for t in range(blocks * wide // TILE):
            at = (n * blocks * wide) + t * TILE
            value_t[:, at : at + TILE] = transposed(ref[1, t * TILE : (t + 1) * TILE])

    def tile(block, inner, t):
        return (block * 2 + inner) * (wide // TILE) + t

    def finish(i, mixed):
        out_ref[pl.ds(pl.multiple_of(i * bm, bm), bm)] = mixed

    attend_blocks(
        blocks,
        TILE,
        lambda i: q_ref[pl.ds(pl.multiple_of(i * bm, bm), bm)],
        key_at,
        value_t,
        2 * blocks,
        lambda i, a, c, t: mask_ref[tile(i, mine, a), tile(c % blocks, mine if c < blocks else 1 - mine, t)] != 0,
        finish,
        scores,
    )


def whole_kernel(sources, mask_ref, qkv_ref, *refs):
    out_ref, value_t, *scores = refs[-4:]
    rows = qkv_ref.shape[2]
    _, wide, bm = scores[0].shape
    bands, tiles = bm // rows, wide // TILE
    for t in range(sources):
        value_t[:, t * TILE : (t + 1) * TILE] = transposed(qkv_ref[t, 2])

    def finish(i, mixed):
        out_ref[pl.ds(i * bands, bands)] = mixed.reshape(bands, rows, HDIM)

    attend_blocks(
        sources // bands,
        rows,
        lambda i: qkv_ref[pl.ds(i * bands, bands), 0].reshape(bm, HDIM),
        lambda c: qkv_ref[c * tiles : (c + 1) * tiles, 1].reshape(wide, HDIM),
        value_t,
        sources // tiles,
        lambda i, a, c, t: mask_ref[i * bands + a, c * tiles + t] != 0,
        finish,
        scores,
    )


def swap(piece, axes, d, count):
    return lax.ppermute(piece, axes, [(i, i ^ d) for i in range(count)]) if d else piece


def halved(far, near):
    order = [*range(near // 2, near), *range(near // 2)]

    def per_device(query_rows, key_rows, value_rows, q_gain, k_gain, tile_mask):
        rows, features = query_rows.shape

        def write(which, block, outs, kept):
            near_heads, far_heads, near_sems, far_sems = kept
            for h in range(near):
                near_heads[h, which] = block[:, h * HDIM : (h + 1) * HDIM]
            for h in range(far):
                far_heads[h, which] = block[:, (near + h) * HDIM : (near + h + 1) * HDIM]
            me = lax.axis_index(NEAR)
            copies = [
                pltpu.make_async_copy(near_heads.at[me ^ d, which], outs[n].at[which], near_sems.at[which, n])
                for n, d in enumerate(order)
            ]
            copies.append(pltpu.make_async_copy(far_heads.at[:, which], outs[-1].at[:, which], far_sems.at[which]))
            for copy in copies:
                copy.start()
            return copies

        def read(shared, whole, out_ref):
            for d in range(near):
                out_ref[:, d * HDIM : (d + 1) * HDIM] = shared[d]
            for d in range(far):
                out_ref[:, (near + d) * HDIM : (near + d + 1) * HDIM] = whole[d]

        *shared, whole = pack(
            write,
            [shape(3, rows, HDIM)] * near + [shape(far, 3, rows, HDIM)],
            rows,
            features,
            (query_rows, key_rows, value_rows, q_gain, k_gain),
            [
                pltpu.VMEM((near, 3, rows, HDIM), BF16),
                pltpu.VMEM((far, 3, rows, HDIM), BF16),
                pltpu.SemaphoreType.DMA((3, near)),
                pltpu.SemaphoreType.DMA((3,)),
            ],
        )
        shared = [swap(piece, NEAR, d, near) for d, piece in zip(order, shared)]
        whole = exchange(whole, FAR)
        q_near, kv_near = pl.pallas_call(
            functools.partial(collect_kernel, order, rows),
            out_shape=[shape(near * rows, HDIM), shape(2, near * rows, HDIM)],
            compiler_params=PARAMS,
            name="collect",
        )(*shared)
        kv_other = lax.ppermute(kv_near, "inner", [(0, 1), (1, 0)])

        wide = 2 * TILE
        blocks = far * rows // wide
        smem, vmem = pl.BlockSpec(memory_space=pltpu.SMEM), pl.BlockSpec(memory_space=pltpu.VMEM)
        scratch = [pltpu.VMEM((HDIM, far * rows), BF16)]
        scores = [pltpu.VMEM((blocks, wide, wide), jnp.float32)] * 2
        shared = pl.pallas_call(
            shared_kernel,
            in_specs=[smem] + [vmem] * 3,
            out_shape=shape(near * rows, HDIM),
            scratch_shapes=scratch + scores,
            compiler_params=PARAMS,
            cost_estimate=pl.CostEstimate(flops=SHARED_COST, bytes_accessed=2**21, transcendentals=0),
            name="attend_shared",
        )(tile_mask, q_near, kv_near, kv_other)

        whole = pl.pallas_call(
            functools.partial(whole_kernel, far),
            in_specs=[smem, vmem, pl.BlockSpec(memory_space=pl.ANY)],
            out_shape=shape(far, rows, HDIM),
            scratch_shapes=scratch + scores,
            compiler_params=PARAMS,
            cost_estimate=pl.CostEstimate(flops=2**33, bytes_accessed=2**22, transcendentals=0),
            name="attend_whole",
        )(tile_mask, whole, shared)
        shared = exchange(shared.reshape(near, rows, HDIM), NEAR)
        return pl.pallas_call(
            read, out_shape=shape(rows, features), compiler_params=PARAMS, name="unpack"
        )(shared, exchange(whole, FAR))

    return per_device


def gathered_kernel(outer, inner, mask_ref, q_ref, kv_ref, out_ref, scores_ref):
    i = pl.program_id(0)
    block = out_ref.shape[0] * out_ref.shape[1] * out_ref.shape[2]
    tiles = block // TILE
    q_tile = (i * inner + lax.axis_index("inner")) * tiles
    mixed = attend(
        q_ref[0, :, 0].reshape(block, HDIM),
        TILE,
        lambda c: kv_ref[lax.rem(c, inner), lax.div(c, inner), :, 1].reshape(block, HDIM),
        lambda c: kv_ref[lax.rem(c, inner), lax.div(c, inner), :, 2].reshape(block, HDIM),
        outer * inner,
        lambda a, t: mask_ref[q_tile + a, t] != 0,
        scores_ref,
    )
    out_ref[...] = mixed.reshape(out_ref.shape)


def gathered(outer, inner, n_head, near):
    width = HEADS // near * HDIM

    def per_device(query_rows, key_rows, value_rows, q_gain, k_gain, tile_mask):
        rows, features = query_rows.shape
        block = rows * n_head

        def write(which, block, outs, kept):
            packed, sems = kept
            for d in range(near):
                packed[d, which] = block[:, d * width : (d + 1) * width]
            copy = pltpu.make_async_copy(packed.at[:, which], outs[0].at[:, which], sems.at[which])
            copy.start()
            return [copy]

        def read(got_ref, out_ref):
            for d in range(near):
                out_ref[:, d * width : (d + 1) * width] = got_ref[d]

        (packed,) = pack(
            write,
            [shape(near, 3, rows, width)],
            rows,
            features,
            (query_rows, key_rows, value_rows, q_gain, k_gain),
            [pltpu.VMEM((near, 3, rows, width), BF16), pltpu.SemaphoreType.DMA((3,))],
        )
        own = exchange(packed, NEAR).reshape(outer, n_head, 3, rows, width)
        every = lax.all_gather(own, "inner")
        mixed = pl.pallas_call(
            functools.partial(gathered_kernel, outer, inner),
            grid=(outer, HEADS // near),
            in_specs=[
                pl.BlockSpec(memory_space=pltpu.SMEM),
                pl.BlockSpec((1, n_head, 1, rows, HDIM), lambda i, h: (i, 0, 0, 0, h)),
                pl.BlockSpec((inner, outer, n_head, 3, rows, HDIM), lambda i, h: (0, 0, 0, 0, 0, h)),
            ],
            out_specs=pl.BlockSpec((1, n_head, rows, HDIM), lambda i, h: (i, 0, 0, h)),
            out_shape=shape(outer, n_head, rows, width),
            scratch_shapes=[pltpu.VMEM((outer * inner, block, block), jnp.float32)],
            compiler_params=PARAMS,
            name="attend",
        )(tile_mask, own, every)
        return pl.pallas_call(
            read, out_shape=shape(rows, features), compiler_params=PARAMS, name="unpack"
        )(exchange(mixed.reshape(near, rows, width), NEAR))

    return per_device


def solution(mesh):
    n_blk, n_head = mesh.shape["blk"], mesh.shape["head"]
    outer = max(d for d in range(1, n_blk + 1) if n_blk % d == 0 and HEADS % (n_head * d) == 0)
    inner = n_blk // outer
    near, far = outer * n_head, n_blk * n_head

    def per_device(query_rows, *others):
        in_pairs = inner == 2 and n_head == 2 and near & (near - 1) == 0
        if in_pairs and HEADS == near + far and query_rows.shape[0] == TILE:
            return halved(far, near)(query_rows, *others)
        return gathered(outer, inner, n_head, near)(query_rows, *others)

    split = P(("batch", "outer", "inner", "head"), None)
    return jax.shard_map(
        per_device,
        mesh=Mesh(
            mesh.devices.reshape(outer, inner, n_head, mesh.shape["batch"]), ("outer", "inner", "head", "batch")
        ),
        in_specs=(split, split, split, P(), P(), P()),
        out_specs=split,
        check_vma=False,
    )
```

```python
import functools

import jax
import jax.numpy as jnp
from jax import lax
from jax.experimental import pallas as pl
from jax.experimental.pallas import tpu as pltpu
from jax.sharding import Mesh, PartitionSpec as P

HEADS = 24
HDIM = 128
TILE = 128
EPS = 1e-06
MASKED = -1e30
NEAR = ("outer", "head")
FAR = ("outer", "inner", "head")
PARAMS = pltpu.CompilerParams(vmem_limit_bytes=48 * 1024 * 1024)
PACK_PARAMS = pltpu.CompilerParams(vmem_limit_bytes=61 * 1024 * 1024)
BF16 = jnp.bfloat16
SHARED_COST = 24 * 2**30
SCALE = 1.4426950408889634 * HDIM ** (-0.5)


def shape(*dims):
    return jax.ShapeDtypeStruct(dims, BF16)


def exchange(x, axes):
    return lax.all_to_all(x, axes, split_axis=0, concat_axis=0, tiled=True)


def pack_kernel(write, inputs, outputs, scratch):
    q_hbm, k_hbm, v_hbm, qg_hbm, kg_hbm = inputs
    q_in, k_in, v_in, qg, kg, sems, *kept = scratch
    copies = [
        pltpu.make_async_copy(src, dst, sems.at[n])
        for n, (src, dst) in enumerate(
            ((v_hbm, v_in), (q_hbm, q_in), (qg_hbm, qg), (k_hbm, k_in), (kg_hbm, kg))
        )
    ]
    for copy in copies:
        copy.start()

    def normalize(first, ref, gain):
        copies[first].wait()
        copies[first + 1].wait()
        widened = ref[...].astype(jnp.float32)
        mean_square = jnp.mean(widened * widened, axis=-1, keepdims=True)
        return (widened * lax.rsqrt(mean_square + EPS) * gain[...]).astype(BF16)

    copies[0].wait()
    sent = write(2, v_in[...], outputs, kept)
    sent += write(0, normalize(1, q_in, qg), outputs, kept)
    sent += write(1, normalize(3, k_in, kg), outputs, kept)
    for copy in sent:
        copy.wait()


def pack(write, out_shape, rows, features, arrays, kept=()):
    q, k, v, q_gain, k_gain = arrays
    hbm = pl.BlockSpec(memory_space=pltpu.HBM)

    def kernel(*refs):
        pack_kernel(write, refs[:5], refs[5 : 5 + len(out_shape)], refs[5 + len(out_shape) :])

    return pl.pallas_call(
        kernel,
        in_specs=[hbm] * 5,
        out_specs=[hbm] * len(out_shape),
        out_shape=out_shape,
        scratch_shapes=[pltpu.VMEM((rows, features), BF16)] * 3
        + [pltpu.VMEM((1, features), jnp.float32)] * 2
        + [pltpu.SemaphoreType.DMA((5,)), *kept],
        compiler_params=PACK_PARAMS,
        name="pack",
    )(q, k, v, q_gain.reshape(1, -1), k_gain.reshape(1, -1))


def first_pass(query, key, bias_at, scores_ref, c, largest):
    s = lax.dot_general(key, query, (((1,), (1,)), ((), ())), preferred_element_type=jnp.float32)
    for t in range(key.shape[0] // TILE):
        down = slice(t * TILE, (t + 1) * TILE)
        masked = s[down].reshape(TILE // 8, 8, -1) + bias_at(t)[None]
        scores_ref[c, down] = masked.reshape(TILE, -1)
        largest = jnp.maximum(largest, jnp.max(masked, axis=0))
    return largest


def second_pass(scores_ref, c, col_max, value_t, state):
    total, mixed = state
    wide, bm = scores_ref.shape[1:]
    weights = jnp.exp2(scores_ref[c].reshape(wide // 8, 8, bm) * SCALE - col_max[None])
    total = total + jnp.sum(weights, axis=0)
    weights = weights.reshape(wide, bm).astype(BF16)
    return total, mixed + jnp.dot(value_t, weights, preferred_element_type=jnp.float32)


def over_all(largest):
    return jnp.broadcast_to(jnp.max(largest, axis=0, keepdims=True) * SCALE, largest.shape)


def divide(total, mixed):
    return (mixed / jnp.sum(total, axis=0, keepdims=True)).T.astype(BF16)


def bias_of(band, bm, live_at):
    lane = lax.broadcasted_iota(jnp.int32, (8, bm), 1)
    bias = jnp.zeros((8, bm), jnp.float32)
    for a in range(bm // band):
        dead = jnp.where(live_at(a), 0.0, MASKED).astype(jnp.float32)
        bias = jnp.where((lane >= a * band) & (lane < (a + 1) * band), dead, bias)
    return bias


def attend(query, band, key_at, value_at, key_blocks, live_at, scores_ref):
    wide, bm = scores_ref.shape[1:]

    def score(c, largest):
        def bias_at(t):
            return bias_of(band, bm, lambda a: live_at(a, c * (wide // TILE) + t))

        return first_pass(query, key_at(c), bias_at, scores_ref, c, largest)

    largest = lax.fori_loop(0, key_blocks, score, jnp.full((8, bm), MASKED, jnp.float32))
    col_max = over_all(largest)

    def mix(c, state):
        return second_pass(scores_ref, c, col_max, transposed(value_at(c)), state)

    state = jnp.zeros((8, bm), jnp.float32), jnp.zeros((HDIM, bm), jnp.float32)
    return divide(*lax.fori_loop(0, key_blocks, mix, state))


def transposed(block):
    return block.astype(jnp.float32).T.astype(BF16)


def attend_blocks(blocks, band, query_at, key_at, value_t, key_blocks, live_at, finish, scores):
    wide, bm = scores[0].shape[1:]
    empty = jnp.full((8, bm), MASKED, jnp.float32)
    nothing = jnp.zeros((8, bm), jnp.float32), jnp.zeros((HDIM, bm), jnp.float32)

    def bias_at(i, c):
        return lambda t: bias_of(band, bm, lambda a: live_at(i, a, c, t))

    def both(i, col_max, now, following):
        later = jnp.minimum(i + 1, blocks - 1)
        query = query_at(later)
        largest, state = empty, nothing
        for c in range(key_blocks):
            largest = first_pass(query, key_at(c), bias_at(later, c), following, c, largest)
            state = second_pass(now, c, col_max, value_t[:, c * wide : (c + 1) * wide], state)
        finish(i, divide(*state))
        return over_all(largest)

    largest = empty
    query = query_at(0)
    for c in range(key_blocks):
        largest = first_pass(query, key_at(c), bias_at(0, c), scores[0], c, largest)

    def pair(n, col_max):
        col_max = both(2 * n, col_max, scores[0], scores[1])
        return both(2 * n + 1, col_max, scores[1], scores[0])

    lax.fori_loop(0, blocks // 2, pair, over_all(largest))


def partner(me, step):
    first, second = step
    return me ^ jnp.where(lax.axis_index("batch") == 0, first, second)


def collect_kernel(steps, rows, *refs):
    pieces, (q_out, kv_out) = refs[:-2], refs[-2:]
    me = lax.axis_index(NEAR)
    for step, piece in zip(steps, pieces):
        at = pl.ds(pl.multiple_of(partner(me, step) * rows, rows), rows)
        q_out[at] = piece[0]
        kv_out[:, at] = piece[1:]


def shared_kernel(mask_ref, q_ref, own_ref, other_ref, out_ref, value_t, *scores):
    mine = lax.axis_index("inner")
    _, wide, bm = scores[0].shape
    blocks = q_ref.shape[0] // wide

    def key_at(c):
        ref = own_ref if c < blocks else other_ref
        return ref[0, c % blocks * wide : (c % blocks + 1) * wide]

    for n, ref in enumerate((own_ref, other_ref)):
        for t in range(blocks * wide // TILE):
            at = (n * blocks * wide) + t * TILE
            value_t[:, at : at + TILE] = transposed(ref[1, t * TILE : (t + 1) * TILE])

    def tile(block, inner, t):
        return (block * 2 + inner) * (wide // TILE) + t

    def finish(i, mixed):
        out_ref[pl.ds(pl.multiple_of(i * bm, bm), bm)] = mixed

    attend_blocks(
        blocks,
        TILE,
        lambda i: q_ref[pl.ds(pl.multiple_of(i * bm, bm), bm)],
        key_at,
        value_t,
        2 * blocks,
        lambda i, a, c, t: mask_ref[tile(i, mine, a), tile(c % blocks, mine if c < blocks else 1 - mine, t)] != 0,
        finish,
        scores,
    )


def whole_kernel(sources, mask_ref, qkv_ref, *refs):
    out_ref, value_t, *scores = refs[-4:]
    rows = qkv_ref.shape[2]
    _, wide, bm = scores[0].shape
    bands, tiles = bm // rows, wide // TILE
    for t in range(sources):
        value_t[:, t * TILE : (t + 1) * TILE] = transposed(qkv_ref[t, 2])

    def finish(i, mixed):
        out_ref[pl.ds(i * bands, bands)] = mixed.reshape(bands, rows, HDIM)

    attend_blocks(
        sources // bands,
        rows,
        lambda i: qkv_ref[pl.ds(i * bands, bands), 0].reshape(bm, HDIM),
        lambda c: qkv_ref[c * tiles : (c + 1) * tiles, 1].reshape(wide, HDIM),
        value_t,
        sources // tiles,
        lambda i, a, c, t: mask_ref[i * bands + a, c * tiles + t] != 0,
        finish,
        scores,
    )


def halved(far, near):
    steps = []
    for d in range(near // 2):
        steps += [(near // 2 + d, d), (d, near // 2 + d)]

    def swap(piece, step):
        pairs = [(2 * i + b, 2 * (i ^ step[b]) + b) for i in range(near) for b in range(2)]
        return lax.ppermute(piece, (*NEAR, "batch"), pairs)

    def per_device(query_rows, key_rows, value_rows, q_gain, k_gain, tile_mask):
        rows, features = query_rows.shape

        def write(which, block, outs, kept):
            near_heads, far_heads, near_sems, far_sems = kept
            for h in range(near):
                near_heads[h, which] = block[:, h * HDIM : (h + 1) * HDIM]
            for h in range(far):
                far_heads[h, which] = block[:, (near + h) * HDIM : (near + h + 1) * HDIM]
            me = lax.axis_index(NEAR)
            copies = [
                pltpu.make_async_copy(near_heads.at[partner(me, step), which], outs[n].at[which], near_sems.at[which, n])
                for n, step in enumerate(steps)
            ]
            copies.append(pltpu.make_async_copy(far_heads.at[:, which], outs[-1].at[:, which], far_sems.at[which]))
            for copy in copies:
                copy.start()
            return copies

        def read(shared, whole, out_ref):
            for d in range(near):
                out_ref[:, d * HDIM : (d + 1) * HDIM] = shared[d]
            for d in range(far):
                out_ref[:, (near + d) * HDIM : (near + d + 1) * HDIM] = whole[d]

        *shared, whole = pack(
            write,
            [shape(3, rows, HDIM)] * near + [shape(far, 3, rows, HDIM)],
            rows,
            features,
            (query_rows, key_rows, value_rows, q_gain, k_gain),
            [
                pltpu.VMEM((near, 3, rows, HDIM), BF16),
                pltpu.VMEM((far, 3, rows, HDIM), BF16),
                pltpu.SemaphoreType.DMA((3, near)),
                pltpu.SemaphoreType.DMA((3,)),
            ],
        )
        shared = [swap(piece, step) for step, piece in zip(steps, shared)]
        whole = exchange(whole, FAR)
        q_near, kv_near = pl.pallas_call(
            functools.partial(collect_kernel, steps, rows),
            out_shape=[shape(near * rows, HDIM), shape(2, near * rows, HDIM)],
            compiler_params=PARAMS,
            name="collect",
        )(*shared)
        kv_other = lax.ppermute(kv_near, "inner", [(0, 1), (1, 0)])

        wide = 2 * TILE
        blocks = far * rows // wide
        smem, vmem = pl.BlockSpec(memory_space=pltpu.SMEM), pl.BlockSpec(memory_space=pltpu.VMEM)
        scratch = [pltpu.VMEM((HDIM, far * rows), BF16)]
        scores = [pltpu.VMEM((blocks, wide, wide), jnp.float32)] * 2
        shared = pl.pallas_call(
            shared_kernel,
            in_specs=[smem] + [vmem] * 3,
            out_shape=shape(near * rows, HDIM),
            scratch_shapes=scratch + scores,
            compiler_params=PARAMS,
            cost_estimate=pl.CostEstimate(flops=SHARED_COST, bytes_accessed=2**21, transcendentals=0),
            name="attend_shared",
        )(tile_mask, q_near, kv_near, kv_other)

        whole = pl.pallas_call(
            functools.partial(whole_kernel, far),
            in_specs=[smem, vmem, pl.BlockSpec(memory_space=pl.ANY)],
            out_shape=shape(far, rows, HDIM),
            scratch_shapes=scratch + scores,
            compiler_params=PARAMS,
            cost_estimate=pl.CostEstimate(flops=2**33, bytes_accessed=2**22, transcendentals=0),
            name="attend_whole",
        )(tile_mask, whole, shared)
        shared = exchange(shared.reshape(near, rows, HDIM), NEAR)
        return pl.pallas_call(
            read, out_shape=shape(rows, features), compiler_params=PARAMS, name="unpack"
        )(shared, exchange(whole, FAR))

    return per_device


def gathered_kernel(outer, inner, mask_ref, q_ref, kv_ref, out_ref, scores_ref):
    i = pl.program_id(0)
    block = out_ref.shape[0] * out_ref.shape[1] * out_ref.shape[2]
    tiles = block // TILE
    q_tile = (i * inner + lax.axis_index("inner")) * tiles
    mixed = attend(
        q_ref[0, :, 0].reshape(block, HDIM),
        TILE,
        lambda c: kv_ref[lax.rem(c, inner), lax.div(c, inner), :, 1].reshape(block, HDIM),
        lambda c: kv_ref[lax.rem(c, inner), lax.div(c, inner), :, 2].reshape(block, HDIM),
        outer * inner,
        lambda a, t: mask_ref[q_tile + a, t] != 0,
        scores_ref,
    )
    out_ref[...] = mixed.reshape(out_ref.shape)


def gathered(outer, inner, n_head, near):
    width = HEADS // near * HDIM

    def per_device(query_rows, key_rows, value_rows, q_gain, k_gain, tile_mask):
        rows, features = query_rows.shape
        block = rows * n_head

        def write(which, block, outs, kept):
            packed, sems = kept
            for d in range(near):
                packed[d, which] = block[:, d * width : (d + 1) * width]
            copy = pltpu.make_async_copy(packed.at[:, which], outs[0].at[:, which], sems.at[which])
            copy.start()
            return [copy]

        def read(got_ref, out_ref):
            for d in range(near):
                out_ref[:, d * width : (d + 1) * width] = got_ref[d]

        (packed,) = pack(
            write,
            [shape(near, 3, rows, width)],
            rows,
            features,
            (query_rows, key_rows, value_rows, q_gain, k_gain),
            [pltpu.VMEM((near, 3, rows, width), BF16), pltpu.SemaphoreType.DMA((3,))],
        )
        own = exchange(packed, NEAR).reshape(outer, n_head, 3, rows, width)
        every = lax.all_gather(own, "inner")
        mixed = pl.pallas_call(
            functools.partial(gathered_kernel, outer, inner),
            grid=(outer, HEADS // near),
            in_specs=[
                pl.BlockSpec(memory_space=pltpu.SMEM),
                pl.BlockSpec((1, n_head, 1, rows, HDIM), lambda i, h: (i, 0, 0, 0, h)),
                pl.BlockSpec((inner, outer, n_head, 3, rows, HDIM), lambda i, h: (0, 0, 0, 0, 0, h)),
            ],
            out_specs=pl.BlockSpec((1, n_head, rows, HDIM), lambda i, h: (i, 0, 0, h)),
            out_shape=shape(outer, n_head, rows, width),
            scratch_shapes=[pltpu.VMEM((outer * inner, block, block), jnp.float32)],
            compiler_params=PARAMS,
            name="attend",
        )(tile_mask, own, every)
        return pl.pallas_call(
            read, out_shape=shape(rows, features), compiler_params=PARAMS, name="unpack"
        )(exchange(mixed.reshape(near, rows, width), NEAR))

    return per_device


def solution(mesh):
    n_blk, n_head = mesh.shape["blk"], mesh.shape["head"]
    outer = max(d for d in range(1, n_blk + 1) if n_blk % d == 0 and HEADS % (n_head * d) == 0)
    inner = n_blk // outer
    near, far = outer * n_head, n_blk * n_head

    def per_device(query_rows, *others):
        in_pairs = inner == 2 and n_head == 2 and mesh.shape["batch"] == 2 and near & (near - 1) == 0
        if in_pairs and HEADS == near + far and query_rows.shape[0] == TILE:
            return halved(far, near)(query_rows, *others)
        return gathered(outer, inner, n_head, near)(query_rows, *others)

    split = P(("batch", "outer", "inner", "head"), None)
    return jax.shard_map(
        per_device,
        mesh=Mesh(
            mesh.devices.reshape(outer, inner, n_head, mesh.shape["batch"]), ("outer", "inner", "head", "batch")
        ),
        in_specs=(split, split, split, P(), P(), P()),
        out_specs=split,
        check_vma=False,
    )
```

```python
import functools

import jax
import jax.numpy as jnp
from jax import lax
from jax.experimental import pallas as pl
from jax.experimental.pallas import tpu as pltpu
from jax.sharding import Mesh, PartitionSpec as P

HEADS = 24
HDIM = 128
TILE = 128
EPS = 1e-06
MASKED = -1e30
NEAR = ("outer", "head")
FAR = ("outer", "inner", "head")
PARAMS = pltpu.CompilerParams(vmem_limit_bytes=48 * 1024 * 1024)
PACK_PARAMS = pltpu.CompilerParams(vmem_limit_bytes=61 * 1024 * 1024)
BF16 = jnp.bfloat16
SHARED_COST = 2**30
SCALE = 1.4426950408889634 * HDIM ** (-0.5)


def shape(*dims):
    return jax.ShapeDtypeStruct(dims, BF16)


def exchange(x, axes):
    return lax.all_to_all(x, axes, split_axis=0, concat_axis=0, tiled=True)


def pack_kernel(write, inputs, outputs, scratch):
    q_hbm, k_hbm, v_hbm, qg_hbm, kg_hbm = inputs
    q_in, k_in, v_in, qg, kg, sems, *kept = scratch
    copies = [
        pltpu.make_async_copy(src, dst, sems.at[n])
        for n, (src, dst) in enumerate(
            ((v_hbm, v_in), (q_hbm, q_in), (qg_hbm, qg), (k_hbm, k_in), (kg_hbm, kg))
        )
    ]
    for copy in copies:
        copy.start()

    def normalize(first, ref, gain):
        copies[first].wait()
        copies[first + 1].wait()
        widened = ref[...].astype(jnp.float32)
        mean_square = jnp.mean(widened * widened, axis=-1, keepdims=True)
        return (widened * lax.rsqrt(mean_square + EPS) * gain[...]).astype(BF16)

    copies[0].wait()
    sent = write(2, v_in[...], outputs, kept)
    sent += write(0, normalize(1, q_in, qg), outputs, kept)
    sent += write(1, normalize(3, k_in, kg), outputs, kept)
    for copy in sent:
        copy.wait()


def pack(write, out_shape, rows, features, arrays, kept=()):
    q, k, v, q_gain, k_gain = arrays
    hbm = pl.BlockSpec(memory_space=pltpu.HBM)

    def kernel(*refs):
        pack_kernel(write, refs[:5], refs[5 : 5 + len(out_shape)], refs[5 + len(out_shape) :])

    return pl.pallas_call(
        kernel,
        in_specs=[hbm] * 5,
        out_specs=[hbm] * len(out_shape),
        out_shape=out_shape,
        scratch_shapes=[pltpu.VMEM((rows, features), BF16)] * 3
        + [pltpu.VMEM((1, features), jnp.float32)] * 2
        + [pltpu.SemaphoreType.DMA((5,)), *kept],
        compiler_params=PACK_PARAMS,
        name="pack",
    )(q, k, v, q_gain.reshape(1, -1), k_gain.reshape(1, -1))


def first_pass(query, key, bias_at, scores_ref, c, largest):
    s = lax.dot_general(key, query, (((1,), (1,)), ((), ())), preferred_element_type=jnp.float32)
    for t in range(key.shape[0] // TILE):
        down = slice(t * TILE, (t + 1) * TILE)
        masked = s[down].reshape(TILE // 8, 8, -1) + bias_at(t)[None]
        scores_ref[c, down] = masked.reshape(TILE, -1)
        largest = jnp.maximum(largest, jnp.max(masked, axis=0))
    return largest


def second_pass(scores_ref, c, col_max, value_t, state):
    total, mixed = state
    wide, bm = scores_ref.shape[1:]
    weights = jnp.exp2(scores_ref[c].reshape(wide // 8, 8, bm) * SCALE - col_max[None])
    total = total + jnp.sum(weights, axis=0)
    weights = weights.reshape(wide, bm).astype(BF16)
    return total, mixed + jnp.dot(value_t, weights, preferred_element_type=jnp.float32)


def over_all(largest):
    return jnp.broadcast_to(jnp.max(largest, axis=0, keepdims=True) * SCALE, largest.shape)


def divide(total, mixed):
    return (mixed / jnp.sum(total, axis=0, keepdims=True)).T.astype(BF16)


def bias_of(band, bm, live_at):
    lane = lax.broadcasted_iota(jnp.int32, (8, bm), 1)
    bias = jnp.zeros((8, bm), jnp.float32)
    for a in range(bm // band):
        dead = jnp.where(live_at(a), 0.0, MASKED).astype(jnp.float32)
        bias = jnp.where((lane >= a * band) & (lane < (a + 1) * band), dead, bias)
    return bias


def attend(query, band, key_at, value_at, key_blocks, live_at, scores_ref):
    wide, bm = scores_ref.shape[1:]

    def score(c, largest):
        def bias_at(t):
            return bias_of(band, bm, lambda a: live_at(a, c * (wide // TILE) + t))

        return first_pass(query, key_at(c), bias_at, scores_ref, c, largest)

    largest = lax.fori_loop(0, key_blocks, score, jnp.full((8, bm), MASKED, jnp.float32))
    col_max = over_all(largest)

    def mix(c, state):
        return second_pass(scores_ref, c, col_max, transposed(value_at(c)), state)

    state = jnp.zeros((8, bm), jnp.float32), jnp.zeros((HDIM, bm), jnp.float32)
    return divide(*lax.fori_loop(0, key_blocks, mix, state))


def transposed(block):
    return block.astype(jnp.float32).T.astype(BF16)


def attend_blocks(blocks, band, query_at, key_at, value_t, key_blocks, live_at, finish, scores):
    wide, bm = scores[0].shape[1:]
    empty = jnp.full((8, bm), MASKED, jnp.float32)
    nothing = jnp.zeros((8, bm), jnp.float32), jnp.zeros((HDIM, bm), jnp.float32)

    def bias_at(i, c):
        return lambda t: bias_of(band, bm, lambda a: live_at(i, a, c, t))

    def both(i, col_max, now, following):
        later = jnp.minimum(i + 1, blocks - 1)
        query = query_at(later)
        largest, state = empty, nothing
        for c in range(key_blocks):
            largest = first_pass(query, key_at(c), bias_at(later, c), following, c, largest)
            state = second_pass(now, c, col_max, value_t[:, c * wide : (c + 1) * wide], state)
        finish(i, divide(*state))
        return over_all(largest)

    largest = empty
    query = query_at(0)
    for c in range(key_blocks):
        largest = first_pass(query, key_at(c), bias_at(0, c), scores[0], c, largest)

    def pair(n, col_max):
        col_max = both(2 * n, col_max, scores[0], scores[1])
        return both(2 * n + 1, col_max, scores[1], scores[0])

    lax.fori_loop(0, blocks // 2, pair, over_all(largest))


def partner(me, step):
    first, second = step
    return me ^ jnp.where(lax.axis_index("batch") == 0, first, second)


def rows_in_part(step, n_head, rows):
    d = partner(0, step)
    slot = lax.div(d, 2 * n_head) * n_head + partner(lax.axis_index("head"), tuple(e % n_head for e in step))
    return pl.ds(pl.multiple_of(slot * rows, rows), rows)


def collect_kernel(steps, n_head, rows, *refs):
    pieces, (q_out, kv_out) = refs[: len(steps)], refs[-2:]
    for step, piece in zip(steps, pieces):
        at = rows_in_part(step, n_head, rows)
        q_out[at] = piece[0]
        kv_out[:, at] = piece[1:]


def shared_kernel(mask_ref, *refs):
    q_refs, kv_refs, (out_ref, query, value_t, *scores) = refs[:2], refs[2:6], refs[6:]
    mine, outer = lax.axis_index("inner"), lax.axis_index("outer")
    _, wide, bm = scores[0].shape
    part = q_refs[0].shape[0] // wide
    blocks = 2 * part

    for n, ref in enumerate(q_refs):
        query[n * part * wide : (n + 1) * part * wide] = ref[...]
    for n, ref in enumerate(kv_refs):
        for t in range(part * wide // TILE):
            at = n * part * wide + t * TILE
            value_t[:, at : at + TILE] = transposed(ref[1, t * TILE : (t + 1) * TILE])

    def outer_of(i):
        return outer ^ (lax.rem(i, part) * 2 + lax.div(i, part))

    def tile(block, inner, t):
        return (block * 2 + inner) * (wide // TILE) + t

    def finish(i, mixed):
        out_ref[pl.ds(pl.multiple_of(outer_of(i) * bm, bm), bm)] = mixed

    attend_blocks(
        blocks,
        TILE,
        lambda i: query[pl.ds(pl.multiple_of(i * bm, bm), bm)],
        lambda c: kv_refs[c // part][0, c % part * wide : (c % part + 1) * wide],
        value_t,
        2 * blocks,
        lambda i, a, c, t: mask_ref[
            tile(outer_of(i), mine, a), tile(outer_of(c % blocks), mine if c < blocks else 1 - mine, t)
        ]
        != 0,
        finish,
        scores,
    )


def whole_kernel(sources, mask_ref, qkv_ref, *refs):
    out_ref, value_t, *scores = refs
    rows = qkv_ref.shape[2]
    _, wide, bm = scores[0].shape
    bands, tiles = bm // rows, wide // TILE
    for t in range(sources):
        value_t[:, t * TILE : (t + 1) * TILE] = transposed(qkv_ref[t, 2])

    def finish(i, mixed):
        out_ref[pl.ds(i * bands, bands)] = mixed.reshape(bands, rows, HDIM)

    attend_blocks(
        sources // bands,
        rows,
        lambda i: qkv_ref[pl.ds(i * bands, bands), 0].reshape(bm, HDIM),
        lambda c: qkv_ref[c * tiles : (c + 1) * tiles, 1].reshape(wide, HDIM),
        value_t,
        sources // tiles,
        lambda i, a, c, t: mask_ref[i * bands + a, c * tiles + t] != 0,
        finish,
        scores,
    )


def halved(n_head, far, near):
    steps = []
    for d in range(near // 2):
        steps += [(near // 2 + d, d), (d, near // 2 + d)]

    def swap(piece, step):
        pairs = [(2 * i + b, 2 * (i ^ step[b]) + b) for i in range(near) for b in range(2)]
        return lax.ppermute(piece, (*NEAR, "batch"), pairs)

    def per_device(query_rows, key_rows, value_rows, q_gain, k_gain, tile_mask):
        rows, features = query_rows.shape

        def write(which, block, outs, kept):
            near_heads, far_heads, near_sems, far_sems = kept
            for h in range(near):
                near_heads[h, which] = block[:, h * HDIM : (h + 1) * HDIM]
            for h in range(far):
                far_heads[h, which] = block[:, (near + h) * HDIM : (near + h + 1) * HDIM]
            me = lax.axis_index(NEAR)
            copies = [
                pltpu.make_async_copy(near_heads.at[partner(me, step), which], outs[n].at[which], near_sems.at[which, n])
                for n, step in enumerate(steps)
            ]
            copies.append(pltpu.make_async_copy(far_heads.at[:, which], outs[-1].at[:, which], far_sems.at[which]))
            for copy in copies:
                copy.start()
            return copies

        def read(shared, whole, out_ref):
            for d in range(near):
                out_ref[:, d * HDIM : (d + 1) * HDIM] = shared[d]
            for d in range(far):
                out_ref[:, (near + d) * HDIM : (near + d + 1) * HDIM] = whole[d]

        *shared, whole = pack(
            write,
            [shape(3, rows, HDIM)] * near + [shape(far, 3, rows, HDIM)],
            rows,
            features,
            (query_rows, key_rows, value_rows, q_gain, k_gain),
            [
                pltpu.VMEM((near, 3, rows, HDIM), BF16),
                pltpu.VMEM((far, 3, rows, HDIM), BF16),
                pltpu.SemaphoreType.DMA((3, near)),
                pltpu.SemaphoreType.DMA((3,)),
            ],
        )
        shared = [swap(piece, step) for step, piece in zip(steps, shared)]
        whole = exchange(whole, FAR)
        wide = 2 * TILE
        blocks = far * rows // wide
        smem, vmem = pl.BlockSpec(memory_space=pltpu.SMEM), pl.BlockSpec(memory_space=pltpu.VMEM)
        after = pl.BlockSpec(memory_space=pl.ANY)
        scratch = [pltpu.VMEM((HDIM, far * rows), BF16)]
        scores = [pltpu.VMEM((blocks, wide, wide), jnp.float32)] * 2
        whole = pl.pallas_call(
            functools.partial(whole_kernel, far),
            in_specs=[smem, vmem],
            out_shape=shape(far, rows, HDIM),
            scratch_shapes=scratch + scores,
            compiler_params=PARAMS,
            cost_estimate=pl.CostEstimate(flops=2**33, bytes_accessed=2**22, transcendentals=0),
            name="attend_whole",
        )(tile_mask, whole)

        queries, keys_values = [], []
        part = near // 2
        for n in range(2):
            q_near, kv_near = pl.pallas_call(
                functools.partial(collect_kernel, steps[n * part : (n + 1) * part], n_head, rows),
                in_specs=[vmem] * part + [after],
                out_shape=[shape(part * rows, HDIM), shape(2, part * rows, HDIM)],
                compiler_params=PARAMS,
                name="collect",
            )(*shared[n * part : (n + 1) * part], whole)
            queries.append(q_near)
            keys_values.append(kv_near)
        keys_values += [lax.ppermute(kv, "inner", [(0, 1), (1, 0)]) for kv in keys_values]
        shared = pl.pallas_call(
            shared_kernel,
            in_specs=[smem] + [vmem] * 6,
            out_shape=shape(near * rows, HDIM),
            scratch_shapes=[pltpu.VMEM((near * rows, HDIM), BF16)] + scratch + scores,
            compiler_params=PARAMS,
            cost_estimate=pl.CostEstimate(flops=SHARED_COST, bytes_accessed=2**21, transcendentals=0),
            name="attend_shared",
        )(tile_mask, *queries, *keys_values)
        shared = exchange(shared.reshape(near, rows, HDIM), NEAR)
        return pl.pallas_call(
            read, out_shape=shape(rows, features), compiler_params=PARAMS, name="unpack"
        )(shared, exchange(whole, FAR))

    return per_device


def gathered_kernel(outer, inner, mask_ref, q_ref, kv_ref, out_ref, scores_ref):
    i = pl.program_id(0)
    block = out_ref.shape[0] * out_ref.shape[1] * out_ref.shape[2]
    tiles = block // TILE
    q_tile = (i * inner + lax.axis_index("inner")) * tiles
    mixed = attend(
        q_ref[0, :, 0].reshape(block, HDIM),
        TILE,
        lambda c: kv_ref[lax.rem(c, inner), lax.div(c, inner), :, 1].reshape(block, HDIM),
        lambda c: kv_ref[lax.rem(c, inner), lax.div(c, inner), :, 2].reshape(block, HDIM),
        outer * inner,
        lambda a, t: mask_ref[q_tile + a, t] != 0,
        scores_ref,
    )
    out_ref[...] = mixed.reshape(out_ref.shape)


def gathered(outer, inner, n_head, near):
    width = HEADS // near * HDIM

    def per_device(query_rows, key_rows, value_rows, q_gain, k_gain, tile_mask):
        rows, features = query_rows.shape
        block = rows * n_head

        def write(which, block, outs, kept):
            packed, sems = kept
            for d in range(near):
                packed[d, which] = block[:, d * width : (d + 1) * width]
            copy = pltpu.make_async_copy(packed.at[:, which], outs[0].at[:, which], sems.at[which])
            copy.start()
            return [copy]

        def read(got_ref, out_ref):
            for d in range(near):
                out_ref[:, d * width : (d + 1) * width] = got_ref[d]

        (packed,) = pack(
            write,
            [shape(near, 3, rows, width)],
            rows,
            features,
            (query_rows, key_rows, value_rows, q_gain, k_gain),
            [pltpu.VMEM((near, 3, rows, width), BF16), pltpu.SemaphoreType.DMA((3,))],
        )
        own = exchange(packed, NEAR).reshape(outer, n_head, 3, rows, width)
        every = lax.all_gather(own, "inner")
        mixed = pl.pallas_call(
            functools.partial(gathered_kernel, outer, inner),
            grid=(outer, HEADS // near),
            in_specs=[
                pl.BlockSpec(memory_space=pltpu.SMEM),
                pl.BlockSpec((1, n_head, 1, rows, HDIM), lambda i, h: (i, 0, 0, 0, h)),
                pl.BlockSpec((inner, outer, n_head, 3, rows, HDIM), lambda i, h: (0, 0, 0, 0, 0, h)),
            ],
            out_specs=pl.BlockSpec((1, n_head, rows, HDIM), lambda i, h: (i, 0, 0, h)),
            out_shape=shape(outer, n_head, rows, width),
            scratch_shapes=[pltpu.VMEM((outer * inner, block, block), jnp.float32)],
            compiler_params=PARAMS,
            name="attend",
        )(tile_mask, own, every)
        return pl.pallas_call(
            read, out_shape=shape(rows, features), compiler_params=PARAMS, name="unpack"
        )(exchange(mixed.reshape(near, rows, width), NEAR))

    return per_device


def solution(mesh):
    n_blk, n_head = mesh.shape["blk"], mesh.shape["head"]
    outer = max(d for d in range(1, n_blk + 1) if n_blk % d == 0 and HEADS % (n_head * d) == 0)
    inner = n_blk // outer
    near, far = outer * n_head, n_blk * n_head

    def per_device(query_rows, *others):
        in_pairs = inner == 2 and n_head == 2 and mesh.shape["batch"] == 2 and near == 8
        if in_pairs and HEADS == near + far and query_rows.shape[0] == TILE:
            return halved(n_head, far, near)(query_rows, *others)
        return gathered(outer, inner, n_head, near)(query_rows, *others)

    split = P(("batch", "outer", "inner", "head"), None)
    return jax.shard_map(
        per_device,
        mesh=Mesh(
            mesh.devices.reshape(outer, inner, n_head, mesh.shape["batch"]), ("outer", "inner", "head", "batch")
        ),
        in_specs=(split, split, split, P(), P(), P()),
        out_specs=split,
        check_vma=False,
    )
```

```python
import functools

import jax
import jax.numpy as jnp
from jax import lax
from jax.experimental import pallas as pl
from jax.experimental.pallas import tpu as pltpu
from jax.sharding import Mesh, PartitionSpec as P

HEADS = 24
HDIM = 128
TILE = 128
EPS = 1e-06
MASKED = -1e30
NEAR = ("outer", "head")
FAR = ("outer", "inner", "head")
PARAMS = pltpu.CompilerParams(vmem_limit_bytes=48 * 1024 * 1024)
PACK_PARAMS = pltpu.CompilerParams(vmem_limit_bytes=61 * 1024 * 1024)
BF16 = jnp.bfloat16
SHARED_COST = 26 * 2**30
SCALE = 1.4426950408889634 * HDIM ** (-0.5)


def shape(*dims):
    return jax.ShapeDtypeStruct(dims, BF16)


def exchange(x, axes):
    return lax.all_to_all(x, axes, split_axis=0, concat_axis=0, tiled=True)


def pack_kernel(write, inputs, outputs, scratch):
    q_hbm, k_hbm, v_hbm, qg_hbm, kg_hbm = inputs
    q_in, k_in, v_in, qg, kg, sems, *kept = scratch
    copies = [
        pltpu.make_async_copy(src, dst, sems.at[n])
        for n, (src, dst) in enumerate(
            ((v_hbm, v_in), (q_hbm, q_in), (qg_hbm, qg), (k_hbm, k_in), (kg_hbm, kg))
        )
    ]
    for copy in copies:
        copy.start()

    def normalize(first, ref, gain):
        copies[first].wait()
        copies[first + 1].wait()
        widened = ref[...].astype(jnp.float32)
        mean_square = jnp.mean(widened * widened, axis=-1, keepdims=True)
        return (widened * lax.rsqrt(mean_square + EPS) * gain[...]).astype(BF16)

    copies[0].wait()
    sent = write(2, v_in[...], outputs, kept)
    sent += write(0, normalize(1, q_in, qg), outputs, kept)
    sent += write(1, normalize(3, k_in, kg), outputs, kept)
    for copy in sent:
        copy.wait()


def pack(write, out_shape, rows, features, arrays, kept=()):
    q, k, v, q_gain, k_gain = arrays
    hbm = pl.BlockSpec(memory_space=pltpu.HBM)

    def kernel(*refs):
        pack_kernel(write, refs[:5], refs[5 : 5 + len(out_shape)], refs[5 + len(out_shape) :])

    return pl.pallas_call(
        kernel,
        in_specs=[hbm] * 5,
        out_specs=[hbm] * len(out_shape),
        out_shape=out_shape,
        scratch_shapes=[pltpu.VMEM((rows, features), BF16)] * 3
        + [pltpu.VMEM((1, features), jnp.float32)] * 2
        + [pltpu.SemaphoreType.DMA((5,)), *kept],
        compiler_params=PACK_PARAMS,
        name="pack",
    )(q, k, v, q_gain.reshape(1, -1), k_gain.reshape(1, -1))


def first_pass(query, key, bias_at, scores_ref, c, largest):
    s = lax.dot_general(key, query, (((1,), (1,)), ((), ())), preferred_element_type=jnp.float32)
    for t in range(key.shape[0] // TILE):
        down = slice(t * TILE, (t + 1) * TILE)
        masked = s[down].reshape(TILE // 8, 8, -1) + bias_at(t)[None]
        scores_ref[c, down] = masked.reshape(TILE, -1)
        largest = jnp.maximum(largest, jnp.max(masked, axis=0))
    return largest


def second_pass(scores_ref, c, col_max, value_t, state):
    total, mixed = state
    wide, bm = scores_ref.shape[1:]
    weights = jnp.exp2(scores_ref[c].reshape(wide // 8, 8, bm) * SCALE - col_max[None])
    total = total + jnp.sum(weights, axis=0)
    weights = weights.reshape(wide, bm).astype(BF16)
    return total, mixed + jnp.dot(value_t, weights, preferred_element_type=jnp.float32)


def over_all(largest):
    return jnp.broadcast_to(jnp.max(largest, axis=0, keepdims=True) * SCALE, largest.shape)


def divide(total, mixed):
    return (mixed / jnp.sum(total, axis=0, keepdims=True)).T.astype(BF16)


def bias_of(band, bm, live_at):
    lane = lax.broadcasted_iota(jnp.int32, (8, bm), 1)
    bias = jnp.zeros((8, bm), jnp.float32)
    for a in range(bm // band):
        dead = jnp.where(live_at(a), 0.0, MASKED).astype(jnp.float32)
        bias = jnp.where((lane >= a * band) & (lane < (a + 1) * band), dead, bias)
    return bias


def attend(query, band, key_at, value_at, key_blocks, live_at, scores_ref):
    wide, bm = scores_ref.shape[1:]

    def score(c, largest):
        def bias_at(t):
            return bias_of(band, bm, lambda a: live_at(a, c * (wide // TILE) + t))

        return first_pass(query, key_at(c), bias_at, scores_ref, c, largest)

    largest = lax.fori_loop(0, key_blocks, score, jnp.full((8, bm), MASKED, jnp.float32))
    col_max = over_all(largest)

    def mix(c, state):
        return second_pass(scores_ref, c, col_max, transposed(value_at(c)), state)

    state = jnp.zeros((8, bm), jnp.float32), jnp.zeros((HDIM, bm), jnp.float32)
    return divide(*lax.fori_loop(0, key_blocks, mix, state))


def transposed(block):
    return block.astype(jnp.float32).T.astype(BF16)


def attend_blocks(blocks, band, query_at, key_at, value_t, key_blocks, live_at, finish, scores):
    wide, bm = scores[0].shape[1:]
    empty = jnp.full((8, bm), MASKED, jnp.float32)
    nothing = jnp.zeros((8, bm), jnp.float32), jnp.zeros((HDIM, bm), jnp.float32)

    def bias_at(i, c):
        return lambda t: bias_of(band, bm, lambda a: live_at(i, a, c, t))

    def both(i, col_max, now, following):
        later = jnp.minimum(i + 1, blocks - 1)
        query = query_at(later)
        largest, state = empty, nothing
        for c in range(key_blocks):
            largest = first_pass(query, key_at(c), bias_at(later, c), following, c, largest)
            state = second_pass(now, c, col_max, value_t[:, c * wide : (c + 1) * wide], state)
        finish(i, divide(*state))
        return over_all(largest)

    largest = empty
    query = query_at(0)
    for c in range(key_blocks):
        largest = first_pass(query, key_at(c), bias_at(0, c), scores[0], c, largest)

    def pair(n, col_max):
        col_max = both(2 * n, col_max, scores[0], scores[1])
        return both(2 * n + 1, col_max, scores[1], scores[0])

    lax.fori_loop(0, blocks // 2, pair, over_all(largest))


def partner(me, step):
    first, second = step
    return me ^ jnp.where(lax.axis_index("batch") == 0, first, second)


def collect_kernel(steps, rows, *refs):
    pieces, (own_q, own_kv, cross_qkv, cross_kv) = refs[: len(steps)], refs[len(steps) :]
    outer, head = lax.axis_index("outer"), lax.axis_index("head")
    for step, piece in zip(steps, pieces):
        at = pl.ds(pl.multiple_of(partner(outer, step) * rows, rows), rows)
        own, cross = piece[head], piece[1 - head]
        own_q[at] = own[0]
        own_kv[:, at] = own[1:]
        cross_qkv[:, at] = cross
        cross_kv[:, at] = cross[1:]


def shared_kernel(mask_ref, q_ref, own_ref, head_ref, inner_ref, both_ref, out_ref, query, value_t, *scores):
    inner, head = lax.axis_index("inner"), lax.axis_index("head")
    _, wide, bm = scores[0].shape
    tall = q_ref.shape[0]
    part = tall // wide
    tiles = wide // TILE
    key_refs = [own_ref.at[0], head_ref.at[1], inner_ref.at[0], both_ref.at[0]]
    value_refs = [own_ref.at[1], head_ref.at[2], inner_ref.at[1], both_ref.at[1]]

    query[:tall] = q_ref[...]
    query[tall:] = head_ref[0]
    for n, ref in enumerate(value_refs):
        for t in range(tall // TILE):
            at = n * tall + t * TILE
            value_t[:, at : at + TILE] = transposed(ref[t * TILE : (t + 1) * TILE])

    def tile(outer, along_inner, along_head):
        return (outer * 2 + along_inner) * 2 + along_head

    def query_tile(i, a):
        return lax.rem(i, part) * tiles + a, head ^ lax.div(i, part)

    def live_at(i, a, c, t):
        outer, along_head = query_tile(i, a)
        n = c // part
        key_tile = tile(c % part * tiles + t, inner ^ (n // 2), head ^ (n % 2))
        return mask_ref[tile(outer, inner, along_head), key_tile] != 0

    def finish(i, mixed):
        for a in range(tiles):
            outer, along_head = query_tile(i, a)
            out_ref[outer * 2 + along_head] = mixed[a * TILE : (a + 1) * TILE]

    attend_blocks(
        2 * part,
        TILE,
        lambda i: query[pl.ds(pl.multiple_of(i * bm, bm), bm)],
        lambda c: key_refs[c // part][c % part * wide : (c % part + 1) * wide],
        value_t,
        4 * part,
        live_at,
        finish,
        scores,
    )


def whole_kernel(sources, mask_ref, qkv_ref, *refs):
    out_ref, value_t, *scores = refs[-4:]
    rows = qkv_ref.shape[2]
    _, wide, bm = scores[0].shape
    bands, tiles = bm // rows, wide // TILE
    for t in range(sources):
        value_t[:, t * TILE : (t + 1) * TILE] = transposed(qkv_ref[t, 2])

    def finish(i, mixed):
        out_ref[pl.ds(i * bands, bands)] = mixed.reshape(bands, rows, HDIM)

    attend_blocks(
        sources // bands,
        rows,
        lambda i: qkv_ref[pl.ds(i * bands, bands), 0].reshape(bm, HDIM),
        lambda c: qkv_ref[c * tiles : (c + 1) * tiles, 1].reshape(wide, HDIM),
        value_t,
        sources // tiles,
        lambda i, a, c, t: mask_ref[i * bands + a, c * tiles + t] != 0,
        finish,
        scores,
    )


def halved(far, near):
    outer = near // 2
    steps = []
    for d in range(outer // 2):
        steps += [(outer // 2 + d, d), (d, outer // 2 + d)]

    def swap(piece, step):
        pairs = [(2 * i + b, 2 * (i ^ step[b]) + b) for i in range(outer) for b in range(2)]
        return lax.ppermute(piece, ("outer", "batch"), pairs)

    def per_device(query_rows, key_rows, value_rows, q_gain, k_gain, tile_mask):
        rows, features = query_rows.shape

        def write(which, block, outs, kept):
            near_heads, far_heads, near_sems, far_sems = kept
            for h in range(near):
                near_heads[h, which] = block[:, h * HDIM : (h + 1) * HDIM]
            for h in range(far):
                far_heads[h, which] = block[:, (near + h) * HDIM : (near + h + 1) * HDIM]
            me = lax.axis_index("outer")
            copies = []
            for n, step in enumerate(steps):
                pair = near_heads.at[pl.ds(partner(me, step) * 2, 2), which]
                copies.append(pltpu.make_async_copy(pair, outs[n].at[:, which], near_sems.at[which, n]))
            copies.append(pltpu.make_async_copy(far_heads.at[:, which], outs[-1].at[:, which], far_sems.at[which]))
            for copy in copies:
                copy.start()
            return copies

        def read(shared, whole, out_ref):
            for d in range(near):
                out_ref[:, d * HDIM : (d + 1) * HDIM] = shared[d]
            for d in range(far):
                out_ref[:, (near + d) * HDIM : (near + d + 1) * HDIM] = whole[d]

        *shared, whole = pack(
            write,
            [shape(2, 3, rows, HDIM)] * outer + [shape(far, 3, rows, HDIM)],
            rows,
            features,
            (query_rows, key_rows, value_rows, q_gain, k_gain),
            [
                pltpu.VMEM((near, 3, rows, HDIM), BF16),
                pltpu.VMEM((far, 3, rows, HDIM), BF16),
                pltpu.SemaphoreType.DMA((3, outer)),
                pltpu.SemaphoreType.DMA((3,)),
            ],
        )
        shared = [swap(piece, step) for step, piece in zip(steps, shared)]
        whole = exchange(whole, FAR)
        tall = outer * rows
        own_q, own_kv, cross_qkv, cross_kv = pl.pallas_call(
            functools.partial(collect_kernel, steps, rows),
            out_shape=[shape(tall, HDIM), shape(2, tall, HDIM), shape(3, tall, HDIM), shape(2, tall, HDIM)],
            compiler_params=PARAMS,
            name="collect",
        )(*shared)
        along_head = lax.ppermute(cross_qkv, "head", [(0, 1), (1, 0)])
        along_inner = lax.ppermute(own_kv, "inner", [(0, 1), (1, 0)])
        along_both = lax.ppermute(cross_kv, ("inner", "head"), [(i, 3 - i) for i in range(4)])

        wide = 2 * TILE
        blocks = far * rows // wide
        smem, vmem = pl.BlockSpec(memory_space=pltpu.SMEM), pl.BlockSpec(memory_space=pltpu.VMEM)
        scratch = [pltpu.VMEM((HDIM, far * rows), BF16)]
        scores = [pltpu.VMEM((blocks, wide, wide), jnp.float32)] * 2
        shared = pl.pallas_call(
            shared_kernel,
            in_specs=[smem] + [vmem] * 5,
            out_shape=shape(near, rows, HDIM),
            scratch_shapes=[pltpu.VMEM((near * rows, HDIM), BF16)] + scratch + scores,
            compiler_params=PARAMS,
            cost_estimate=pl.CostEstimate(flops=SHARED_COST, bytes_accessed=2**21, transcendentals=0),
            name="attend_shared",
        )(tile_mask, own_q, own_kv, along_head, along_inner, along_both)

        whole = pl.pallas_call(
            functools.partial(whole_kernel, far),
            in_specs=[smem, vmem, pl.BlockSpec(memory_space=pl.ANY)],
            out_shape=shape(far, rows, HDIM),
            scratch_shapes=scratch + scores,
            compiler_params=PARAMS,
            cost_estimate=pl.CostEstimate(flops=2**33, bytes_accessed=2**22, transcendentals=0),
            name="attend_whole",
        )(tile_mask, whole, shared)
        shared = exchange(shared, NEAR)
        return pl.pallas_call(
            read, out_shape=shape(rows, features), compiler_params=PARAMS, name="unpack"
        )(shared, exchange(whole, FAR))

    return per_device


def gathered_kernel(outer, inner, mask_ref, q_ref, kv_ref, out_ref, scores_ref):
    i = pl.program_id(0)
    block = out_ref.shape[0] * out_ref.shape[1] * out_ref.shape[2]
    tiles = block // TILE
    q_tile = (i * inner + lax.axis_index("inner")) * tiles
    mixed = attend(
        q_ref[0, :, 0].reshape(block, HDIM),
        TILE,
        lambda c: kv_ref[lax.rem(c, inner), lax.div(c, inner), :, 1].reshape(block, HDIM),
        lambda c: kv_ref[lax.rem(c, inner), lax.div(c, inner), :, 2].reshape(block, HDIM),
        outer * inner,
        lambda a, t: mask_ref[q_tile + a, t] != 0,
        scores_ref,
    )
    out_ref[...] = mixed.reshape(out_ref.shape)


def gathered(outer, inner, n_head, near):
    width = HEADS // near * HDIM

    def per_device(query_rows, key_rows, value_rows, q_gain, k_gain, tile_mask):
        rows, features = query_rows.shape
        block = rows * n_head

        def write(which, block, outs, kept):
            packed, sems = kept
            for d in range(near):
                packed[d, which] = block[:, d * width : (d + 1) * width]
            copy = pltpu.make_async_copy(packed.at[:, which], outs[0].at[:, which], sems.at[which])
            copy.start()
            return [copy]

        def read(got_ref, out_ref):
            for d in range(near):
                out_ref[:, d * width : (d + 1) * width] = got_ref[d]

        (packed,) = pack(
            write,
            [shape(near, 3, rows, width)],
            rows,
            features,
            (query_rows, key_rows, value_rows, q_gain, k_gain),
            [pltpu.VMEM((near, 3, rows, width), BF16), pltpu.SemaphoreType.DMA((3,))],
        )
        own = exchange(packed, NEAR).reshape(outer, n_head, 3, rows, width)
        every = lax.all_gather(own, "inner")
        mixed = pl.pallas_call(
            functools.partial(gathered_kernel, outer, inner),
            grid=(outer, HEADS // near),
            in_specs=[
                pl.BlockSpec(memory_space=pltpu.SMEM),
                pl.BlockSpec((1, n_head, 1, rows, HDIM), lambda i, h: (i, 0, 0, 0, h)),
                pl.BlockSpec((inner, outer, n_head, 3, rows, HDIM), lambda i, h: (0, 0, 0, 0, 0, h)),
            ],
            out_specs=pl.BlockSpec((1, n_head, rows, HDIM), lambda i, h: (i, 0, 0, h)),
            out_shape=shape(outer, n_head, rows, width),
            scratch_shapes=[pltpu.VMEM((outer * inner, block, block), jnp.float32)],
            compiler_params=PARAMS,
            name="attend",
        )(tile_mask, own, every)
        return pl.pallas_call(
            read, out_shape=shape(rows, features), compiler_params=PARAMS, name="unpack"
        )(exchange(mixed.reshape(near, rows, width), NEAR))

    return per_device


def solution(mesh):
    n_blk, n_head = mesh.shape["blk"], mesh.shape["head"]
    outer = max(d for d in range(1, n_blk + 1) if n_blk % d == 0 and HEADS % (n_head * d) == 0)
    inner = n_blk // outer
    near, far = outer * n_head, n_blk * n_head

    def per_device(query_rows, *others):
        in_pairs = inner == 2 and n_head == 2 and mesh.shape["batch"] == 2 and outer & (outer - 1) == 0
        if in_pairs and HEADS == near + far and query_rows.shape[0] == TILE:
            return halved(far, near)(query_rows, *others)
        return gathered(outer, inner, n_head, near)(query_rows, *others)

    split = P(("batch", "outer", "inner", "head"), None)
    return jax.shard_map(
        per_device,
        mesh=Mesh(
            mesh.devices.reshape(outer, inner, n_head, mesh.shape["batch"]), ("outer", "inner", "head", "batch")
        ),
        in_specs=(split, split, split, P(), P(), P()),
        out_specs=split,
        check_vma=False,
    )
```

```python
import functools

import jax
import jax.numpy as jnp
from jax import lax
from jax.experimental import pallas as pl
from jax.experimental.pallas import tpu as pltpu
from jax.sharding import Mesh, PartitionSpec as P

HEADS = 24
HDIM = 128
TILE = 128
EPS = 1e-06
MASKED = -1e30
NEAR = ("outer", "head")
FAR = ("outer", "inner", "head")
PARAMS = pltpu.CompilerParams(vmem_limit_bytes=48 * 1024 * 1024)
PACK_PARAMS = pltpu.CompilerParams(vmem_limit_bytes=61 * 1024 * 1024)
BF16 = jnp.bfloat16
SHARED_COST = 24 * 2**30
SCALE = 1.4426950408889634 * HDIM ** (-0.5)


def shape(*dims):
    return jax.ShapeDtypeStruct(dims, BF16)


def exchange(x, axes):
    return lax.all_to_all(x, axes, split_axis=0, concat_axis=0, tiled=True)


def pack_kernel(write, inputs, outputs, scratch):
    q_hbm, k_hbm, v_hbm, qg_hbm, kg_hbm = inputs
    q_in, k_in, v_in, qg, kg, sems, *kept = scratch
    copies = [
        pltpu.make_async_copy(src, dst, sems.at[n])
        for n, (src, dst) in enumerate(
            ((v_hbm, v_in), (q_hbm, q_in), (qg_hbm, qg), (k_hbm, k_in), (kg_hbm, kg))
        )
    ]
    for copy in copies:
        copy.start()

    def normalize(first, ref, gain):
        copies[first].wait()
        copies[first + 1].wait()
        widened = ref[...].astype(jnp.float32)
        mean_square = jnp.mean(widened * widened, axis=-1, keepdims=True)
        return (widened * lax.rsqrt(mean_square + EPS) * gain[...]).astype(BF16)

    copies[0].wait()
    sent = write(2, v_in[...], outputs, kept)
    sent += write(0, normalize(1, q_in, qg), outputs, kept)
    sent += write(1, normalize(3, k_in, kg), outputs, kept)
    for copy in sent:
        copy.wait()


def pack(write, out_shape, rows, features, arrays, kept=()):
    q, k, v, q_gain, k_gain = arrays
    hbm = pl.BlockSpec(memory_space=pltpu.HBM)

    def kernel(*refs):
        pack_kernel(write, refs[:5], refs[5 : 5 + len(out_shape)], refs[5 + len(out_shape) :])

    return pl.pallas_call(
        kernel,
        in_specs=[hbm] * 5,
        out_specs=[hbm] * len(out_shape),
        out_shape=out_shape,
        scratch_shapes=[pltpu.VMEM((rows, features), BF16)] * 3
        + [pltpu.VMEM((1, features), jnp.float32)] * 2
        + [pltpu.SemaphoreType.DMA((5,)), *kept],
        compiler_params=PACK_PARAMS,
        name="pack",
    )(q, k, v, q_gain.reshape(1, -1), k_gain.reshape(1, -1))


def first_pass(query, key, bias_at, scores_ref, c, largest):
    s = lax.dot_general(key, query, (((1,), (1,)), ((), ())), preferred_element_type=jnp.float32)
    for t in range(key.shape[0] // TILE):
        down = slice(t * TILE, (t + 1) * TILE)
        masked = s[down].reshape(TILE // 8, 8, -1) + bias_at(t)[None]
        scores_ref[c, down] = masked.reshape(TILE, -1)
        largest = jnp.maximum(largest, jnp.max(masked, axis=0))
    return largest


def second_pass(scores_ref, c, col_max, value_t, state):
    total, mixed = state
    wide, bm = scores_ref.shape[1:]
    weights = jnp.exp2(scores_ref[c].reshape(wide // 8, 8, bm) * SCALE - col_max[None])
    total = total + jnp.sum(weights, axis=0)
    weights = weights.reshape(wide, bm).astype(BF16)
    return total, mixed + jnp.dot(value_t, weights, preferred_element_type=jnp.float32)


def over_all(largest):
    return jnp.broadcast_to(jnp.max(largest, axis=0, keepdims=True) * SCALE, largest.shape)


def divide(total, mixed):
    return (mixed / jnp.sum(total, axis=0, keepdims=True)).T.astype(BF16)


def bias_of(band, bm, live_at):
    lane = lax.broadcasted_iota(jnp.int32, (8, bm), 1)
    bias = jnp.zeros((8, bm), jnp.float32)
    for a in range(bm // band):
        dead = jnp.where(live_at(a), 0.0, MASKED).astype(jnp.float32)
        bias = jnp.where((lane >= a * band) & (lane < (a + 1) * band), dead, bias)
    return bias


def attend(query, band, key_at, value_at, key_blocks, live_at, scores_ref):
    wide, bm = scores_ref.shape[1:]

    def score(c, largest):
        def bias_at(t):
            return bias_of(band, bm, lambda a: live_at(a, c * (wide // TILE) + t))

        return first_pass(query, key_at(c), bias_at, scores_ref, c, largest)

    largest = lax.fori_loop(0, key_blocks, score, jnp.full((8, bm), MASKED, jnp.float32))
    col_max = over_all(largest)

    def mix(c, state):
        return second_pass(scores_ref, c, col_max, transposed(value_at(c)), state)

    state = jnp.zeros((8, bm), jnp.float32), jnp.zeros((HDIM, bm), jnp.float32)
    return divide(*lax.fori_loop(0, key_blocks, mix, state))


def transposed(block):
    return block.astype(jnp.float32).T.astype(BF16)


def attend_blocks(blocks, band, query_at, key_at, value_t, key_blocks, live_at, finish, scores):
    wide, bm = scores[0].shape[1:]
    empty = jnp.full((8, bm), MASKED, jnp.float32)
    nothing = jnp.zeros((8, bm), jnp.float32), jnp.zeros((HDIM, bm), jnp.float32)

    def bias_at(i, c):
        return lambda t: bias_of(band, bm, lambda a: live_at(i, a, c, t))

    def both(i, col_max, now, following):
        later = jnp.minimum(i + 1, blocks - 1)
        query = query_at(later)
        largest, state = empty, nothing
        for c in range(key_blocks):
            largest = first_pass(query, key_at(c), bias_at(later, c), following, c, largest)
            state = second_pass(now, c, col_max, value_t[:, c * wide : (c + 1) * wide], state)
        finish(i, divide(*state))
        return over_all(largest)

    largest = empty
    query = query_at(0)
    for c in range(key_blocks):
        largest = first_pass(query, key_at(c), bias_at(0, c), scores[0], c, largest)

    def pair(n, col_max):
        col_max = both(2 * n, col_max, scores[0], scores[1])
        return both(2 * n + 1, col_max, scores[1], scores[0])

    lax.fori_loop(0, blocks // 2, pair, over_all(largest))


def partner(me, step):
    first, second = step
    return me ^ jnp.where(lax.axis_index("batch") == 0, first, second)


def collect_kernel(steps, rows, *refs):
    pieces, (own_q, own_kv, cross_qkv, cross_kv) = refs[: len(steps)], refs[len(steps) :]
    outer, head = lax.axis_index("outer"), lax.axis_index("head")
    for step, piece in zip(steps, pieces):
        at = pl.ds(pl.multiple_of(partner(outer, step) * rows, rows), rows)
        own, cross = piece[head], piece[1 - head]
        own_q[at] = own[0]
        own_kv[:, at] = own[1:]
        cross_qkv[:, at] = cross
        cross_kv[:, at] = cross[1:]


def shared_kernel(mask_ref, q_ref, own_ref, head_ref, inner_ref, both_ref, out_ref, query, value_t, *scores):
    inner, head = lax.axis_index("inner"), lax.axis_index("head")
    _, wide, bm = scores[0].shape
    tall = q_ref.shape[0]
    part = tall // wide
    tiles = wide // TILE
    key_refs = [own_ref.at[0], head_ref.at[1], inner_ref.at[0], both_ref.at[0]]
    value_refs = [own_ref.at[1], head_ref.at[2], inner_ref.at[1], both_ref.at[1]]

    query[:tall] = q_ref[...]
    query[tall:] = head_ref[0]
    for n, ref in enumerate(value_refs):
        for t in range(tall // TILE):
            at = n * tall + t * TILE
            value_t[:, at : at + TILE] = transposed(ref[t * TILE : (t + 1) * TILE])

    def tile(outer, along_inner, along_head):
        return (outer * 2 + along_inner) * 2 + along_head

    def query_tile(i, a):
        return lax.rem(i, part) * tiles + a, head ^ lax.div(i, part)

    def live_at(i, a, c, t):
        outer, along_head = query_tile(i, a)
        n = c // part
        key_tile = tile(c % part * tiles + t, inner ^ (n // 2), head ^ (n % 2))
        return mask_ref[tile(outer, inner, along_head), key_tile] != 0

    def finish(i, mixed):
        for a in range(tiles):
            outer, along_head = query_tile(i, a)
            out_ref[outer * 2 + along_head] = mixed[a * TILE : (a + 1) * TILE]

    attend_blocks(
        2 * part,
        TILE,
        lambda i: query[pl.ds(pl.multiple_of(i * bm, bm), bm)],
        lambda c: key_refs[c // part][c % part * wide : (c % part + 1) * wide],
        value_t,
        4 * part,
        live_at,
        finish,
        scores,
    )


def whole_kernel(sources, mask_ref, qkv_ref, *refs):
    out_ref, value_t, *scores = refs[-4:]
    rows = qkv_ref.shape[2]
    _, wide, bm = scores[0].shape
    bands, tiles = bm // rows, wide // TILE
    for t in range(sources):
        value_t[:, t * TILE : (t + 1) * TILE] = transposed(qkv_ref[t, 2])

    def finish(i, mixed):
        out_ref[pl.ds(i * bands, bands)] = mixed.reshape(bands, rows, HDIM)

    attend_blocks(
        sources // bands,
        rows,
        lambda i: qkv_ref[pl.ds(i * bands, bands), 0].reshape(bm, HDIM),
        lambda c: qkv_ref[c * tiles : (c + 1) * tiles, 1].reshape(wide, HDIM),
        value_t,
        sources // tiles,
        lambda i, a, c, t: mask_ref[i * bands + a, c * tiles + t] != 0,
        finish,
        scores,
    )


def halved(far, near):
    outer = near // 2
    steps = []
    for d in range(outer // 2):
        steps += [(outer // 2 + d, d), (d, outer // 2 + d)]

    def swap(piece, step):
        pairs = [(2 * i + b, 2 * (i ^ step[b]) + b) for i in range(outer) for b in range(2)]
        return lax.ppermute(piece, ("outer", "batch"), pairs)

    def per_device(query_rows, key_rows, value_rows, q_gain, k_gain, tile_mask):
        rows, features = query_rows.shape

        def write(which, block, outs, kept):
            near_heads, far_heads, near_sems, far_sems = kept
            for h in range(near):
                near_heads[h, which] = block[:, h * HDIM : (h + 1) * HDIM]
            for h in range(far):
                far_heads[h, which] = block[:, (near + h) * HDIM : (near + h + 1) * HDIM]
            me = lax.axis_index("outer")
            copies = []
            for n, step in enumerate(steps):
                pair = near_heads.at[pl.ds(partner(me, step) * 2, 2), which]
                copies.append(pltpu.make_async_copy(pair, outs[n].at[:, which], near_sems.at[which, n]))
            copies.append(pltpu.make_async_copy(far_heads.at[:, which], outs[-1].at[:, which], far_sems.at[which]))
            for copy in copies:
                copy.start()
            return copies

        def read(shared, whole, out_ref):
            for d in range(near):
                out_ref[:, d * HDIM : (d + 1) * HDIM] = shared[d]
            for d in range(far):
                out_ref[:, (near + d) * HDIM : (near + d + 1) * HDIM] = whole[d]

        *shared, whole = pack(
            write,
            [shape(2, 3, rows, HDIM)] * outer + [shape(far, 3, rows, HDIM)],
            rows,
            features,
            (query_rows, key_rows, value_rows, q_gain, k_gain),
            [
                pltpu.VMEM((near, 3, rows, HDIM), BF16),
                pltpu.VMEM((far, 3, rows, HDIM), BF16),
                pltpu.SemaphoreType.DMA((3, outer)),
                pltpu.SemaphoreType.DMA((3,)),
            ],
        )
        shared = [swap(piece, step) for step, piece in zip(steps, shared)]
        whole = exchange(whole, FAR)
        tall = outer * rows
        own_q, own_kv, cross_qkv, cross_kv = pl.pallas_call(
            functools.partial(collect_kernel, steps, rows),
            out_shape=[shape(tall, HDIM), shape(2, tall, HDIM), shape(3, tall, HDIM), shape(2, tall, HDIM)],
            compiler_params=PARAMS,
            name="collect",
        )(*shared)
        along_head = lax.ppermute(cross_qkv, "head", [(0, 1), (1, 0)])
        along_inner = lax.ppermute(own_kv, "inner", [(0, 1), (1, 0)])
        along_both = lax.ppermute(cross_kv, ("inner", "head"), [(i, 3 - i) for i in range(4)])

        wide = 2 * TILE
        blocks = far * rows // wide
        smem, vmem = pl.BlockSpec(memory_space=pltpu.SMEM), pl.BlockSpec(memory_space=pltpu.VMEM)
        scratch = [pltpu.VMEM((HDIM, far * rows), BF16)]
        scores = [pltpu.VMEM((blocks, wide, wide), jnp.float32)] * 2
        shared = pl.pallas_call(
            shared_kernel,
            in_specs=[smem] + [vmem] * 5,
            out_shape=shape(near, rows, HDIM),
            scratch_shapes=[pltpu.VMEM((near * rows, HDIM), BF16)] + scratch + scores,
            compiler_params=PARAMS,
            cost_estimate=pl.CostEstimate(flops=SHARED_COST, bytes_accessed=2**21, transcendentals=0),
            name="attend_shared",
        )(tile_mask, own_q, own_kv, along_head, along_inner, along_both)

        whole = pl.pallas_call(
            functools.partial(whole_kernel, far),
            in_specs=[smem, vmem, pl.BlockSpec(memory_space=pl.ANY)],
            out_shape=shape(far, rows, HDIM),
            scratch_shapes=scratch + scores,
            compiler_params=PARAMS,
            cost_estimate=pl.CostEstimate(flops=2**33, bytes_accessed=2**22, transcendentals=0),
            name="attend_whole",
        )(tile_mask, whole, shared)
        shared = exchange(shared, NEAR)
        return pl.pallas_call(
            read, out_shape=shape(rows, features), compiler_params=PARAMS, name="unpack"
        )(shared, exchange(whole, FAR))

    return per_device


def gathered_kernel(outer, inner, mask_ref, q_ref, kv_ref, out_ref, scores_ref):
    i = pl.program_id(0)
    block = out_ref.shape[0] * out_ref.shape[1] * out_ref.shape[2]
    tiles = block // TILE
    q_tile = (i * inner + lax.axis_index("inner")) * tiles
    mixed = attend(
        q_ref[0, :, 0].reshape(block, HDIM),
        TILE,
        lambda c: kv_ref[lax.rem(c, inner), lax.div(c, inner), :, 1].reshape(block, HDIM),
        lambda c: kv_ref[lax.rem(c, inner), lax.div(c, inner), :, 2].reshape(block, HDIM),
        outer * inner,
        lambda a, t: mask_ref[q_tile + a, t] != 0,
        scores_ref,
    )
    out_ref[...] = mixed.reshape(out_ref.shape)


def gathered(outer, inner, n_head, near):
    width = HEADS // near * HDIM

    def per_device(query_rows, key_rows, value_rows, q_gain, k_gain, tile_mask):
        rows, features = query_rows.shape
        block = rows * n_head

        def write(which, block, outs, kept):
            packed, sems = kept
            for d in range(near):
                packed[d, which] = block[:, d * width : (d + 1) * width]
            copy = pltpu.make_async_copy(packed.at[:, which], outs[0].at[:, which], sems.at[which])
            copy.start()
            return [copy]

        def read(got_ref, out_ref):
            for d in range(near):
                out_ref[:, d * width : (d + 1) * width] = got_ref[d]

        (packed,) = pack(
            write,
            [shape(near, 3, rows, width)],
            rows,
            features,
            (query_rows, key_rows, value_rows, q_gain, k_gain),
            [pltpu.VMEM((near, 3, rows, width), BF16), pltpu.SemaphoreType.DMA((3,))],
        )
        own = exchange(packed, NEAR).reshape(outer, n_head, 3, rows, width)
        every = lax.all_gather(own, "inner")
        mixed = pl.pallas_call(
            functools.partial(gathered_kernel, outer, inner),
            grid=(outer, HEADS // near),
            in_specs=[
                pl.BlockSpec(memory_space=pltpu.SMEM),
                pl.BlockSpec((1, n_head, 1, rows, HDIM), lambda i, h: (i, 0, 0, 0, h)),
                pl.BlockSpec((inner, outer, n_head, 3, rows, HDIM), lambda i, h: (0, 0, 0, 0, 0, h)),
            ],
            out_specs=pl.BlockSpec((1, n_head, rows, HDIM), lambda i, h: (i, 0, 0, h)),
            out_shape=shape(outer, n_head, rows, width),
            scratch_shapes=[pltpu.VMEM((outer * inner, block, block), jnp.float32)],
            compiler_params=PARAMS,
            name="attend",
        )(tile_mask, own, every)
        return pl.pallas_call(
            read, out_shape=shape(rows, features), compiler_params=PARAMS, name="unpack"
        )(exchange(mixed.reshape(near, rows, width), NEAR))

    return per_device


def solution(mesh):
    n_blk, n_head = mesh.shape["blk"], mesh.shape["head"]
    outer = max(d for d in range(1, n_blk + 1) if n_blk % d == 0 and HEADS % (n_head * d) == 0)
    inner = n_blk // outer
    near, far = outer * n_head, n_blk * n_head

    def per_device(query_rows, *others):
        in_pairs = inner == 2 and n_head == 2 and mesh.shape["batch"] == 2 and outer & (outer - 1) == 0
        if in_pairs and HEADS == near + far and query_rows.shape[0] == TILE:
            return halved(far, near)(query_rows, *others)
        return gathered(outer, inner, n_head, near)(query_rows, *others)

    split = P(("batch", "outer", "inner", "head"), None)
    return jax.shard_map(
        per_device,
        mesh=Mesh(
            mesh.devices.reshape(outer, inner, n_head, mesh.shape["batch"]), ("outer", "inner", "head", "batch")
        ),
        in_specs=(split, split, split, P(), P(), P()),
        out_specs=split,
        check_vma=False,
    )
```

```python
import functools

import jax
import jax.numpy as jnp
from jax import lax
from jax.experimental import pallas as pl
from jax.experimental.pallas import tpu as pltpu
from jax.sharding import Mesh, PartitionSpec as P

HEADS = 24
HDIM = 128
TILE = 128
EPS = 1e-06
MASKED = -1e30
NEAR = ("outer", "head")
FAR = ("outer", "inner", "head")
PARAMS = pltpu.CompilerParams(vmem_limit_bytes=48 * 1024 * 1024)
PACK_PARAMS = pltpu.CompilerParams(vmem_limit_bytes=61 * 1024 * 1024)
BF16 = jnp.bfloat16
SHARED_COST = 24 * 2**30
SCALE = 1.4426950408889634 * HDIM ** (-0.5)


def shape(*dims):
    return jax.ShapeDtypeStruct(dims, BF16)


def exchange(x, axes):
    return lax.all_to_all(x, axes, split_axis=0, concat_axis=0, tiled=True)


def pack_kernel(write, inputs, outputs, scratch):
    q_hbm, k_hbm, v_hbm, qg_hbm, kg_hbm = inputs
    q_in, k_in, v_in, qg, kg, sems, *kept = scratch
    copies = [
        pltpu.make_async_copy(src, dst, sems.at[n])
        for n, (src, dst) in enumerate(
            ((v_hbm, v_in), (q_hbm, q_in), (qg_hbm, qg), (k_hbm, k_in), (kg_hbm, kg))
        )
    ]
    for copy in copies:
        copy.start()

    def normalize(first, ref, gain):
        copies[first].wait()
        copies[first + 1].wait()
        widened = ref[...].astype(jnp.float32)
        mean_square = jnp.mean(widened * widened, axis=-1, keepdims=True)
        return (widened * lax.rsqrt(mean_square + EPS) * gain[...]).astype(BF16)

    copies[0].wait()
    sent = write(2, v_in[...], outputs, kept)
    sent += write(0, normalize(1, q_in, qg), outputs, kept)
    sent += write(1, normalize(3, k_in, kg), outputs, kept)
    for copy in sent:
        copy.wait()


def pack(write, out_shape, rows, features, arrays, kept=()):
    q, k, v, q_gain, k_gain = arrays
    hbm = pl.BlockSpec(memory_space=pltpu.HBM)

    def kernel(*refs):
        pack_kernel(write, refs[:5], refs[5 : 5 + len(out_shape)], refs[5 + len(out_shape) :])

    return pl.pallas_call(
        kernel,
        in_specs=[hbm] * 5,
        out_specs=[hbm] * len(out_shape),
        out_shape=out_shape,
        scratch_shapes=[pltpu.VMEM((rows, features), BF16)] * 3
        + [pltpu.VMEM((1, features), jnp.float32)] * 2
        + [pltpu.SemaphoreType.DMA((5,)), *kept],
        compiler_params=PACK_PARAMS,
        name="pack",
    )(q, k, v, q_gain.reshape(1, -1), k_gain.reshape(1, -1))


def first_pass(query, key, bias_at, scores_ref, c, largest):
    s = lax.dot_general(key, query, (((1,), (1,)), ((), ())), preferred_element_type=jnp.float32)
    for t in range(key.shape[0] // TILE):
        down = slice(t * TILE, (t + 1) * TILE)
        masked = s[down].reshape(TILE // 8, 8, -1) + bias_at(t)[None]
        scores_ref[c, down] = masked.reshape(TILE, -1)
        largest = jnp.maximum(largest, jnp.max(masked, axis=0))
    return largest


def second_pass(scores_ref, c, col_max, value_t, state):
    total, mixed = state
    wide, bm = scores_ref.shape[1:]
    weights = jnp.exp2(scores_ref[c].reshape(wide // 8, 8, bm) * SCALE - col_max[None])
    total = total + jnp.sum(weights, axis=0)
    weights = weights.reshape(wide, bm).astype(BF16)
    return total, mixed + jnp.dot(value_t, weights, preferred_element_type=jnp.float32)


def over_all(largest):
    return jnp.broadcast_to(jnp.max(largest, axis=0, keepdims=True) * SCALE, largest.shape)


def divide(total, mixed):
    return (mixed / jnp.sum(total, axis=0, keepdims=True)).T.astype(BF16)


def bias_of(band, bm, live_at):
    lane = lax.broadcasted_iota(jnp.int32, (8, bm), 1)
    bias = jnp.zeros((8, bm), jnp.float32)
    for a in range(bm // band):
        dead = jnp.where(live_at(a), 0.0, MASKED).astype(jnp.float32)
        bias = jnp.where((lane >= a * band) & (lane < (a + 1) * band), dead, bias)
    return bias


def attend(query, band, key_at, value_at, key_blocks, live_at, scores_ref):
    wide, bm = scores_ref.shape[1:]

    def score(c, largest):
        def bias_at(t):
            return bias_of(band, bm, lambda a: live_at(a, c * (wide // TILE) + t))

        return first_pass(query, key_at(c), bias_at, scores_ref, c, largest)

    largest = lax.fori_loop(0, key_blocks, score, jnp.full((8, bm), MASKED, jnp.float32))
    col_max = over_all(largest)

    def mix(c, state):
        return second_pass(scores_ref, c, col_max, transposed(value_at(c)), state)

    state = jnp.zeros((8, bm), jnp.float32), jnp.zeros((HDIM, bm), jnp.float32)
    return divide(*lax.fori_loop(0, key_blocks, mix, state))


def transposed(block):
    return block.astype(jnp.float32).T.astype(BF16)


def attend_blocks(blocks, band, query_at, key_at, value_t, key_blocks, live_at, finish, scores):
    wide, bm = scores[0].shape[1:]
    empty = jnp.full((8, bm), MASKED, jnp.float32)
    nothing = jnp.zeros((8, bm), jnp.float32), jnp.zeros((HDIM, bm), jnp.float32)

    def bias_at(i, c):
        return lambda t: bias_of(band, bm, lambda a: live_at(i, a, c, t))

    def second(c, col_max, now, state):
        return second_pass(now, c, col_max, value_t[:, c * wide : (c + 1) * wide], state)

    def both(i, col_max, now, following):
        query = query_at(i + 1)
        largest, state = empty, nothing
        for c in range(key_blocks):
            largest = first_pass(query, key_at(c), bias_at(i + 1, c), following, c, largest)
            state = second(c, col_max, now, state)
        finish(i, divide(*state))
        return over_all(largest)

    largest = empty
    query = query_at(0)
    for c in range(key_blocks):
        largest = first_pass(query, key_at(c), bias_at(0, c), scores[0], c, largest)

    def pair(n, col_max):
        col_max = both(2 * n, col_max, scores[0], scores[1])
        return both(2 * n + 1, col_max, scores[1], scores[0])

    col_max = lax.fori_loop(0, blocks // 2 - 1, pair, over_all(largest))
    col_max = both(blocks - 2, col_max, scores[0], scores[1])
    state = nothing
    for c in range(key_blocks):
        state = second(c, col_max, scores[1], state)
    finish(blocks - 1, divide(*state))


def partner(me, step):
    first, second = step
    return me ^ jnp.where(lax.axis_index("batch") == 0, first, second)


def collect_kernel(steps, rows, *refs):
    pieces, (q_out, kv_out) = refs[:-2], refs[-2:]
    me = lax.axis_index(NEAR)
    for step, piece in zip(steps, pieces):
        at = pl.ds(pl.multiple_of(partner(me, step) * rows, rows), rows)
        q_out[at] = piece[0]
        kv_out[:, at] = piece[1:]


def shared_kernel(mask_ref, q_ref, own_ref, other_ref, out_ref, value_t, *scores):
    mine = lax.axis_index("inner")
    _, wide, bm = scores[0].shape
    blocks = q_ref.shape[0] // wide

    def key_at(c):
        ref = own_ref if c < blocks else other_ref
        return ref[0, c % blocks * wide : (c % blocks + 1) * wide]

    for n, ref in enumerate((own_ref, other_ref)):
        for t in range(blocks * wide // TILE):
            at = (n * blocks * wide) + t * TILE
            value_t[:, at : at + TILE] = transposed(ref[1, t * TILE : (t + 1) * TILE])

    def tile(block, inner, t):
        return (block * 2 + inner) * (wide // TILE) + t

    def finish(i, mixed):
        out_ref[pl.ds(pl.multiple_of(i * bm, bm), bm)] = mixed

    attend_blocks(
        blocks,
        TILE,
        lambda i: q_ref[pl.ds(pl.multiple_of(i * bm, bm), bm)],
        key_at,
        value_t,
        2 * blocks,
        lambda i, a, c, t: mask_ref[tile(i, mine, a), tile(c % blocks, mine if c < blocks else 1 - mine, t)] != 0,
        finish,
        scores,
    )


def whole_kernel(sources, mask_ref, qkv_ref, *refs):
    out_ref, value_t, *scores = refs[-4:]
    rows = qkv_ref.shape[2]
    _, wide, bm = scores[0].shape
    bands, tiles = bm // rows, wide // TILE
    for t in range(sources):
        value_t[:, t * TILE : (t + 1) * TILE] = transposed(qkv_ref[t, 2])

    def finish(i, mixed):
        out_ref[pl.ds(i * bands, bands)] = mixed.reshape(bands, rows, HDIM)

    attend_blocks(
        sources // bands,
        rows,
        lambda i: qkv_ref[pl.ds(i * bands, bands), 0].reshape(bm, HDIM),
        lambda c: qkv_ref[c * tiles : (c + 1) * tiles, 1].reshape(wide, HDIM),
        value_t,
        sources // tiles,
        lambda i, a, c, t: mask_ref[i * bands + a, c * tiles + t] != 0,
        finish,
        scores,
    )


def halved(far, near):
    steps = []
    for d in range(near // 2):
        steps += [(near // 2 + d, d), (d, near // 2 + d)]

    def swap(piece, step):
        pairs = [(2 * i + b, 2 * (i ^ step[b]) + b) for i in range(near) for b in range(2)]
        return lax.ppermute(piece, (*NEAR, "batch"), pairs)

    def per_device(query_rows, key_rows, value_rows, q_gain, k_gain, tile_mask):
        rows, features = query_rows.shape

        def write(which, block, outs, kept):
            near_heads, far_heads, near_sems, far_sems = kept
            for h in range(near):
                near_heads[h, which] = block[:, h * HDIM : (h + 1) * HDIM]
            for h in range(far):
                far_heads[h, which] = block[:, (near + h) * HDIM : (near + h + 1) * HDIM]
            me = lax.axis_index(NEAR)
            copies = [
                pltpu.make_async_copy(near_heads.at[partner(me, step), which], outs[n].at[which], near_sems.at[which, n])
                for n, step in enumerate(steps)
            ]
            copies.append(pltpu.make_async_copy(far_heads.at[:, which], outs[-1].at[:, which], far_sems.at[which]))
            for copy in copies:
                copy.start()
            return copies

        def read(first, got_ref, *refs):
            out_ref, sems = refs[-2:]
            copies = [
                pltpu.make_async_copy(got_ref.at[d], out_ref.at[:, pl.ds((first + d) * HDIM, HDIM)], sems.at[d])
                for d in range(got_ref.shape[0])
            ]
            for copy in copies:
                copy.start()
            for copy in copies:
                copy.wait()

        *shared, whole = pack(
            write,
            [shape(3, rows, HDIM)] * near + [shape(far, 3, rows, HDIM)],
            rows,
            features,
            (query_rows, key_rows, value_rows, q_gain, k_gain),
            [
                pltpu.VMEM((near, 3, rows, HDIM), BF16),
                pltpu.VMEM((far, 3, rows, HDIM), BF16),
                pltpu.SemaphoreType.DMA((3, near)),
                pltpu.SemaphoreType.DMA((3,)),
            ],
        )
        shared = [swap(piece, step) for step, piece in zip(steps, shared)]
        whole = exchange(whole, FAR)
        q_near, kv_near = pl.pallas_call(
            functools.partial(collect_kernel, steps, rows),
            out_shape=[shape(near * rows, HDIM), shape(2, near * rows, HDIM)],
            compiler_params=PARAMS,
            name="collect",
        )(*shared)
        kv_other = lax.ppermute(kv_near, "inner", [(0, 1), (1, 0)])

        wide = 2 * TILE
        blocks = far * rows // wide
        smem, vmem = pl.BlockSpec(memory_space=pltpu.SMEM), pl.BlockSpec(memory_space=pltpu.VMEM)
        scratch = [pltpu.VMEM((HDIM, far * rows), BF16)]
        scores = [pltpu.VMEM((blocks, wide, wide), jnp.float32)] * 2
        shared = pl.pallas_call(
            shared_kernel,
            in_specs=[smem] + [vmem] * 3,
            out_shape=shape(near * rows, HDIM),
            scratch_shapes=scratch + scores,
            compiler_params=PARAMS,
            cost_estimate=pl.CostEstimate(flops=SHARED_COST, bytes_accessed=2**21, transcendentals=0),
            name="attend_shared",
        )(tile_mask, q_near, kv_near, kv_other)

        whole = pl.pallas_call(
            functools.partial(whole_kernel, far),
            in_specs=[smem, vmem, pl.BlockSpec(memory_space=pl.ANY)],
            out_shape=shape(far, rows, HDIM),
            scratch_shapes=scratch + scores,
            compiler_params=PARAMS,
            cost_estimate=pl.CostEstimate(flops=2**33, bytes_accessed=2**22, transcendentals=0),
            name="attend_whole",
        )(tile_mask, whole, shared)
        shared = exchange(shared.reshape(near, rows, HDIM), NEAR)
        whole = exchange(whole, FAR)
        result, hbm = (), pl.BlockSpec(memory_space=pltpu.HBM)
        for first, got in ((0, shared), (near, whole)):
            result = pl.pallas_call(
                functools.partial(read, first),
                in_specs=[vmem] + [hbm] * len(result),
                out_specs=hbm,
                out_shape=shape(rows, features),
                input_output_aliases={1: 0} if result else {},
                scratch_shapes=[pltpu.SemaphoreType.DMA((got.shape[0],))],
                compiler_params=PARAMS,
                name="unpack_whole" if result else "unpack_shared",
            )(got, *result)
            result = (result,)
        return result[0]

    return per_device


def gathered_kernel(outer, inner, mask_ref, q_ref, kv_ref, out_ref, scores_ref):
    i = pl.program_id(0)
    block = out_ref.shape[0] * out_ref.shape[1] * out_ref.shape[2]
    tiles = block // TILE
    q_tile = (i * inner + lax.axis_index("inner")) * tiles
    mixed = attend(
        q_ref[0, :, 0].reshape(block, HDIM),
        TILE,
        lambda c: kv_ref[lax.rem(c, inner), lax.div(c, inner), :, 1].reshape(block, HDIM),
        lambda c: kv_ref[lax.rem(c, inner), lax.div(c, inner), :, 2].reshape(block, HDIM),
        outer * inner,
        lambda a, t: mask_ref[q_tile + a, t] != 0,
        scores_ref,
    )
    out_ref[...] = mixed.reshape(out_ref.shape)


def gathered(outer, inner, n_head, near):
    width = HEADS // near * HDIM

    def per_device(query_rows, key_rows, value_rows, q_gain, k_gain, tile_mask):
        rows, features = query_rows.shape
        block = rows * n_head

        def write(which, block, outs, kept):
            packed, sems = kept
            for d in range(near):
                packed[d, which] = block[:, d * width : (d + 1) * width]
            copy = pltpu.make_async_copy(packed.at[:, which], outs[0].at[:, which], sems.at[which])
            copy.start()
            return [copy]

        def read(got_ref, out_ref):
            for d in range(near):
                out_ref[:, d * width : (d + 1) * width] = got_ref[d]

        (packed,) = pack(
            write,
            [shape(near, 3, rows, width)],
            rows,
            features,
            (query_rows, key_rows, value_rows, q_gain, k_gain),
            [pltpu.VMEM((near, 3, rows, width), BF16), pltpu.SemaphoreType.DMA((3,))],
        )
        own = exchange(packed, NEAR).reshape(outer, n_head, 3, rows, width)
        every = lax.all_gather(own, "inner")
        mixed = pl.pallas_call(
            functools.partial(gathered_kernel, outer, inner),
            grid=(outer, HEADS // near),
            in_specs=[
                pl.BlockSpec(memory_space=pltpu.SMEM),
                pl.BlockSpec((1, n_head, 1, rows, HDIM), lambda i, h: (i, 0, 0, 0, h)),
                pl.BlockSpec((inner, outer, n_head, 3, rows, HDIM), lambda i, h: (0, 0, 0, 0, 0, h)),
            ],
            out_specs=pl.BlockSpec((1, n_head, rows, HDIM), lambda i, h: (i, 0, 0, h)),
            out_shape=shape(outer, n_head, rows, width),
            scratch_shapes=[pltpu.VMEM((outer * inner, block, block), jnp.float32)],
            compiler_params=PARAMS,
            name="attend",
        )(tile_mask, own, every)
        return pl.pallas_call(
            read, out_shape=shape(rows, features), compiler_params=PARAMS, name="unpack"
        )(exchange(mixed.reshape(near, rows, width), NEAR))

    return per_device


def solution(mesh):
    n_blk, n_head = mesh.shape["blk"], mesh.shape["head"]
    outer = max(d for d in range(1, n_blk + 1) if n_blk % d == 0 and HEADS % (n_head * d) == 0)
    inner = n_blk // outer
    near, far = outer * n_head, n_blk * n_head

    def per_device(query_rows, *others):
        in_pairs = inner == 2 and n_head == 2 and mesh.shape["batch"] == 2 and near & (near - 1) == 0
        if in_pairs and HEADS == near + far and query_rows.shape[0] == TILE:
            return halved(far, near)(query_rows, *others)
        return gathered(outer, inner, n_head, near)(query_rows, *others)

    split = P(("batch", "outer", "inner", "head"), None)
    return jax.shard_map(
        per_device,
        mesh=Mesh(
            mesh.devices.reshape(outer, inner, n_head, mesh.shape["batch"]), ("outer", "inner", "head", "batch")
        ),
        in_specs=(split, split, split, P(), P(), P()),
        out_specs=split,
        check_vma=False,
    )
```

```python
import functools

import jax
import jax.numpy as jnp
from jax import lax
from jax.experimental import pallas as pl
from jax.experimental.pallas import tpu as pltpu
from jax.sharding import Mesh, PartitionSpec as P

HEADS = 24
HDIM = 128
TILE = 128
EPS = 1e-06
MASKED = -1e30
NEAR = ("outer", "head")
FAR = ("outer", "inner", "head")
PARAMS = pltpu.CompilerParams(vmem_limit_bytes=48 * 1024 * 1024)
PACK_PARAMS = pltpu.CompilerParams(vmem_limit_bytes=61 * 1024 * 1024)
BF16 = jnp.bfloat16
SHARED_COST = 24 * 2**30
SCALE = 1.4426950408889634 * HDIM ** (-0.5)


def shape(*dims):
    return jax.ShapeDtypeStruct(dims, BF16)


def exchange(x, axes):
    return lax.all_to_all(x, axes, split_axis=0, concat_axis=0, tiled=True)


def pack_kernel(write, inputs, outputs, scratch):
    q_hbm, k_hbm, v_hbm, qg_hbm, kg_hbm = inputs
    q_in, k_in, v_in, qg, kg, sems, *kept = scratch
    copies = [
        pltpu.make_async_copy(src, dst, sems.at[n])
        for n, (src, dst) in enumerate(
            ((v_hbm, v_in), (q_hbm, q_in), (qg_hbm, qg), (k_hbm, k_in), (kg_hbm, kg))
        )
    ]
    for copy in copies:
        copy.start()

    def normalize(first, ref, gain):
        copies[first].wait()
        copies[first + 1].wait()
        widened = ref[...].astype(jnp.float32)
        mean_square = jnp.mean(widened * widened, axis=-1, keepdims=True)
        return (widened * lax.rsqrt(mean_square + EPS) * gain[...]).astype(BF16)

    copies[0].wait()
    sent = write(2, v_in[...], outputs, kept)
    sent += write(0, normalize(1, q_in, qg), outputs, kept)
    sent += write(1, normalize(3, k_in, kg), outputs, kept)
    for copy in sent:
        copy.wait()


def pack(write, out_shape, rows, features, arrays, kept, name="pack", after=()):
    q, k, v, q_gain, k_gain = arrays
    hbm = pl.BlockSpec(memory_space=pltpu.HBM)

    def kernel(*refs):
        refs = refs[:5] + refs[5 + len(after) :]
        pack_kernel(write, refs[:5], refs[5 : 5 + len(out_shape)], refs[5 + len(out_shape) :])

    return pl.pallas_call(
        kernel,
        in_specs=[hbm] * 5 + [pl.BlockSpec(memory_space=pl.ANY)] * len(after),
        out_specs=[hbm] * len(out_shape),
        out_shape=out_shape,
        scratch_shapes=[pltpu.VMEM((rows, features), BF16)] * 3
        + [pltpu.VMEM((1, features), jnp.float32)] * 2
        + [pltpu.SemaphoreType.DMA((5,)), *kept],
        compiler_params=PACK_PARAMS,
        name=name,
    )(q, k, v, q_gain.reshape(1, -1), k_gain.reshape(1, -1), *after)


def first_pass(query, key, bias_at, scores_ref, c, largest):
    s = lax.dot_general(key, query, (((1,), (1,)), ((), ())), preferred_element_type=jnp.float32)
    for t in range(key.shape[0] // TILE):
        down = slice(t * TILE, (t + 1) * TILE)
        masked = s[down].reshape(TILE // 8, 8, -1) + bias_at(t)[None]
        scores_ref[c, down] = masked.reshape(TILE, -1)
        largest = jnp.maximum(largest, jnp.max(masked, axis=0))
    return largest


def second_pass(scores_ref, c, col_max, value_t, state):
    total, mixed = state
    wide, bm = scores_ref.shape[1:]
    weights = jnp.exp2(scores_ref[c].reshape(wide // 8, 8, bm) * SCALE - col_max[None])
    total = total + jnp.sum(weights, axis=0)
    weights = weights.reshape(wide, bm).astype(BF16)
    return total, mixed + jnp.dot(value_t, weights, preferred_element_type=jnp.float32)


def over_all(largest):
    return jnp.broadcast_to(jnp.max(largest, axis=0, keepdims=True) * SCALE, largest.shape)


def divide(total, mixed):
    return (mixed / jnp.sum(total, axis=0, keepdims=True)).T.astype(BF16)


def bias_of(band, bm, live_at):
    lane = lax.broadcasted_iota(jnp.int32, (8, bm), 1)
    bias = jnp.zeros((8, bm), jnp.float32)
    for a in range(bm // band):
        dead = jnp.where(live_at(a), 0.0, MASKED).astype(jnp.float32)
        bias = jnp.where((lane >= a * band) & (lane < (a + 1) * band), dead, bias)
    return bias


def attend(query, band, key_at, value_at, key_blocks, live_at, scores_ref):
    wide, bm = scores_ref.shape[1:]

    def score(c, largest):
        def bias_at(t):
            return bias_of(band, bm, lambda a: live_at(a, c * (wide // TILE) + t))

        return first_pass(query, key_at(c), bias_at, scores_ref, c, largest)

    largest = lax.fori_loop(0, key_blocks, score, jnp.full((8, bm), MASKED, jnp.float32))
    col_max = over_all(largest)

    def mix(c, state):
        return second_pass(scores_ref, c, col_max, transposed(value_at(c)), state)

    state = jnp.zeros((8, bm), jnp.float32), jnp.zeros((HDIM, bm), jnp.float32)
    return divide(*lax.fori_loop(0, key_blocks, mix, state))


def transposed(block):
    return block.astype(jnp.float32).T.astype(BF16)


def attend_blocks(blocks, band, query_at, key_at, value_t, key_blocks, live_at, finish, scores):
    wide, bm = scores[0].shape[1:]
    empty = jnp.full((8, bm), MASKED, jnp.float32)
    nothing = jnp.zeros((8, bm), jnp.float32), jnp.zeros((HDIM, bm), jnp.float32)

    def bias_at(i, c):
        return lambda t: bias_of(band, bm, lambda a: live_at(i, a, c, t))

    def both(i, col_max, now, following):
        later = jnp.minimum(i + 1, blocks - 1)
        query = query_at(later)
        largest, state = empty, nothing
        for c in range(key_blocks):
            largest = first_pass(query, key_at(c), bias_at(later, c), following, c, largest)
            state = second_pass(now, c, col_max, value_t[:, c * wide : (c + 1) * wide], state)
        finish(i, divide(*state))
        return over_all(largest)

    largest = empty
    query = query_at(0)
    for c in range(key_blocks):
        largest = first_pass(query, key_at(c), bias_at(0, c), scores[0], c, largest)

    def pair(n, col_max):
        col_max = both(2 * n, col_max, scores[0], scores[1])
        return both(2 * n + 1, col_max, scores[1], scores[0])

    lax.fori_loop(0, blocks // 2, pair, over_all(largest))


def partner(me, step):
    first, second = step
    return me ^ jnp.where(lax.axis_index("batch") == 0, first, second)


def collect_kernel(steps, rows, *refs):
    pieces, (q_out, kv_out) = refs[:-2], refs[-2:]
    me = lax.axis_index(NEAR)
    for step, piece in zip(steps, pieces):
        at = pl.ds(pl.multiple_of(partner(me, step) * rows, rows), rows)
        q_out[at] = piece[0]
        kv_out[:, at] = piece[1:]


def shared_kernel(mask_ref, q_ref, own_ref, other_ref, out_ref, value_t, *scores):
    mine = lax.axis_index("inner")
    _, wide, bm = scores[0].shape
    blocks = q_ref.shape[0] // wide

    def key_at(c):
        ref = own_ref if c < blocks else other_ref
        return ref[0, c % blocks * wide : (c % blocks + 1) * wide]

    for n, ref in enumerate((own_ref, other_ref)):
        for t in range(blocks * wide // TILE):
            at = (n * blocks * wide) + t * TILE
            value_t[:, at : at + TILE] = transposed(ref[1, t * TILE : (t + 1) * TILE])

    def tile(block, inner, t):
        return (block * 2 + inner) * (wide // TILE) + t

    def finish(i, mixed):
        out_ref[pl.ds(pl.multiple_of(i * bm, bm), bm)] = mixed

    attend_blocks(
        blocks,
        TILE,
        lambda i: q_ref[pl.ds(pl.multiple_of(i * bm, bm), bm)],
        key_at,
        value_t,
        2 * blocks,
        lambda i, a, c, t: mask_ref[tile(i, mine, a), tile(c % blocks, mine if c < blocks else 1 - mine, t)] != 0,
        finish,
        scores,
    )


def whole_kernel(sources, mask_ref, qkv_ref, *refs):
    out_ref, value_t, *scores = refs[-4:]
    rows = qkv_ref.shape[2]
    _, wide, bm = scores[0].shape
    bands, tiles = bm // rows, wide // TILE
    for t in range(sources):
        value_t[:, t * TILE : (t + 1) * TILE] = transposed(qkv_ref[t, 2])

    def finish(i, mixed):
        out_ref[pl.ds(i * bands, bands)] = mixed.reshape(bands, rows, HDIM)

    attend_blocks(
        sources // bands,
        rows,
        lambda i: qkv_ref[pl.ds(i * bands, bands), 0].reshape(bm, HDIM),
        lambda c: qkv_ref[c * tiles : (c + 1) * tiles, 1].reshape(wide, HDIM),
        value_t,
        sources // tiles,
        lambda i, a, c, t: mask_ref[i * bands + a, c * tiles + t] != 0,
        finish,
        scores,
    )


def halved(far, near):
    steps = []
    for d in range(near // 2):
        steps += [(near // 2 + d, d), (d, near // 2 + d)]

    def swap(piece, step):
        pairs = [(2 * i + b, 2 * (i ^ step[b]) + b) for i in range(near) for b in range(2)]
        return lax.ppermute(piece, (*NEAR, "batch"), pairs)

    def per_device(query_rows, key_rows, value_rows, q_gain, k_gain, tile_mask):
        rows, features = query_rows.shape

        def write_shared(which, block, outs, kept):
            by_head, sems = kept
            for h in range(near):
                by_head[h, which] = block[:, h * HDIM : (h + 1) * HDIM]
            me = lax.axis_index(NEAR)
            copies = [
                pltpu.make_async_copy(by_head.at[partner(me, step), which], outs[n].at[which], sems.at[which, n])
                for n, step in enumerate(steps)
            ]
            for copy in copies:
                copy.start()
            return copies

        def write_whole(which, block, outs, kept):
            by_head, sems = kept
            for h in range(far):
                by_head[h, which] = block[:, (near + h) * HDIM : (near + h + 1) * HDIM]
            copy = pltpu.make_async_copy(by_head.at[:, which], outs[0].at[:, which], sems.at[which])
            copy.start()
            return [copy]

        def read(first, got_ref, *refs):
            out_ref, sems = refs[-2:]
            copies = [
                pltpu.make_async_copy(got_ref.at[d], out_ref.at[:, pl.ds((first + d) * HDIM, HDIM)], sems.at[d])
                for d in range(got_ref.shape[0])
            ]
            for copy in copies:
                copy.start()
            for copy in copies:
                copy.wait()

        arrays = query_rows, key_rows, value_rows, q_gain, k_gain
        shared = pack(
            write_shared,
            [shape(3, rows, HDIM)] * near,
            rows,
            features,
            arrays,
            [pltpu.VMEM((near, 3, rows, HDIM), BF16), pltpu.SemaphoreType.DMA((3, near))],
            "pack_shared",
        )
        shared = [swap(piece, step) for step, piece in zip(steps, shared)]
        (whole,) = pack(
            write_whole,
            [shape(far, 3, rows, HDIM)],
            rows,
            features,
            arrays,
            [pltpu.VMEM((far, 3, rows, HDIM), BF16), pltpu.SemaphoreType.DMA((3,))],
            "pack_whole",
            shared[:1],
        )
        whole = exchange(whole, FAR)
        q_near, kv_near = pl.pallas_call(
            functools.partial(collect_kernel, steps, rows),
            out_shape=[shape(near * rows, HDIM), shape(2, near * rows, HDIM)],
            compiler_params=PARAMS,
            name="collect",
        )(*shared)
        kv_other = lax.ppermute(kv_near, "inner", [(0, 1), (1, 0)])

        wide = 2 * TILE
        blocks = far * rows // wide
        smem, vmem = pl.BlockSpec(memory_space=pltpu.SMEM), pl.BlockSpec(memory_space=pltpu.VMEM)
        scratch = [pltpu.VMEM((HDIM, far * rows), BF16)]
        scores = [pltpu.VMEM((blocks, wide, wide), jnp.float32)] * 2
        shared = pl.pallas_call(
            shared_kernel,
            in_specs=[smem] + [vmem] * 3,
            out_shape=shape(near * rows, HDIM),
            scratch_shapes=scratch + scores,
            compiler_params=PARAMS,
            cost_estimate=pl.CostEstimate(flops=SHARED_COST, bytes_accessed=2**21, transcendentals=0),
            name="attend_shared",
        )(tile_mask, q_near, kv_near, kv_other)

        whole = pl.pallas_call(
            functools.partial(whole_kernel, far),
            in_specs=[smem, vmem, pl.BlockSpec(memory_space=pl.ANY)],
            out_shape=shape(far, rows, HDIM),
            scratch_shapes=scratch + scores,
            compiler_params=PARAMS,
            cost_estimate=pl.CostEstimate(flops=2**33, bytes_accessed=2**22, transcendentals=0),
            name="attend_whole",
        )(tile_mask, whole, shared)
        shared = exchange(shared.reshape(near, rows, HDIM), NEAR)
        whole = exchange(whole, FAR)
        result, hbm = (), pl.BlockSpec(memory_space=pltpu.HBM)
        for first, got in ((0, shared), (near, whole)):
            result = pl.pallas_call(
                functools.partial(read, first),
                in_specs=[vmem] + [hbm] * len(result),
                out_specs=hbm,
                out_shape=shape(rows, features),
                input_output_aliases={1: 0} if result else {},
                scratch_shapes=[pltpu.SemaphoreType.DMA((got.shape[0],))],
                compiler_params=PARAMS,
                name="unpack_whole" if result else "unpack_shared",
            )(got, *result)
            result = (result,)
        return result[0]

    return per_device


def gathered_kernel(outer, inner, mask_ref, q_ref, kv_ref, out_ref, scores_ref):
    i = pl.program_id(0)
    block = out_ref.shape[0] * out_ref.shape[1] * out_ref.shape[2]
    tiles = block // TILE
    q_tile = (i * inner + lax.axis_index("inner")) * tiles
    mixed = attend(
        q_ref[0, :, 0].reshape(block, HDIM),
        TILE,
        lambda c: kv_ref[lax.rem(c, inner), lax.div(c, inner), :, 1].reshape(block, HDIM),
        lambda c: kv_ref[lax.rem(c, inner), lax.div(c, inner), :, 2].reshape(block, HDIM),
        outer * inner,
        lambda a, t: mask_ref[q_tile + a, t] != 0,
        scores_ref,
    )
    out_ref[...] = mixed.reshape(out_ref.shape)


def gathered(outer, inner, n_head, near):
    width = HEADS // near * HDIM

    def per_device(query_rows, key_rows, value_rows, q_gain, k_gain, tile_mask):
        rows, features = query_rows.shape
        block = rows * n_head

        def write(which, block, outs, kept):
            packed, sems = kept
            for d in range(near):
                packed[d, which] = block[:, d * width : (d + 1) * width]
            copy = pltpu.make_async_copy(packed.at[:, which], outs[0].at[:, which], sems.at[which])
            copy.start()
            return [copy]

        def read(got_ref, out_ref):
            for d in range(near):
                out_ref[:, d * width : (d + 1) * width] = got_ref[d]

        (packed,) = pack(
            write,
            [shape(near, 3, rows, width)],
            rows,
            features,
            (query_rows, key_rows, value_rows, q_gain, k_gain),
            [pltpu.VMEM((near, 3, rows, width), BF16), pltpu.SemaphoreType.DMA((3,))],
        )
        own = exchange(packed, NEAR).reshape(outer, n_head, 3, rows, width)
        every = lax.all_gather(own, "inner")
        mixed = pl.pallas_call(
            functools.partial(gathered_kernel, outer, inner),
            grid=(outer, HEADS // near),
            in_specs=[
                pl.BlockSpec(memory_space=pltpu.SMEM),
                pl.BlockSpec((1, n_head, 1, rows, HDIM), lambda i, h: (i, 0, 0, 0, h)),
                pl.BlockSpec((inner, outer, n_head, 3, rows, HDIM), lambda i, h: (0, 0, 0, 0, 0, h)),
            ],
            out_specs=pl.BlockSpec((1, n_head, rows, HDIM), lambda i, h: (i, 0, 0, h)),
            out_shape=shape(outer, n_head, rows, width),
            scratch_shapes=[pltpu.VMEM((outer * inner, block, block), jnp.float32)],
            compiler_params=PARAMS,
            name="attend",
        )(tile_mask, own, every)
        return pl.pallas_call(
            read, out_shape=shape(rows, features), compiler_params=PARAMS, name="unpack"
        )(exchange(mixed.reshape(near, rows, width), NEAR))

    return per_device


def solution(mesh):
    n_blk, n_head = mesh.shape["blk"], mesh.shape["head"]
    outer = max(d for d in range(1, n_blk + 1) if n_blk % d == 0 and HEADS % (n_head * d) == 0)
    inner = n_blk // outer
    near, far = outer * n_head, n_blk * n_head

    def per_device(query_rows, *others):
        in_pairs = inner == 2 and n_head == 2 and mesh.shape["batch"] == 2 and near & (near - 1) == 0
        if in_pairs and HEADS == near + far and query_rows.shape[0] == TILE:
            return halved(far, near)(query_rows, *others)
        return gathered(outer, inner, n_head, near)(query_rows, *others)

    split = P(("batch", "outer", "inner", "head"), None)
    return jax.shard_map(
        per_device,
        mesh=Mesh(
            mesh.devices.reshape(outer, inner, n_head, mesh.shape["batch"]), ("outer", "inner", "head", "batch")
        ),
        in_specs=(split, split, split, P(), P(), P()),
        out_specs=split,
        check_vma=False,
    )
```

```python
import functools

import jax
import jax.numpy as jnp
from jax import lax
from jax.experimental import pallas as pl
from jax.experimental.pallas import tpu as pltpu
from jax.sharding import Mesh, PartitionSpec as P

HEADS = 24
HDIM = 128
TILE = 128
EPS = 1e-06
MASKED = -1e30
NEAR = ("outer", "head")
FAR = ("outer", "inner", "head")
PARAMS = pltpu.CompilerParams(vmem_limit_bytes=20 * 1024 * 1024)
GATHERED_PARAMS = pltpu.CompilerParams(vmem_limit_bytes=48 * 1024 * 1024)
PACK_PARAMS = pltpu.CompilerParams(vmem_limit_bytes=61 * 1024 * 1024)
BF16 = jnp.bfloat16
SHARED_COST = 23 * 2**30
SCALE = 1.4426950408889634 * HDIM ** (-0.5)


def shape(*dims):
    return jax.ShapeDtypeStruct(dims, BF16)


def exchange(x, axes):
    return lax.all_to_all(x, axes, split_axis=0, concat_axis=0, tiled=True)


def pack_kernel(write, inputs, outputs, scratch):
    q_hbm, k_hbm, v_hbm, qg_hbm, kg_hbm = inputs
    q_in, k_in, v_in, qg, kg, sems, *kept = scratch
    copies = [
        pltpu.make_async_copy(src, dst, sems.at[n])
        for n, (src, dst) in enumerate(
            ((v_hbm, v_in), (q_hbm, q_in), (qg_hbm, qg), (k_hbm, k_in), (kg_hbm, kg))
        )
    ]
    for copy in copies:
        copy.start()

    def normalize(first, ref, gain):
        copies[first].wait()
        copies[first + 1].wait()
        widened = ref[...].astype(jnp.float32)
        mean_square = jnp.mean(widened * widened, axis=-1, keepdims=True)
        return (widened * lax.rsqrt(mean_square + EPS) * gain[...]).astype(BF16)

    copies[0].wait()
    sent = write(2, v_in[...], outputs, kept)
    sent += write(0, normalize(1, q_in, qg), outputs, kept)
    sent += write(1, normalize(3, k_in, kg), outputs, kept)
    for copy in sent:
        copy.wait()


def pack(write, out_shape, rows, features, arrays, kept=()):
    q, k, v, q_gain, k_gain = arrays
    hbm = pl.BlockSpec(memory_space=pltpu.HBM)

    def kernel(*refs):
        pack_kernel(write, refs[:5], refs[5 : 5 + len(out_shape)], refs[5 + len(out_shape) :])

    return pl.pallas_call(
        kernel,
        in_specs=[hbm] * 5,
        out_specs=[hbm] * len(out_shape),
        out_shape=out_shape,
        scratch_shapes=[pltpu.VMEM((rows, features), BF16)] * 3
        + [pltpu.VMEM((1, features), jnp.float32)] * 2
        + [pltpu.SemaphoreType.DMA((5,)), *kept],
        compiler_params=PACK_PARAMS,
        name="pack",
    )(q, k, v, q_gain.reshape(1, -1), k_gain.reshape(1, -1))


def first_pass(query, key, bias_at, scores_ref, c, largest):
    s = lax.dot_general(key, query, (((1,), (1,)), ((), ())), preferred_element_type=jnp.float32)
    for t in range(key.shape[0] // TILE):
        down = slice(t * TILE, (t + 1) * TILE)
        masked = s[down].reshape(TILE // 8, 8, -1) + bias_at(t)[None]
        scores_ref[c, down] = masked.reshape(TILE, -1)
        largest = jnp.maximum(largest, jnp.max(masked, axis=0))
    return largest


def second_pass(scores_ref, c, col_max, value_t, state):
    total, mixed = state
    wide, bm = scores_ref.shape[1:]
    weights = jnp.exp2(scores_ref[c].reshape(wide // 8, 8, bm) * SCALE - col_max[None])
    total = total + jnp.sum(weights, axis=0)
    weights = weights.reshape(wide, bm).astype(BF16)
    return total, mixed + jnp.dot(value_t, weights, preferred_element_type=jnp.float32)


def over_all(largest):
    return jnp.broadcast_to(jnp.max(largest, axis=0, keepdims=True) * SCALE, largest.shape)


def divide(total, mixed):
    return (mixed / jnp.sum(total, axis=0, keepdims=True)).T.astype(BF16)


def bias_of(band, bm, live_at):
    lane = lax.broadcasted_iota(jnp.int32, (8, bm), 1)
    bias = jnp.zeros((8, bm), jnp.float32)
    for a in range(bm // band):
        dead = jnp.where(live_at(a), 0.0, MASKED).astype(jnp.float32)
        bias = jnp.where((lane >= a * band) & (lane < (a + 1) * band), dead, bias)
    return bias


def attend(query, band, key_at, value_at, key_blocks, live_at, scores_ref):
    wide, bm = scores_ref.shape[1:]

    def score(c, largest):
        def bias_at(t):
            return bias_of(band, bm, lambda a: live_at(a, c * (wide // TILE) + t))

        return first_pass(query, key_at(c), bias_at, scores_ref, c, largest)

    largest = lax.fori_loop(0, key_blocks, score, jnp.full((8, bm), MASKED, jnp.float32))
    col_max = over_all(largest)

    def mix(c, state):
        return second_pass(scores_ref, c, col_max, transposed(value_at(c)), state)

    state = jnp.zeros((8, bm), jnp.float32), jnp.zeros((HDIM, bm), jnp.float32)
    return divide(*lax.fori_loop(0, key_blocks, mix, state))


def transposed(block):
    return block.astype(jnp.float32).T.astype(BF16)


def attend_blocks(blocks, band, query_at, key_at, value_t, key_blocks, live_at, finish, scores):
    wide, bm = scores[0].shape[1:]
    empty = jnp.full((8, bm), MASKED, jnp.float32)
    nothing = jnp.zeros((8, bm), jnp.float32), jnp.zeros((HDIM, bm), jnp.float32)

    def bias_at(i, c):
        return lambda t: bias_of(band, bm, lambda a: live_at(i, a, c, t))

    def both(i, col_max, now, following):
        later = jnp.minimum(i + 1, blocks - 1)
        query = query_at(later)
        largest, state = empty, nothing
        for c in range(key_blocks):
            largest = first_pass(query, key_at(c), bias_at(later, c), following, c, largest)
            state = second_pass(now, c, col_max, value_t[:, c * wide : (c + 1) * wide], state)
        finish(i, divide(*state))
        return over_all(largest)

    largest = empty
    query = query_at(0)
    for c in range(key_blocks):
        largest = first_pass(query, key_at(c), bias_at(0, c), scores[0], c, largest)

    def pair(n, col_max):
        col_max = both(2 * n, col_max, scores[0], scores[1])
        return both(2 * n + 1, col_max, scores[1], scores[0])

    lax.fori_loop(0, blocks // 2, pair, over_all(largest))


def partner(me, step):
    first, second = step
    return me ^ jnp.where(lax.axis_index("batch") == 0, first, second)


def collect_kernel(steps, rows, *refs):
    pieces, (q_out, kv_out) = refs[:-2], refs[-2:]
    me = lax.axis_index(NEAR)
    for step, piece in zip(steps, pieces):
        at = pl.ds(pl.multiple_of(partner(me, step) * rows, rows), rows)
        q_out[at] = piece[0]
        kv_out[:, at] = piece[1:]


def shared_kernel(mask_ref, q_ref, own_ref, other_ref, out_ref, value_t, *scores):
    mine = lax.axis_index("inner")
    _, wide, bm = scores[0].shape
    blocks = q_ref.shape[0] // wide

    def key_at(c):
        ref = own_ref if c < blocks else other_ref
        return ref[0, c % blocks * wide : (c % blocks + 1) * wide]

    for n, ref in enumerate((own_ref, other_ref)):
        for t in range(blocks * wide // TILE):
            at = (n * blocks * wide) + t * TILE
            value_t[:, at : at + TILE] = transposed(ref[1, t * TILE : (t + 1) * TILE])

    def tile(block, inner, t):
        return (block * 2 + inner) * (wide // TILE) + t

    def finish(i, mixed):
        out_ref[pl.ds(pl.multiple_of(i * bm, bm), bm)] = mixed

    attend_blocks(
        blocks,
        TILE,
        lambda i: q_ref[pl.ds(pl.multiple_of(i * bm, bm), bm)],
        key_at,
        value_t,
        2 * blocks,
        lambda i, a, c, t: mask_ref[tile(i, mine, a), tile(c % blocks, mine if c < blocks else 1 - mine, t)] != 0,
        finish,
        scores,
    )


def whole_kernel(sources, mask_ref, qkv_ref, *refs):
    out_ref, value_t, *scores = refs[-4:]
    rows = qkv_ref.shape[2]
    _, wide, bm = scores[0].shape
    bands, tiles = bm // rows, wide // TILE
    for t in range(sources):
        value_t[:, t * TILE : (t + 1) * TILE] = transposed(qkv_ref[t, 2])

    def finish(i, mixed):
        out_ref[pl.ds(i * bands, bands)] = mixed.reshape(bands, rows, HDIM)

    attend_blocks(
        sources // bands,
        rows,
        lambda i: qkv_ref[pl.ds(i * bands, bands), 0].reshape(bm, HDIM),
        lambda c: qkv_ref[c * tiles : (c + 1) * tiles, 1].reshape(wide, HDIM),
        value_t,
        sources // tiles,
        lambda i, a, c, t: mask_ref[i * bands + a, c * tiles + t] != 0,
        finish,
        scores,
    )


def halved(far, near):
    steps = []
    for d in range(near // 2):
        steps += [(near // 2 + d, d), (d, near // 2 + d)]

    def swap(piece, step):
        pairs = [(2 * i + b, 2 * (i ^ step[b]) + b) for i in range(near) for b in range(2)]
        return lax.ppermute(piece, (*NEAR, "batch"), pairs)

    def per_device(query_rows, key_rows, value_rows, q_gain, k_gain, tile_mask):
        rows, features = query_rows.shape

        def write(which, block, outs, kept):
            near_heads, far_heads, near_sems, far_sems = kept
            for h in range(near):
                near_heads[h, which] = block[:, h * HDIM : (h + 1) * HDIM]
            for h in range(far):
                far_heads[h, which] = block[:, (near + h) * HDIM : (near + h + 1) * HDIM]
            me = lax.axis_index(NEAR)
            copies = [
                pltpu.make_async_copy(near_heads.at[partner(me, step), which], outs[n].at[which], near_sems.at[which, n])
                for n, step in enumerate(steps)
            ]
            copies.append(pltpu.make_async_copy(far_heads.at[:, which], outs[-1].at[:, which], far_sems.at[which]))
            for copy in copies:
                copy.start()
            return copies

        def read(shared, whole, out_ref):
            for d in range(near):
                out_ref[:, d * HDIM : (d + 1) * HDIM] = shared[d]
            for d in range(far):
                out_ref[:, (near + d) * HDIM : (near + d + 1) * HDIM] = whole[d]

        *shared, whole = pack(
            write,
            [shape(3, rows, HDIM)] * near + [shape(far, 3, rows, HDIM)],
            rows,
            features,
            (query_rows, key_rows, value_rows, q_gain, k_gain),
            [
                pltpu.VMEM((near, 3, rows, HDIM), BF16),
                pltpu.VMEM((far, 3, rows, HDIM), BF16),
                pltpu.SemaphoreType.DMA((3, near)),
                pltpu.SemaphoreType.DMA((3,)),
            ],
        )
        shared = [swap(piece, step) for step, piece in zip(steps, shared)]
        whole = exchange(whole, FAR)
        q_near, kv_near = pl.pallas_call(
            functools.partial(collect_kernel, steps, rows),
            out_shape=[shape(near * rows, HDIM), shape(2, near * rows, HDIM)],
            compiler_params=PARAMS,
            name="collect",
        )(*shared)
        kv_other = lax.ppermute(kv_near, "inner", [(0, 1), (1, 0)])

        wide = 2 * TILE
        blocks = far * rows // wide
        smem, vmem = pl.BlockSpec(memory_space=pltpu.SMEM), pl.BlockSpec(memory_space=pltpu.VMEM)
        scratch = [pltpu.VMEM((HDIM, far * rows), BF16)]
        scores = [pltpu.VMEM((blocks, wide, wide), jnp.float32)] * 2
        shared = pl.pallas_call(
            shared_kernel,
            in_specs=[smem] + [vmem] * 3,
            out_shape=shape(near * rows, HDIM),
            scratch_shapes=scratch + scores,
            compiler_params=PARAMS,
            cost_estimate=pl.CostEstimate(flops=SHARED_COST, bytes_accessed=2**21, transcendentals=0),
            name="attend_shared",
        )(tile_mask, q_near, kv_near, kv_other)

        whole = pl.pallas_call(
            functools.partial(whole_kernel, far),
            in_specs=[smem, vmem, pl.BlockSpec(memory_space=pl.ANY)],
            out_shape=shape(far, rows, HDIM),
            scratch_shapes=scratch + scores,
            compiler_params=PARAMS,
            cost_estimate=pl.CostEstimate(flops=2**33, bytes_accessed=2**22, transcendentals=0),
            name="attend_whole",
        )(tile_mask, whole, shared)
        shared = exchange(shared.reshape(near, rows, HDIM), NEAR)
        return pl.pallas_call(
            read, out_shape=shape(rows, features), compiler_params=PARAMS, name="unpack"
        )(shared, exchange(whole, FAR))

    return per_device


def gathered_kernel(outer, inner, mask_ref, q_ref, kv_ref, out_ref, scores_ref):
    i = pl.program_id(0)
    block = out_ref.shape[0] * out_ref.shape[1] * out_ref.shape[2]
    tiles = block // TILE
    q_tile = (i * inner + lax.axis_index("inner")) * tiles
    mixed = attend(
        q_ref[0, :, 0].reshape(block, HDIM),
        TILE,
        lambda c: kv_ref[lax.rem(c, inner), lax.div(c, inner), :, 1].reshape(block, HDIM),
        lambda c: kv_ref[lax.rem(c, inner), lax.div(c, inner), :, 2].reshape(block, HDIM),
        outer * inner,
        lambda a, t: mask_ref[q_tile + a, t] != 0,
        scores_ref,
    )
    out_ref[...] = mixed.reshape(out_ref.shape)


def gathered(outer, inner, n_head, near):
    width = HEADS // near * HDIM

    def per_device(query_rows, key_rows, value_rows, q_gain, k_gain, tile_mask):
        rows, features = query_rows.shape
        block = rows * n_head

        def write(which, block, outs, kept):
            packed, sems = kept
            for d in range(near):
                packed[d, which] = block[:, d * width : (d + 1) * width]
            copy = pltpu.make_async_copy(packed.at[:, which], outs[0].at[:, which], sems.at[which])
            copy.start()
            return [copy]

        def read(got_ref, out_ref):
            for d in range(near):
                out_ref[:, d * width : (d + 1) * width] = got_ref[d]

        (packed,) = pack(
            write,
            [shape(near, 3, rows, width)],
            rows,
            features,
            (query_rows, key_rows, value_rows, q_gain, k_gain),
            [pltpu.VMEM((near, 3, rows, width), BF16), pltpu.SemaphoreType.DMA((3,))],
        )
        own = exchange(packed, NEAR).reshape(outer, n_head, 3, rows, width)
        every = lax.all_gather(own, "inner")
        mixed = pl.pallas_call(
            functools.partial(gathered_kernel, outer, inner),
            grid=(outer, HEADS // near),
            in_specs=[
                pl.BlockSpec(memory_space=pltpu.SMEM),
                pl.BlockSpec((1, n_head, 1, rows, HDIM), lambda i, h: (i, 0, 0, 0, h)),
                pl.BlockSpec((inner, outer, n_head, 3, rows, HDIM), lambda i, h: (0, 0, 0, 0, 0, h)),
            ],
            out_specs=pl.BlockSpec((1, n_head, rows, HDIM), lambda i, h: (i, 0, 0, h)),
            out_shape=shape(outer, n_head, rows, width),
            scratch_shapes=[pltpu.VMEM((outer * inner, block, block), jnp.float32)],
            compiler_params=GATHERED_PARAMS,
            name="attend",
        )(tile_mask, own, every)
        return pl.pallas_call(
            read, out_shape=shape(rows, features), compiler_params=GATHERED_PARAMS, name="unpack"
        )(exchange(mixed.reshape(near, rows, width), NEAR))

    return per_device


def solution(mesh):
    n_blk, n_head = mesh.shape["blk"], mesh.shape["head"]
    outer = max(d for d in range(1, n_blk + 1) if n_blk % d == 0 and HEADS % (n_head * d) == 0)
    inner = n_blk // outer
    near, far = outer * n_head, n_blk * n_head

    def per_device(query_rows, *others):
        in_pairs = inner == 2 and n_head == 2 and mesh.shape["batch"] == 2 and near & (near - 1) == 0
        if in_pairs and HEADS == near + far and query_rows.shape[0] == TILE:
            return halved(far, near)(query_rows, *others)
        return gathered(outer, inner, n_head, near)(query_rows, *others)

    split = P(("batch", "outer", "inner", "head"), None)
    return jax.shard_map(
        per_device,
        mesh=Mesh(
            mesh.devices.reshape(outer, inner, n_head, mesh.shape["batch"]), ("outer", "inner", "head", "batch")
        ),
        in_specs=(split, split, split, P(), P(), P()),
        out_specs=split,
        check_vma=False,
    )
```

```python
import functools

import jax
import jax.numpy as jnp
from jax import lax
from jax.experimental import pallas as pl
from jax.experimental.pallas import tpu as pltpu
from jax.sharding import Mesh, PartitionSpec as P

HEADS = 24
HDIM = 128
TILE = 128
EPS = 1e-06
MASKED = -1e30
NEAR = ("outer", "head")
FAR = ("outer", "inner", "head")
PARAMS = pltpu.CompilerParams(vmem_limit_bytes=48 * 1024 * 1024)
PACK_PARAMS = pltpu.CompilerParams(vmem_limit_bytes=61 * 1024 * 1024)
BF16 = jnp.bfloat16
SHARED_COST = 24 * 2**30
SCALE = 1.4426950408889634 * HDIM ** (-0.5)


def shape(*dims):
    return jax.ShapeDtypeStruct(dims, BF16)


def exchange(x, axes):
    return lax.all_to_all(x, axes, split_axis=0, concat_axis=0, tiled=True)


def pack_kernel(write, inputs, outputs, scratch):
    q_hbm, k_hbm, v_hbm, qg_hbm, kg_hbm = inputs
    q_in, k_in, v_in, qg, kg, sems, *kept = scratch
    copies = [
        pltpu.make_async_copy(src, dst, sems.at[n])
        for n, (src, dst) in enumerate(
            ((v_hbm, v_in), (q_hbm, q_in), (qg_hbm, qg), (k_hbm, k_in), (kg_hbm, kg))
        )
    ]
    for copy in copies:
        copy.start()

    def normalize(first, ref, gain):
        copies[first].wait()
        copies[first + 1].wait()
        widened = ref[...].astype(jnp.float32)
        mean_square = jnp.mean(widened * widened, axis=-1, keepdims=True)
        return (widened * lax.rsqrt(mean_square + EPS) * gain[...]).astype(BF16)

    copies[0].wait()
    sent = write(2, v_in[...], outputs, kept)
    sent += write(0, normalize(1, q_in, qg), outputs, kept)
    sent += write(1, normalize(3, k_in, kg), outputs, kept)
    for copy in sent:
        copy.wait()


def pack(write, out_shape, rows, features, arrays, kept=()):
    q, k, v, q_gain, k_gain = arrays
    hbm = pl.BlockSpec(memory_space=pltpu.HBM)

    def kernel(*refs):
        pack_kernel(write, refs[:5], refs[5 : 5 + len(out_shape)], refs[5 + len(out_shape) :])

    return pl.pallas_call(
        kernel,
        in_specs=[hbm] * 5,
        out_specs=[hbm] * len(out_shape),
        out_shape=out_shape,
        scratch_shapes=[pltpu.VMEM((rows, features), BF16)] * 3
        + [pltpu.VMEM((1, features), jnp.float32)] * 2
        + [pltpu.SemaphoreType.DMA((5,)), *kept],
        compiler_params=PACK_PARAMS,
        name="pack",
    )(q, k, v, q_gain.reshape(1, -1), k_gain.reshape(1, -1))


def first_pass(query, key, bias_at, scores_ref, c, largest):
    s = lax.dot_general(key, query, (((1,), (1,)), ((), ())), preferred_element_type=jnp.float32)
    scores_ref[c] = s
    for t in range(key.shape[0] // TILE):
        tile = s[t * TILE : (t + 1) * TILE].reshape(TILE // 8, 8, -1)
        largest = jnp.maximum(largest, jnp.max(tile, axis=0) + bias_at(t))
    return largest


def second_pass(scores_ref, c, col_max, bias_at, value_t, state):
    total, mixed = state
    wide, bm = scores_ref.shape[1:]
    weights = []
    for t in range(wide // TILE):
        tile = scores_ref[c, t * TILE : (t + 1) * TILE].reshape(TILE // 8, 8, bm)
        tile = jnp.exp2(tile * SCALE - (col_max - bias_at(t))[None])
        total = total + jnp.sum(tile, axis=0)
        weights.append(tile.reshape(TILE, bm).astype(BF16))
    weights = jnp.concatenate(weights, axis=0)
    return total, mixed + jnp.dot(value_t, weights, preferred_element_type=jnp.float32)


def over_all(largest):
    return jnp.broadcast_to(jnp.max(largest, axis=0, keepdims=True) * SCALE, largest.shape)


def divide(total, mixed):
    return (mixed / jnp.sum(total, axis=0, keepdims=True)).T.astype(BF16)


def bias_of(band, bm, live_at):
    lane = lax.broadcasted_iota(jnp.int32, (8, bm), 1)
    bias = jnp.zeros((8, bm), jnp.float32)
    for a in range(bm // band):
        dead = jnp.where(live_at(a), 0.0, MASKED).astype(jnp.float32)
        bias = jnp.where((lane >= a * band) & (lane < (a + 1) * band), dead, bias)
    return bias


def attend(query, band, key_at, value_at, key_blocks, live_at, scores_ref):
    wide, bm = scores_ref.shape[1:]

    def bias_at(c):
        return lambda t: bias_of(band, bm, lambda a: live_at(a, c * (wide // TILE) + t))

    def score(c, largest):
        return first_pass(query, key_at(c), bias_at(c), scores_ref, c, largest)

    largest = lax.fori_loop(0, key_blocks, score, jnp.full((8, bm), MASKED, jnp.float32))
    col_max = over_all(largest)

    def mix(c, state):
        return second_pass(scores_ref, c, col_max, bias_at(c), transposed(value_at(c)), state)

    state = jnp.zeros((8, bm), jnp.float32), jnp.zeros((HDIM, bm), jnp.float32)
    return divide(*lax.fori_loop(0, key_blocks, mix, state))


def transposed(block):
    return block.astype(jnp.float32).T.astype(BF16)


def attend_blocks(blocks, band, query_at, key_at, value_t, key_blocks, live_at, finish, scores):
    wide, bm = scores[0].shape[1:]
    empty = jnp.full((8, bm), MASKED, jnp.float32)
    nothing = jnp.zeros((8, bm), jnp.float32), jnp.zeros((HDIM, bm), jnp.float32)

    def bias_at(i, c):
        return lambda t: bias_of(band, bm, lambda a: live_at(i, a, c, t))

    def both(i, col_max, now, following):
        later = jnp.minimum(i + 1, blocks - 1)
        query = query_at(later)
        largest, state = empty, nothing
        for c in range(key_blocks):
            largest = first_pass(query, key_at(c), bias_at(later, c), following, c, largest)
            state = second_pass(now, c, col_max, bias_at(i, c), value_t[:, c * wide : (c + 1) * wide], state)
        finish(i, divide(*state))
        return over_all(largest)

    largest = empty
    query = query_at(0)
    for c in range(key_blocks):
        largest = first_pass(query, key_at(c), bias_at(0, c), scores[0], c, largest)

    def pair(n, col_max):
        col_max = both(2 * n, col_max, scores[0], scores[1])
        return both(2 * n + 1, col_max, scores[1], scores[0])

    lax.fori_loop(0, blocks // 2, pair, over_all(largest))


def partner(me, step):
    first, second = step
    return me ^ jnp.where(lax.axis_index("batch") == 0, first, second)


def collect_kernel(steps, rows, *refs):
    pieces, (q_out, kv_out) = refs[:-2], refs[-2:]
    me = lax.axis_index(NEAR)
    for step, piece in zip(steps, pieces):
        at = pl.ds(pl.multiple_of(partner(me, step) * rows, rows), rows)
        q_out[at] = piece[0]
        kv_out[:, at] = piece[1:]


def shared_kernel(mask_ref, q_ref, own_ref, other_ref, out_ref, value_t, *scores):
    mine = lax.axis_index("inner")
    _, wide, bm = scores[0].shape
    blocks = q_ref.shape[0] // wide

    def key_at(c):
        ref = own_ref if c < blocks else other_ref
        return ref[0, c % blocks * wide : (c % blocks + 1) * wide]

    for n, ref in enumerate((own_ref, other_ref)):
        for t in range(blocks * wide // TILE):
            at = (n * blocks * wide) + t * TILE
            value_t[:, at : at + TILE] = transposed(ref[1, t * TILE : (t + 1) * TILE])

    def tile(block, inner, t):
        return (block * 2 + inner) * (wide // TILE) + t

    def finish(i, mixed):
        out_ref[pl.ds(pl.multiple_of(i * bm, bm), bm)] = mixed

    attend_blocks(
        blocks,
        TILE,
        lambda i: q_ref[pl.ds(pl.multiple_of(i * bm, bm), bm)],
        key_at,
        value_t,
        2 * blocks,
        lambda i, a, c, t: mask_ref[tile(i, mine, a), tile(c % blocks, mine if c < blocks else 1 - mine, t)] != 0,
        finish,
        scores,
    )


def whole_kernel(sources, mask_ref, qkv_ref, *refs):
    out_ref, value_t, *scores = refs[-4:]
    rows = qkv_ref.shape[2]
    _, wide, bm = scores[0].shape
    bands, tiles = bm // rows, wide // TILE
    for t in range(sources):
        value_t[:, t * TILE : (t + 1) * TILE] = transposed(qkv_ref[t, 2])

    def finish(i, mixed):
        out_ref[pl.ds(i * bands, bands)] = mixed.reshape(bands, rows, HDIM)

    attend_blocks(
        sources // bands,
        rows,
        lambda i: qkv_ref[pl.ds(i * bands, bands), 0].reshape(bm, HDIM),
        lambda c: qkv_ref[c * tiles : (c + 1) * tiles, 1].reshape(wide, HDIM),
        value_t,
        sources // tiles,
        lambda i, a, c, t: mask_ref[i * bands + a, c * tiles + t] != 0,
        finish,
        scores,
    )


def halved(far, near):
    steps = []
    for d in range(near // 2):
        steps += [(near // 2 + d, d), (d, near // 2 + d)]

    def swap(piece, step):
        pairs = [(2 * i + b, 2 * (i ^ step[b]) + b) for i in range(near) for b in range(2)]
        return lax.ppermute(piece, (*NEAR, "batch"), pairs)

    def per_device(query_rows, key_rows, value_rows, q_gain, k_gain, tile_mask):
        rows, features = query_rows.shape

        def write(which, block, outs, kept):
            near_heads, far_heads, near_sems, far_sems = kept
            for h in range(near):
                near_heads[h, which] = block[:, h * HDIM : (h + 1) * HDIM]
            for h in range(far):
                far_heads[h, which] = block[:, (near + h) * HDIM : (near + h + 1) * HDIM]
            me = lax.axis_index(NEAR)
            copies = [
                pltpu.make_async_copy(near_heads.at[partner(me, step), which], outs[n].at[which], near_sems.at[which, n])
                for n, step in enumerate(steps)
            ]
            copies.append(pltpu.make_async_copy(far_heads.at[:, which], outs[-1].at[:, which], far_sems.at[which]))
            for copy in copies:
                copy.start()
            return copies

        def read(shared, whole, out_ref):
            for d in range(near):
                out_ref[:, d * HDIM : (d + 1) * HDIM] = shared[d]
            for d in range(far):
                out_ref[:, (near + d) * HDIM : (near + d + 1) * HDIM] = whole[d]

        *shared, whole = pack(
            write,
            [shape(3, rows, HDIM)] * near + [shape(far, 3, rows, HDIM)],
            rows,
            features,
            (query_rows, key_rows, value_rows, q_gain, k_gain),
            [
                pltpu.VMEM((near, 3, rows, HDIM), BF16),
                pltpu.VMEM((far, 3, rows, HDIM), BF16),
                pltpu.SemaphoreType.DMA((3, near)),
                pltpu.SemaphoreType.DMA((3,)),
            ],
        )
        shared = [swap(piece, step) for step, piece in zip(steps, shared)]
        whole = exchange(whole, FAR)
        q_near, kv_near = pl.pallas_call(
            functools.partial(collect_kernel, steps, rows),
            out_shape=[shape(near * rows, HDIM), shape(2, near * rows, HDIM)],
            compiler_params=PARAMS,
            name="collect",
        )(*shared)
        kv_other = lax.ppermute(kv_near, "inner", [(0, 1), (1, 0)])

        wide = 2 * TILE
        blocks = far * rows // wide
        smem, vmem = pl.BlockSpec(memory_space=pltpu.SMEM), pl.BlockSpec(memory_space=pltpu.VMEM)
        scratch = [pltpu.VMEM((HDIM, far * rows), BF16)]
        scores = [pltpu.VMEM((blocks, wide, wide), jnp.float32)] * 2
        shared = pl.pallas_call(
            shared_kernel,
            in_specs=[smem] + [vmem] * 3,
            out_shape=shape(near * rows, HDIM),
            scratch_shapes=scratch + scores,
            compiler_params=PARAMS,
            cost_estimate=pl.CostEstimate(flops=SHARED_COST, bytes_accessed=2**21, transcendentals=0),
            name="attend_shared",
        )(tile_mask, q_near, kv_near, kv_other)

        whole = pl.pallas_call(
            functools.partial(whole_kernel, far),
            in_specs=[smem, vmem, pl.BlockSpec(memory_space=pl.ANY)],
            out_shape=shape(far, rows, HDIM),
            scratch_shapes=scratch + [pltpu.VMEM((blocks // 2, 2 * wide, wide), jnp.float32)] * 2,
            compiler_params=PARAMS,
            cost_estimate=pl.CostEstimate(flops=2**33, bytes_accessed=2**22, transcendentals=0),
            name="attend_whole",
        )(tile_mask, whole, shared)
        shared = exchange(shared.reshape(near, rows, HDIM), NEAR)
        return pl.pallas_call(
            read, out_shape=shape(rows, features), compiler_params=PARAMS, name="unpack"
        )(shared, exchange(whole, FAR))

    return per_device


def gathered_kernel(outer, inner, mask_ref, q_ref, kv_ref, out_ref, scores_ref):
    i = pl.program_id(0)
    block = out_ref.shape[0] * out_ref.shape[1] * out_ref.shape[2]
    tiles = block // TILE
    q_tile = (i * inner + lax.axis_index("inner")) * tiles
    mixed = attend(
        q_ref[0, :, 0].reshape(block, HDIM),
        TILE,
        lambda c: kv_ref[lax.rem(c, inner), lax.div(c, inner), :, 1].reshape(block, HDIM),
        lambda c: kv_ref[lax.rem(c, inner), lax.div(c, inner), :, 2].reshape(block, HDIM),
        outer * inner,
        lambda a, t: mask_ref[q_tile + a, t] != 0,
        scores_ref,
    )
    out_ref[...] = mixed.reshape(out_ref.shape)


def gathered(outer, inner, n_head, near):
    width = HEADS // near * HDIM

    def per_device(query_rows, key_rows, value_rows, q_gain, k_gain, tile_mask):
        rows, features = query_rows.shape
        block = rows * n_head

        def write(which, block, outs, kept):
            packed, sems = kept
            for d in range(near):
                packed[d, which] = block[:, d * width : (d + 1) * width]
            copy = pltpu.make_async_copy(packed.at[:, which], outs[0].at[:, which], sems.at[which])
            copy.start()
            return [copy]

        def read(got_ref, out_ref):
            for d in range(near):
                out_ref[:, d * width : (d + 1) * width] = got_ref[d]

        (packed,) = pack(
            write,
            [shape(near, 3, rows, width)],
            rows,
            features,
            (query_rows, key_rows, value_rows, q_gain, k_gain),
            [pltpu.VMEM((near, 3, rows, width), BF16), pltpu.SemaphoreType.DMA((3,))],
        )
        own = exchange(packed, NEAR).reshape(outer, n_head, 3, rows, width)
        every = lax.all_gather(own, "inner")
        mixed = pl.pallas_call(
            functools.partial(gathered_kernel, outer, inner),
            grid=(outer, HEADS // near),
            in_specs=[
                pl.BlockSpec(memory_space=pltpu.SMEM),
                pl.BlockSpec((1, n_head, 1, rows, HDIM), lambda i, h: (i, 0, 0, 0, h)),
                pl.BlockSpec((inner, outer, n_head, 3, rows, HDIM), lambda i, h: (0, 0, 0, 0, 0, h)),
            ],
            out_specs=pl.BlockSpec((1, n_head, rows, HDIM), lambda i, h: (i, 0, 0, h)),
            out_shape=shape(outer, n_head, rows, width),
            scratch_shapes=[pltpu.VMEM((outer * inner, block, block), jnp.float32)],
            compiler_params=PARAMS,
            name="attend",
        )(tile_mask, own, every)
        return pl.pallas_call(
            read, out_shape=shape(rows, features), compiler_params=PARAMS, name="unpack"
        )(exchange(mixed.reshape(near, rows, width), NEAR))

    return per_device


def solution(mesh):
    n_blk, n_head = mesh.shape["blk"], mesh.shape["head"]
    outer = max(d for d in range(1, n_blk + 1) if n_blk % d == 0 and HEADS % (n_head * d) == 0)
    inner = n_blk // outer
    near, far = outer * n_head, n_blk * n_head

    def per_device(query_rows, *others):
        in_pairs = inner == 2 and n_head == 2 and mesh.shape["batch"] == 2 and near & (near - 1) == 0
        if in_pairs and HEADS == near + far and query_rows.shape[0] == TILE:
            return halved(far, near)(query_rows, *others)
        return gathered(outer, inner, n_head, near)(query_rows, *others)

    split = P(("batch", "outer", "inner", "head"), None)
    return jax.shard_map(
        per_device,
        mesh=Mesh(
            mesh.devices.reshape(outer, inner, n_head, mesh.shape["batch"]), ("outer", "inner", "head", "batch")
        ),
        in_specs=(split, split, split, P(), P(), P()),
        out_specs=split,
        check_vma=False,
    )
```

```python
import functools

import jax
import jax.numpy as jnp
from jax import lax
from jax.experimental import pallas as pl
from jax.experimental.pallas import tpu as pltpu
from jax.sharding import Mesh, PartitionSpec as P

HEADS = 24
HDIM = 128
TILE = 128
EPS = 1e-06
MASKED = -1e30
NEAR = ("outer", "head")
FAR = ("outer", "inner", "head")
PARAMS = pltpu.CompilerParams(vmem_limit_bytes=48 * 1024 * 1024)
PACK_PARAMS = pltpu.CompilerParams(vmem_limit_bytes=61 * 1024 * 1024)
BF16 = jnp.bfloat16
SHARED_COST = 24 * 2**30
SCALE = 1.4426950408889634 * HDIM ** (-0.5)


def shape(*dims):
    return jax.ShapeDtypeStruct(dims, BF16)


def exchange(x, axes):
    return lax.all_to_all(x, axes, split_axis=0, concat_axis=0, tiled=True)


def pack_kernel(store, send, inputs, outputs, scratch):
    *arrays, qg_hbm, kg_hbm = inputs
    *arrived, qg, kg, row_sems, gain_sems = scratch[:7]
    half = arrived[0].shape[1]
    rows = [
        [
            pltpu.make_async_copy(src.at[n * half : (n + 1) * half], dst.at[n], row_sems.at[n, which])
            for which, (src, dst) in enumerate(zip(arrays, arrived))
        ]
        for n in range(2)
    ]
    gains = [
        pltpu.make_async_copy(src, dst, gain_sems.at[n]) for n, (src, dst) in enumerate(((qg_hbm, qg), (kg_hbm, kg)))
    ]
    for copy in rows[0] + gains + rows[1]:
        copy.start()

    def normalize(block, gain):
        widened = block.astype(jnp.float32)
        mean_square = jnp.mean(widened * widened, axis=-1, keepdims=True)
        return (widened * lax.rsqrt(mean_square + EPS) * gain[...]).astype(BF16)

    sent = []
    for n in range(2):
        rows[n][2].wait()
        store(n, 2, arrived[2][n], scratch[7:])
        for which, gain in enumerate((qg, kg)):
            rows[n][which].wait()
            if n == 0:
                gains[which].wait()
            store(n, which, normalize(arrived[which][n], gain), scratch[7:])
        sent += send(n, pl.ds(n * half, half), outputs, scratch[7:])
    for copy in sent:
        copy.wait()


def pack(store, send, out_shape, rows, features, arrays, kept):
    q, k, v, q_gain, k_gain = arrays
    hbm = pl.BlockSpec(memory_space=pltpu.HBM)

    def kernel(*refs):
        pack_kernel(store, send, refs[:5], refs[5 : 5 + len(out_shape)], refs[5 + len(out_shape) :])

    return pl.pallas_call(
        kernel,
        in_specs=[hbm] * 5,
        out_specs=[hbm] * len(out_shape),
        out_shape=out_shape,
        scratch_shapes=[pltpu.VMEM((2, rows // 2, features), BF16)] * 3
        + [pltpu.VMEM((1, features), jnp.float32)] * 2
        + [pltpu.SemaphoreType.DMA((2, 3)), pltpu.SemaphoreType.DMA((2,)), *kept],
        compiler_params=PACK_PARAMS,
        name="pack",
    )(q, k, v, q_gain.reshape(1, -1), k_gain.reshape(1, -1))


def first_pass(query, key, bias_at, scores_ref, c, largest):
    s = lax.dot_general(key, query, (((1,), (1,)), ((), ())), preferred_element_type=jnp.float32)
    scores_ref[c] = s
    for t in range(key.shape[0] // TILE):
        tile = s[t * TILE : (t + 1) * TILE].reshape(TILE // 8, 8, -1)
        largest = jnp.maximum(largest, jnp.max(tile, axis=0) + bias_at(t))
    return largest


def second_pass(scores_ref, c, col_max, bias_at, value_t, state):
    total, mixed = state
    wide, bm = scores_ref.shape[1:]
    weights = []
    for t in range(wide // TILE):
        tile = scores_ref[c, t * TILE : (t + 1) * TILE].reshape(TILE // 8, 8, bm)
        tile = jnp.exp2(tile * SCALE - (col_max - bias_at(t))[None])
        total = total + jnp.sum(tile, axis=0)
        weights.append(tile.reshape(TILE, bm).astype(BF16))
    weights = jnp.concatenate(weights, axis=0)
    return total, mixed + jnp.dot(value_t, weights, preferred_element_type=jnp.float32)


def over_all(largest):
    return jnp.broadcast_to(jnp.max(largest, axis=0, keepdims=True) * SCALE, largest.shape)


def divide(total, mixed):
    return (mixed / jnp.sum(total, axis=0, keepdims=True)).T.astype(BF16)


def bias_of(band, bm, live_at):
    lane = lax.broadcasted_iota(jnp.int32, (8, bm), 1)
    bias = jnp.zeros((8, bm), jnp.float32)
    for a in range(bm // band):
        dead = jnp.where(live_at(a), 0.0, MASKED).astype(jnp.float32)
        bias = jnp.where((lane >= a * band) & (lane < (a + 1) * band), dead, bias)
    return bias


def attend(query, band, key_at, value_at, key_blocks, live_at, scores_ref):
    wide, bm = scores_ref.shape[1:]

    def bias_at(c):
        return lambda t: bias_of(band, bm, lambda a: live_at(a, c * (wide // TILE) + t))

    def score(c, largest):
        return first_pass(query, key_at(c), bias_at(c), scores_ref, c, largest)

    largest = lax.fori_loop(0, key_blocks, score, jnp.full((8, bm), MASKED, jnp.float32))
    col_max = over_all(largest)

    def mix(c, state):
        return second_pass(scores_ref, c, col_max, bias_at(c), transposed(value_at(c)), state)

    state = jnp.zeros((8, bm), jnp.float32), jnp.zeros((HDIM, bm), jnp.float32)
    return divide(*lax.fori_loop(0, key_blocks, mix, state))


def transposed(block):
    return block.astype(jnp.float32).T.astype(BF16)


def attend_blocks(blocks, band, query_at, key_at, value_t, key_blocks, live_at, finish, scores):
    wide, bm = scores[0].shape[1:]
    empty = jnp.full((8, bm), MASKED, jnp.float32)
    nothing = jnp.zeros((8, bm), jnp.float32), jnp.zeros((HDIM, bm), jnp.float32)

    def bias_at(i, c):
        return lambda t: bias_of(band, bm, lambda a: live_at(i, a, c, t))

    def both(i, col_max, now, following):
        later = jnp.minimum(i + 1, blocks - 1)
        query = query_at(later)
        largest, state = empty, nothing
        for c in range(key_blocks):
            largest = first_pass(query, key_at(c), bias_at(later, c), following, c, largest)
            state = second_pass(now, c, col_max, bias_at(i, c), value_t[:, c * wide : (c + 1) * wide], state)
        finish(i, divide(*state))
        return over_all(largest)

    largest = empty
    query = query_at(0)
    for c in range(key_blocks):
        largest = first_pass(query, key_at(c), bias_at(0, c), scores[0], c, largest)

    def pair(n, col_max):
        col_max = both(2 * n, col_max, scores[0], scores[1])
        return both(2 * n + 1, col_max, scores[1], scores[0])

    lax.fori_loop(0, blocks // 2, pair, over_all(largest))


def partner(me, step):
    first, second = step
    return me ^ jnp.where(lax.axis_index("batch") == 0, first, second)


def collect_kernel(steps, rows, *refs):
    pieces, (q_out, kv_out) = refs[:-2], refs[-2:]
    me = lax.axis_index(NEAR)
    for step, piece in zip(steps, pieces):
        at = pl.ds(pl.multiple_of(partner(me, step) * rows, rows), rows)
        q_out[at] = piece[0]
        kv_out[:, at] = piece[1:]


def shared_kernel(mask_ref, q_ref, own_ref, other_ref, out_ref, value_t, *scores):
    mine = lax.axis_index("inner")
    _, wide, bm = scores[0].shape
    blocks = q_ref.shape[0] // wide

    def key_at(c):
        ref = own_ref if c < blocks else other_ref
        return ref[0, c % blocks * wide : (c % blocks + 1) * wide]

    for n, ref in enumerate((own_ref, other_ref)):
        for t in range(blocks * wide // TILE):
            at = (n * blocks * wide) + t * TILE
            value_t[:, at : at + TILE] = transposed(ref[1, t * TILE : (t + 1) * TILE])

    def tile(block, inner, t):
        return (block * 2 + inner) * (wide // TILE) + t

    def finish(i, mixed):
        out_ref[pl.ds(pl.multiple_of(i * bm, bm), bm)] = mixed

    attend_blocks(
        blocks,
        TILE,
        lambda i: q_ref[pl.ds(pl.multiple_of(i * bm, bm), bm)],
        key_at,
        value_t,
        2 * blocks,
        lambda i, a, c, t: mask_ref[tile(i, mine, a), tile(c % blocks, mine if c < blocks else 1 - mine, t)] != 0,
        finish,
        scores,
    )


def whole_kernel(sources, mask_ref, qkv_ref, *refs):
    out_ref, value_t, *scores = refs[-4:]
    rows = qkv_ref.shape[2]
    _, wide, bm = scores[0].shape
    bands, tiles = bm // rows, wide // TILE
    for t in range(sources):
        value_t[:, t * TILE : (t + 1) * TILE] = transposed(qkv_ref[t, 2])

    def finish(i, mixed):
        out_ref[pl.ds(i * bands, bands)] = mixed.reshape(bands, rows, HDIM)

    attend_blocks(
        sources // bands,
        rows,
        lambda i: qkv_ref[pl.ds(i * bands, bands), 0].reshape(bm, HDIM),
        lambda c: qkv_ref[c * tiles : (c + 1) * tiles, 1].reshape(wide, HDIM),
        value_t,
        sources // tiles,
        lambda i, a, c, t: mask_ref[i * bands + a, c * tiles + t] != 0,
        finish,
        scores,
    )


def halved(far, near):
    steps = []
    for d in range(near // 2):
        steps += [(near // 2 + d, d), (d, near // 2 + d)]

    def swap(piece, step):
        pairs = [(2 * i + b, 2 * (i ^ step[b]) + b) for i in range(near) for b in range(2)]
        return lax.ppermute(piece, (*NEAR, "batch"), pairs)

    def per_device(query_rows, key_rows, value_rows, q_gain, k_gain, tile_mask):
        rows, features = query_rows.shape

        def store(n, which, block, kept):
            near_heads, far_heads = kept[n], kept[2 + n]
            for h in range(near):
                near_heads[h, which] = block[:, h * HDIM : (h + 1) * HDIM]
            for h in range(far):
                far_heads[h, which] = block[:, (near + h) * HDIM : (near + h + 1) * HDIM]

        def send(n, at, outs, kept):
            near_heads, far_heads, sems = kept[n], kept[2 + n], kept[4]
            me = lax.axis_index(NEAR)
            copies = [
                pltpu.make_async_copy(near_heads.at[partner(me, step)], out.at[:, at], sems.at[n, i])
                for i, (step, out) in enumerate(zip(steps, outs))
            ]
            copies.append(pltpu.make_async_copy(far_heads, outs[-1].at[:, :, at], sems.at[n, near]))
            for copy in copies:
                copy.start()
            return copies

        def read(shared, whole, out_ref):
            for d in range(near):
                out_ref[:, d * HDIM : (d + 1) * HDIM] = shared[d]
            for d in range(far):
                out_ref[:, (near + d) * HDIM : (near + d + 1) * HDIM] = whole[d]

        *shared, whole = pack(
            store,
            send,
            [shape(3, rows, HDIM)] * near + [shape(far, 3, rows, HDIM)],
            rows,
            features,
            (query_rows, key_rows, value_rows, q_gain, k_gain),
            [pltpu.VMEM((near, 3, rows // 2, HDIM), BF16)] * 2
            + [pltpu.VMEM((far, 3, rows // 2, HDIM), BF16)] * 2
            + [pltpu.SemaphoreType.DMA((2, near + 1))],
        )
        shared = [swap(piece, step) for step, piece in zip(steps, shared)]
        whole = exchange(whole, FAR)
        q_near, kv_near = pl.pallas_call(
            functools.partial(collect_kernel, steps, rows),
            out_shape=[shape(near * rows, HDIM), shape(2, near * rows, HDIM)],
            compiler_params=PARAMS,
            name="collect",
        )(*shared)
        kv_other = lax.ppermute(kv_near, "inner", [(0, 1), (1, 0)])

        wide = 2 * TILE
        blocks = far * rows // wide
        smem, vmem = pl.BlockSpec(memory_space=pltpu.SMEM), pl.BlockSpec(memory_space=pltpu.VMEM)
        scratch = [pltpu.VMEM((HDIM, far * rows), BF16)]
        scores = [pltpu.VMEM((blocks, wide, wide), jnp.float32)] * 2
        shared = pl.pallas_call(
            shared_kernel,
            in_specs=[smem] + [vmem] * 3,
            out_shape=shape(near * rows, HDIM),
            scratch_shapes=scratch + scores,
            compiler_params=PARAMS,
            cost_estimate=pl.CostEstimate(flops=SHARED_COST, bytes_accessed=2**21, transcendentals=0),
            name="attend_shared",
        )(tile_mask, q_near, kv_near, kv_other)

        whole = pl.pallas_call(
            functools.partial(whole_kernel, far),
            in_specs=[smem, vmem, pl.BlockSpec(memory_space=pl.ANY)],
            out_shape=shape(far, rows, HDIM),
            scratch_shapes=scratch + [pltpu.VMEM((blocks // 2, 2 * wide, wide), jnp.float32)] * 2,
            compiler_params=PARAMS,
            cost_estimate=pl.CostEstimate(flops=2**33, bytes_accessed=2**22, transcendentals=0),
            name="attend_whole",
        )(tile_mask, whole, shared)
        shared = exchange(shared.reshape(near, rows, HDIM), NEAR)
        return pl.pallas_call(
            read, out_shape=shape(rows, features), compiler_params=PARAMS, name="unpack"
        )(shared, exchange(whole, FAR))

    return per_device


def gathered_kernel(outer, inner, mask_ref, q_ref, kv_ref, out_ref, scores_ref):
    i = pl.program_id(0)
    block = out_ref.shape[0] * out_ref.shape[1] * out_ref.shape[2]
    tiles = block // TILE
    q_tile = (i * inner + lax.axis_index("inner")) * tiles
    mixed = attend(
        q_ref[0, :, 0].reshape(block, HDIM),
        TILE,
        lambda c: kv_ref[lax.rem(c, inner), lax.div(c, inner), :, 1].reshape(block, HDIM),
        lambda c: kv_ref[lax.rem(c, inner), lax.div(c, inner), :, 2].reshape(block, HDIM),
        outer * inner,
        lambda a, t: mask_ref[q_tile + a, t] != 0,
        scores_ref,
    )
    out_ref[...] = mixed.reshape(out_ref.shape)


def gathered(outer, inner, n_head, near):
    width = HEADS // near * HDIM

    def per_device(query_rows, key_rows, value_rows, q_gain, k_gain, tile_mask):
        rows, features = query_rows.shape
        block = rows * n_head

        def store(n, which, block, kept):
            for d in range(near):
                kept[n][d, which] = block[:, d * width : (d + 1) * width]

        def send(n, at, outs, kept):
            copy = pltpu.make_async_copy(kept[n], outs[0].at[:, :, at], kept[2].at[n])
            copy.start()
            return [copy]

        def read(got_ref, out_ref):
            for d in range(near):
                out_ref[:, d * width : (d + 1) * width] = got_ref[d]

        (packed,) = pack(
            store,
            send,
            [shape(near, 3, rows, width)],
            rows,
            features,
            (query_rows, key_rows, value_rows, q_gain, k_gain),
            [pltpu.VMEM((near, 3, rows // 2, width), BF16)] * 2 + [pltpu.SemaphoreType.DMA((2,))],
        )
        own = exchange(packed, NEAR).reshape(outer, n_head, 3, rows, width)
        every = lax.all_gather(own, "inner")
        mixed = pl.pallas_call(
            functools.partial(gathered_kernel, outer, inner),
            grid=(outer, HEADS // near),
            in_specs=[
                pl.BlockSpec(memory_space=pltpu.SMEM),
                pl.BlockSpec((1, n_head, 1, rows, HDIM), lambda i, h: (i, 0, 0, 0, h)),
                pl.BlockSpec((inner, outer, n_head, 3, rows, HDIM), lambda i, h: (0, 0, 0, 0, 0, h)),
            ],
            out_specs=pl.BlockSpec((1, n_head, rows, HDIM), lambda i, h: (i, 0, 0, h)),
            out_shape=shape(outer, n_head, rows, width),
            scratch_shapes=[pltpu.VMEM((outer * inner, block, block), jnp.float32)],
            compiler_params=PARAMS,
            name="attend",
        )(tile_mask, own, every)
        return pl.pallas_call(
            read, out_shape=shape(rows, features), compiler_params=PARAMS, name="unpack"
        )(exchange(mixed.reshape(near, rows, width), NEAR))

    return per_device


def solution(mesh):
    n_blk, n_head = mesh.shape["blk"], mesh.shape["head"]
    outer = max(d for d in range(1, n_blk + 1) if n_blk % d == 0 and HEADS % (n_head * d) == 0)
    inner = n_blk // outer
    near, far = outer * n_head, n_blk * n_head

    def per_device(query_rows, *others):
        in_pairs = inner == 2 and n_head == 2 and mesh.shape["batch"] == 2 and near & (near - 1) == 0
        if in_pairs and HEADS == near + far and query_rows.shape[0] == TILE:
            return halved(far, near)(query_rows, *others)
        return gathered(outer, inner, n_head, near)(query_rows, *others)

    split = P(("batch", "outer", "inner", "head"), None)
    return jax.shard_map(
        per_device,
        mesh=Mesh(
            mesh.devices.reshape(outer, inner, n_head, mesh.shape["batch"]), ("outer", "inner", "head", "batch")
        ),
        in_specs=(split, split, split, P(), P(), P()),
        out_specs=split,
        check_vma=False,
    )
```

```python
import functools

import jax
import jax.numpy as jnp
from jax import lax
from jax.experimental import pallas as pl
from jax.experimental.pallas import tpu as pltpu
from jax.sharding import Mesh, PartitionSpec as P

HEADS = 24
HDIM = 128
TILE = 128
EPS = 1e-06
MASKED = -1e30
NEAR = ("outer", "head")
FAR = ("outer", "inner", "head")
PARAMS = pltpu.CompilerParams(vmem_limit_bytes=48 * 1024 * 1024)
PACK_PARAMS = pltpu.CompilerParams(vmem_limit_bytes=61 * 1024 * 1024)
BF16 = jnp.bfloat16
SHARED_COST = 24 * 2**30
SCALE = 1.4426950408889634 * HDIM ** (-0.5)


def shape(*dims):
    return jax.ShapeDtypeStruct(dims, BF16)


def exchange(x, axes):
    return lax.all_to_all(x, axes, split_axis=0, concat_axis=0, tiled=True)


def pack_kernel(store, send, inputs, outputs, scratch):
    q_hbm, k_hbm, v_hbm, qg_hbm, kg_hbm = inputs
    q_in, k_in, v_in, qg, kg, sems, *kept = scratch
    copies = [
        pltpu.make_async_copy(src, dst, sems.at[n])
        for n, (src, dst) in enumerate(
            ((v_hbm, v_in), (q_hbm, q_in), (qg_hbm, qg), (k_hbm, k_in), (kg_hbm, kg))
        )
    ]
    for copy in copies:
        copy.start()

    group = 16

    def normalize(block, gain):
        widened = block.astype(jnp.float32)
        mean_square = jnp.mean(widened * widened, axis=-1, keepdims=True)
        return (widened * lax.rsqrt(mean_square + EPS) * gain[...]).astype(BF16)

    sent = []
    for first, which, ref, gain in ((0, 2, v_in, None), (1, 0, q_in, qg), (3, 1, k_in, kg)):
        copies[first].wait()
        if gain is not None:
            copies[first + 1].wait()
        for row in range(0, ref.shape[0], group):
            at = slice(row, row + group)
            store(which, at, ref[at] if gain is None else normalize(ref[at], gain), kept)
        sent += send(which, outputs, kept)
    for copy in sent:
        copy.wait()


def pack(store, send, out_shape, rows, features, arrays, kept=()):
    q, k, v, q_gain, k_gain = arrays
    hbm = pl.BlockSpec(memory_space=pltpu.HBM)

    def kernel(*refs):
        pack_kernel(store, send, refs[:5], refs[5 : 5 + len(out_shape)], refs[5 + len(out_shape) :])

    return pl.pallas_call(
        kernel,
        in_specs=[hbm] * 5,
        out_specs=[hbm] * len(out_shape),
        out_shape=out_shape,
        scratch_shapes=[pltpu.VMEM((rows, features), BF16)] * 3
        + [pltpu.VMEM((1, features), jnp.float32)] * 2
        + [pltpu.SemaphoreType.DMA((5,)), *kept],
        compiler_params=PACK_PARAMS,
        name="pack",
    )(q, k, v, q_gain.reshape(1, -1), k_gain.reshape(1, -1))


def first_pass(query, key, bias_at, scores_ref, c, largest):
    s = lax.dot_general(key, query, (((1,), (1,)), ((), ())), preferred_element_type=jnp.float32)
    scores_ref[c] = s
    for t in range(key.shape[0] // TILE):
        tile = s[t * TILE : (t + 1) * TILE].reshape(TILE // 8, 8, -1)
        largest = jnp.maximum(largest, jnp.max(tile, axis=0) + bias_at(t))
    return largest


def second_pass(scores_ref, c, col_max, bias_at, value_t, state):
    total, mixed = state
    wide, bm = scores_ref.shape[1:]
    weights = []
    for t in range(wide // TILE):
        tile = scores_ref[c, t * TILE : (t + 1) * TILE].reshape(TILE // 8, 8, bm)
        tile = jnp.exp2(tile * SCALE - (col_max - bias_at(t))[None])
        total = total + jnp.sum(tile, axis=0)
        weights.append(tile.reshape(TILE, bm).astype(BF16))
    weights = jnp.concatenate(weights, axis=0)
    return total, mixed + jnp.dot(value_t, weights, preferred_element_type=jnp.float32)


def over_all(largest):
    return jnp.broadcast_to(jnp.max(largest, axis=0, keepdims=True) * SCALE, largest.shape)


def divide(total, mixed):
    return (mixed / jnp.sum(total, axis=0, keepdims=True)).T.astype(BF16)


def bias_of(band, bm, live_at):
    lane = lax.broadcasted_iota(jnp.int32, (8, bm), 1)
    bias = jnp.zeros((8, bm), jnp.float32)
    for a in range(bm // band):
        dead = jnp.where(live_at(a), 0.0, MASKED).astype(jnp.float32)
        bias = jnp.where((lane >= a * band) & (lane < (a + 1) * band), dead, bias)
    return bias


def attend(query, band, key_at, value_at, key_blocks, live_at, scores_ref):
    wide, bm = scores_ref.shape[1:]

    def bias_at(c):
        return lambda t: bias_of(band, bm, lambda a: live_at(a, c * (wide // TILE) + t))

    def score(c, largest):
        return first_pass(query, key_at(c), bias_at(c), scores_ref, c, largest)

    largest = lax.fori_loop(0, key_blocks, score, jnp.full((8, bm), MASKED, jnp.float32))
    col_max = over_all(largest)

    def mix(c, state):
        return second_pass(scores_ref, c, col_max, bias_at(c), transposed(value_at(c)), state)

    state = jnp.zeros((8, bm), jnp.float32), jnp.zeros((HDIM, bm), jnp.float32)
    return divide(*lax.fori_loop(0, key_blocks, mix, state))


def transposed(block):
    return block.astype(jnp.float32).T.astype(BF16)


def attend_blocks(blocks, band, query_at, key_at, value_t, key_blocks, live_at, finish, scores):
    wide, bm = scores[0].shape[1:]
    empty = jnp.full((8, bm), MASKED, jnp.float32)
    nothing = jnp.zeros((8, bm), jnp.float32), jnp.zeros((HDIM, bm), jnp.float32)

    def bias_at(i, c):
        return lambda t: bias_of(band, bm, lambda a: live_at(i, a, c, t))

    def both(i, col_max, now, following):
        later = jnp.minimum(i + 1, blocks - 1)
        query = query_at(later)
        largest, state = empty, nothing
        for c in range(key_blocks):
            largest = first_pass(query, key_at(c), bias_at(later, c), following, c, largest)
            state = second_pass(now, c, col_max, bias_at(i, c), value_t[:, c * wide : (c + 1) * wide], state)
        finish(i, divide(*state))
        return over_all(largest)

    largest = empty
    query = query_at(0)
    for c in range(key_blocks):
        largest = first_pass(query, key_at(c), bias_at(0, c), scores[0], c, largest)

    def pair(n, col_max):
        col_max = both(2 * n, col_max, scores[0], scores[1])
        return both(2 * n + 1, col_max, scores[1], scores[0])

    lax.fori_loop(0, blocks // 2, pair, over_all(largest))


def partner(me, step):
    first, second = step
    return me ^ jnp.where(lax.axis_index("batch") == 0, first, second)


def collect_kernel(steps, rows, *refs):
    pieces, (q_out, kv_out) = refs[:-2], refs[-2:]
    me = lax.axis_index(NEAR)
    for step, piece in zip(steps, pieces):
        at = pl.ds(pl.multiple_of(partner(me, step) * rows, rows), rows)
        q_out[at] = piece[0]
        kv_out[:, at] = piece[1:]


def shared_kernel(mask_ref, q_ref, own_ref, other_ref, out_ref, value_t, *scores):
    mine = lax.axis_index("inner")
    _, wide, bm = scores[0].shape
    blocks = q_ref.shape[0] // wide

    def key_at(c):
        ref = own_ref if c < blocks else other_ref
        return ref[0, c % blocks * wide : (c % blocks + 1) * wide]

    for n, ref in enumerate((own_ref, other_ref)):
        for t in range(blocks * wide // TILE):
            at = (n * blocks * wide) + t * TILE
            value_t[:, at : at + TILE] = transposed(ref[1, t * TILE : (t + 1) * TILE])

    def tile(block, inner, t):
        return (block * 2 + inner) * (wide // TILE) + t

    def finish(i, mixed):
        out_ref[pl.ds(pl.multiple_of(i * bm, bm), bm)] = mixed

    attend_blocks(
        blocks,
        TILE,
        lambda i: q_ref[pl.ds(pl.multiple_of(i * bm, bm), bm)],
        key_at,
        value_t,
        2 * blocks,
        lambda i, a, c, t: mask_ref[tile(i, mine, a), tile(c % blocks, mine if c < blocks else 1 - mine, t)] != 0,
        finish,
        scores,
    )


def whole_kernel(sources, mask_ref, qkv_ref, *refs):
    out_ref, value_t, *scores = refs[-4:]
    rows = qkv_ref.shape[2]
    _, wide, bm = scores[0].shape
    bands, tiles = bm // rows, wide // TILE
    for t in range(sources):
        value_t[:, t * TILE : (t + 1) * TILE] = transposed(qkv_ref[t, 2])

    def finish(i, mixed):
        out_ref[pl.ds(i * bands, bands)] = mixed.reshape(bands, rows, HDIM)

    attend_blocks(
        sources // bands,
        rows,
        lambda i: qkv_ref[pl.ds(i * bands, bands), 0].reshape(bm, HDIM),
        lambda c: qkv_ref[c * tiles : (c + 1) * tiles, 1].reshape(wide, HDIM),
        value_t,
        sources // tiles,
        lambda i, a, c, t: mask_ref[i * bands + a, c * tiles + t] != 0,
        finish,
        scores,
    )


def halved(far, near):
    steps = []
    for d in range(near // 2):
        steps += [(near // 2 + d, d), (d, near // 2 + d)]

    def swap(piece, step):
        pairs = [(2 * i + b, 2 * (i ^ step[b]) + b) for i in range(near) for b in range(2)]
        return lax.ppermute(piece, (*NEAR, "batch"), pairs)

    def per_device(query_rows, key_rows, value_rows, q_gain, k_gain, tile_mask):
        rows, features = query_rows.shape

        def store(which, at, block, kept):
            near_heads, far_heads = kept[:2]
            for h in range(near):
                near_heads[h, which, at] = block[:, h * HDIM : (h + 1) * HDIM]
            for h in range(far):
                far_heads[h, which, at] = block[:, (near + h) * HDIM : (near + h + 1) * HDIM]

        def send(which, outs, kept):
            near_heads, far_heads, near_sems, far_sems = kept
            me = lax.axis_index(NEAR)
            copies = [
                pltpu.make_async_copy(near_heads.at[partner(me, step), which], outs[n].at[which], near_sems.at[which, n])
                for n, step in enumerate(steps)
            ]
            copies.append(pltpu.make_async_copy(far_heads.at[:, which], outs[-1].at[:, which], far_sems.at[which]))
            for copy in copies:
                copy.start()
            return copies

        def read(shared, whole, out_ref):
            for d in range(near):
                out_ref[:, d * HDIM : (d + 1) * HDIM] = shared[d]
            for d in range(far):
                out_ref[:, (near + d) * HDIM : (near + d + 1) * HDIM] = whole[d]

        *shared, whole = pack(
            store,
            send,
            [shape(3, rows, HDIM)] * near + [shape(far, 3, rows, HDIM)],
            rows,
            features,
            (query_rows, key_rows, value_rows, q_gain, k_gain),
            [
                pltpu.VMEM((near, 3, rows, HDIM), BF16),
                pltpu.VMEM((far, 3, rows, HDIM), BF16),
                pltpu.SemaphoreType.DMA((3, near)),
                pltpu.SemaphoreType.DMA((3,)),
            ],
        )
        shared = [swap(piece, step) for step, piece in zip(steps, shared)]
        whole = exchange(whole, FAR)
        q_near, kv_near = pl.pallas_call(
            functools.partial(collect_kernel, steps, rows),
            out_shape=[shape(near * rows, HDIM), shape(2, near * rows, HDIM)],
            compiler_params=PARAMS,
            name="collect",
        )(*shared)
        kv_other = lax.ppermute(kv_near, "inner", [(0, 1), (1, 0)])

        wide = 2 * TILE
        blocks = far * rows // wide
        smem, vmem = pl.BlockSpec(memory_space=pltpu.SMEM), pl.BlockSpec(memory_space=pltpu.VMEM)
        scratch = [pltpu.VMEM((HDIM, far * rows), BF16)]
        scores = [pltpu.VMEM((blocks, wide, wide), jnp.float32)] * 2
        shared = pl.pallas_call(
            shared_kernel,
            in_specs=[smem] + [vmem] * 3,
            out_shape=shape(near * rows, HDIM),
            scratch_shapes=scratch + scores,
            compiler_params=PARAMS,
            cost_estimate=pl.CostEstimate(flops=SHARED_COST, bytes_accessed=2**21, transcendentals=0),
            name="attend_shared",
        )(tile_mask, q_near, kv_near, kv_other)

        whole = pl.pallas_call(
            functools.partial(whole_kernel, far),
            in_specs=[smem, vmem, pl.BlockSpec(memory_space=pl.ANY)],
            out_shape=shape(far, rows, HDIM),
            scratch_shapes=scratch + [pltpu.VMEM((blocks // 2, 2 * wide, wide), jnp.float32)] * 2,
            compiler_params=PARAMS,
            cost_estimate=pl.CostEstimate(flops=2**33, bytes_accessed=2**22, transcendentals=0),
            name="attend_whole",
        )(tile_mask, whole, shared)
        shared = exchange(shared.reshape(near, rows, HDIM), NEAR)
        return pl.pallas_call(
            read, out_shape=shape(rows, features), compiler_params=PARAMS, name="unpack"
        )(shared, exchange(whole, FAR))

    return per_device


def gathered_kernel(outer, inner, mask_ref, q_ref, kv_ref, out_ref, scores_ref):
    i = pl.program_id(0)
    block = out_ref.shape[0] * out_ref.shape[1] * out_ref.shape[2]
    tiles = block // TILE
    q_tile = (i * inner + lax.axis_index("inner")) * tiles
    mixed = attend(
        q_ref[0, :, 0].reshape(block, HDIM),
        TILE,
        lambda c: kv_ref[lax.rem(c, inner), lax.div(c, inner), :, 1].reshape(block, HDIM),
        lambda c: kv_ref[lax.rem(c, inner), lax.div(c, inner), :, 2].reshape(block, HDIM),
        outer * inner,
        lambda a, t: mask_ref[q_tile + a, t] != 0,
        scores_ref,
    )
    out_ref[...] = mixed.reshape(out_ref.shape)


def gathered(outer, inner, n_head, near):
    width = HEADS // near * HDIM

    def per_device(query_rows, key_rows, value_rows, q_gain, k_gain, tile_mask):
        rows, features = query_rows.shape
        block = rows * n_head

        def store(which, at, block, kept):
            for d in range(near):
                kept[0][d, which, at] = block[:, d * width : (d + 1) * width]

        def send(which, outs, kept):
            packed, sems = kept
            copy = pltpu.make_async_copy(packed.at[:, which], outs[0].at[:, which], sems.at[which])
            copy.start()
            return [copy]

        def read(got_ref, out_ref):
            for d in range(near):
                out_ref[:, d * width : (d + 1) * width] = got_ref[d]

        (packed,) = pack(
            store,
            send,
            [shape(near, 3, rows, width)],
            rows,
            features,
            (query_rows, key_rows, value_rows, q_gain, k_gain),
            [pltpu.VMEM((near, 3, rows, width), BF16), pltpu.SemaphoreType.DMA((3,))],
        )
        own = exchange(packed, NEAR).reshape(outer, n_head, 3, rows, width)
        every = lax.all_gather(own, "inner")
        mixed = pl.pallas_call(
            functools.partial(gathered_kernel, outer, inner),
            grid=(outer, HEADS // near),
            in_specs=[
                pl.BlockSpec(memory_space=pltpu.SMEM),
                pl.BlockSpec((1, n_head, 1, rows, HDIM), lambda i, h: (i, 0, 0, 0, h)),
                pl.BlockSpec((inner, outer, n_head, 3, rows, HDIM), lambda i, h: (0, 0, 0, 0, 0, h)),
            ],
            out_specs=pl.BlockSpec((1, n_head, rows, HDIM), lambda i, h: (i, 0, 0, h)),
            out_shape=shape(outer, n_head, rows, width),
            scratch_shapes=[pltpu.VMEM((outer * inner, block, block), jnp.float32)],
            compiler_params=PARAMS,
            name="attend",
        )(tile_mask, own, every)
        return pl.pallas_call(
            read, out_shape=shape(rows, features), compiler_params=PARAMS, name="unpack"
        )(exchange(mixed.reshape(near, rows, width), NEAR))

    return per_device


def solution(mesh):
    n_blk, n_head = mesh.shape["blk"], mesh.shape["head"]
    outer = max(d for d in range(1, n_blk + 1) if n_blk % d == 0 and HEADS % (n_head * d) == 0)
    inner = n_blk // outer
    near, far = outer * n_head, n_blk * n_head

    def per_device(query_rows, *others):
        in_pairs = inner == 2 and n_head == 2 and mesh.shape["batch"] == 2 and near & (near - 1) == 0
        if in_pairs and HEADS == near + far and query_rows.shape[0] == TILE:
            return halved(far, near)(query_rows, *others)
        return gathered(outer, inner, n_head, near)(query_rows, *others)

    split = P(("batch", "outer", "inner", "head"), None)
    return jax.shard_map(
        per_device,
        mesh=Mesh(
            mesh.devices.reshape(outer, inner, n_head, mesh.shape["batch"]), ("outer", "inner", "head", "batch")
        ),
        in_specs=(split, split, split, P(), P(), P()),
        out_specs=split,
        check_vma=False,
    )
```

```python
import functools

import jax
import jax.numpy as jnp
from jax import lax
from jax.experimental import pallas as pl
from jax.experimental.pallas import tpu as pltpu
from jax.sharding import Mesh, PartitionSpec as P

HEADS = 24
HDIM = 128
TILE = 128
EPS = 1e-06
MASKED = -1e30
NEAR = ("outer", "head")
FAR = ("outer", "inner", "head")
PARAMS = pltpu.CompilerParams(vmem_limit_bytes=48 * 1024 * 1024)
PACK_PARAMS = pltpu.CompilerParams(vmem_limit_bytes=61 * 1024 * 1024)
BF16 = jnp.bfloat16
SHARED_COST = 24 * 2**30
SCALE = 1.4426950408889634 * HDIM ** (-0.5)


def shape(*dims):
    return jax.ShapeDtypeStruct(dims, BF16)


def exchange(x, axes):
    return lax.all_to_all(x, axes, split_axis=0, concat_axis=0, tiled=True)


def pack_kernel(store, send, inputs, outputs, scratch):
    q_hbm, k_hbm, v_hbm, qg_hbm, kg_hbm = inputs
    q_in, k_in, v_in, qg, kg, sems, *kept = scratch
    copies = [
        pltpu.make_async_copy(src, dst, sems.at[n])
        for n, (src, dst) in enumerate(
            ((v_hbm, v_in), (q_hbm, q_in), (qg_hbm, qg), (k_hbm, k_in), (kg_hbm, kg))
        )
    ]
    for copy in copies:
        copy.start()

    group = 16

    def normalize(block, gain):
        widened = block.astype(jnp.float32)
        mean_square = jnp.mean(widened * widened, axis=-1, keepdims=True)
        return (widened * lax.rsqrt(mean_square + EPS) * gain[...]).astype(BF16)

    sent = []
    for first, which, ref, gain in ((0, 2, v_in, None), (1, 0, q_in, qg), (3, 1, k_in, kg)):
        copies[first].wait()
        if gain is not None:
            copies[first + 1].wait()
        for row in range(0, ref.shape[0], group):
            at = slice(row, row + group)
            store(which, at, ref[at] if gain is None else normalize(ref[at], gain), kept)
        sent += send(which, outputs, kept)
    for copy in sent:
        copy.wait()


def pack(store, send, out_shape, rows, features, arrays, kept=()):
    q, k, v, q_gain, k_gain = arrays
    hbm = pl.BlockSpec(memory_space=pltpu.HBM)

    def kernel(*refs):
        pack_kernel(store, send, refs[:5], refs[5 : 5 + len(out_shape)], refs[5 + len(out_shape) :])

    return pl.pallas_call(
        kernel,
        in_specs=[hbm] * 5,
        out_specs=[hbm] * len(out_shape),
        out_shape=out_shape,
        scratch_shapes=[pltpu.VMEM((rows, features), BF16)] * 3
        + [pltpu.VMEM((1, features), jnp.float32)] * 2
        + [pltpu.SemaphoreType.DMA((5,)), *kept],
        compiler_params=PACK_PARAMS,
        name="pack",
    )(q, k, v, q_gain.reshape(1, -1), k_gain.reshape(1, -1))


def first_pass(query, key, bias_at, scores_ref, c, largest):
    s = lax.dot_general(key, query, (((1,), (1,)), ((), ())), preferred_element_type=jnp.float32)
    scores_ref[c] = s
    for t in range(key.shape[0] // TILE):
        tile = s[t * TILE : (t + 1) * TILE].reshape(TILE // 8, 8, -1)
        largest = jnp.maximum(largest, jnp.max(tile, axis=0) + bias_at(t))
    return largest


def second_pass(scores_ref, c, col_max, bias_at, value_t, state):
    total, mixed = state
    wide, bm = scores_ref.shape[1:]
    weights = []
    for t in range(wide // TILE):
        tile = scores_ref[c, t * TILE : (t + 1) * TILE].reshape(TILE // 8, 8, bm)
        tile = jnp.exp2(tile * SCALE - (col_max - bias_at(t))[None])
        total = total + jnp.sum(tile, axis=0)
        weights.append(tile.reshape(TILE, bm).astype(BF16))
    weights = jnp.concatenate(weights, axis=0)
    return total, mixed + jnp.dot(value_t, weights, preferred_element_type=jnp.float32)


def over_all(largest):
    return jnp.broadcast_to(jnp.max(largest, axis=0, keepdims=True) * SCALE, largest.shape)


def divide(total, mixed):
    return (mixed / jnp.sum(total, axis=0, keepdims=True)).T.astype(BF16)


def bias_of(band, bm, live_at):
    lane = lax.broadcasted_iota(jnp.int32, (8, bm), 1)
    bias = jnp.zeros((8, bm), jnp.float32)
    for a in range(bm // band):
        dead = jnp.where(live_at(a), 0.0, MASKED).astype(jnp.float32)
        bias = jnp.where((lane >= a * band) & (lane < (a + 1) * band), dead, bias)
    return bias


def attend(query, band, key_at, value_at, key_blocks, live_at, scores_ref):
    wide, bm = scores_ref.shape[1:]

    def bias_at(c):
        return lambda t: bias_of(band, bm, lambda a: live_at(a, c * (wide // TILE) + t))

    def score(c, largest):
        return first_pass(query, key_at(c), bias_at(c), scores_ref, c, largest)

    largest = lax.fori_loop(0, key_blocks, score, jnp.full((8, bm), MASKED, jnp.float32))
    col_max = over_all(largest)

    def mix(c, state):
        return second_pass(scores_ref, c, col_max, bias_at(c), transposed(value_at(c)), state)

    state = jnp.zeros((8, bm), jnp.float32), jnp.zeros((HDIM, bm), jnp.float32)
    return divide(*lax.fori_loop(0, key_blocks, mix, state))


def transposed(block):
    return block.astype(jnp.float32).T.astype(BF16)


def attend_blocks(blocks, band, query_at, key_at, value_t, key_blocks, live_at, finish, scores):
    wide, bm = scores[0].shape[1:]
    empty = jnp.full((8, bm), MASKED, jnp.float32)
    nothing = jnp.zeros((8, bm), jnp.float32), jnp.zeros((HDIM, bm), jnp.float32)

    def bias_at(i, c):
        return lambda t: bias_of(band, bm, lambda a: live_at(i, a, c, t))

    def both(i, col_max, now, following):
        later = jnp.minimum(i + 1, blocks - 1)
        query = query_at(later)
        largest, state = empty, nothing
        for c in range(key_blocks):
            largest = first_pass(query, key_at(c), bias_at(later, c), following, c, largest)
            state = second_pass(now, c, col_max, bias_at(i, c), value_t[:, c * wide : (c + 1) * wide], state)
        finish(i, divide(*state))
        return over_all(largest)

    largest = empty
    query = query_at(0)
    for c in range(key_blocks):
        largest = first_pass(query, key_at(c), bias_at(0, c), scores[0], c, largest)

    def pair(n, col_max):
        col_max = both(2 * n, col_max, scores[0], scores[1])
        return both(2 * n + 1, col_max, scores[1], scores[0])

    lax.fori_loop(0, blocks // 2, pair, over_all(largest))


def partner(me, step):
    first, second = step
    return me ^ jnp.where(lax.axis_index("batch") == 0, first, second)


def collect_kernel(steps, rows, *refs):
    pieces, (q_out, kv_out) = refs[:-2], refs[-2:]
    me = lax.axis_index(NEAR)
    for step, piece in zip(steps, pieces):
        at = pl.ds(pl.multiple_of(partner(me, step) * rows, rows), rows)
        q_out[at] = piece[0]
        kv_out[:, at] = piece[1:]


def shared_kernel(mask_ref, q_ref, own_ref, other_ref, out_ref, value_t, *scores):
    mine = lax.axis_index("inner")
    _, wide, bm = scores[0].shape
    blocks = q_ref.shape[0] // wide

    def key_at(c):
        ref = own_ref if c < blocks else other_ref
        return ref[0, c % blocks * wide : (c % blocks + 1) * wide]

    for n, ref in enumerate((own_ref, other_ref)):
        for t in range(blocks * wide // TILE):
            at = (n * blocks * wide) + t * TILE
            value_t[:, at : at + TILE] = transposed(ref[1, t * TILE : (t + 1) * TILE])

    def tile(block, inner, t):
        return (block * 2 + inner) * (wide // TILE) + t

    def finish(i, mixed):
        out_ref[pl.ds(pl.multiple_of(i * bm, bm), bm)] = mixed

    attend_blocks(
        blocks,
        TILE,
        lambda i: q_ref[pl.ds(pl.multiple_of(i * bm, bm), bm)],
        key_at,
        value_t,
        2 * blocks,
        lambda i, a, c, t: mask_ref[tile(i, mine, a), tile(c % blocks, mine if c < blocks else 1 - mine, t)] != 0,
        finish,
        scores,
    )


def whole_kernel(sources, mask_ref, qkv_ref, *refs):
    out_ref, value_t, *scores = refs[-4:]
    rows = qkv_ref.shape[2]
    _, wide, bm = scores[0].shape
    bands, tiles = bm // rows, wide // TILE
    for t in range(sources):
        value_t[:, t * TILE : (t + 1) * TILE] = transposed(qkv_ref[t, 2])

    def finish(i, mixed):
        out_ref[pl.ds(i * bands, bands)] = mixed.reshape(bands, rows, HDIM)

    attend_blocks(
        sources // bands,
        rows,
        lambda i: qkv_ref[pl.ds(i * bands, bands), 0].reshape(bm, HDIM),
        lambda c: qkv_ref[c * tiles : (c + 1) * tiles, 1].reshape(wide, HDIM),
        value_t,
        sources // tiles,
        lambda i, a, c, t: mask_ref[i * bands + a, c * tiles + t] != 0,
        finish,
        scores,
    )


def halved(far, near):
    steps = [(d, d) for d in (*range(near // 2, near), *range(near // 2))]

    def swap(piece, step):
        if step == (0, 0):
            return piece
        pairs = [(2 * i + b, 2 * (i ^ step[b]) + b) for i in range(near) for b in range(2)]
        return lax.ppermute(piece, (*NEAR, "batch"), pairs)

    def per_device(query_rows, key_rows, value_rows, q_gain, k_gain, tile_mask):
        rows, features = query_rows.shape

        def store(which, at, block, kept):
            near_heads, far_heads = kept[:2]
            for h in range(near):
                near_heads[h, which, at] = block[:, h * HDIM : (h + 1) * HDIM]
            for h in range(far):
                far_heads[h, which, at] = block[:, (near + h) * HDIM : (near + h + 1) * HDIM]

        def send(which, outs, kept):
            near_heads, far_heads, near_sems, far_sems = kept
            me = lax.axis_index(NEAR)
            copies = [
                pltpu.make_async_copy(near_heads.at[partner(me, step), which], outs[n].at[which], near_sems.at[which, n])
                for n, step in enumerate(steps)
            ]
            copies.append(pltpu.make_async_copy(far_heads.at[:, which], outs[-1].at[:, which], far_sems.at[which]))
            for copy in copies:
                copy.start()
            return copies

        def read(shared, whole, out_ref):
            for d in range(near):
                out_ref[:, d * HDIM : (d + 1) * HDIM] = shared[d]
            for d in range(far):
                out_ref[:, (near + d) * HDIM : (near + d + 1) * HDIM] = whole[d]

        *shared, whole = pack(
            store,
            send,
            [shape(3, rows, HDIM)] * near + [shape(far, 3, rows, HDIM)],
            rows,
            features,
            (query_rows, key_rows, value_rows, q_gain, k_gain),
            [
                pltpu.VMEM((near, 3, rows, HDIM), BF16),
                pltpu.VMEM((far, 3, rows, HDIM), BF16),
                pltpu.SemaphoreType.DMA((3, near)),
                pltpu.SemaphoreType.DMA((3,)),
            ],
        )
        shared = [swap(piece, step) for step, piece in zip(steps, shared)]
        whole = exchange(whole, FAR)
        q_near, kv_near = pl.pallas_call(
            functools.partial(collect_kernel, steps, rows),
            out_shape=[shape(near * rows, HDIM), shape(2, near * rows, HDIM)],
            compiler_params=PARAMS,
            name="collect",
        )(*shared)
        kv_other = lax.ppermute(kv_near, "inner", [(0, 1), (1, 0)])

        wide = 2 * TILE
        blocks = far * rows // wide
        smem, vmem = pl.BlockSpec(memory_space=pltpu.SMEM), pl.BlockSpec(memory_space=pltpu.VMEM)
        scratch = [pltpu.VMEM((HDIM, far * rows), BF16)]
        scores = [pltpu.VMEM((blocks, wide, wide), jnp.float32)] * 2
        shared = pl.pallas_call(
            shared_kernel,
            in_specs=[smem] + [vmem] * 3,
            out_shape=shape(near * rows, HDIM),
            scratch_shapes=scratch + scores,
            compiler_params=PARAMS,
            cost_estimate=pl.CostEstimate(flops=SHARED_COST, bytes_accessed=2**21, transcendentals=0),
            name="attend_shared",
        )(tile_mask, q_near, kv_near, kv_other)

        whole = pl.pallas_call(
            functools.partial(whole_kernel, far),
            in_specs=[smem, vmem, pl.BlockSpec(memory_space=pl.ANY)],
            out_shape=shape(far, rows, HDIM),
            scratch_shapes=scratch + [pltpu.VMEM((blocks // 2, 2 * wide, wide), jnp.float32)] * 2,
            compiler_params=PARAMS,
            cost_estimate=pl.CostEstimate(flops=2**33, bytes_accessed=2**22, transcendentals=0),
            name="attend_whole",
        )(tile_mask, whole, shared)
        shared = exchange(shared.reshape(near, rows, HDIM), NEAR)
        return pl.pallas_call(
            read, out_shape=shape(rows, features), compiler_params=PARAMS, name="unpack"
        )(shared, exchange(whole, FAR))

    return per_device


def gathered_kernel(outer, inner, mask_ref, q_ref, kv_ref, out_ref, scores_ref):
    i = pl.program_id(0)
    block = out_ref.shape[0] * out_ref.shape[1] * out_ref.shape[2]
    tiles = block // TILE
    q_tile = (i * inner + lax.axis_index("inner")) * tiles
    mixed = attend(
        q_ref[0, :, 0].reshape(block, HDIM),
        TILE,
        lambda c: kv_ref[lax.rem(c, inner), lax.div(c, inner), :, 1].reshape(block, HDIM),
        lambda c: kv_ref[lax.rem(c, inner), lax.div(c, inner), :, 2].reshape(block, HDIM),
        outer * inner,
        lambda a, t: mask_ref[q_tile + a, t] != 0,
        scores_ref,
    )
    out_ref[...] = mixed.reshape(out_ref.shape)


def gathered(outer, inner, n_head, near):
    width = HEADS // near * HDIM

    def per_device(query_rows, key_rows, value_rows, q_gain, k_gain, tile_mask):
        rows, features = query_rows.shape
        block = rows * n_head

        def store(which, at, block, kept):
            for d in range(near):
                kept[0][d, which, at] = block[:, d * width : (d + 1) * width]

        def send(which, outs, kept):
            packed, sems = kept
            copy = pltpu.make_async_copy(packed.at[:, which], outs[0].at[:, which], sems.at[which])
            copy.start()
            return [copy]

        def read(got_ref, out_ref):
            for d in range(near):
                out_ref[:, d * width : (d + 1) * width] = got_ref[d]

        (packed,) = pack(
            store,
            send,
            [shape(near, 3, rows, width)],
            rows,
            features,
            (query_rows, key_rows, value_rows, q_gain, k_gain),
            [pltpu.VMEM((near, 3, rows, width), BF16), pltpu.SemaphoreType.DMA((3,))],
        )
        own = exchange(packed, NEAR).reshape(outer, n_head, 3, rows, width)
        every = lax.all_gather(own, "inner")
        mixed = pl.pallas_call(
            functools.partial(gathered_kernel, outer, inner),
            grid=(outer, HEADS // near),
            in_specs=[
                pl.BlockSpec(memory_space=pltpu.SMEM),
                pl.BlockSpec((1, n_head, 1, rows, HDIM), lambda i, h: (i, 0, 0, 0, h)),
                pl.BlockSpec((inner, outer, n_head, 3, rows, HDIM), lambda i, h: (0, 0, 0, 0, 0, h)),
            ],
            out_specs=pl.BlockSpec((1, n_head, rows, HDIM), lambda i, h: (i, 0, 0, h)),
            out_shape=shape(outer, n_head, rows, width),
            scratch_shapes=[pltpu.VMEM((outer * inner, block, block), jnp.float32)],
            compiler_params=PARAMS,
            name="attend",
        )(tile_mask, own, every)
        return pl.pallas_call(
            read, out_shape=shape(rows, features), compiler_params=PARAMS, name="unpack"
        )(exchange(mixed.reshape(near, rows, width), NEAR))

    return per_device


def solution(mesh):
    n_blk, n_head = mesh.shape["blk"], mesh.shape["head"]
    outer = max(d for d in range(1, n_blk + 1) if n_blk % d == 0 and HEADS % (n_head * d) == 0)
    inner = n_blk // outer
    near, far = outer * n_head, n_blk * n_head

    def per_device(query_rows, *others):
        in_pairs = inner == 2 and n_head == 2 and mesh.shape["batch"] == 2 and near & (near - 1) == 0
        if in_pairs and HEADS == near + far and query_rows.shape[0] == TILE:
            return halved(far, near)(query_rows, *others)
        return gathered(outer, inner, n_head, near)(query_rows, *others)

    split = P(("batch", "outer", "inner", "head"), None)
    return jax.shard_map(
        per_device,
        mesh=Mesh(
            mesh.devices.reshape(outer, inner, n_head, mesh.shape["batch"]), ("outer", "inner", "head", "batch")
        ),
        in_specs=(split, split, split, P(), P(), P()),
        out_specs=split,
        check_vma=False,
    )
```

```python
import functools

import jax
import jax.numpy as jnp
from jax import lax
from jax.experimental import pallas as pl
from jax.experimental.pallas import tpu as pltpu
from jax.sharding import Mesh, PartitionSpec as P

HEADS = 24
HDIM = 128
TILE = 128
EPS = 1e-06
MASKED = -1e30
NEAR = ("outer_hi", "outer_lo", "head")
FAR = ("outer_hi", "inner", "outer_lo", "head")
PARAMS = pltpu.CompilerParams(vmem_limit_bytes=48 * 1024 * 1024)
PACK_PARAMS = pltpu.CompilerParams(vmem_limit_bytes=61 * 1024 * 1024)
BF16 = jnp.bfloat16
SHARED_COST = 24 * 2**30
SCALE = 1.4426950408889634 * HDIM ** (-0.5)


def shape(*dims):
    return jax.ShapeDtypeStruct(dims, BF16)


def exchange(x, axes):
    return lax.all_to_all(x, axes, split_axis=0, concat_axis=0, tiled=True)


def pack_kernel(store, send, inputs, outputs, scratch):
    q_hbm, k_hbm, v_hbm, qg_hbm, kg_hbm = inputs
    q_in, k_in, v_in, qg, kg, sems, *kept = scratch
    copies = [
        pltpu.make_async_copy(src, dst, sems.at[n])
        for n, (src, dst) in enumerate(
            ((v_hbm, v_in), (q_hbm, q_in), (qg_hbm, qg), (k_hbm, k_in), (kg_hbm, kg))
        )
    ]
    for copy in copies:
        copy.start()

    group = 16

    def normalize(block, gain):
        widened = block.astype(jnp.float32)
        mean_square = jnp.mean(widened * widened, axis=-1, keepdims=True)
        return (widened * lax.rsqrt(mean_square + EPS) * gain[...]).astype(BF16)

    sent = []
    for first, which, ref, gain in ((0, 2, v_in, None), (1, 0, q_in, qg), (3, 1, k_in, kg)):
        copies[first].wait()
        if gain is not None:
            copies[first + 1].wait()
        for row in range(0, ref.shape[0], group):
            at = slice(row, row + group)
            store(which, at, ref[at] if gain is None else normalize(ref[at], gain), kept)
        sent += send(which, outputs, kept)
    for copy in sent:
        copy.wait()


def pack(store, send, out_shape, rows, features, arrays, kept=()):
    q, k, v, q_gain, k_gain = arrays
    hbm = pl.BlockSpec(memory_space=pltpu.HBM)

    def kernel(*refs):
        pack_kernel(store, send, refs[:5], refs[5 : 5 + len(out_shape)], refs[5 + len(out_shape) :])

    return pl.pallas_call(
        kernel,
        in_specs=[hbm] * 5,
        out_specs=[hbm] * len(out_shape),
        out_shape=out_shape,
        scratch_shapes=[pltpu.VMEM((rows, features), BF16)] * 3
        + [pltpu.VMEM((1, features), jnp.float32)] * 2
        + [pltpu.SemaphoreType.DMA((5,)), *kept],
        compiler_params=PACK_PARAMS,
        name="pack",
    )(q, k, v, q_gain.reshape(1, -1), k_gain.reshape(1, -1))


def first_pass(query, key, bias_at, scores_ref, c, largest):
    s = lax.dot_general(key, query, (((1,), (1,)), ((), ())), preferred_element_type=jnp.float32)
    scores_ref[c] = s
    for t in range(key.shape[0] // TILE):
        tile = s[t * TILE : (t + 1) * TILE].reshape(TILE // 8, 8, -1)
        largest = jnp.maximum(largest, jnp.max(tile, axis=0) + bias_at(t))
    return largest


def second_pass(scores_ref, c, col_max, bias_at, value_t, state):
    total, mixed = state
    wide, bm = scores_ref.shape[1:]
    weights = []
    for t in range(wide // TILE):
        tile = scores_ref[c, t * TILE : (t + 1) * TILE].reshape(TILE // 8, 8, bm)
        tile = jnp.exp2(tile * SCALE - (col_max - bias_at(t))[None])
        total = total + jnp.sum(tile, axis=0)
        weights.append(tile.reshape(TILE, bm).astype(BF16))
    weights = jnp.concatenate(weights, axis=0)
    return total, mixed + jnp.dot(value_t, weights, preferred_element_type=jnp.float32)


def over_all(largest):
    return jnp.broadcast_to(jnp.max(largest, axis=0, keepdims=True) * SCALE, largest.shape)


def divide(total, mixed):
    return (mixed / jnp.sum(total, axis=0, keepdims=True)).T.astype(BF16)


def bias_of(band, bm, live_at):
    lane = lax.broadcasted_iota(jnp.int32, (8, bm), 1)
    bias = jnp.zeros((8, bm), jnp.float32)
    for a in range(bm // band):
        dead = jnp.where(live_at(a), 0.0, MASKED).astype(jnp.float32)
        bias = jnp.where((lane >= a * band) & (lane < (a + 1) * band), dead, bias)
    return bias


def attend(query, band, key_at, value_at, key_blocks, live_at, scores_ref):
    wide, bm = scores_ref.shape[1:]

    def bias_at(c):
        return lambda t: bias_of(band, bm, lambda a: live_at(a, c * (wide // TILE) + t))

    def score(c, largest):
        return first_pass(query, key_at(c), bias_at(c), scores_ref, c, largest)

    largest = lax.fori_loop(0, key_blocks, score, jnp.full((8, bm), MASKED, jnp.float32))
    col_max = over_all(largest)

    def mix(c, state):
        return second_pass(scores_ref, c, col_max, bias_at(c), transposed(value_at(c)), state)

    state = jnp.zeros((8, bm), jnp.float32), jnp.zeros((HDIM, bm), jnp.float32)
    return divide(*lax.fori_loop(0, key_blocks, mix, state))


def transposed(block):
    return block.astype(jnp.float32).T.astype(BF16)


def attend_blocks(blocks, band, query_at, key_at, value_t, key_blocks, live_at, finish, scores):
    wide, bm = scores[0].shape[1:]
    empty = jnp.full((8, bm), MASKED, jnp.float32)
    nothing = jnp.zeros((8, bm), jnp.float32), jnp.zeros((HDIM, bm), jnp.float32)

    def bias_at(i, c):
        return lambda t: bias_of(band, bm, lambda a: live_at(i, a, c, t))

    def both(i, col_max, now, following):
        later = jnp.minimum(i + 1, blocks - 1)
        query = query_at(later)
        largest, state = empty, nothing
        for c in range(key_blocks):
            largest = first_pass(query, key_at(c), bias_at(later, c), following, c, largest)
            state = second_pass(now, c, col_max, bias_at(i, c), value_t[:, c * wide : (c + 1) * wide], state)
        finish(i, divide(*state))
        return over_all(largest)

    largest = empty
    query = query_at(0)
    for c in range(key_blocks):
        largest = first_pass(query, key_at(c), bias_at(0, c), scores[0], c, largest)

    def pair(n, col_max):
        col_max = both(2 * n, col_max, scores[0], scores[1])
        return both(2 * n + 1, col_max, scores[1], scores[0])

    lax.fori_loop(0, blocks // 2, pair, over_all(largest))


def partner(me, step):
    first, second = step
    return me ^ jnp.where(lax.axis_index("batch") == 0, first, second)


def collect_kernel(steps, rows, *refs):
    pieces, (q_out, kv_out) = refs[:-2], refs[-2:]
    me = lax.axis_index(NEAR)
    for step, piece in zip(steps, pieces):
        at = pl.ds(pl.multiple_of(partner(me, step) * rows, rows), rows)
        q_out[at] = piece[0]
        kv_out[:, at] = piece[1:]


def shared_kernel(mask_ref, q_ref, own_ref, other_ref, out_ref, value_t, *scores):
    mine = lax.axis_index("inner")
    _, wide, bm = scores[0].shape
    blocks = q_ref.shape[0] // wide

    def key_at(c):
        ref = own_ref if c < blocks else other_ref
        return ref[0, c % blocks * wide : (c % blocks + 1) * wide]

    for n, ref in enumerate((own_ref, other_ref)):
        for t in range(blocks * wide // TILE):
            at = (n * blocks * wide) + t * TILE
            value_t[:, at : at + TILE] = transposed(ref[1, t * TILE : (t + 1) * TILE])

    def tile(block, inner, t):
        return ((block // 2 * 2 + inner) * 2 + block % 2) * (wide // TILE) + t

    def finish(i, mixed):
        out_ref[pl.ds(pl.multiple_of(i * bm, bm), bm)] = mixed

    attend_blocks(
        blocks,
        TILE,
        lambda i: q_ref[pl.ds(pl.multiple_of(i * bm, bm), bm)],
        key_at,
        value_t,
        2 * blocks,
        lambda i, a, c, t: mask_ref[tile(i, mine, a), tile(c % blocks, mine if c < blocks else 1 - mine, t)] != 0,
        finish,
        scores,
    )


def whole_kernel(sources, mask_ref, qkv_ref, *refs):
    out_ref, value_t, *scores = refs[-4:]
    rows = qkv_ref.shape[2]
    _, wide, bm = scores[0].shape
    bands, tiles = bm // rows, wide // TILE
    for t in range(sources):
        value_t[:, t * TILE : (t + 1) * TILE] = transposed(qkv_ref[t, 2])

    def finish(i, mixed):
        out_ref[pl.ds(i * bands, bands)] = mixed.reshape(bands, rows, HDIM)

    attend_blocks(
        sources // bands,
        rows,
        lambda i: qkv_ref[pl.ds(i * bands, bands), 0].reshape(bm, HDIM),
        lambda c: qkv_ref[c * tiles : (c + 1) * tiles, 1].reshape(wide, HDIM),
        value_t,
        sources // tiles,
        lambda i, a, c, t: mask_ref[i * bands + a, c * tiles + t] != 0,
        finish,
        scores,
    )


def halved(far, near):
    steps = []
    for d in range(near // 2):
        steps += [(near // 2 + d, d), (d, near // 2 + d)]

    def swap(piece, step):
        pairs = [(2 * i + b, 2 * (i ^ step[b]) + b) for i in range(near) for b in range(2)]
        return lax.ppermute(piece, (*NEAR, "batch"), pairs)

    def per_device(query_rows, key_rows, value_rows, q_gain, k_gain, tile_mask):
        rows, features = query_rows.shape

        def store(which, at, block, kept):
            near_heads, far_heads = kept[:2]
            for h in range(near):
                near_heads[h, which, at] = block[:, h * HDIM : (h + 1) * HDIM]
            for h in range(far):
                far_heads[h, which, at] = block[:, (near + h) * HDIM : (near + h + 1) * HDIM]

        def send(which, outs, kept):
            near_heads, far_heads, near_sems, far_sems = kept
            me = lax.axis_index(NEAR)
            copies = [
                pltpu.make_async_copy(near_heads.at[partner(me, step), which], outs[n].at[which], near_sems.at[which, n])
                for n, step in enumerate(steps)
            ]
            copies.append(pltpu.make_async_copy(far_heads.at[:, which], outs[-1].at[:, which], far_sems.at[which]))
            for copy in copies:
                copy.start()
            return copies

        def read(shared, whole, out_ref):
            for d in range(near):
                out_ref[:, d * HDIM : (d + 1) * HDIM] = shared[d]
            for d in range(far):
                out_ref[:, (near + d) * HDIM : (near + d + 1) * HDIM] = whole[d]

        *shared, whole = pack(
            store,
            send,
            [shape(3, rows, HDIM)] * near + [shape(far, 3, rows, HDIM)],
            rows,
            features,
            (query_rows, key_rows, value_rows, q_gain, k_gain),
            [
                pltpu.VMEM((near, 3, rows, HDIM), BF16),
                pltpu.VMEM((far, 3, rows, HDIM), BF16),
                pltpu.SemaphoreType.DMA((3, near)),
                pltpu.SemaphoreType.DMA((3,)),
            ],
        )
        shared = [swap(piece, step) for step, piece in zip(steps, shared)]
        whole = exchange(whole, FAR)
        q_near, kv_near = pl.pallas_call(
            functools.partial(collect_kernel, steps, rows),
            out_shape=[shape(near * rows, HDIM), shape(2, near * rows, HDIM)],
            compiler_params=PARAMS,
            name="collect",
        )(*shared)
        kv_other = lax.ppermute(kv_near, "inner", [(0, 1), (1, 0)])

        wide = 2 * TILE
        blocks = far * rows // wide
        smem, vmem = pl.BlockSpec(memory_space=pltpu.SMEM), pl.BlockSpec(memory_space=pltpu.VMEM)
        scratch = [pltpu.VMEM((HDIM, far * rows), BF16)]
        scores = [pltpu.VMEM((blocks, wide, wide), jnp.float32)] * 2
        shared = pl.pallas_call(
            shared_kernel,
            in_specs=[smem] + [vmem] * 3,
            out_shape=shape(near * rows, HDIM),
            scratch_shapes=scratch + scores,
            compiler_params=PARAMS,
            cost_estimate=pl.CostEstimate(flops=SHARED_COST, bytes_accessed=2**21, transcendentals=0),
            name="attend_shared",
        )(tile_mask, q_near, kv_near, kv_other)

        whole = pl.pallas_call(
            functools.partial(whole_kernel, far),
            in_specs=[smem, vmem, pl.BlockSpec(memory_space=pl.ANY)],
            out_shape=shape(far, rows, HDIM),
            scratch_shapes=scratch + [pltpu.VMEM((blocks // 2, 2 * wide, wide), jnp.float32)] * 2,
            compiler_params=PARAMS,
            cost_estimate=pl.CostEstimate(flops=2**33, bytes_accessed=2**22, transcendentals=0),
            name="attend_whole",
        )(tile_mask, whole, shared)
        shared = exchange(shared.reshape(near, rows, HDIM), NEAR)
        return pl.pallas_call(
            read, out_shape=shape(rows, features), compiler_params=PARAMS, name="unpack"
        )(shared, exchange(whole, FAR))

    return per_device


def gathered_kernel(outer, inner, mask_ref, q_ref, kv_ref, out_ref, scores_ref):
    i = pl.program_id(0)
    block = out_ref.shape[0] * out_ref.shape[1] * out_ref.shape[2]
    tiles = block // TILE
    q_tile = (i * inner + lax.axis_index("inner")) * tiles
    mixed = attend(
        q_ref[0, :, 0].reshape(block, HDIM),
        TILE,
        lambda c: kv_ref[lax.rem(c, inner), lax.div(c, inner), :, 1].reshape(block, HDIM),
        lambda c: kv_ref[lax.rem(c, inner), lax.div(c, inner), :, 2].reshape(block, HDIM),
        outer * inner,
        lambda a, t: mask_ref[q_tile + a, t] != 0,
        scores_ref,
    )
    out_ref[...] = mixed.reshape(out_ref.shape)


def gathered(outer, inner, n_head, near):
    width = HEADS // near * HDIM

    def per_device(query_rows, key_rows, value_rows, q_gain, k_gain, tile_mask):
        rows, features = query_rows.shape
        block = rows * n_head

        def store(which, at, block, kept):
            for d in range(near):
                kept[0][d, which, at] = block[:, d * width : (d + 1) * width]

        def send(which, outs, kept):
            packed, sems = kept
            copy = pltpu.make_async_copy(packed.at[:, which], outs[0].at[:, which], sems.at[which])
            copy.start()
            return [copy]

        def read(got_ref, out_ref):
            for d in range(near):
                out_ref[:, d * width : (d + 1) * width] = got_ref[d]

        (packed,) = pack(
            store,
            send,
            [shape(near, 3, rows, width)],
            rows,
            features,
            (query_rows, key_rows, value_rows, q_gain, k_gain),
            [pltpu.VMEM((near, 3, rows, width), BF16), pltpu.SemaphoreType.DMA((3,))],
        )
        own = exchange(packed, ("outer", "head")).reshape(outer, n_head, 3, rows, width)
        every = lax.all_gather(own, "inner")
        mixed = pl.pallas_call(
            functools.partial(gathered_kernel, outer, inner),
            grid=(outer, HEADS // near),
            in_specs=[
                pl.BlockSpec(memory_space=pltpu.SMEM),
                pl.BlockSpec((1, n_head, 1, rows, HDIM), lambda i, h: (i, 0, 0, 0, h)),
                pl.BlockSpec((inner, outer, n_head, 3, rows, HDIM), lambda i, h: (0, 0, 0, 0, 0, h)),
            ],
            out_specs=pl.BlockSpec((1, n_head, rows, HDIM), lambda i, h: (i, 0, 0, h)),
            out_shape=shape(outer, n_head, rows, width),
            scratch_shapes=[pltpu.VMEM((outer * inner, block, block), jnp.float32)],
            compiler_params=PARAMS,
            name="attend",
        )(tile_mask, own, every)
        return pl.pallas_call(
            read, out_shape=shape(rows, features), compiler_params=PARAMS, name="unpack"
        )(exchange(mixed.reshape(near, rows, width), ("outer", "head")))

    return per_device


def solution(mesh):
    n_blk, n_head = mesh.shape["blk"], mesh.shape["head"]
    outer = max(d for d in range(1, n_blk + 1) if n_blk % d == 0 and HEADS % (n_head * d) == 0)
    inner = n_blk // outer
    near, far = outer * n_head, n_blk * n_head

    in_pairs = inner == 2 and outer == 4 and n_head == 2 and mesh.shape["batch"] == 2 and HEADS == near + far
    if in_pairs:
        per_device, sizes, names = halved(far, near), (2, inner, 2, n_head), FAR
    else:
        per_device, sizes, names = gathered(outer, inner, n_head, near), (outer, inner, n_head), ("outer", "inner", "head")
    split = P(("batch", *names), None)
    return jax.shard_map(
        per_device,
        mesh=Mesh(mesh.devices.reshape(*sizes, mesh.shape["batch"]), (*names, "batch")),
        in_specs=(split, split, split, P(), P(), P()),
        out_specs=split,
        check_vma=False,
    )
```

```python
import functools

import jax
import jax.numpy as jnp
from jax import lax
from jax.experimental import pallas as pl
from jax.experimental.pallas import tpu as pltpu
from jax.sharding import Mesh, PartitionSpec as P

HEADS = 24
HDIM = 128
TILE = 128
EPS = 1e-06
MASKED = -1e30
NEAR = ("outer", "head")
FAR = ("outer", "inner", "head")
PARAMS = pltpu.CompilerParams(vmem_limit_bytes=48 * 1024 * 1024)
PACK_PARAMS = pltpu.CompilerParams(vmem_limit_bytes=61 * 1024 * 1024)
BF16 = jnp.bfloat16
SHARED_COST = 25 * 2**30
SCALE = 1.4426950408889634 * HDIM ** (-0.5)


def shape(*dims):
    return jax.ShapeDtypeStruct(dims, BF16)


def exchange(x, axes):
    return lax.all_to_all(x, axes, split_axis=0, concat_axis=0, tiled=True)


def pack_kernel(store, send, inputs, outputs, scratch):
    q_hbm, k_hbm, v_hbm, qg_hbm, kg_hbm = inputs
    q_in, k_in, v_in, qg, kg, sems, *kept = scratch
    copies = [
        pltpu.make_async_copy(src, dst, sems.at[n])
        for n, (src, dst) in enumerate(
            ((v_hbm, v_in), (q_hbm, q_in), (qg_hbm, qg), (k_hbm, k_in), (kg_hbm, kg))
        )
    ]
    for copy in copies:
        copy.start()

    group = 16

    def normalize(block, gain):
        widened = block.astype(jnp.float32)
        mean_square = jnp.mean(widened * widened, axis=-1, keepdims=True)
        return (widened * lax.rsqrt(mean_square + EPS) * gain[...]).astype(BF16)

    sent = []
    for first, which, ref, gain in ((0, 2, v_in, None), (1, 0, q_in, qg), (3, 1, k_in, kg)):
        copies[first].wait()
        if gain is not None:
            copies[first + 1].wait()
        for row in range(0, ref.shape[0], group):
            at = slice(row, row + group)
            store(which, at, ref[at] if gain is None else normalize(ref[at], gain), kept)
        sent += send(which, outputs, kept)
    for copy in sent:
        copy.wait()


def pack(store, send, out_shape, rows, features, arrays, kept=()):
    q, k, v, q_gain, k_gain = arrays
    hbm = pl.BlockSpec(memory_space=pltpu.HBM)

    def kernel(*refs):
        pack_kernel(store, send, refs[:5], refs[5 : 5 + len(out_shape)], refs[5 + len(out_shape) :])

    return pl.pallas_call(
        kernel,
        in_specs=[hbm] * 5,
        out_specs=[hbm] * len(out_shape),
        out_shape=out_shape,
        scratch_shapes=[pltpu.VMEM((rows, features), BF16)] * 3
        + [pltpu.VMEM((1, features), jnp.float32)] * 2
        + [pltpu.SemaphoreType.DMA((5,)), *kept],
        compiler_params=PACK_PARAMS,
        name="pack",
    )(q, k, v, q_gain.reshape(1, -1), k_gain.reshape(1, -1))


def first_pass(query, key, bias_at, scores_ref, c, largest):
    s = lax.dot_general(key, query, (((1,), (1,)), ((), ())), preferred_element_type=jnp.float32)
    scores_ref[c] = s
    for t in range(key.shape[0] // TILE):
        tile = s[t * TILE : (t + 1) * TILE].reshape(TILE // 8, 8, -1)
        largest = jnp.maximum(largest, jnp.max(tile, axis=0) + bias_at(t))
    return largest


def second_pass(scores_ref, c, col_max, bias_at, value_t, state):
    total, mixed = state
    wide, bm = scores_ref.shape[1:]
    weights = []
    for t in range(wide // TILE):
        tile = scores_ref[c, t * TILE : (t + 1) * TILE].reshape(TILE // 8, 8, bm)
        tile = jnp.exp2(tile * SCALE - (col_max - bias_at(t))[None])
        total = total + jnp.sum(tile, axis=0)
        weights.append(tile.reshape(TILE, bm).astype(BF16))
    weights = jnp.concatenate(weights, axis=0)
    return total, mixed + jnp.dot(value_t, weights, preferred_element_type=jnp.float32)


def over_all(largest):
    return jnp.broadcast_to(jnp.max(largest, axis=0, keepdims=True) * SCALE, largest.shape)


def divide(total, mixed):
    return (mixed / jnp.sum(total, axis=0, keepdims=True)).T.astype(BF16)


def bias_of(band, bm, live_at):
    lane = lax.broadcasted_iota(jnp.int32, (8, bm), 1)
    bias = jnp.zeros((8, bm), jnp.float32)
    for a in range(bm // band):
        dead = jnp.where(live_at(a), 0.0, MASKED).astype(jnp.float32)
        bias = jnp.where((lane >= a * band) & (lane < (a + 1) * band), dead, bias)
    return bias


def attend(query, band, key_at, value_at, key_blocks, live_at, scores_ref):
    wide, bm = scores_ref.shape[1:]

    def bias_at(c):
        return lambda t: bias_of(band, bm, lambda a: live_at(a, c * (wide // TILE) + t))

    def score(c, largest):
        return first_pass(query, key_at(c), bias_at(c), scores_ref, c, largest)

    largest = lax.fori_loop(0, key_blocks, score, jnp.full((8, bm), MASKED, jnp.float32))
    col_max = over_all(largest)

    def mix(c, state):
        return second_pass(scores_ref, c, col_max, bias_at(c), transposed(value_at(c)), state)

    state = jnp.zeros((8, bm), jnp.float32), jnp.zeros((HDIM, bm), jnp.float32)
    return divide(*lax.fori_loop(0, key_blocks, mix, state))


def transposed(block):
    return block.astype(jnp.float32).T.astype(BF16)


def attend_blocks(blocks, band, query_at, key_at, value_t, key_blocks, live_at, finish, scores):
    wide, bm = scores[0].shape[1:]
    empty = jnp.full((8, bm), MASKED, jnp.float32)
    nothing = jnp.zeros((8, bm), jnp.float32), jnp.zeros((HDIM, bm), jnp.float32)

    def bias_at(i, c):
        return lambda t: bias_of(band, bm, lambda a: live_at(i, a, c, t))

    def both(i, col_max, now, following):
        later = jnp.minimum(i + 1, blocks - 1)
        query = query_at(later)
        largest, state = empty, nothing
        for c in range(key_blocks):
            largest = first_pass(query, key_at(c), bias_at(later, c), following, c, largest)
            state = second_pass(now, c, col_max, bias_at(i, c), value_t[:, c * wide : (c + 1) * wide], state)
        finish(i, divide(*state))
        return over_all(largest)

    largest = empty
    query = query_at(0)
    for c in range(key_blocks):
        largest = first_pass(query, key_at(c), bias_at(0, c), scores[0], c, largest)

    def pair(n, col_max):
        col_max = both(2 * n, col_max, scores[0], scores[1])
        return both(2 * n + 1, col_max, scores[1], scores[0])

    lax.fori_loop(0, blocks // 2, pair, over_all(largest))


def partner(me, step):
    first, second = step
    return me ^ jnp.where(lax.axis_index("batch") == 0, first, second)


def rows_in_part(step, n_head, rows):
    d = partner(0, step)
    slot = lax.div(d, 2 * n_head) * n_head + partner(lax.axis_index("head"), tuple(e % n_head for e in step))
    return pl.ds(pl.multiple_of(slot * rows, rows), rows)


def collect_kernel(steps, n_head, rows, *refs):
    pieces, (q_out, kv_out) = refs[: len(steps)], refs[-2:]
    for step, piece in zip(steps, pieces):
        at = rows_in_part(step, n_head, rows)
        q_out[at] = piece[0]
        kv_out[:, at] = piece[1:]


def shared_kernel(mask_ref, *refs):
    q_refs, kv_refs, (out_ref, query, value_t, *scores) = refs[:2], refs[2:6], refs[6:]
    mine, outer = lax.axis_index("inner"), lax.axis_index("outer")
    _, wide, bm = scores[0].shape
    part = q_refs[0].shape[0] // wide
    blocks = 2 * part

    for n, ref in enumerate(q_refs):
        query[n * part * wide : (n + 1) * part * wide] = ref[...]
    for n, ref in enumerate(kv_refs):
        for t in range(part * wide // TILE):
            at = n * part * wide + t * TILE
            value_t[:, at : at + TILE] = transposed(ref[1, t * TILE : (t + 1) * TILE])

    def outer_of(i):
        return outer ^ (lax.rem(i, part) * 2 + lax.div(i, part))

    def tile(block, inner, t):
        return (block * 2 + inner) * (wide // TILE) + t

    def finish(i, mixed):
        out_ref[pl.ds(pl.multiple_of(outer_of(i) * bm, bm), bm)] = mixed

    attend_blocks(
        blocks,
        TILE,
        lambda i: query[pl.ds(pl.multiple_of(i * bm, bm), bm)],
        lambda c: kv_refs[c // part][0, c % part * wide : (c % part + 1) * wide],
        value_t,
        2 * blocks,
        lambda i, a, c, t: mask_ref[
            tile(outer_of(i), mine, a), tile(outer_of(c % blocks), mine if c < blocks else 1 - mine, t)
        ]
        != 0,
        finish,
        scores,
    )


def whole_kernel(sources, mask_ref, qkv_ref, *refs):
    out_ref, value_t, *scores = refs[-4:]
    rows = qkv_ref.shape[2]
    _, wide, bm = scores[0].shape
    bands, tiles = bm // rows, wide // TILE
    for t in range(sources):
        value_t[:, t * TILE : (t + 1) * TILE] = transposed(qkv_ref[t, 2])

    def finish(i, mixed):
        out_ref[pl.ds(i * bands, bands)] = mixed.reshape(bands, rows, HDIM)

    attend_blocks(
        sources // bands,
        rows,
        lambda i: qkv_ref[pl.ds(i * bands, bands), 0].reshape(bm, HDIM),
        lambda c: qkv_ref[c * tiles : (c + 1) * tiles, 1].reshape(wide, HDIM),
        value_t,
        sources // tiles,
        lambda i, a, c, t: mask_ref[i * bands + a, c * tiles + t] != 0,
        finish,
        scores,
    )


def halved(n_head, far, near):
    steps = []
    for d in range(near // 2):
        steps += [(near // 2 + d, d), (d, near // 2 + d)]

    def swap(piece, step):
        pairs = [(2 * i + b, 2 * (i ^ step[b]) + b) for i in range(near) for b in range(2)]
        return lax.ppermute(piece, (*NEAR, "batch"), pairs)

    def per_device(query_rows, key_rows, value_rows, q_gain, k_gain, tile_mask):
        rows, features = query_rows.shape

        def store(which, at, block, kept):
            near_heads, far_heads = kept[:2]
            for h in range(near):
                near_heads[h, which, at] = block[:, h * HDIM : (h + 1) * HDIM]
            for h in range(far):
                far_heads[h, which, at] = block[:, (near + h) * HDIM : (near + h + 1) * HDIM]

        def send(which, outs, kept):
            near_heads, far_heads, near_sems, far_sems = kept
            me = lax.axis_index(NEAR)
            copies = [
                pltpu.make_async_copy(near_heads.at[partner(me, step), which], outs[n].at[which], near_sems.at[which, n])
                for n, step in enumerate(steps)
            ]
            copies.append(pltpu.make_async_copy(far_heads.at[:, which], outs[-1].at[:, which], far_sems.at[which]))
            for copy in copies:
                copy.start()
            return copies

        def read(shared, whole, out_ref):
            for d in range(near):
                out_ref[:, d * HDIM : (d + 1) * HDIM] = shared[d]
            for d in range(far):
                out_ref[:, (near + d) * HDIM : (near + d + 1) * HDIM] = whole[d]

        *shared, whole = pack(
            store,
            send,
            [shape(3, rows, HDIM)] * near + [shape(far, 3, rows, HDIM)],
            rows,
            features,
            (query_rows, key_rows, value_rows, q_gain, k_gain),
            [
                pltpu.VMEM((near, 3, rows, HDIM), BF16),
                pltpu.VMEM((far, 3, rows, HDIM), BF16),
                pltpu.SemaphoreType.DMA((3, near)),
                pltpu.SemaphoreType.DMA((3,)),
            ],
        )
        shared = [swap(piece, step) for step, piece in zip(steps, shared)]
        whole = exchange(whole, FAR)
        queries, own, other = [], [], []
        part = near // 2
        for n in range(2):
            q_near, kv_near = pl.pallas_call(
                functools.partial(collect_kernel, steps[n * part : (n + 1) * part], n_head, rows),
                in_specs=[pl.BlockSpec(memory_space=pltpu.VMEM)] * part + [pl.BlockSpec(memory_space=pl.ANY)] * n,
                out_shape=[shape(part * rows, HDIM), shape(2, part * rows, HDIM)],
                compiler_params=PARAMS,
                name="collect",
            )(*shared[n * part : (n + 1) * part], *other)
            queries.append(q_near)
            own.append(kv_near)
            other.append(lax.ppermute(kv_near, "inner", [(0, 1), (1, 0)]))

        wide = 2 * TILE
        blocks = far * rows // wide
        smem, vmem = pl.BlockSpec(memory_space=pltpu.SMEM), pl.BlockSpec(memory_space=pltpu.VMEM)
        scratch = [pltpu.VMEM((HDIM, far * rows), BF16)]
        scores = [pltpu.VMEM((blocks, wide, wide), jnp.float32)] * 2
        shared = pl.pallas_call(
            shared_kernel,
            in_specs=[smem] + [vmem] * 6,
            out_shape=shape(near * rows, HDIM),
            scratch_shapes=[pltpu.VMEM((near * rows, HDIM), BF16)] + scratch + scores,
            compiler_params=PARAMS,
            cost_estimate=pl.CostEstimate(flops=SHARED_COST, bytes_accessed=2**21, transcendentals=0),
            name="attend_shared",
        )(tile_mask, *queries, *own, *other)

        whole = pl.pallas_call(
            functools.partial(whole_kernel, far),
            in_specs=[smem, vmem, pl.BlockSpec(memory_space=pl.ANY)],
            out_shape=shape(far, rows, HDIM),
            scratch_shapes=scratch + [pltpu.VMEM((blocks // 2, 2 * wide, wide), jnp.float32)] * 2,
            compiler_params=PARAMS,
            cost_estimate=pl.CostEstimate(flops=2**33, bytes_accessed=2**22, transcendentals=0),
            name="attend_whole",
        )(tile_mask, whole, shared)
        shared = exchange(shared.reshape(near, rows, HDIM), NEAR)
        return pl.pallas_call(
            read, out_shape=shape(rows, features), compiler_params=PARAMS, name="unpack"
        )(shared, exchange(whole, FAR))

    return per_device


def gathered_kernel(outer, inner, mask_ref, q_ref, kv_ref, out_ref, scores_ref):
    i = pl.program_id(0)
    block = out_ref.shape[0] * out_ref.shape[1] * out_ref.shape[2]
    tiles = block // TILE
    q_tile = (i * inner + lax.axis_index("inner")) * tiles
    mixed = attend(
        q_ref[0, :, 0].reshape(block, HDIM),
        TILE,
        lambda c: kv_ref[lax.rem(c, inner), lax.div(c, inner), :, 1].reshape(block, HDIM),
        lambda c: kv_ref[lax.rem(c, inner), lax.div(c, inner), :, 2].reshape(block, HDIM),
        outer * inner,
        lambda a, t: mask_ref[q_tile + a, t] != 0,
        scores_ref,
    )
    out_ref[...] = mixed.reshape(out_ref.shape)


def gathered(outer, inner, n_head, near):
    width = HEADS // near * HDIM

    def per_device(query_rows, key_rows, value_rows, q_gain, k_gain, tile_mask):
        rows, features = query_rows.shape
        block = rows * n_head

        def store(which, at, block, kept):
            for d in range(near):
                kept[0][d, which, at] = block[:, d * width : (d + 1) * width]

        def send(which, outs, kept):
            packed, sems = kept
            copy = pltpu.make_async_copy(packed.at[:, which], outs[0].at[:, which], sems.at[which])
            copy.start()
            return [copy]

        def read(got_ref, out_ref):
            for d in range(near):
                out_ref[:, d * width : (d + 1) * width] = got_ref[d]

        (packed,) = pack(
            store,
            send,
            [shape(near, 3, rows, width)],
            rows,
            features,
            (query_rows, key_rows, value_rows, q_gain, k_gain),
            [pltpu.VMEM((near, 3, rows, width), BF16), pltpu.SemaphoreType.DMA((3,))],
        )
        own = exchange(packed, NEAR).reshape(outer, n_head, 3, rows, width)
        every = lax.all_gather(own, "inner")
        mixed = pl.pallas_call(
            functools.partial(gathered_kernel, outer, inner),
            grid=(outer, HEADS // near),
            in_specs=[
                pl.BlockSpec(memory_space=pltpu.SMEM),
                pl.BlockSpec((1, n_head, 1, rows, HDIM), lambda i, h: (i, 0, 0, 0, h)),
                pl.BlockSpec((inner, outer, n_head, 3, rows, HDIM), lambda i, h: (0, 0, 0, 0, 0, h)),
            ],
            out_specs=pl.BlockSpec((1, n_head, rows, HDIM), lambda i, h: (i, 0, 0, h)),
            out_shape=shape(outer, n_head, rows, width),
            scratch_shapes=[pltpu.VMEM((outer * inner, block, block), jnp.float32)],
            compiler_params=PARAMS,
            name="attend",
        )(tile_mask, own, every)
        return pl.pallas_call(
            read, out_shape=shape(rows, features), compiler_params=PARAMS, name="unpack"
        )(exchange(mixed.reshape(near, rows, width), NEAR))

    return per_device


def solution(mesh):
    n_blk, n_head = mesh.shape["blk"], mesh.shape["head"]
    outer = max(d for d in range(1, n_blk + 1) if n_blk % d == 0 and HEADS % (n_head * d) == 0)
    inner = n_blk // outer
    near, far = outer * n_head, n_blk * n_head

    def per_device(query_rows, *others):
        in_pairs = inner == 2 and n_head == 2 and mesh.shape["batch"] == 2 and near == 8
        if in_pairs and HEADS == near + far and query_rows.shape[0] == TILE:
            return halved(n_head, far, near)(query_rows, *others)
        return gathered(outer, inner, n_head, near)(query_rows, *others)

    split = P(("batch", "outer", "inner", "head"), None)
    return jax.shard_map(
        per_device,
        mesh=Mesh(
            mesh.devices.reshape(outer, inner, n_head, mesh.shape["batch"]), ("outer", "inner", "head", "batch")
        ),
        in_specs=(split, split, split, P(), P(), P()),
        out_specs=split,
        check_vma=False,
    )
```

```python
import functools

import jax
import jax.numpy as jnp
from jax import lax
from jax.experimental import pallas as pl
from jax.experimental.pallas import tpu as pltpu
from jax.sharding import Mesh, PartitionSpec as P

HEADS = 24
HDIM = 128
TILE = 128
EPS = 1e-06
MASKED = -1e30
NEAR = ("outer", "head")
FAR = ("outer", "inner", "head")
PARAMS = pltpu.CompilerParams(vmem_limit_bytes=48 * 1024 * 1024)
PACK_PARAMS = pltpu.CompilerParams(vmem_limit_bytes=61 * 1024 * 1024)
BF16 = jnp.bfloat16
SHARED_COST = 24 * 2**30
SCALE = 1.4426950408889634 * HDIM ** (-0.5)


def shape(*dims):
    return jax.ShapeDtypeStruct(dims, BF16)


def exchange(x, axes):
    return lax.all_to_all(x, axes, split_axis=0, concat_axis=0, tiled=True)


def pack_kernel(store, send, inputs, outputs, scratch):
    q_hbm, k_hbm, v_hbm, qg_hbm, kg_hbm = inputs
    q_in, k_in, v_in, qg, kg, sems, *kept = scratch
    copies = [
        pltpu.make_async_copy(src, dst, sems.at[n])
        for n, (src, dst) in enumerate(
            ((v_hbm, v_in), (q_hbm, q_in), (qg_hbm, qg), (k_hbm, k_in), (kg_hbm, kg))
        )
    ]
    for copy in copies:
        copy.start()

    group = 16

    def normalize(block, gain):
        widened = block.astype(jnp.float32)
        mean_square = jnp.mean(widened * widened, axis=-1, keepdims=True)
        return (widened * lax.rsqrt(mean_square + EPS) * gain[...]).astype(BF16)

    sent = []
    for first, which, ref, gain in ((0, 2, v_in, None), (1, 0, q_in, qg), (3, 1, k_in, kg)):
        copies[first].wait()
        if gain is not None:
            copies[first + 1].wait()
        for row in range(0, ref.shape[0], group):
            at = slice(row, row + group)
            store(which, at, ref[at] if gain is None else normalize(ref[at], gain), kept)
        sent += send(which, outputs, kept)
    for copy in sent:
        copy.wait()


def pack(store, send, out_shape, rows, features, arrays, kept=()):
    q, k, v, q_gain, k_gain = arrays
    hbm = pl.BlockSpec(memory_space=pltpu.HBM)

    def kernel(*refs):
        pack_kernel(store, send, refs[:5], refs[5 : 5 + len(out_shape)], refs[5 + len(out_shape) :])

    return pl.pallas_call(
        kernel,
        in_specs=[hbm] * 5,
        out_specs=[hbm] * len(out_shape),
        out_shape=out_shape,
        scratch_shapes=[pltpu.VMEM((rows, features), BF16)] * 3
        + [pltpu.VMEM((1, features), jnp.float32)] * 2
        + [pltpu.SemaphoreType.DMA((5,)), *kept],
        compiler_params=PACK_PARAMS,
        name="pack",
    )(q, k, v, q_gain.reshape(1, -1), k_gain.reshape(1, -1))


def first_pass(query, key, bias_at, scores_ref, c, largest):
    s = lax.dot_general(key, query, (((1,), (1,)), ((), ())), preferred_element_type=jnp.float32)
    scores_ref[c] = s
    for t in range(key.shape[0] // TILE):
        tile = s[t * TILE : (t + 1) * TILE].reshape(TILE // 8, 8, -1)
        largest = jnp.maximum(largest, jnp.max(tile, axis=0) + bias_at(t))
    return largest


def second_pass(scores_ref, c, col_max, bias_at, value_t, state):
    total, mixed = state
    wide, bm = scores_ref.shape[1:]
    weights = []
    for t in range(wide // TILE):
        tile = scores_ref[c, t * TILE : (t + 1) * TILE].reshape(TILE // 8, 8, bm)
        tile = jnp.exp2(tile * SCALE - (col_max - bias_at(t))[None])
        total = total + jnp.sum(tile, axis=0)
        weights.append(tile.reshape(TILE, bm).astype(BF16))
    weights = jnp.concatenate(weights, axis=0)
    return total, mixed + jnp.dot(value_t, weights, preferred_element_type=jnp.float32)


def over_all(largest):
    return jnp.broadcast_to(jnp.max(largest, axis=0, keepdims=True) * SCALE, largest.shape)


def divide(total, mixed):
    return (mixed / jnp.sum(total, axis=0, keepdims=True)).T.astype(BF16)


def bias_of(band, bm, live_at):
    lane = lax.broadcasted_iota(jnp.int32, (8, bm), 1)
    bias = jnp.zeros((8, bm), jnp.float32)
    for a in range(bm // band):
        dead = jnp.where(live_at(a), 0.0, MASKED).astype(jnp.float32)
        bias = jnp.where((lane >= a * band) & (lane < (a + 1) * band), dead, bias)
    return bias


def attend(query, band, key_at, value_at, key_blocks, live_at, scores_ref):
    wide, bm = scores_ref.shape[1:]

    def bias_at(c):
        return lambda t: bias_of(band, bm, lambda a: live_at(a, c * (wide // TILE) + t))

    def score(c, largest):
        return first_pass(query, key_at(c), bias_at(c), scores_ref, c, largest)

    largest = lax.fori_loop(0, key_blocks, score, jnp.full((8, bm), MASKED, jnp.float32))
    col_max = over_all(largest)

    def mix(c, state):
        return second_pass(scores_ref, c, col_max, bias_at(c), transposed(value_at(c)), state)

    state = jnp.zeros((8, bm), jnp.float32), jnp.zeros((HDIM, bm), jnp.float32)
    return divide(*lax.fori_loop(0, key_blocks, mix, state))


def transposed(block):
    return block.astype(jnp.float32).T.astype(BF16)


def attend_blocks(blocks, band, query_at, key_at, value_t, key_blocks, live_at, finish, scores):
    wide, bm = scores[0].shape[1:]
    empty = jnp.full((8, bm), MASKED, jnp.float32)
    nothing = jnp.zeros((8, bm), jnp.float32), jnp.zeros((HDIM, bm), jnp.float32)

    def bias_at(i, c):
        return lambda t: bias_of(band, bm, lambda a: live_at(i, a, c, t))

    def both(i, col_max, now, following):
        later = jnp.minimum(i + 1, blocks - 1)
        query = query_at(later)
        largest, state = empty, nothing
        for c in range(key_blocks):
            largest = first_pass(query, key_at(c), bias_at(later, c), following, c, largest)
            state = second_pass(now, c, col_max, bias_at(i, c), value_t[:, c * wide : (c + 1) * wide], state)
        finish(i, divide(*state))
        return over_all(largest)

    largest = empty
    query = query_at(0)
    for c in range(key_blocks):
        largest = first_pass(query, key_at(c), bias_at(0, c), scores[0], c, largest)

    def pair(n, col_max):
        col_max = both(2 * n, col_max, scores[0], scores[1])
        return both(2 * n + 1, col_max, scores[1], scores[0])

    lax.fori_loop(0, blocks // 2, pair, over_all(largest))


def partner(me, step):
    first, second = step
    return me ^ jnp.where(lax.axis_index("batch") == 0, first, second)


def collect_kernel(steps, rows, *refs):
    pieces, (q_out, kv_out) = refs[:-2], refs[-2:]
    me = lax.axis_index(NEAR)
    for step, piece in zip(steps, pieces):
        at = pl.ds(pl.multiple_of(partner(me, step) * rows, rows), rows)
        q_out[at] = piece[0]
        kv_out[:, at] = piece[1:]


def shared_kernel(mask_ref, q_ref, own_ref, other_ref, out_ref, value_t, *scores):
    mine = lax.axis_index("inner")
    _, wide, bm = scores[0].shape
    blocks = q_ref.shape[0] // wide

    def key_at(c):
        ref = own_ref if c < blocks else other_ref
        return ref[0, c % blocks * wide : (c % blocks + 1) * wide]

    for n, ref in enumerate((own_ref, other_ref)):
        for t in range(blocks * wide // TILE):
            at = (n * blocks * wide) + t * TILE
            value_t[:, at : at + TILE] = transposed(ref[1, t * TILE : (t + 1) * TILE])

    def tile(block, inner, t):
        return (block * 2 + inner) * (wide // TILE) + t

    def finish(i, mixed):
        out_ref[pl.ds(pl.multiple_of(i * bm, bm), bm)] = mixed

    attend_blocks(
        blocks,
        TILE,
        lambda i: q_ref[pl.ds(pl.multiple_of(i * bm, bm), bm)],
        key_at,
        value_t,
        2 * blocks,
        lambda i, a, c, t: mask_ref[tile(i, mine, a), tile(c % blocks, mine if c < blocks else 1 - mine, t)] != 0,
        finish,
        scores,
    )


def whole_kernel(sources, mask_ref, qkv_ref, *refs):
    out_ref, value_t, *scores = refs[-4:]
    rows = qkv_ref.shape[2]
    _, wide, bm = scores[0].shape
    bands, tiles = bm // rows, wide // TILE
    for t in range(sources):
        value_t[:, t * TILE : (t + 1) * TILE] = transposed(qkv_ref[t, 2])

    def finish(i, mixed):
        out_ref[pl.ds(i * bands, bands)] = mixed.reshape(bands, rows, HDIM)

    attend_blocks(
        sources // bands,
        rows,
        lambda i: qkv_ref[pl.ds(i * bands, bands), 0].reshape(bm, HDIM),
        lambda c: qkv_ref[c * tiles : (c + 1) * tiles, 1].reshape(wide, HDIM),
        value_t,
        sources // tiles,
        lambda i, a, c, t: mask_ref[i * bands + a, c * tiles + t] != 0,
        finish,
        scores,
    )


def halved(far, near):
    steps = []
    for d in (*range(near // 4, near // 2), *range(near // 4)):
        steps += [(near // 2 + d, d), (d, near // 2 + d)]

    def swap(piece, step):
        pairs = [(2 * i + b, 2 * (i ^ step[b]) + b) for i in range(near) for b in range(2)]
        return lax.ppermute(piece, (*NEAR, "batch"), pairs)

    def per_device(query_rows, key_rows, value_rows, q_gain, k_gain, tile_mask):
        rows, features = query_rows.shape

        def store(which, at, block, kept):
            near_heads, far_heads = kept[:2]
            for h in range(near):
                near_heads[h, which, at] = block[:, h * HDIM : (h + 1) * HDIM]
            for h in range(far):
                far_heads[h, which, at] = block[:, (near + h) * HDIM : (near + h + 1) * HDIM]

        def send(which, outs, kept):
            near_heads, far_heads, near_sems, far_sems = kept
            me = lax.axis_index(NEAR)
            copies = [
                pltpu.make_async_copy(near_heads.at[partner(me, step), which], outs[n].at[which], near_sems.at[which, n])
                for n, step in enumerate(steps)
            ]
            copies.append(pltpu.make_async_copy(far_heads.at[:, which], outs[-1].at[:, which], far_sems.at[which]))
            for copy in copies:
                copy.start()
            return copies

        def read(shared, whole, out_ref):
            for d in range(near):
                out_ref[:, d * HDIM : (d + 1) * HDIM] = shared[d]
            for d in range(far):
                out_ref[:, (near + d) * HDIM : (near + d + 1) * HDIM] = whole[d]

        *shared, whole = pack(
            store,
            send,
            [shape(3, rows, HDIM)] * near + [shape(far, 3, rows, HDIM)],
            rows,
            features,
            (query_rows, key_rows, value_rows, q_gain, k_gain),
            [
                pltpu.VMEM((near, 3, rows, HDIM), BF16),
                pltpu.VMEM((far, 3, rows, HDIM), BF16),
                pltpu.SemaphoreType.DMA((3, near)),
                pltpu.SemaphoreType.DMA((3,)),
            ],
        )
        shared = [swap(piece, step) for step, piece in zip(steps, shared)]
        whole = exchange(whole, FAR)
        q_near, kv_near = pl.pallas_call(
            functools.partial(collect_kernel, steps, rows),
            out_shape=[shape(near * rows, HDIM), shape(2, near * rows, HDIM)],
            compiler_params=PARAMS,
            name="collect",
        )(*shared)
        kv_other = lax.ppermute(kv_near, "inner", [(0, 1), (1, 0)])

        wide = 2 * TILE
        blocks = far * rows // wide
        smem, vmem = pl.BlockSpec(memory_space=pltpu.SMEM), pl.BlockSpec(memory_space=pltpu.VMEM)
        scratch = [pltpu.VMEM((HDIM, far * rows), BF16)]
        scores = [pltpu.VMEM((blocks, wide, wide), jnp.float32)] * 2
        shared = pl.pallas_call(
            shared_kernel,
            in_specs=[smem] + [vmem] * 3,
            out_shape=shape(near * rows, HDIM),
            scratch_shapes=scratch + scores,
            compiler_params=PARAMS,
            cost_estimate=pl.CostEstimate(flops=SHARED_COST, bytes_accessed=2**21, transcendentals=0),
            name="attend_shared",
        )(tile_mask, q_near, kv_near, kv_other)

        whole = pl.pallas_call(
            functools.partial(whole_kernel, far),
            in_specs=[smem, vmem, pl.BlockSpec(memory_space=pl.ANY)],
            out_shape=shape(far, rows, HDIM),
            scratch_shapes=scratch + [pltpu.VMEM((blocks // 2, 2 * wide, wide), jnp.float32)] * 2,
            compiler_params=PARAMS,
            cost_estimate=pl.CostEstimate(flops=2**33, bytes_accessed=2**22, transcendentals=0),
            name="attend_whole",
        )(tile_mask, whole, shared)
        shared = exchange(shared.reshape(near, rows, HDIM), NEAR)
        return pl.pallas_call(
            read, out_shape=shape(rows, features), compiler_params=PARAMS, name="unpack"
        )(shared, exchange(whole, FAR))

    return per_device


def gathered_kernel(outer, inner, mask_ref, q_ref, kv_ref, out_ref, scores_ref):
    i = pl.program_id(0)
    block = out_ref.shape[0] * out_ref.shape[1] * out_ref.shape[2]
    tiles = block // TILE
    q_tile = (i * inner + lax.axis_index("inner")) * tiles
    mixed = attend(
        q_ref[0, :, 0].reshape(block, HDIM),
        TILE,
        lambda c: kv_ref[lax.rem(c, inner), lax.div(c, inner), :, 1].reshape(block, HDIM),
        lambda c: kv_ref[lax.rem(c, inner), lax.div(c, inner), :, 2].reshape(block, HDIM),
        outer * inner,
        lambda a, t: mask_ref[q_tile + a, t] != 0,
        scores_ref,
    )
    out_ref[...] = mixed.reshape(out_ref.shape)


def gathered(outer, inner, n_head, near):
    width = HEADS // near * HDIM

    def per_device(query_rows, key_rows, value_rows, q_gain, k_gain, tile_mask):
        rows, features = query_rows.shape
        block = rows * n_head

        def store(which, at, block, kept):
            for d in range(near):
                kept[0][d, which, at] = block[:, d * width : (d + 1) * width]

        def send(which, outs, kept):
            packed, sems = kept
            copy = pltpu.make_async_copy(packed.at[:, which], outs[0].at[:, which], sems.at[which])
            copy.start()
            return [copy]

        def read(got_ref, out_ref):
            for d in range(near):
                out_ref[:, d * width : (d + 1) * width] = got_ref[d]

        (packed,) = pack(
            store,
            send,
            [shape(near, 3, rows, width)],
            rows,
            features,
            (query_rows, key_rows, value_rows, q_gain, k_gain),
            [pltpu.VMEM((near, 3, rows, width), BF16), pltpu.SemaphoreType.DMA((3,))],
        )
        own = exchange(packed, NEAR).reshape(outer, n_head, 3, rows, width)
        every = lax.all_gather(own, "inner")
        mixed = pl.pallas_call(
            functools.partial(gathered_kernel, outer, inner),
            grid=(outer, HEADS // near),
            in_specs=[
                pl.BlockSpec(memory_space=pltpu.SMEM),
                pl.BlockSpec((1, n_head, 1, rows, HDIM), lambda i, h: (i, 0, 0, 0, h)),
                pl.BlockSpec((inner, outer, n_head, 3, rows, HDIM), lambda i, h: (0, 0, 0, 0, 0, h)),
            ],
            out_specs=pl.BlockSpec((1, n_head, rows, HDIM), lambda i, h: (i, 0, 0, h)),
            out_shape=shape(outer, n_head, rows, width),
            scratch_shapes=[pltpu.VMEM((outer * inner, block, block), jnp.float32)],
            compiler_params=PARAMS,
            name="attend",
        )(tile_mask, own, every)
        return pl.pallas_call(
            read, out_shape=shape(rows, features), compiler_params=PARAMS, name="unpack"
        )(exchange(mixed.reshape(near, rows, width), NEAR))

    return per_device


def solution(mesh):
    n_blk, n_head = mesh.shape["blk"], mesh.shape["head"]
    outer = max(d for d in range(1, n_blk + 1) if n_blk % d == 0 and HEADS % (n_head * d) == 0)
    inner = n_blk // outer
    near, far = outer * n_head, n_blk * n_head

    def per_device(query_rows, *others):
        in_pairs = inner == 2 and n_head == 2 and mesh.shape["batch"] == 2 and near & (near - 1) == 0
        if in_pairs and HEADS == near + far and query_rows.shape[0] == TILE:
            return halved(far, near)(query_rows, *others)
        return gathered(outer, inner, n_head, near)(query_rows, *others)

    split = P(("batch", "outer", "inner", "head"), None)
    return jax.shard_map(
        per_device,
        mesh=Mesh(
            mesh.devices.reshape(outer, inner, n_head, mesh.shape["batch"]), ("outer", "inner", "head", "batch")
        ),
        in_specs=(split, split, split, P(), P(), P()),
        out_specs=split,
        check_vma=False,
    )
```

```python
import functools

import jax
import jax.numpy as jnp
from jax import lax
from jax.experimental import pallas as pl
from jax.experimental.pallas import tpu as pltpu
from jax.sharding import Mesh, PartitionSpec as P

HEADS = 24
HDIM = 128
TILE = 128
EPS = 1e-06
MASKED = -1e30
NEAR = ("outer", "head")
FAR = ("outer", "inner", "head")
PARAMS = pltpu.CompilerParams(vmem_limit_bytes=48 * 1024 * 1024)
PACK_PARAMS = pltpu.CompilerParams(vmem_limit_bytes=61 * 1024 * 1024)
BF16 = jnp.bfloat16
SHARED_COST = 24 * 2**30
SCALE = 1.4426950408889634 * HDIM ** (-0.5)


def shape(*dims):
    return jax.ShapeDtypeStruct(dims, BF16)


def exchange(x, axes):
    return lax.all_to_all(x, axes, split_axis=0, concat_axis=0, tiled=True)


def pack_kernel(store, send, inputs, outputs, scratch):
    q_hbm, k_hbm, v_hbm, qg_hbm, kg_hbm = inputs
    q_in, k_in, v_in, qg, kg, sems, *kept = scratch
    copies = [
        pltpu.make_async_copy(src, dst, sems.at[n])
        for n, (src, dst) in enumerate(
            ((v_hbm, v_in), (q_hbm, q_in), (qg_hbm, qg), (k_hbm, k_in), (kg_hbm, kg))
        )
    ]
    for copy in copies:
        copy.start()

    group = 16

    def normalize(block, gain):
        widened = block.astype(jnp.float32)
        mean_square = jnp.mean(widened * widened, axis=-1, keepdims=True)
        return (widened * lax.rsqrt(mean_square + EPS) * gain[...]).astype(BF16)

    sent = []
    for first, which, ref, gain in ((0, 2, v_in, None), (1, 0, q_in, qg), (3, 1, k_in, kg)):
        copies[first].wait()
        if gain is not None:
            copies[first + 1].wait()
        for row in range(0, ref.shape[0], group):
            at = slice(row, row + group)
            store(which, at, ref[at] if gain is None else normalize(ref[at], gain), kept)
        sent += send(which, outputs, kept)
    for copy in sent:
        copy.wait()


def pack(store, send, out_shape, rows, features, arrays, kept=()):
    q, k, v, q_gain, k_gain = arrays
    hbm = pl.BlockSpec(memory_space=pltpu.HBM)

    def kernel(*refs):
        pack_kernel(store, send, refs[:5], refs[5 : 5 + len(out_shape)], refs[5 + len(out_shape) :])

    return pl.pallas_call(
        kernel,
        in_specs=[hbm] * 5,
        out_specs=[hbm] * len(out_shape),
        out_shape=out_shape,
        scratch_shapes=[pltpu.VMEM((rows, features), BF16)] * 3
        + [pltpu.VMEM((1, features), jnp.float32)] * 2
        + [pltpu.SemaphoreType.DMA((5,)), *kept],
        compiler_params=PACK_PARAMS,
        name="pack",
    )(q, k, v, q_gain.reshape(1, -1), k_gain.reshape(1, -1))


def first_pass(query, key, bias_at, scores_ref, c, largest):
    s = lax.dot_general(key, query, (((1,), (1,)), ((), ())), preferred_element_type=jnp.float32)
    scores_ref[c] = s
    for t in range(key.shape[0] // TILE):
        tile = s[t * TILE : (t + 1) * TILE].reshape(TILE // 8, 8, -1)
        largest = jnp.maximum(largest, jnp.max(tile, axis=0) + bias_at(t))
    return largest


def second_pass(scores_ref, c, col_max, bias_at, value_t, state):
    total, mixed = state
    wide, bm = scores_ref.shape[1:]
    weights = []
    for t in range(wide // TILE):
        tile = scores_ref[c, t * TILE : (t + 1) * TILE].reshape(TILE // 8, 8, bm)
        tile = jnp.exp2(tile * SCALE - (col_max - bias_at(t))[None])
        total = total + jnp.sum(tile, axis=0)
        weights.append(tile.reshape(TILE, bm).astype(BF16))
    weights = jnp.concatenate(weights, axis=0)
    return total, mixed + jnp.dot(value_t, weights, preferred_element_type=jnp.float32)


def over_all(largest):
    return jnp.broadcast_to(jnp.max(largest, axis=0, keepdims=True) * SCALE, largest.shape)


def divide(total, mixed):
    return (mixed / jnp.sum(total, axis=0, keepdims=True)).T.astype(BF16)


def bias_of(band, bm, live_at):
    lane = lax.broadcasted_iota(jnp.int32, (8, bm), 1)
    bias = jnp.zeros((8, bm), jnp.float32)
    for a in range(bm // band):
        dead = jnp.where(live_at(a), 0.0, MASKED).astype(jnp.float32)
        bias = jnp.where((lane >= a * band) & (lane < (a + 1) * band), dead, bias)
    return bias


def attend(query, band, key_at, value_at, key_blocks, live_at, scores_ref):
    wide, bm = scores_ref.shape[1:]

    def bias_at(c):
        return lambda t: bias_of(band, bm, lambda a: live_at(a, c * (wide // TILE) + t))

    def score(c, largest):
        return first_pass(query, key_at(c), bias_at(c), scores_ref, c, largest)

    largest = lax.fori_loop(0, key_blocks, score, jnp.full((8, bm), MASKED, jnp.float32))
    col_max = over_all(largest)

    def mix(c, state):
        return second_pass(scores_ref, c, col_max, bias_at(c), transposed(value_at(c)), state)

    state = jnp.zeros((8, bm), jnp.float32), jnp.zeros((HDIM, bm), jnp.float32)
    return divide(*lax.fori_loop(0, key_blocks, mix, state))


def transposed(block):
    return block.astype(jnp.float32).T.astype(BF16)


def attend_blocks(blocks, band, query_at, key_at, value_t, key_blocks, live_at, finish, scores):
    wide, bm = scores[0].shape[1:]
    empty = jnp.full((8, bm), MASKED, jnp.float32)
    nothing = jnp.zeros((8, bm), jnp.float32), jnp.zeros((HDIM, bm), jnp.float32)

    def bias_at(i, c):
        return lambda t: bias_of(band, bm, lambda a: live_at(i, a, c, t))

    def both(i, col_max, now, following):
        later = jnp.minimum(i + 1, blocks - 1)
        query = query_at(later)
        largest, state = empty, nothing
        for c in range(key_blocks):
            largest = first_pass(query, key_at(c), bias_at(later, c), following, c, largest)
            state = second_pass(now, c, col_max, bias_at(i, c), value_t[:, c * wide : (c + 1) * wide], state)
        finish(i, divide(*state))
        return over_all(largest)

    largest = empty
    query = query_at(0)
    for c in range(key_blocks):
        largest = first_pass(query, key_at(c), bias_at(0, c), scores[0], c, largest)

    def pair(n, col_max):
        col_max = both(2 * n, col_max, scores[0], scores[1])
        return both(2 * n + 1, col_max, scores[1], scores[0])

    lax.fori_loop(0, blocks // 2, pair, over_all(largest))


def partner(me, step):
    first, second = step
    return me ^ jnp.where(lax.axis_index("batch") == 0, first, second)


def collect_kernel(steps, rows, *refs):
    pieces, (q_out, kv_out) = refs[:-2], refs[-2:]
    me = lax.axis_index(NEAR)
    for step, piece in zip(steps, pieces):
        at = pl.ds(pl.multiple_of(partner(me, step) * rows, rows), rows)
        q_out[at] = piece[0]
        kv_out[:, at] = piece[1:]


def shared_kernel(mask_ref, q_ref, own_ref, other_ref, out_ref, value_t, *scores):
    mine = lax.axis_index("inner")
    _, wide, bm = scores[0].shape
    blocks = q_ref.shape[0] // wide

    def key_at(c):
        ref = own_ref if c < blocks else other_ref
        return ref[0, c % blocks * wide : (c % blocks + 1) * wide]

    for n, ref in enumerate((own_ref, other_ref)):
        for t in range(blocks * wide // TILE):
            at = (n * blocks * wide) + t * TILE
            value_t[:, at : at + TILE] = transposed(ref[1, t * TILE : (t + 1) * TILE])

    def tile(block, inner, t):
        return (block * 2 + inner) * (wide // TILE) + t

    def finish(i, mixed):
        out_ref[pl.ds(pl.multiple_of(i * bm, bm), bm)] = mixed

    attend_blocks(
        blocks,
        TILE,
        lambda i: q_ref[pl.ds(pl.multiple_of(i * bm, bm), bm)],
        key_at,
        value_t,
        2 * blocks,
        lambda i, a, c, t: mask_ref[tile(i, mine, a), tile(c % blocks, mine if c < blocks else 1 - mine, t)] != 0,
        finish,
        scores,
    )


def whole_kernel(sources, mask_ref, qkv_ref, *refs):
    out_ref, value_t, *scores = refs[-4:]
    rows = qkv_ref.shape[2]
    _, wide, bm = scores[0].shape
    bands, tiles = bm // rows, wide // TILE
    for t in range(sources):
        value_t[:, t * TILE : (t + 1) * TILE] = transposed(qkv_ref[t, 2])

    def finish(i, mixed):
        out_ref[pl.ds(i * bands, bands)] = mixed.reshape(bands, rows, HDIM)

    attend_blocks(
        sources // bands,
        rows,
        lambda i: qkv_ref[pl.ds(i * bands, bands), 0].reshape(bm, HDIM),
        lambda c: qkv_ref[c * tiles : (c + 1) * tiles, 1].reshape(wide, HDIM),
        value_t,
        sources // tiles,
        lambda i, a, c, t: mask_ref[i * bands + a, c * tiles + t] != 0,
        finish,
        scores,
    )


def halved(far, near):
    steps = []
    for d in range(near // 2):
        crossing = near // 2 + (d ^ near // 4)
        steps += [(crossing, d), (d, crossing)]

    def swap(piece, step):
        pairs = [(2 * i + b, 2 * (i ^ step[b]) + b) for i in range(near) for b in range(2)]
        return lax.ppermute(piece, (*NEAR, "batch"), pairs)

    def per_device(query_rows, key_rows, value_rows, q_gain, k_gain, tile_mask):
        rows, features = query_rows.shape

        def store(which, at, block, kept):
            near_heads, far_heads = kept[:2]
            for h in range(near):
                near_heads[h, which, at] = block[:, h * HDIM : (h + 1) * HDIM]
            for h in range(far):
                far_heads[h, which, at] = block[:, (near + h) * HDIM : (near + h + 1) * HDIM]

        def send(which, outs, kept):
            near_heads, far_heads, near_sems, far_sems = kept
            me = lax.axis_index(NEAR)
            copies = [
                pltpu.make_async_copy(near_heads.at[partner(me, step), which], outs[n].at[which], near_sems.at[which, n])
                for n, step in enumerate(steps)
            ]
            copies.append(pltpu.make_async_copy(far_heads.at[:, which], outs[-1].at[:, which], far_sems.at[which]))
            for copy in copies:
                copy.start()
            return copies

        def read(shared, whole, out_ref):
            for d in range(near):
                out_ref[:, d * HDIM : (d + 1) * HDIM] = shared[d]
            for d in range(far):
                out_ref[:, (near + d) * HDIM : (near + d + 1) * HDIM] = whole[d]

        *shared, whole = pack(
            store,
            send,
            [shape(3, rows, HDIM)] * near + [shape(far, 3, rows, HDIM)],
            rows,
            features,
            (query_rows, key_rows, value_rows, q_gain, k_gain),
            [
                pltpu.VMEM((near, 3, rows, HDIM), BF16),
                pltpu.VMEM((far, 3, rows, HDIM), BF16),
                pltpu.SemaphoreType.DMA((3, near)),
                pltpu.SemaphoreType.DMA((3,)),
            ],
        )
        shared = [swap(piece, step) for step, piece in zip(steps, shared)]
        whole = exchange(whole, FAR)
        q_near, kv_near = pl.pallas_call(
            functools.partial(collect_kernel, steps, rows),
            out_shape=[shape(near * rows, HDIM), shape(2, near * rows, HDIM)],
            compiler_params=PARAMS,
            name="collect",
        )(*shared)
        kv_other = lax.ppermute(kv_near, "inner", [(0, 1), (1, 0)])

        wide = 2 * TILE
        blocks = far * rows // wide
        smem, vmem = pl.BlockSpec(memory_space=pltpu.SMEM), pl.BlockSpec(memory_space=pltpu.VMEM)
        scratch = [pltpu.VMEM((HDIM, far * rows), BF16)]
        scores = [pltpu.VMEM((blocks, wide, wide), jnp.float32)] * 2
        shared = pl.pallas_call(
            shared_kernel,
            in_specs=[smem] + [vmem] * 3,
            out_shape=shape(near * rows, HDIM),
            scratch_shapes=scratch + scores,
            compiler_params=PARAMS,
            cost_estimate=pl.CostEstimate(flops=SHARED_COST, bytes_accessed=2**21, transcendentals=0),
            name="attend_shared",
        )(tile_mask, q_near, kv_near, kv_other)

        whole = pl.pallas_call(
            functools.partial(whole_kernel, far),
            in_specs=[smem, vmem, pl.BlockSpec(memory_space=pl.ANY)],
            out_shape=shape(far, rows, HDIM),
            scratch_shapes=scratch + [pltpu.VMEM((blocks // 2, 2 * wide, wide), jnp.float32)] * 2,
            compiler_params=PARAMS,
            cost_estimate=pl.CostEstimate(flops=2**33, bytes_accessed=2**22, transcendentals=0),
            name="attend_whole",
        )(tile_mask, whole, shared)
        shared = exchange(shared.reshape(near, rows, HDIM), NEAR)
        return pl.pallas_call(
            read, out_shape=shape(rows, features), compiler_params=PARAMS, name="unpack"
        )(shared, exchange(whole, FAR))

    return per_device


def gathered_kernel(outer, inner, mask_ref, q_ref, kv_ref, out_ref, scores_ref):
    i = pl.program_id(0)
    block = out_ref.shape[0] * out_ref.shape[1] * out_ref.shape[2]
    tiles = block // TILE
    q_tile = (i * inner + lax.axis_index("inner")) * tiles
    mixed = attend(
        q_ref[0, :, 0].reshape(block, HDIM),
        TILE,
        lambda c: kv_ref[lax.rem(c, inner), lax.div(c, inner), :, 1].reshape(block, HDIM),
        lambda c: kv_ref[lax.rem(c, inner), lax.div(c, inner), :, 2].reshape(block, HDIM),
        outer * inner,
        lambda a, t: mask_ref[q_tile + a, t] != 0,
        scores_ref,
    )
    out_ref[...] = mixed.reshape(out_ref.shape)


def gathered(outer, inner, n_head, near):
    width = HEADS // near * HDIM

    def per_device(query_rows, key_rows, value_rows, q_gain, k_gain, tile_mask):
        rows, features = query_rows.shape
        block = rows * n_head

        def store(which, at, block, kept):
            for d in range(near):
                kept[0][d, which, at] = block[:, d * width : (d + 1) * width]

        def send(which, outs, kept):
            packed, sems = kept
            copy = pltpu.make_async_copy(packed.at[:, which], outs[0].at[:, which], sems.at[which])
            copy.start()
            return [copy]

        def read(got_ref, out_ref):
            for d in range(near):
                out_ref[:, d * width : (d + 1) * width] = got_ref[d]

        (packed,) = pack(
            store,
            send,
            [shape(near, 3, rows, width)],
            rows,
            features,
            (query_rows, key_rows, value_rows, q_gain, k_gain),
            [pltpu.VMEM((near, 3, rows, width), BF16), pltpu.SemaphoreType.DMA((3,))],
        )
        own = exchange(packed, NEAR).reshape(outer, n_head, 3, rows, width)
        every = lax.all_gather(own, "inner")
        mixed = pl.pallas_call(
            functools.partial(gathered_kernel, outer, inner),
            grid=(outer, HEADS // near),
            in_specs=[
                pl.BlockSpec(memory_space=pltpu.SMEM),
                pl.BlockSpec((1, n_head, 1, rows, HDIM), lambda i, h: (i, 0, 0, 0, h)),
                pl.BlockSpec((inner, outer, n_head, 3, rows, HDIM), lambda i, h: (0, 0, 0, 0, 0, h)),
            ],
            out_specs=pl.BlockSpec((1, n_head, rows, HDIM), lambda i, h: (i, 0, 0, h)),
            out_shape=shape(outer, n_head, rows, width),
            scratch_shapes=[pltpu.VMEM((outer * inner, block, block), jnp.float32)],
            compiler_params=PARAMS,
            name="attend",
        )(tile_mask, own, every)
        return pl.pallas_call(
            read, out_shape=shape(rows, features), compiler_params=PARAMS, name="unpack"
        )(exchange(mixed.reshape(near, rows, width), NEAR))

    return per_device


def solution(mesh):
    n_blk, n_head = mesh.shape["blk"], mesh.shape["head"]
    outer = max(d for d in range(1, n_blk + 1) if n_blk % d == 0 and HEADS % (n_head * d) == 0)
    inner = n_blk // outer
    near, far = outer * n_head, n_blk * n_head

    def per_device(query_rows, *others):
        in_pairs = inner == 2 and n_head == 2 and mesh.shape["batch"] == 2 and near & (near - 1) == 0
        if in_pairs and HEADS == near + far and query_rows.shape[0] == TILE:
            return halved(far, near)(query_rows, *others)
        return gathered(outer, inner, n_head, near)(query_rows, *others)

    split = P(("batch", "outer", "inner", "head"), None)
    return jax.shard_map(
        per_device,
        mesh=Mesh(
            mesh.devices.reshape(outer, inner, n_head, mesh.shape["batch"]), ("outer", "inner", "head", "batch")
        ),
        in_specs=(split, split, split, P(), P(), P()),
        out_specs=split,
        check_vma=False,
    )
```

```python
import functools

import jax
import jax.numpy as jnp
from jax import lax
from jax.experimental import pallas as pl
from jax.experimental.pallas import tpu as pltpu
from jax.sharding import Mesh, PartitionSpec as P

HEADS = 24
HDIM = 128
TILE = 128
EPS = 1e-06
MASKED = -1e30
NEAR = ("outer", "head")
FAR = ("outer", "inner", "head")
PARAMS = pltpu.CompilerParams(vmem_limit_bytes=48 * 1024 * 1024)
PACK_PARAMS = pltpu.CompilerParams(vmem_limit_bytes=61 * 1024 * 1024)
BF16 = jnp.bfloat16
SHARED_COST = 24 * 2**30
SCALE = 1.4426950408889634 * HDIM ** (-0.5)


def shape(*dims):
    return jax.ShapeDtypeStruct(dims, BF16)


def exchange(x, axes):
    return lax.all_to_all(x, axes, split_axis=0, concat_axis=0, tiled=True)


def pack_kernel(store, send, inputs, outputs, scratch):
    q_hbm, k_hbm, v_hbm, qg_hbm, kg_hbm = inputs
    q_in, k_in, v_in, qg, kg, sems, *kept = scratch
    copies = [
        pltpu.make_async_copy(src, dst, sems.at[n])
        for n, (src, dst) in enumerate(
            ((v_hbm, v_in), (q_hbm, q_in), (qg_hbm, qg), (k_hbm, k_in), (kg_hbm, kg))
        )
    ]
    for copy in copies:
        copy.start()

    group = 16

    def normalize(block, gain):
        widened = block.astype(jnp.float32)
        mean_square = jnp.mean(widened * widened, axis=-1, keepdims=True)
        return (widened * lax.rsqrt(mean_square + EPS) * gain[...]).astype(BF16)

    sent = []
    for first, which, ref, gain in ((0, 2, v_in, None), (1, 0, q_in, qg), (3, 1, k_in, kg)):
        copies[first].wait()
        if gain is not None:
            copies[first + 1].wait()
        for row in range(0, ref.shape[0], group):
            at = slice(row, row + group)
            store(which, at, ref[at] if gain is None else normalize(ref[at], gain), kept)
        sent += send(which, outputs, kept)
    for copy in sent:
        copy.wait()


def pack(store, send, out_shape, rows, features, arrays, kept=()):
    q, k, v, q_gain, k_gain = arrays
    hbm = pl.BlockSpec(memory_space=pltpu.HBM)

    def kernel(*refs):
        pack_kernel(store, send, refs[:5], refs[5 : 5 + len(out_shape)], refs[5 + len(out_shape) :])

    return pl.pallas_call(
        kernel,
        in_specs=[hbm] * 5,
        out_specs=[hbm] * len(out_shape),
        out_shape=out_shape,
        scratch_shapes=[pltpu.VMEM((rows, features), BF16)] * 3
        + [pltpu.VMEM((1, features), jnp.float32)] * 2
        + [pltpu.SemaphoreType.DMA((5,)), *kept],
        compiler_params=PACK_PARAMS,
        name="pack",
    )(q, k, v, q_gain.reshape(1, -1), k_gain.reshape(1, -1))


def first_pass(query, key, bias_at, scores_ref, c, largest):
    s = lax.dot_general(key, query, (((1,), (1,)), ((), ())), preferred_element_type=jnp.float32)
    scores_ref[c] = s
    for t in range(key.shape[0] // TILE):
        tile = s[t * TILE : (t + 1) * TILE].reshape(TILE // 8, 8, -1)
        largest = jnp.maximum(largest, jnp.max(tile, axis=0) + bias_at(t))
    return largest


def second_pass(scores_ref, c, col_max, bias_at, value_t, state):
    total, mixed = state
    wide, bm = scores_ref.shape[1:]
    weights = []
    for t in range(wide // TILE):
        tile = scores_ref[c, t * TILE : (t + 1) * TILE].reshape(TILE // 8, 8, bm)
        tile = jnp.exp2(tile * SCALE - (col_max - bias_at(t))[None])
        total = total + jnp.sum(tile, axis=0)
        weights.append(tile.reshape(TILE, bm).astype(BF16))
    weights = jnp.concatenate(weights, axis=0)
    return total, mixed + jnp.dot(value_t, weights, preferred_element_type=jnp.float32)


def over_all(largest):
    return jnp.broadcast_to(jnp.max(largest, axis=0, keepdims=True) * SCALE, largest.shape)


def divide(total, mixed):
    return (mixed / jnp.sum(total, axis=0, keepdims=True)).T.astype(BF16)


def bias_of(band, bm, live_at):
    lane = lax.broadcasted_iota(jnp.int32, (8, bm), 1)
    bias = jnp.zeros((8, bm), jnp.float32)
    for a in range(bm // band):
        dead = jnp.where(live_at(a), 0.0, MASKED).astype(jnp.float32)
        bias = jnp.where((lane >= a * band) & (lane < (a + 1) * band), dead, bias)
    return bias


def attend(query, band, key_at, value_at, key_blocks, live_at, scores_ref):
    wide, bm = scores_ref.shape[1:]

    def bias_at(c):
        return lambda t: bias_of(band, bm, lambda a: live_at(a, c * (wide // TILE) + t))

    def score(c, largest):
        return first_pass(query, key_at(c), bias_at(c), scores_ref, c, largest)

    largest = lax.fori_loop(0, key_blocks, score, jnp.full((8, bm), MASKED, jnp.float32))
    col_max = over_all(largest)

    def mix(c, state):
        return second_pass(scores_ref, c, col_max, bias_at(c), transposed(value_at(c)), state)

    state = jnp.zeros((8, bm), jnp.float32), jnp.zeros((HDIM, bm), jnp.float32)
    return divide(*lax.fori_loop(0, key_blocks, mix, state))


def transposed(block):
    return block.astype(jnp.float32).T.astype(BF16)


def attend_blocks(blocks, band, query_at, key_at, value_t, key_blocks, live_at, finish, scores):
    wide, bm = scores[0].shape[1:]
    empty = jnp.full((8, bm), MASKED, jnp.float32)
    nothing = jnp.zeros((8, bm), jnp.float32), jnp.zeros((HDIM, bm), jnp.float32)

    def bias_at(i, c):
        return lambda t: bias_of(band, bm, lambda a: live_at(i, a, c, t))

    def both(i, col_max, now, following):
        later = jnp.minimum(i + 1, blocks - 1)
        query = query_at(later)
        largest, state = empty, nothing
        for c in range(key_blocks):
            largest = first_pass(query, key_at(c), bias_at(later, c), following, c, largest)
            state = second_pass(now, c, col_max, bias_at(i, c), value_t[:, c * wide : (c + 1) * wide], state)
        finish(i, divide(*state))
        return over_all(largest)

    largest = empty
    query = query_at(0)
    for c in range(key_blocks):
        largest = first_pass(query, key_at(c), bias_at(0, c), scores[0], c, largest)

    def pair(n, col_max):
        col_max = both(2 * n, col_max, scores[0], scores[1])
        return both(2 * n + 1, col_max, scores[1], scores[0])

    lax.fori_loop(0, blocks // 2, pair, over_all(largest))


def partner(me, step):
    first, second = step
    return me ^ jnp.where(lax.axis_index("batch") == 0, first, second)


def collect_kernel(steps, rows, *refs):
    pieces, (q_out, kv_out) = refs[:-2], refs[-2:]
    me = lax.axis_index(NEAR)
    for step, piece in zip(steps, pieces):
        at = pl.ds(pl.multiple_of(partner(me, step) * rows, rows), rows)
        q_out[at] = piece[0]
        kv_out[:, at] = piece[1:]


def shared_kernel(mask_ref, q_ref, own_ref, other_ref, out_ref, value_t, *scores):
    mine = lax.axis_index("inner")
    _, wide, bm = scores[0].shape
    blocks = q_ref.shape[0] // wide

    def key_at(c):
        ref = own_ref if c < blocks else other_ref
        return ref[0, c % blocks * wide : (c % blocks + 1) * wide]

    for n, ref in enumerate((own_ref, other_ref)):
        for t in range(blocks * wide // TILE):
            at = (n * blocks * wide) + t * TILE
            value_t[:, at : at + TILE] = transposed(ref[1, t * TILE : (t + 1) * TILE])

    def tile(block, inner, t):
        return (block * 2 + inner) * (wide // TILE) + t

    def finish(i, mixed):
        out_ref[pl.ds(pl.multiple_of(i * bm, bm), bm)] = mixed

    attend_blocks(
        blocks,
        TILE,
        lambda i: q_ref[pl.ds(pl.multiple_of(i * bm, bm), bm)],
        key_at,
        value_t,
        2 * blocks,
        lambda i, a, c, t: mask_ref[tile(i, mine, a), tile(c % blocks, mine if c < blocks else 1 - mine, t)] != 0,
        finish,
        scores,
    )


def whole_kernel(sources, mask_ref, qkv_ref, *refs):
    out_ref, value_t, *scores = refs[-4:]
    rows = qkv_ref.shape[2]
    _, wide, bm = scores[0].shape
    bands, tiles = bm // rows, wide // TILE
    for t in range(sources):
        value_t[:, t * TILE : (t + 1) * TILE] = transposed(qkv_ref[t, 2])

    def finish(i, mixed):
        out_ref[pl.ds(i * bands, bands)] = mixed.reshape(bands, rows, HDIM)

    attend_blocks(
        sources // bands,
        rows,
        lambda i: qkv_ref[pl.ds(i * bands, bands), 0].reshape(bm, HDIM),
        lambda c: qkv_ref[c * tiles : (c + 1) * tiles, 1].reshape(wide, HDIM),
        value_t,
        sources // tiles,
        lambda i, a, c, t: mask_ref[i * bands + a, c * tiles + t] != 0,
        finish,
        scores,
    )


def halved(far, near):
    steps = []
    for d in reversed(range(near // 2)):
        steps += [(near // 2 + d, d), (d, near // 2 + d)]

    def swap(piece, step):
        pairs = [(2 * i + b, 2 * (i ^ step[b]) + b) for i in range(near) for b in range(2)]
        return lax.ppermute(piece, (*NEAR, "batch"), pairs)

    def per_device(query_rows, key_rows, value_rows, q_gain, k_gain, tile_mask):
        rows, features = query_rows.shape

        def store(which, at, block, kept):
            near_heads, far_heads = kept[:2]
            for h in range(near):
                near_heads[h, which, at] = block[:, h * HDIM : (h + 1) * HDIM]
            for h in range(far):
                far_heads[h, which, at] = block[:, (near + h) * HDIM : (near + h + 1) * HDIM]

        def send(which, outs, kept):
            near_heads, far_heads, near_sems, far_sems = kept
            me = lax.axis_index(NEAR)
            copies = [
                pltpu.make_async_copy(near_heads.at[partner(me, step), which], outs[n].at[which], near_sems.at[which, n])
                for n, step in enumerate(steps)
            ]
            copies.append(pltpu.make_async_copy(far_heads.at[:, which], outs[-1].at[:, which], far_sems.at[which]))
            for copy in copies:
                copy.start()
            return copies

        def read(shared, whole, out_ref):
            for d in range(near):
                out_ref[:, d * HDIM : (d + 1) * HDIM] = shared[d]
            for d in range(far):
                out_ref[:, (near + d) * HDIM : (near + d + 1) * HDIM] = whole[d]

        *shared, whole = pack(
            store,
            send,
            [shape(3, rows, HDIM)] * near + [shape(far, 3, rows, HDIM)],
            rows,
            features,
            (query_rows, key_rows, value_rows, q_gain, k_gain),
            [
                pltpu.VMEM((near, 3, rows, HDIM), BF16),
                pltpu.VMEM((far, 3, rows, HDIM), BF16),
                pltpu.SemaphoreType.DMA((3, near)),
                pltpu.SemaphoreType.DMA((3,)),
            ],
        )
        shared = [swap(piece, step) for step, piece in zip(steps, shared)]
        whole = exchange(whole, FAR)
        q_near, kv_near = pl.pallas_call(
            functools.partial(collect_kernel, steps, rows),
            out_shape=[shape(near * rows, HDIM), shape(2, near * rows, HDIM)],
            compiler_params=PARAMS,
            name="collect",
        )(*shared)
        kv_other = lax.ppermute(kv_near, "inner", [(0, 1), (1, 0)])

        wide = 2 * TILE
        blocks = far * rows // wide
        smem, vmem = pl.BlockSpec(memory_space=pltpu.SMEM), pl.BlockSpec(memory_space=pltpu.VMEM)
        scratch = [pltpu.VMEM((HDIM, far * rows), BF16)]
        scores = [pltpu.VMEM((blocks, wide, wide), jnp.float32)] * 2
        shared = pl.pallas_call(
            shared_kernel,
            in_specs=[smem] + [vmem] * 3,
            out_shape=shape(near * rows, HDIM),
            scratch_shapes=scratch + scores,
            compiler_params=PARAMS,
            cost_estimate=pl.CostEstimate(flops=SHARED_COST, bytes_accessed=2**21, transcendentals=0),
            name="attend_shared",
        )(tile_mask, q_near, kv_near, kv_other)

        whole = pl.pallas_call(
            functools.partial(whole_kernel, far),
            in_specs=[smem, vmem, pl.BlockSpec(memory_space=pl.ANY)],
            out_shape=shape(far, rows, HDIM),
            scratch_shapes=scratch + [pltpu.VMEM((blocks // 2, 2 * wide, wide), jnp.float32)] * 2,
            compiler_params=PARAMS,
            cost_estimate=pl.CostEstimate(flops=2**33, bytes_accessed=2**22, transcendentals=0),
            name="attend_whole",
        )(tile_mask, whole, shared)
        shared = exchange(shared.reshape(near, rows, HDIM), NEAR)
        return pl.pallas_call(
            read, out_shape=shape(rows, features), compiler_params=PARAMS, name="unpack"
        )(shared, exchange(whole, FAR))

    return per_device


def gathered_kernel(outer, inner, mask_ref, q_ref, kv_ref, out_ref, scores_ref):
    i = pl.program_id(0)
    block = out_ref.shape[0] * out_ref.shape[1] * out_ref.shape[2]
    tiles = block // TILE
    q_tile = (i * inner + lax.axis_index("inner")) * tiles
    mixed = attend(
        q_ref[0, :, 0].reshape(block, HDIM),
        TILE,
        lambda c: kv_ref[lax.rem(c, inner), lax.div(c, inner), :, 1].reshape(block, HDIM),
        lambda c: kv_ref[lax.rem(c, inner), lax.div(c, inner), :, 2].reshape(block, HDIM),
        outer * inner,
        lambda a, t: mask_ref[q_tile + a, t] != 0,
        scores_ref,
    )
    out_ref[...] = mixed.reshape(out_ref.shape)


def gathered(outer, inner, n_head, near):
    width = HEADS // near * HDIM

    def per_device(query_rows, key_rows, value_rows, q_gain, k_gain, tile_mask):
        rows, features = query_rows.shape
        block = rows * n_head

        def store(which, at, block, kept):
            for d in range(near):
                kept[0][d, which, at] = block[:, d * width : (d + 1) * width]

        def send(which, outs, kept):
            packed, sems = kept
            copy = pltpu.make_async_copy(packed.at[:, which], outs[0].at[:, which], sems.at[which])
            copy.start()
            return [copy]

        def read(got_ref, out_ref):
            for d in range(near):
                out_ref[:, d * width : (d + 1) * width] = got_ref[d]

        (packed,) = pack(
            store,
            send,
            [shape(near, 3, rows, width)],
            rows,
            features,
            (query_rows, key_rows, value_rows, q_gain, k_gain),
            [pltpu.VMEM((near, 3, rows, width), BF16), pltpu.SemaphoreType.DMA((3,))],
        )
        own = exchange(packed, NEAR).reshape(outer, n_head, 3, rows, width)
        every = lax.all_gather(own, "inner")
        mixed = pl.pallas_call(
            functools.partial(gathered_kernel, outer, inner),
            grid=(outer, HEADS // near),
            in_specs=[
                pl.BlockSpec(memory_space=pltpu.SMEM),
                pl.BlockSpec((1, n_head, 1, rows, HDIM), lambda i, h: (i, 0, 0, 0, h)),
                pl.BlockSpec((inner, outer, n_head, 3, rows, HDIM), lambda i, h: (0, 0, 0, 0, 0, h)),
            ],
            out_specs=pl.BlockSpec((1, n_head, rows, HDIM), lambda i, h: (i, 0, 0, h)),
            out_shape=shape(outer, n_head, rows, width),
            scratch_shapes=[pltpu.VMEM((outer * inner, block, block), jnp.float32)],
            compiler_params=PARAMS,
            name="attend",
        )(tile_mask, own, every)
        return pl.pallas_call(
            read, out_shape=shape(rows, features), compiler_params=PARAMS, name="unpack"
        )(exchange(mixed.reshape(near, rows, width), NEAR))

    return per_device


def solution(mesh):
    n_blk, n_head = mesh.shape["blk"], mesh.shape["head"]
    outer = max(d for d in range(1, n_blk + 1) if n_blk % d == 0 and HEADS % (n_head * d) == 0)
    inner = n_blk // outer
    near, far = outer * n_head, n_blk * n_head

    def per_device(query_rows, *others):
        in_pairs = inner == 2 and n_head == 2 and mesh.shape["batch"] == 2 and near & (near - 1) == 0
        if in_pairs and HEADS == near + far and query_rows.shape[0] == TILE:
            return halved(far, near)(query_rows, *others)
        return gathered(outer, inner, n_head, near)(query_rows, *others)

    split = P(("batch", "outer", "inner", "head"), None)
    return jax.shard_map(
        per_device,
        mesh=Mesh(
            mesh.devices.reshape(outer, inner, n_head, mesh.shape["batch"]), ("outer", "inner", "head", "batch")
        ),
        in_specs=(split, split, split, P(), P(), P()),
        out_specs=split,
        check_vma=False,
    )
```

```python
import functools

import jax
import jax.numpy as jnp
from jax import lax
from jax.experimental import pallas as pl
from jax.experimental.pallas import tpu as pltpu
from jax.sharding import Mesh, PartitionSpec as P

HEADS = 24
HDIM = 128
TILE = 128
EPS = 1e-06
MASKED = -1e30
NEAR = ("outer", "head")
FAR = ("outer", "inner", "head")
PARAMS = pltpu.CompilerParams(vmem_limit_bytes=48 * 1024 * 1024)
PACK_PARAMS = pltpu.CompilerParams(vmem_limit_bytes=61 * 1024 * 1024)
BF16 = jnp.bfloat16
SHARED_COST = 24 * 2**30
SCALE = 1.4426950408889634 * HDIM ** (-0.5)


def shape(*dims):
    return jax.ShapeDtypeStruct(dims, BF16)


def exchange(x, axes):
    return lax.all_to_all(x, axes, split_axis=0, concat_axis=0, tiled=True)


def pack_kernel(store, send, inputs, outputs, scratch):
    q_hbm, k_hbm, v_hbm, qg_hbm, kg_hbm = inputs
    q_in, k_in, v_in, qg, kg, sems, *kept = scratch
    copies = [
        pltpu.make_async_copy(src, dst, sems.at[n])
        for n, (src, dst) in enumerate(
            ((v_hbm, v_in), (q_hbm, q_in), (qg_hbm, qg), (k_hbm, k_in), (kg_hbm, kg))
        )
    ]
    for copy in copies:
        copy.start()

    group = 16

    def normalize(block, gain):
        widened = block.astype(jnp.float32)
        mean_square = jnp.mean(widened * widened, axis=-1, keepdims=True)
        return (widened * lax.rsqrt(mean_square + EPS) * gain[...]).astype(BF16)

    sent = []
    for first, which, ref, gain in ((0, 2, v_in, None), (1, 0, q_in, qg), (3, 1, k_in, kg)):
        copies[first].wait()
        if gain is not None:
            copies[first + 1].wait()
        for row in range(0, ref.shape[0], group):
            at = slice(row, row + group)
            store(which, at, ref[at] if gain is None else normalize(ref[at], gain), kept)
        sent += send(which, outputs, kept)
    for copy in sent:
        copy.wait()


def pack(store, send, out_shape, rows, features, arrays, kept=()):
    q, k, v, q_gain, k_gain = arrays
    hbm = pl.BlockSpec(memory_space=pltpu.HBM)

    def kernel(*refs):
        pack_kernel(store, send, refs[:5], refs[5 : 5 + len(out_shape)], refs[5 + len(out_shape) :])

    return pl.pallas_call(
        kernel,
        in_specs=[hbm] * 5,
        out_specs=[hbm] * len(out_shape),
        out_shape=out_shape,
        scratch_shapes=[pltpu.VMEM((rows, features), BF16)] * 3
        + [pltpu.VMEM((1, features), jnp.float32)] * 2
        + [pltpu.SemaphoreType.DMA((5,)), *kept],
        compiler_params=PACK_PARAMS,
        name="pack",
    )(q, k, v, q_gain.reshape(1, -1), k_gain.reshape(1, -1))


def first_pass(query, key, bias_at, scores_ref, c, largest):
    s = lax.dot_general(key, query, (((1,), (1,)), ((), ())), preferred_element_type=jnp.float32)
    scores_ref[c] = s
    for t in range(key.shape[0] // TILE):
        tile = s[t * TILE : (t + 1) * TILE].reshape(TILE // 8, 8, -1)
        largest = jnp.maximum(largest, jnp.max(tile, axis=0) + bias_at(t))
    return largest


def second_pass(scores_ref, c, col_max, bias_at, value_t, state):
    total, mixed = state
    wide, bm = scores_ref.shape[1:]
    weights = []
    for t in range(wide // TILE):
        tile = scores_ref[c, t * TILE : (t + 1) * TILE].reshape(TILE // 8, 8, bm)
        tile = jnp.exp2(tile * SCALE - (col_max - bias_at(t))[None])
        total = total + jnp.sum(tile, axis=0)
        weights.append(tile.reshape(TILE, bm).astype(BF16))
    weights = jnp.concatenate(weights, axis=0)
    return total, mixed + jnp.dot(value_t, weights, preferred_element_type=jnp.float32)


def over_all(largest):
    return jnp.broadcast_to(jnp.max(largest, axis=0, keepdims=True) * SCALE, largest.shape)


def divide(total, mixed):
    return (mixed / jnp.sum(total, axis=0, keepdims=True)).T.astype(BF16)


def bias_of(band, bm, live_at):
    lane = lax.broadcasted_iota(jnp.int32, (8, bm), 1)
    bias = jnp.zeros((8, bm), jnp.float32)
    for a in range(bm // band):
        dead = jnp.where(live_at(a), 0.0, MASKED).astype(jnp.float32)
        bias = jnp.where((lane >= a * band) & (lane < (a + 1) * band), dead, bias)
    return bias


def attend(query, band, key_at, value_at, key_blocks, live_at, scores_ref):
    wide, bm = scores_ref.shape[1:]

    def bias_at(c):
        return lambda t: bias_of(band, bm, lambda a: live_at(a, c * (wide // TILE) + t))

    def score(c, largest):
        return first_pass(query, key_at(c), bias_at(c), scores_ref, c, largest)

    largest = lax.fori_loop(0, key_blocks, score, jnp.full((8, bm), MASKED, jnp.float32))
    col_max = over_all(largest)

    def mix(c, state):
        return second_pass(scores_ref, c, col_max, bias_at(c), transposed(value_at(c)), state)

    state = jnp.zeros((8, bm), jnp.float32), jnp.zeros((HDIM, bm), jnp.float32)
    return divide(*lax.fori_loop(0, key_blocks, mix, state))


def transposed(block):
    return block.astype(jnp.float32).T.astype(BF16)


def attend_blocks(blocks, band, query_at, key_at, value_t, key_blocks, live_at, finish, scores):
    wide, bm = scores[0].shape[1:]
    empty = jnp.full((8, bm), MASKED, jnp.float32)
    nothing = jnp.zeros((8, bm), jnp.float32), jnp.zeros((HDIM, bm), jnp.float32)

    def bias_at(i, c):
        return lambda t: bias_of(band, bm, lambda a: live_at(i, a, c, t))

    def both(i, col_max, now, following):
        later = jnp.minimum(i + 1, blocks - 1)
        query = query_at(later)
        largest, state = empty, nothing
        for c in range(key_blocks):
            largest = first_pass(query, key_at(c), bias_at(later, c), following, c, largest)
            state = second_pass(now, c, col_max, bias_at(i, c), value_t[:, c * wide : (c + 1) * wide], state)
        finish(i, divide(*state))
        return over_all(largest)

    largest = empty
    query = query_at(0)
    for c in range(key_blocks):
        largest = first_pass(query, key_at(c), bias_at(0, c), scores[0], c, largest)

    def pair(n, col_max):
        col_max = both(2 * n, col_max, scores[0], scores[1])
        return both(2 * n + 1, col_max, scores[1], scores[0])

    lax.fori_loop(0, blocks // 2, pair, over_all(largest))


def partner(me, step):
    first, second = step
    return me ^ jnp.where(lax.axis_index("batch") == 0, first, second)


def collect_kernel(steps, rows, *refs):
    pieces, (q_out, kv_out) = refs[:-2], refs[-2:]
    me = lax.axis_index(NEAR)
    for step, piece in zip(steps, pieces):
        at = pl.ds(pl.multiple_of(partner(me, step) * rows, rows), rows)
        q_out[at] = piece[0]
        kv_out[:, at] = piece[1:]


def shared_kernel(mask_ref, q_ref, own_ref, other_ref, out_ref, value_t, *scores):
    mine = lax.axis_index("inner")
    _, wide, bm = scores[0].shape
    blocks = q_ref.shape[0] // wide

    def key_at(c):
        ref = own_ref if c < blocks else other_ref
        return ref[0, c % blocks * wide : (c % blocks + 1) * wide]

    for n, ref in enumerate((own_ref, other_ref)):
        for t in range(blocks * wide // TILE):
            at = (n * blocks * wide) + t * TILE
            value_t[:, at : at + TILE] = transposed(ref[1, t * TILE : (t + 1) * TILE])

    def tile(block, inner, t):
        return (block * 2 + inner) * (wide // TILE) + t

    def finish(i, mixed):
        out_ref[pl.ds(pl.multiple_of(i * bm, bm), bm)] = mixed

    attend_blocks(
        blocks,
        TILE,
        lambda i: q_ref[pl.ds(pl.multiple_of(i * bm, bm), bm)],
        key_at,
        value_t,
        2 * blocks,
        lambda i, a, c, t: mask_ref[tile(i, mine, a), tile(c % blocks, mine if c < blocks else 1 - mine, t)] != 0,
        finish,
        scores,
    )


def whole_kernel(sources, mask_ref, qkv_ref, *refs):
    out_ref, value_t, *scores = refs[-4:]
    rows = qkv_ref.shape[2]
    _, wide, bm = scores[0].shape
    bands, tiles = bm // rows, wide // TILE
    for t in range(sources):
        value_t[:, t * TILE : (t + 1) * TILE] = transposed(qkv_ref[t, 2])

    def finish(i, mixed):
        out_ref[pl.ds(i * bands, bands)] = mixed.reshape(bands, rows, HDIM)

    attend_blocks(
        sources // bands,
        rows,
        lambda i: qkv_ref[pl.ds(i * bands, bands), 0].reshape(bm, HDIM),
        lambda c: qkv_ref[c * tiles : (c + 1) * tiles, 1].reshape(wide, HDIM),
        value_t,
        sources // tiles,
        lambda i, a, c, t: mask_ref[i * bands + a, c * tiles + t] != 0,
        finish,
        scores,
    )


def halved(far, near):
    steps = []
    for d in (*range(near // 4, near // 2), *reversed(range(near // 4))):
        steps += [(near // 2 + d, d), (d, near // 2 + d)]

    def swap(piece, step):
        pairs = [(2 * i + b, 2 * (i ^ step[b]) + b) for i in range(near) for b in range(2)]
        return lax.ppermute(piece, (*NEAR, "batch"), pairs)

    def per_device(query_rows, key_rows, value_rows, q_gain, k_gain, tile_mask):
        rows, features = query_rows.shape

        def store(which, at, block, kept):
            near_heads, far_heads = kept[:2]
            for h in range(near):
                near_heads[h, which, at] = block[:, h * HDIM : (h + 1) * HDIM]
            for h in range(far):
                far_heads[h, which, at] = block[:, (near + h) * HDIM : (near + h + 1) * HDIM]

        def send(which, outs, kept):
            near_heads, far_heads, near_sems, far_sems = kept
            me = lax.axis_index(NEAR)
            copies = [
                pltpu.make_async_copy(near_heads.at[partner(me, step), which], outs[n].at[which], near_sems.at[which, n])
                for n, step in enumerate(steps)
            ]
            copies.append(pltpu.make_async_copy(far_heads.at[:, which], outs[-1].at[:, which], far_sems.at[which]))
            for copy in copies:
                copy.start()
            return copies

        def read(shared, whole, out_ref):
            for d in range(near):
                out_ref[:, d * HDIM : (d + 1) * HDIM] = shared[d]
            for d in range(far):
                out_ref[:, (near + d) * HDIM : (near + d + 1) * HDIM] = whole[d]

        *shared, whole = pack(
            store,
            send,
            [shape(3, rows, HDIM)] * near + [shape(far, 3, rows, HDIM)],
            rows,
            features,
            (query_rows, key_rows, value_rows, q_gain, k_gain),
            [
                pltpu.VMEM((near, 3, rows, HDIM), BF16),
                pltpu.VMEM((far, 3, rows, HDIM), BF16),
                pltpu.SemaphoreType.DMA((3, near)),
                pltpu.SemaphoreType.DMA((3,)),
            ],
        )
        shared = [swap(piece, step) for step, piece in zip(steps, shared)]
        whole = exchange(whole, FAR)
        q_near, kv_near = pl.pallas_call(
            functools.partial(collect_kernel, steps, rows),
            out_shape=[shape(near * rows, HDIM), shape(2, near * rows, HDIM)],
            compiler_params=PARAMS,
            name="collect",
        )(*shared)
        kv_other = lax.ppermute(kv_near, "inner", [(0, 1), (1, 0)])

        wide = 2 * TILE
        blocks = far * rows // wide
        smem, vmem = pl.BlockSpec(memory_space=pltpu.SMEM), pl.BlockSpec(memory_space=pltpu.VMEM)
        scratch = [pltpu.VMEM((HDIM, far * rows), BF16)]
        scores = [pltpu.VMEM((blocks, wide, wide), jnp.float32)] * 2
        shared = pl.pallas_call(
            shared_kernel,
            in_specs=[smem] + [vmem] * 3,
            out_shape=shape(near * rows, HDIM),
            scratch_shapes=scratch + scores,
            compiler_params=PARAMS,
            cost_estimate=pl.CostEstimate(flops=SHARED_COST, bytes_accessed=2**21, transcendentals=0),
            name="attend_shared",
        )(tile_mask, q_near, kv_near, kv_other)

        whole = pl.pallas_call(
            functools.partial(whole_kernel, far),
            in_specs=[smem, vmem, pl.BlockSpec(memory_space=pl.ANY)],
            out_shape=shape(far, rows, HDIM),
            scratch_shapes=scratch + [pltpu.VMEM((blocks // 2, 2 * wide, wide), jnp.float32)] * 2,
            compiler_params=PARAMS,
            cost_estimate=pl.CostEstimate(flops=2**33, bytes_accessed=2**22, transcendentals=0),
            name="attend_whole",
        )(tile_mask, whole, shared)
        shared = exchange(shared.reshape(near, rows, HDIM), NEAR)
        return pl.pallas_call(
            read, out_shape=shape(rows, features), compiler_params=PARAMS, name="unpack"
        )(shared, exchange(whole, FAR))

    return per_device


def gathered_kernel(outer, inner, mask_ref, q_ref, kv_ref, out_ref, scores_ref):
    i = pl.program_id(0)
    block = out_ref.shape[0] * out_ref.shape[1] * out_ref.shape[2]
    tiles = block // TILE
    q_tile = (i * inner + lax.axis_index("inner")) * tiles
    mixed = attend(
        q_ref[0, :, 0].reshape(block, HDIM),
        TILE,
        lambda c: kv_ref[lax.rem(c, inner), lax.div(c, inner), :, 1].reshape(block, HDIM),
        lambda c: kv_ref[lax.rem(c, inner), lax.div(c, inner), :, 2].reshape(block, HDIM),
        outer * inner,
        lambda a, t: mask_ref[q_tile + a, t] != 0,
        scores_ref,
    )
    out_ref[...] = mixed.reshape(out_ref.shape)


def gathered(outer, inner, n_head, near):
    width = HEADS // near * HDIM

    def per_device(query_rows, key_rows, value_rows, q_gain, k_gain, tile_mask):
        rows, features = query_rows.shape
        block = rows * n_head

        def store(which, at, block, kept):
            for d in range(near):
                kept[0][d, which, at] = block[:, d * width : (d + 1) * width]

        def send(which, outs, kept):
            packed, sems = kept
            copy = pltpu.make_async_copy(packed.at[:, which], outs[0].at[:, which], sems.at[which])
            copy.start()
            return [copy]

        def read(got_ref, out_ref):
            for d in range(near):
                out_ref[:, d * width : (d + 1) * width] = got_ref[d]

        (packed,) = pack(
            store,
            send,
            [shape(near, 3, rows, width)],
            rows,
            features,
            (query_rows, key_rows, value_rows, q_gain, k_gain),
            [pltpu.VMEM((near, 3, rows, width), BF16), pltpu.SemaphoreType.DMA((3,))],
        )
        own = exchange(packed, NEAR).reshape(outer, n_head, 3, rows, width)
        every = lax.all_gather(own, "inner")
        mixed = pl.pallas_call(
            functools.partial(gathered_kernel, outer, inner),
            grid=(outer, HEADS // near),
            in_specs=[
                pl.BlockSpec(memory_space=pltpu.SMEM),
                pl.BlockSpec((1, n_head, 1, rows, HDIM), lambda i, h: (i, 0, 0, 0, h)),
                pl.BlockSpec((inner, outer, n_head, 3, rows, HDIM), lambda i, h: (0, 0, 0, 0, 0, h)),
            ],
            out_specs=pl.BlockSpec((1, n_head, rows, HDIM), lambda i, h: (i, 0, 0, h)),
            out_shape=shape(outer, n_head, rows, width),
            scratch_shapes=[pltpu.VMEM((outer * inner, block, block), jnp.float32)],
            compiler_params=PARAMS,
            name="attend",
        )(tile_mask, own, every)
        return pl.pallas_call(
            read, out_shape=shape(rows, features), compiler_params=PARAMS, name="unpack"
        )(exchange(mixed.reshape(near, rows, width), NEAR))

    return per_device


def solution(mesh):
    n_blk, n_head = mesh.shape["blk"], mesh.shape["head"]
    outer = max(d for d in range(1, n_blk + 1) if n_blk % d == 0 and HEADS % (n_head * d) == 0)
    inner = n_blk // outer
    near, far = outer * n_head, n_blk * n_head

    def per_device(query_rows, *others):
        in_pairs = inner == 2 and n_head == 2 and mesh.shape["batch"] == 2 and near & (near - 1) == 0
        if in_pairs and HEADS == near + far and query_rows.shape[0] == TILE:
            return halved(far, near)(query_rows, *others)
        return gathered(outer, inner, n_head, near)(query_rows, *others)

    split = P(("batch", "outer", "inner", "head"), None)
    return jax.shard_map(
        per_device,
        mesh=Mesh(
            mesh.devices.reshape(outer, inner, n_head, mesh.shape["batch"]), ("outer", "inner", "head", "batch")
        ),
        in_specs=(split, split, split, P(), P(), P()),
        out_specs=split,
        check_vma=False,
    )
```

```python
import functools

import jax
import jax.numpy as jnp
from jax import lax
from jax.experimental import pallas as pl
from jax.experimental.pallas import tpu as pltpu
from jax.sharding import Mesh, PartitionSpec as P

HEADS = 24
HDIM = 128
TILE = 128
EPS = 1e-06
MASKED = -1e30
NEAR = ("outer", "head")
FAR = ("outer", "inner", "head")
PARAMS = pltpu.CompilerParams(vmem_limit_bytes=48 * 1024 * 1024)
PACK_PARAMS = pltpu.CompilerParams(vmem_limit_bytes=61 * 1024 * 1024)
BF16 = jnp.bfloat16
SHARED_COST = 24 * 2**30
SCALE = 1.4426950408889634 * HDIM ** (-0.5)


def shape(*dims):
    return jax.ShapeDtypeStruct(dims, BF16)


def exchange(x, axes):
    return lax.all_to_all(x, axes, split_axis=0, concat_axis=0, tiled=True)


def pack_kernel(store, send, inputs, outputs, scratch):
    q_hbm, k_hbm, v_hbm, qg_hbm, kg_hbm = inputs
    q_in, k_in, v_in, qg, kg, sems, *kept = scratch
    copies = [
        pltpu.make_async_copy(src, dst, sems.at[n])
        for n, (src, dst) in enumerate(
            ((v_hbm, v_in), (q_hbm, q_in), (qg_hbm, qg), (k_hbm, k_in), (kg_hbm, kg))
        )
    ]
    for copy in copies:
        copy.start()

    group = 16

    def normalize(block, gain):
        widened = block.astype(jnp.float32)
        mean_square = jnp.mean(widened * widened, axis=-1, keepdims=True)
        return (widened * lax.rsqrt(mean_square + EPS) * gain[...]).astype(BF16)

    sent = []
    for first, which, ref, gain in ((0, 2, v_in, None), (1, 0, q_in, qg), (3, 1, k_in, kg)):
        copies[first].wait()
        if gain is not None:
            copies[first + 1].wait()
        for row in range(0, ref.shape[0], group):
            at = slice(row, row + group)
            store(which, at, ref[at] if gain is None else normalize(ref[at], gain), kept)
        sent += send(which, outputs, kept)
    for copy in sent:
        copy.wait()


def pack(store, send, out_shape, rows, features, arrays, kept=()):
    q, k, v, q_gain, k_gain = arrays
    hbm = pl.BlockSpec(memory_space=pltpu.HBM)

    def kernel(*refs):
        pack_kernel(store, send, refs[:5], refs[5 : 5 + len(out_shape)], refs[5 + len(out_shape) :])

    return pl.pallas_call(
        kernel,
        in_specs=[hbm] * 5,
        out_specs=[hbm] * len(out_shape),
        out_shape=out_shape,
        scratch_shapes=[pltpu.VMEM((rows, features), BF16)] * 3
        + [pltpu.VMEM((1, features), jnp.float32)] * 2
        + [pltpu.SemaphoreType.DMA((5,)), *kept],
        compiler_params=PACK_PARAMS,
        name="pack",
    )(q, k, v, q_gain.reshape(1, -1), k_gain.reshape(1, -1))


def first_pass(query, key, bias_at, scores_ref, c, largest):
    s = lax.dot_general(key, query, (((1,), (1,)), ((), ())), preferred_element_type=jnp.float32)
    scores_ref[c] = s
    for t in range(key.shape[0] // TILE):
        tile = s[t * TILE : (t + 1) * TILE].reshape(TILE // 8, 8, -1)
        largest = jnp.maximum(largest, jnp.max(tile, axis=0) + bias_at(t))
    return largest


def second_pass(scores_ref, c, col_max, bias_at, value_t, state):
    total, mixed = state
    wide, bm = scores_ref.shape[1:]
    weights = []
    for t in range(wide // TILE):
        tile = scores_ref[c, t * TILE : (t + 1) * TILE].reshape(TILE // 8, 8, bm)
        tile = jnp.exp2(tile * SCALE - (col_max - bias_at(t))[None])
        total = total + jnp.sum(tile, axis=0)
        weights.append(tile.reshape(TILE, bm).astype(BF16))
    weights = jnp.concatenate(weights, axis=0)
    return total, mixed + jnp.dot(value_t, weights, preferred_element_type=jnp.float32)


def over_all(largest):
    return jnp.broadcast_to(jnp.max(largest, axis=0, keepdims=True) * SCALE, largest.shape)


def divide(total, mixed):
    return (mixed / jnp.sum(total, axis=0, keepdims=True)).T.astype(BF16)


def bias_of(band, bm, live_at):
    lane = lax.broadcasted_iota(jnp.int32, (8, bm), 1)
    bias = jnp.zeros((8, bm), jnp.float32)
    for a in range(bm // band):
        dead = jnp.where(live_at(a), 0.0, MASKED).astype(jnp.float32)
        bias = jnp.where((lane >= a * band) & (lane < (a + 1) * band), dead, bias)
    return bias


def attend(query, band, key_at, value_at, key_blocks, live_at, scores_ref):
    wide, bm = scores_ref.shape[1:]

    def bias_at(c):
        return lambda t: bias_of(band, bm, lambda a: live_at(a, c * (wide // TILE) + t))

    def score(c, largest):
        return first_pass(query, key_at(c), bias_at(c), scores_ref, c, largest)

    largest = lax.fori_loop(0, key_blocks, score, jnp.full((8, bm), MASKED, jnp.float32))
    col_max = over_all(largest)

    def mix(c, state):
        return second_pass(scores_ref, c, col_max, bias_at(c), transposed(value_at(c)), state)

    state = jnp.zeros((8, bm), jnp.float32), jnp.zeros((HDIM, bm), jnp.float32)
    return divide(*lax.fori_loop(0, key_blocks, mix, state))


def transposed(block):
    return block.astype(jnp.float32).T.astype(BF16)


def attend_blocks(blocks, band, query_at, key_at, value_t, key_blocks, live_at, finish, scores):
    wide, bm = scores[0].shape[1:]
    empty = jnp.full((8, bm), MASKED, jnp.float32)
    nothing = jnp.zeros((8, bm), jnp.float32), jnp.zeros((HDIM, bm), jnp.float32)

    def bias_at(i, c):
        return lambda t: bias_of(band, bm, lambda a: live_at(i, a, c, t))

    def both(i, col_max, now, following):
        later = jnp.minimum(i + 1, blocks - 1)
        query = query_at(later)
        largest, state = empty, nothing
        for c in range(key_blocks):
            largest = first_pass(query, key_at(c), bias_at(later, c), following, c, largest)
            state = second_pass(now, c, col_max, bias_at(i, c), value_t[:, c * wide : (c + 1) * wide], state)
        finish(i, divide(*state))
        return over_all(largest)

    largest = empty
    query = query_at(0)
    for c in range(key_blocks):
        largest = first_pass(query, key_at(c), bias_at(0, c), scores[0], c, largest)

    def pair(n, col_max):
        col_max = both(2 * n, col_max, scores[0], scores[1])
        return both(2 * n + 1, col_max, scores[1], scores[0])

    lax.fori_loop(0, blocks // 2, pair, over_all(largest))


def partner(me, step):
    first, second = step
    return me ^ jnp.where(lax.axis_index("batch") == 0, first, second)


def collect_kernel(steps, rows, *refs):
    pieces, (q_out, kv_out) = refs[:-2], refs[-2:]
    me = lax.axis_index(NEAR)
    for step, piece in zip(steps, pieces):
        at = pl.ds(pl.multiple_of(partner(me, step) * rows, rows), rows)
        q_out[at] = piece[0]
        kv_out[:, at] = piece[1:]


def shared_kernel(mask_ref, q_ref, own_ref, other_ref, out_ref, value_t, *scores):
    mine = lax.axis_index("inner")
    _, wide, bm = scores[0].shape
    blocks = q_ref.shape[0] // wide

    def key_at(c):
        ref = own_ref if c < blocks else other_ref
        return ref[0, c % blocks * wide : (c % blocks + 1) * wide]

    for n, ref in enumerate((own_ref, other_ref)):
        for t in range(blocks * wide // TILE):
            at = (n * blocks * wide) + t * TILE
            value_t[:, at : at + TILE] = transposed(ref[1, t * TILE : (t + 1) * TILE])

    def tile(block, inner, t):
        return (block * 2 + inner) * (wide // TILE) + t

    def finish(i, mixed):
        out_ref[pl.ds(pl.multiple_of(i * bm, bm), bm)] = mixed

    attend_blocks(
        blocks,
        TILE,
        lambda i: q_ref[pl.ds(pl.multiple_of(i * bm, bm), bm)],
        key_at,
        value_t,
        2 * blocks,
        lambda i, a, c, t: mask_ref[tile(i, mine, a), tile(c % blocks, mine if c < blocks else 1 - mine, t)] != 0,
        finish,
        scores,
    )


def whole_kernel(sources, mask_ref, qkv_ref, *refs):
    out_ref, value_t, *scores = refs[-4:]
    rows = qkv_ref.shape[2]
    _, wide, bm = scores[0].shape
    bands, tiles = bm // rows, wide // TILE
    for t in range(sources):
        value_t[:, t * TILE : (t + 1) * TILE] = transposed(qkv_ref[t, 2])

    def finish(i, mixed):
        out_ref[pl.ds(i * bands, bands)] = mixed.reshape(bands, rows, HDIM)

    attend_blocks(
        sources // bands,
        rows,
        lambda i: qkv_ref[pl.ds(i * bands, bands), 0].reshape(bm, HDIM),
        lambda c: qkv_ref[c * tiles : (c + 1) * tiles, 1].reshape(wide, HDIM),
        value_t,
        sources // tiles,
        lambda i, a, c, t: mask_ref[i * bands + a, c * tiles + t] != 0,
        finish,
        scores,
    )


def halved(far, near):
    steps = []
    for d in (*range(near // 4, near // 2), *reversed(range(near // 4))):
        steps += [(d, near // 2 + d), (near // 2 + d, d)]

    def swap(piece, step):
        pairs = [(2 * i + b, 2 * (i ^ step[b]) + b) for i in range(near) for b in range(2)]
        return lax.ppermute(piece, (*NEAR, "batch"), pairs)

    def per_device(query_rows, key_rows, value_rows, q_gain, k_gain, tile_mask):
        rows, features = query_rows.shape

        def store(which, at, block, kept):
            near_heads, far_heads = kept[:2]
            for h in range(near):
                near_heads[h, which, at] = block[:, h * HDIM : (h + 1) * HDIM]
            for h in range(far):
                far_heads[h, which, at] = block[:, (near + h) * HDIM : (near + h + 1) * HDIM]

        def send(which, outs, kept):
            near_heads, far_heads, near_sems, far_sems = kept
            me = lax.axis_index(NEAR)
            copies = [
                pltpu.make_async_copy(near_heads.at[partner(me, step), which], outs[n].at[which], near_sems.at[which, n])
                for n, step in enumerate(steps)
            ]
            copies.append(pltpu.make_async_copy(far_heads.at[:, which], outs[-1].at[:, which], far_sems.at[which]))
            for copy in copies:
                copy.start()
            return copies

        def read(shared, whole, out_ref):
            for d in range(near):
                out_ref[:, d * HDIM : (d + 1) * HDIM] = shared[d]
            for d in range(far):
                out_ref[:, (near + d) * HDIM : (near + d + 1) * HDIM] = whole[d]

        *shared, whole = pack(
            store,
            send,
            [shape(3, rows, HDIM)] * near + [shape(far, 3, rows, HDIM)],
            rows,
            features,
            (query_rows, key_rows, value_rows, q_gain, k_gain),
            [
                pltpu.VMEM((near, 3, rows, HDIM), BF16),
                pltpu.VMEM((far, 3, rows, HDIM), BF16),
                pltpu.SemaphoreType.DMA((3, near)),
                pltpu.SemaphoreType.DMA((3,)),
            ],
        )
        shared = [swap(piece, step) for step, piece in zip(steps, shared)]
        whole = exchange(whole, FAR)
        q_near, kv_near = pl.pallas_call(
            functools.partial(collect_kernel, steps, rows),
            out_shape=[shape(near * rows, HDIM), shape(2, near * rows, HDIM)],
            compiler_params=PARAMS,
            name="collect",
        )(*shared)
        kv_other = lax.ppermute(kv_near, "inner", [(0, 1), (1, 0)])

        wide = 2 * TILE
        blocks = far * rows // wide
        smem, vmem = pl.BlockSpec(memory_space=pltpu.SMEM), pl.BlockSpec(memory_space=pltpu.VMEM)
        scratch = [pltpu.VMEM((HDIM, far * rows), BF16)]
        scores = [pltpu.VMEM((blocks, wide, wide), jnp.float32)] * 2
        shared = pl.pallas_call(
            shared_kernel,
            in_specs=[smem] + [vmem] * 3,
            out_shape=shape(near * rows, HDIM),
            scratch_shapes=scratch + scores,
            compiler_params=PARAMS,
            cost_estimate=pl.CostEstimate(flops=SHARED_COST, bytes_accessed=2**21, transcendentals=0),
            name="attend_shared",
        )(tile_mask, q_near, kv_near, kv_other)

        whole = pl.pallas_call(
            functools.partial(whole_kernel, far),
            in_specs=[smem, vmem, pl.BlockSpec(memory_space=pl.ANY)],
            out_shape=shape(far, rows, HDIM),
            scratch_shapes=scratch + [pltpu.VMEM((blocks // 2, 2 * wide, wide), jnp.float32)] * 2,
            compiler_params=PARAMS,
            cost_estimate=pl.CostEstimate(flops=2**33, bytes_accessed=2**22, transcendentals=0),
            name="attend_whole",
        )(tile_mask, whole, shared)
        shared = exchange(shared.reshape(near, rows, HDIM), NEAR)
        return pl.pallas_call(
            read, out_shape=shape(rows, features), compiler_params=PARAMS, name="unpack"
        )(shared, exchange(whole, FAR))

    return per_device


def gathered_kernel(outer, inner, mask_ref, q_ref, kv_ref, out_ref, scores_ref):
    i = pl.program_id(0)
    block = out_ref.shape[0] * out_ref.shape[1] * out_ref.shape[2]
    tiles = block // TILE
    q_tile = (i * inner + lax.axis_index("inner")) * tiles
    mixed = attend(
        q_ref[0, :, 0].reshape(block, HDIM),
        TILE,
        lambda c: kv_ref[lax.rem(c, inner), lax.div(c, inner), :, 1].reshape(block, HDIM),
        lambda c: kv_ref[lax.rem(c, inner), lax.div(c, inner), :, 2].reshape(block, HDIM),
        outer * inner,
        lambda a, t: mask_ref[q_tile + a, t] != 0,
        scores_ref,
    )
    out_ref[...] = mixed.reshape(out_ref.shape)


def gathered(outer, inner, n_head, near):
    width = HEADS // near * HDIM

    def per_device(query_rows, key_rows, value_rows, q_gain, k_gain, tile_mask):
        rows, features = query_rows.shape
        block = rows * n_head

        def store(which, at, block, kept):
            for d in range(near):
                kept[0][d, which, at] = block[:, d * width : (d + 1) * width]

        def send(which, outs, kept):
            packed, sems = kept
            copy = pltpu.make_async_copy(packed.at[:, which], outs[0].at[:, which], sems.at[which])
            copy.start()
            return [copy]

        def read(got_ref, out_ref):
            for d in range(near):
                out_ref[:, d * width : (d + 1) * width] = got_ref[d]

        (packed,) = pack(
            store,
            send,
            [shape(near, 3, rows, width)],
            rows,
            features,
            (query_rows, key_rows, value_rows, q_gain, k_gain),
            [pltpu.VMEM((near, 3, rows, width), BF16), pltpu.SemaphoreType.DMA((3,))],
        )
        own = exchange(packed, NEAR).reshape(outer, n_head, 3, rows, width)
        every = lax.all_gather(own, "inner")
        mixed = pl.pallas_call(
            functools.partial(gathered_kernel, outer, inner),
            grid=(outer, HEADS // near),
            in_specs=[
                pl.BlockSpec(memory_space=pltpu.SMEM),
                pl.BlockSpec((1, n_head, 1, rows, HDIM), lambda i, h: (i, 0, 0, 0, h)),
                pl.BlockSpec((inner, outer, n_head, 3, rows, HDIM), lambda i, h: (0, 0, 0, 0, 0, h)),
            ],
            out_specs=pl.BlockSpec((1, n_head, rows, HDIM), lambda i, h: (i, 0, 0, h)),
            out_shape=shape(outer, n_head, rows, width),
            scratch_shapes=[pltpu.VMEM((outer * inner, block, block), jnp.float32)],
            compiler_params=PARAMS,
            name="attend",
        )(tile_mask, own, every)
        return pl.pallas_call(
            read, out_shape=shape(rows, features), compiler_params=PARAMS, name="unpack"
        )(exchange(mixed.reshape(near, rows, width), NEAR))

    return per_device


def solution(mesh):
    n_blk, n_head = mesh.shape["blk"], mesh.shape["head"]
    outer = max(d for d in range(1, n_blk + 1) if n_blk % d == 0 and HEADS % (n_head * d) == 0)
    inner = n_blk // outer
    near, far = outer * n_head, n_blk * n_head

    def per_device(query_rows, *others):
        in_pairs = inner == 2 and n_head == 2 and mesh.shape["batch"] == 2 and near & (near - 1) == 0
        if in_pairs and HEADS == near + far and query_rows.shape[0] == TILE:
            return halved(far, near)(query_rows, *others)
        return gathered(outer, inner, n_head, near)(query_rows, *others)

    split = P(("batch", "outer", "inner", "head"), None)
    return jax.shard_map(
        per_device,
        mesh=Mesh(
            mesh.devices.reshape(outer, inner, n_head, mesh.shape["batch"]), ("outer", "inner", "head", "batch")
        ),
        in_specs=(split, split, split, P(), P(), P()),
        out_specs=split,
        check_vma=False,
    )
```
